32 devices in a mesh: shard: 2 (over y), ctx: 8 (over z, x), tp: 2 (over core).
Axes of the slice: x: 2, y: 2, z: 4, core: 2. Of those that a mesh axis runs over, the one named last changes fastest.
Arguments:
- tokens: bfloat16 [8192, 1024], P(('shard', 'ctx')), may hold values from -6 to 6
- cotangent: bfloat16 [8192, 1024], P(('shard', 'ctx')), may hold values from -6 to 6
- seq_lengths: int32 [2, 4], P('shard'), may hold values from 512 to 2048, as said below
- part_order: int32 [8, 2], replicated, may hold values from 0 to 15, as said below
- w_query: bfloat16 [1024, 2048], P('shard', 'tp'), may hold values from -0.1875 to 0.1875
- key_weight: bfloat16 [1024, 1024], P('shard', 'tp'), may hold values from -0.1875 to 0.1875
- value_weight: bfloat16 [1024, 1024], P('shard', 'tp'), may hold values from -0.1875 to 0.1875
- w_out: bfloat16 [2048, 1024], P('tp', 'shard'), may hold values from -1.5 to 1.5
- w_gate: bfloat16 [1024, 3072], P('shard', 'tp'), may hold values from -0.1875 to 0.1875
- w_up: bfloat16 [1024, 3072], P('shard', 'tp'), may hold values from -0.1875 to 0.1875
- w_down: bfloat16 [3072, 1024], P('tp', 'shard'), may hold values from -0.109375 to 0.109375
- gain_in: bfloat16 [1024], P('shard'), may hold values from 0.25 to 1.75
- gain_post: bfloat16 [1024], P('shard'), may hold values from 0.25 to 1.75
- gain_q: bfloat16 [128], P('shard'), may hold values from 0.25 to 1.75
- gain_k: bfloat16 [128], P('shard'), may hold values from 0.25 to 1.75
Outputs:
- mixed: bfloat16 [8192, 1024], P(('shard', 'ctx'))
- input_grad: float32 [8192, 1024], P(('shard', 'ctx'))
- grad_query: float32 [1024, 2048], P('shard', 'tp')
- grad_key: float32 [1024, 1024], P('shard', 'tp')
- grad_value: float32 [1024, 1024], P('shard', 'tp')
- grad_out: float32 [2048, 1024], P('tp', 'shard')
- grad_gate: float32 [1024, 3072], P('shard', 'tp')
- grad_up: float32 [1024, 3072], P('shard', 'tp')
- grad_down: float32 [3072, 1024], P('tp', 'shard')
- grad_gain_in: float32 [1024], P('shard')
- grad_gain_post: float32 [1024], P('shard')
- grad_gain_q: float32 [128], P('shard')
- grad_gain_k: float32 [128], P('shard')
The draws below stay inside these ranges and needn't reach their ends.
Inputs may be any that keep to these rules, and one draw needn't show every extreme that they name: `seq_lengths`: in each row the 4 lengths add up to 4096; one is 2048 and stands first or last, one is exactly 512, and the other two add up to 1536 with neither under 4096 // 8. Row c names the parts of 256 packed places that device c of ctx holds, in the order of its rows: part_order[c, 0] takes each value of 0 to 7 once over the rows, and part_order[c, 1] = 15 - part_order[c, 0].
All inputs are finite; a program needn't handle non-finite values.
Results may differ from the reference program's by a relative error of at most 0.024.
Values may be sent and summed in bfloat16 or wider, within the bound.
No kernel may reach another device: no remote copies, remote signals or barrier semaphores. Data moves between devices by JAX's collectives and lax.ppermute only.
A program may use at most 128 MiB of HBM per device.

```python
import jax
import jax.numpy as jnp
from jax import lax

MODEL_WIDTH = 1024
QUERY_HEADS = 16
KEY_VALUE_HEADS = 8
HEAD_WIDTH = 128
FF = 3072
TOK_DEV = 512
SEQS = 4
HALF_ROWS = 256
GROUP = 4096
TOKENS = 8192
N_SHARD = 2
N_CTX = 8


def draw_seq_lengths(key, part):
    key = jax.random.fold_in(key, 11)

    def one_row(row_key):
        row_keys = jax.random.split(row_key, 3)
        spread_extra = jax.random.randint(row_keys[0], (), 0, GROUP // 8 + 1, dtype=jnp.int32)
        shorter = jnp.stack([jnp.int32(GROUP // 8) + 0 * spread_extra, GROUP // 8 + spread_extra, GROUP // 4 - spread_extra]).astype(jnp.int32)
        shorter = shorter[jax.random.permutation(row_keys[1], 3)]
        longest = jnp.full((1,), GROUP // 2, dtype=jnp.int32)
        long_first = jax.random.randint(row_keys[2], (), 0, 2, dtype=jnp.int32)
        return jnp.where(long_first == 1, jnp.concatenate([longest, shorter]), jnp.concatenate([shorter, longest]))
    return jax.vmap(one_row)(jax.random.split(key, N_SHARD)).astype(jnp.int32)


def draw_part_order(key, part):
    key = jax.random.fold_in(key, 23)
    early = jax.random.permutation(key, N_CTX).astype(jnp.int32)
    return jnp.stack([early, 2 * N_CTX - 1 - early], axis=1).astype(jnp.int32)


def steps_of(stream_key, shape, shards, least, top_value):
    level = 1.0
    for axis_at, parts in shards:
        steps = jax.random.uniform(jax.random.fold_in(jax.random.fold_in(stream_key, 6), axis_at), (parts,), jnp.float32, least / len(shards), top_value / len(shards))
        level = level * jnp.repeat(jnp.exp(steps), shape[axis_at] // parts).reshape((-1,) + (1,) * (len(shape) - 1 - axis_at))
    return level


def centred(rng, extent, width, reach, cuts=(), held_as=jnp.bfloat16):
    factor_of = steps_of(rng, extent, cuts, -0.22, 0.18) if cuts else 1.0
    entries = jax.random.normal(rng, extent, jnp.float32) * width * factor_of
    return jnp.minimum(jnp.maximum(entries, -reach), reach).astype(held_as)


def setup_inputs(seed: int = 0) -> dict:
    keys = jax.random.split(jax.random.key(seed), 16)
    tokens = centred(keys[0], (TOKENS, MODEL_WIDTH), 1.0, 6.0, ((0, 16),))
    cotangent = centred(keys[1], (TOKENS, MODEL_WIDTH), 1.0, 6.0, ((0, 16),))
    seq_lengths = draw_seq_lengths(jax.random.fold_in(keys[15], 71), 0)
    part_order = draw_part_order(jax.random.fold_in(keys[15], 71), 0)
    w_query = centred(keys[4], (MODEL_WIDTH, QUERY_HEADS * HEAD_WIDTH), MODEL_WIDTH ** -0.5, 0.1875, ((0, 2), (1, 2)))
    key_weight = centred(keys[5], (MODEL_WIDTH, KEY_VALUE_HEADS * HEAD_WIDTH), MODEL_WIDTH ** -0.5, 0.1875, ((0, 2), (1, 2)))
    value_weight = centred(keys[6], (MODEL_WIDTH, KEY_VALUE_HEADS * HEAD_WIDTH), MODEL_WIDTH ** -0.5, 0.1875, ((0, 2), (1, 2)))
    w_out = centred(keys[7], (QUERY_HEADS * HEAD_WIDTH, MODEL_WIDTH), (QUERY_HEADS * HEAD_WIDTH // 128) ** -0.5, 1.5, ((0, 2), (1, 2)))
    w_gate = centred(keys[8], (MODEL_WIDTH, FF), MODEL_WIDTH ** -0.5, 0.1875, ((0, 2), (1, 2)))
    w_up = centred(keys[9], (MODEL_WIDTH, FF), MODEL_WIDTH ** -0.5, 0.1875, ((0, 2), (1, 2)))
    w_down = centred(keys[10], (FF, MODEL_WIDTH), FF ** -0.5, 0.109375, ((0, 2), (1, 2)))
    gain_in = jnp.clip(1.0 + 0.15 * jax.random.normal(keys[11], (MODEL_WIDTH,), jnp.float32), 0.25, 1.75).astype(jnp.bfloat16)
    gain_post = jnp.clip(1.0 + 0.15 * jax.random.normal(keys[12], (MODEL_WIDTH,), jnp.float32), 0.25, 1.75).astype(jnp.bfloat16)
    gain_q = jnp.clip(1.0 + 0.15 * jax.random.normal(keys[13], (HEAD_WIDTH,), jnp.float32), 0.25, 1.75).astype(jnp.bfloat16)
    gain_k = jnp.clip(1.0 + 0.15 * jax.random.normal(keys[14], (HEAD_WIDTH,), jnp.float32), 0.25, 1.75).astype(jnp.bfloat16)
    return {"tokens": tokens, "cotangent": cotangent, "seq_lengths": seq_lengths, "part_order": part_order, "w_query": w_query, "key_weight": key_weight, "value_weight": value_weight, "w_out": w_out, "w_gate": w_gate, "w_up": w_up, "w_down": w_down, "gain_in": gain_in, "gain_post": gain_post, "gain_q": gain_q, "gain_k": gain_k}


EPS = 1e-06
THETA = 1000000.0
HIGH = lax.Precision.HIGHEST
MASKED = -1e+30

@jax.custom_vjp
def low_precision(v):
    return lax.optimization_barrier(v.astype(jnp.bfloat16)).astype(jnp.float32)

@jax.custom_vjp
def low_precision_back(v):
    return v

def low_keep(v):
    return (low_precision(v), None)

def low_pass(kept, grad):
    return (grad,)

def back_keep(v):
    return (v, None)

def back_low(kept, grad):
    return (low_precision(grad),)
low_precision.defvjp(low_keep, low_pass)
low_precision_back.defvjp(back_keep, back_low)

def matrix_product(left, right):
    return jnp.dot(left, right, precision=HIGH)

def rms_gain(values, gain):
    return values * lax.rsqrt(lax.optimization_barrier(jnp.mean(values * values, axis=-1, keepdims=True)) + EPS) * gain

def rotate(values, cosine, sine_table):
    middle = values.shape[-1] // 2
    turned = jnp.concatenate([-values[..., middle:], values[..., :middle]], axis=-1)
    return values * cosine + turned * sine_table

def layout(lengths, part_order):
    row_ids = jnp.arange(GROUP, dtype=jnp.int32)
    device = row_ids // TOK_DEV
    second = row_ids % TOK_DEV // HALF_ROWS
    part_id = part_order[device, second].astype(jnp.int32)
    place_id = part_id * HALF_ROWS + row_ids % HALF_ROWS
    starts = (jnp.cumsum(lengths) - lengths).astype(jnp.int32)
    member = lax.optimization_barrier(jnp.sum((place_id[:, None] >= starts[None, 1:]).astype(jnp.int32), axis=1))
    matches = member[:, None] == jnp.arange(SEQS, dtype=jnp.int32)[None, :]
    doc_begin = lax.optimization_barrier(jnp.sum(jnp.where(matches, starts[None, :], 0), axis=1)).astype(jnp.int32)
    return (place_id, member, place_id - doc_begin)

def forward(params, inputs, place_id, member, in_doc):
    w_query, key_weight, value_weight, w_out, w_gate, w_up, w_down, gain_in, gain_post, gain_q, gain_k = params
    token_rows = inputs.shape[0]
    normed_input = low_precision(rms_gain(inputs, gain_in))
    queries = low_precision_back(matrix_product(normed_input, w_query)).reshape(token_rows, QUERY_HEADS, HEAD_WIDTH)
    key_row_block = low_precision_back(matrix_product(normed_input, key_weight)).reshape(token_rows, KEY_VALUE_HEADS, HEAD_WIDTH)
    value_row_block = low_precision(low_precision_back(matrix_product(normed_input, value_weight))).reshape(token_rows, KEY_VALUE_HEADS, HEAD_WIDTH)
    frequency = THETA ** (-jnp.arange(0, HEAD_WIDTH, 2, dtype=jnp.float32) / HEAD_WIDTH)
    angles = in_doc.astype(jnp.float32)[:, None] * frequency[None, :]
    cosine = jnp.concatenate([jnp.cos(angles), jnp.cos(angles)], axis=-1)[:, None, :]
    sine_table = jnp.concatenate([jnp.sin(angles), jnp.sin(angles)], axis=-1)[:, None, :]
    queries = low_precision(rotate(rms_gain(queries, gain_q), cosine, sine_table))
    key_row_block = low_precision(rotate(rms_gain(key_row_block, gain_k), cosine, sine_table))
    key_expanded = jnp.repeat(key_row_block, QUERY_HEADS // KEY_VALUE_HEADS, axis=1)
    value_expanded = jnp.repeat(value_row_block, QUERY_HEADS // KEY_VALUE_HEADS, axis=1)
    block_rows = min(512, token_rows)
    score_scale = HEAD_WIDTH ** (-0.5)

    def attend(block_args):
        q_block, place_block, member_block = block_args
        scores = low_precision_back(jnp.einsum('qhd,khd->hqk', q_block, key_expanded, precision=HIGH) * score_scale)
        visible = (member_block[:, None] == member[None, :]) & (place_id[None, :] <= place_block[:, None])
        scores = jnp.where(visible[None], scores, MASKED)
        highest = lax.optimization_barrier(jnp.max(scores, axis=-1, keepdims=True))
        weights = jnp.exp(scores - highest)
        weights = low_precision(weights / lax.optimization_barrier(jnp.sum(weights, axis=-1, keepdims=True)))
        return jnp.einsum('hqk,khd->qhd', weights, value_expanded, precision=HIGH)
    blocks = (queries.reshape(token_rows // block_rows, block_rows, QUERY_HEADS, HEAD_WIDTH), place_id.reshape(token_rows // block_rows, block_rows), member.reshape(token_rows // block_rows, block_rows))
    attended = lax.map(jax.checkpoint(attend), blocks).reshape(token_rows, QUERY_HEADS * HEAD_WIDTH)
    attn_out = low_precision(low_precision_back(attended))
    residual = inputs + low_precision_back(matrix_product(attn_out, w_out))
    normed_two = low_precision(rms_gain(residual, gain_post))
    gate_act = low_precision_back(matrix_product(normed_two, w_gate))
    upward = low_precision_back(matrix_product(normed_two, w_up))
    hidden = low_precision(jax.nn.silu(gate_act) * upward)
    return residual + matrix_product(hidden, w_down)

def reference(tokens, cotangent, seq_lengths, part_order, w_query, key_weight, value_weight, w_out, w_gate, w_up, w_down, gain_in, gain_post, gain_q, gain_k):
    params = tuple((weight.astype(jnp.float32) for weight in (w_query, key_weight, value_weight, w_out, w_gate, w_up, w_down, gain_in, gain_post, gain_q, gain_k)))
    inputs = tokens.astype(jnp.float32).reshape(N_SHARD, GROUP, MODEL_WIDTH)
    upstream = cotangent.astype(jnp.float32).reshape(N_SHARD, GROUP, MODEL_WIDTH)

    def one_group(summed, group_args):
        group_inputs, group_upstream, lengths = group_args
        place_id, member, in_doc = layout(lengths, part_order)
        outputs, pullback = jax.vjp(lambda weights, values: forward(weights, values, place_id, member, in_doc), params, group_inputs)
        weight_grads, grad_inputs = pullback(group_upstream)
        return (jax.tree.map(jnp.add, summed, weight_grads), (outputs.astype(jnp.bfloat16), grad_inputs))
    summed, (outputs, grad_inputs) = lax.scan(one_group, jax.tree.map(jnp.zeros_like, params), (inputs, upstream, seq_lengths))
    return (outputs.reshape(TOKENS, MODEL_WIDTH), grad_inputs.reshape(TOKENS, MODEL_WIDTH), summed[0], summed[1], summed[2], summed[3], summed[4], summed[5], summed[6], summed[7], summed[8], summed[9], summed[10])
```

```python
import functools

import jax
import jax.numpy as jnp
from jax import lax
from jax.experimental import pallas as pl
from jax.experimental.pallas import tpu as pltpu
from jax.sharding import PartitionSpec as P

EPS = 1e-06
THETA = 1000000.0
LOG2E = 1.4426950408889634
HEAD = 128
BF16 = jnp.bfloat16
F32 = jnp.float32
VMEM_LIMIT = 48 * 1024 * 1024


def rms_parts(values):
    factor = lax.rsqrt(jnp.mean(values * values, axis=-1, keepdims=True) + EPS)
    return (values * factor, factor)


def rms_back(grad_hat, normal, factor):
    return factor * (grad_hat - normal * jnp.mean(grad_hat * normal, axis=-1, keepdims=True))


def dot(a, b):
    return jnp.dot(a, b, preferred_element_type=F32)


def dot_nt(a, b):
    return lax.dot_general(a, b, (((1,), (1,)), ((), ())), preferred_element_type=F32)


def dot_tn(a, b):
    return lax.dot_general(a, b, (((0,), (0,)), ((), ())), preferred_element_type=F32)


def after(value, *earlier):
    return lax.optimization_barrier((value,) + earlier)[0]


def pieces_of(own, axis):
    count = lax.axis_size(axis)
    return [own] + [
        lax.ppermute(own, axis, [((i + j) % count, i) for i in range(count)])
        for j in range(1, count)
    ]


def join(pieces, dim, index):
    count = len(pieces)
    if count == 1:
        return pieces[0]
    if count == 2:
        return jnp.where(
            index == 0, jnp.concatenate(pieces, dim), jnp.concatenate(pieces[::-1], dim)
        )
    size = pieces[0].shape[dim]
    shape = list(pieces[0].shape)
    shape[dim] = size * count
    whole = jnp.zeros(shape, pieces[0].dtype)
    for j, piece in enumerate(pieces):
        whole = lax.dynamic_update_slice_in_dim(whole, piece, (index + j) % count * size, dim)
    return whole


def pair_total(partial):
    count = lax.axis_size("tp")
    partial = partial.astype(BF16)
    if count != 2:
        return lax.psum(partial, "tp").astype(F32)
    other = lax.ppermute(partial, "tp", [(0, 1), (1, 0)])
    return partial.astype(F32) + other.astype(F32)


def to_shard_owner(grad, dim):
    count = lax.axis_size("shard")
    index = lax.axis_index("shard")
    if count != 2:
        return lax.psum_scatter(grad, "shard", scatter_dimension=dim, tiled=True).astype(F32)
    size = grad.shape[dim] // 2
    sent = lax.dynamic_slice_in_dim(grad, (1 - index) * size, size, dim)
    kept = lax.dynamic_slice_in_dim(grad, index * size, size, dim)
    other = lax.ppermute(sent, "shard", [(0, 1), (1, 0)])
    return kept.astype(F32) + other.astype(F32)


def ctx_total(value):
    count = lax.axis_size("ctx")
    index = lax.axis_index("ctx")
    levels = [1 << b for b in range(count.bit_length() - 1)]
    for level in levels:
        bit = (index // level) % 2
        size = value.shape[0] // 2
        sent = lax.dynamic_slice_in_dim(value, (1 - bit) * size, size, 0).astype(BF16)
        kept = lax.dynamic_slice_in_dim(value, bit * size, size, 0)
        other = lax.ppermute(sent, "ctx", [(i, i ^ level) for i in range(count)])
        value = kept + other.astype(F32)
    value = value.astype(BF16)
    for level in levels[::-1]:
        bit = (index // level) % 2
        other = lax.ppermute(value, "ctx", [(i, i ^ level) for i in range(count)])
        value = join([value, other], 0, bit)
    return value.astype(F32)


def rope_kernel(roped, pre_ref, cos_ref, sin_ref, gain_ref, out_ref):
    pre = pre_ref[...]

    @pl.when(pl.program_id(0) < roped)
    def _():
        factor = lax.rsqrt(jnp.mean(pre * pre, axis=-1, keepdims=True) + EPS)
        scaled = pre * factor * gain_ref[...]
        turned = pltpu.roll(scaled, HEAD // 2, 1)
        out_ref[...] = (scaled * cos_ref[...] + turned * sin_ref[...]).astype(BF16)

    @pl.when(pl.program_id(0) >= roped)
    def _():
        out_ref[...] = pre.astype(BF16)


def rope(pre, roped, cosine, sine, gain):
    rows, width = pre.shape
    column = pl.BlockSpec((rows, HEAD), lambda h: (0, h))
    table = pl.BlockSpec((rows, HEAD), lambda h: (0, 0))
    return pl.pallas_call(
        functools.partial(rope_kernel, roped),
        grid=(width // HEAD,),
        in_specs=[column, table, table, pl.BlockSpec((1, HEAD), lambda h: (0, 0))],
        out_specs=column,
        out_shape=jax.ShapeDtypeStruct((rows, width), BF16),
        compiler_params=pltpu.CompilerParams(vmem_limit_bytes=VMEM_LIMIT),
    )(pre, cosine, sine, gain)


def rope_back_kernel(grad_ref, pre_ref, cos_ref, sin_ref, gain_ref, out_ref, sum_ref):
    pre = pre_ref[...]
    grad = grad_ref[...]
    factor = lax.rsqrt(jnp.mean(pre * pre, axis=-1, keepdims=True) + EPS)
    hat = pre * factor
    back = grad * cos_ref[...] - pltpu.roll(grad, HEAD // 2, 1) * sin_ref[...]
    terms = jnp.sum(back * hat, axis=0, keepdims=True)

    @pl.when(pl.program_id(0) == 0)
    def _():
        sum_ref[...] = terms

    @pl.when(pl.program_id(0) > 0)
    def _():
        sum_ref[...] += terms

    back = back * gain_ref[...]
    inner = jnp.mean(back * hat, axis=-1, keepdims=True)
    out_ref[...] = (factor * (back - hat * inner)).astype(BF16)


def rope_back(grad, pre, cosine, sine, gain):
    rows, width = grad.shape
    column = pl.BlockSpec((rows, HEAD), lambda h: (0, h))
    table = pl.BlockSpec((rows, HEAD), lambda h: (0, 0))
    one_row = pl.BlockSpec((1, HEAD), lambda h: (0, 0))
    return pl.pallas_call(
        rope_back_kernel,
        grid=(width // HEAD,),
        in_specs=[column, column, table, table, one_row],
        out_specs=[column, one_row],
        out_shape=[
            jax.ShapeDtypeStruct((rows, width), BF16),
            jax.ShapeDtypeStruct((1, HEAD), F32),
        ],
        compiler_params=pltpu.CompilerParams(vmem_limit_bytes=VMEM_LIMIT),
    )(grad, pre, cosine, sine, gain)


def doc_begins(meta_ref, docs, place):
    begin = jnp.zeros_like(place)
    for i in range(1, docs):
        start = meta_ref[i]
        begin = jnp.where(place >= start, start, begin)
    return begin


def block_mask(meta_ref, docs, shape, half, q_part, k_part, diagonal):
    row = lax.broadcasted_iota(jnp.int32, (shape[0], 1), 0)
    q_place = q_part * half + jnp.where(row >= half, row - half, row)
    begin = doc_begins(meta_ref, docs, q_place) - k_part * half
    column = lax.broadcasted_iota(jnp.int32, shape, 1)
    visible = column >= begin
    if diagonal:
        visible = visible & (column <= q_place - k_part * half)
    return visible


def any_visible(meta_ref, docs, half, q_part, k_part):
    return (k_part + 1) * half > doc_begins(meta_ref, docs, q_part * half)


def two_heads(ref, start, half):
    rows = pl.ds(start, half)
    return jnp.concatenate([ref[rows, :HEAD], ref[rows, HEAD:]], axis=0)


def forward_kernel(docs, count, meta_ref, q_ref, k_ref, v_ref, *refs):
    others = refs[: 2 * (count - 1)]
    out_ref, out16_ref, lse_ref, acc_ref = refs[2 * (count - 1) :]
    half = q_ref.shape[0] // 2
    factor = HEAD**-0.5 * LOG2E
    ones = jnp.ones((half, HEAD), BF16)
    own = meta_ref[0]

    def block(start, keys, values, q_part, k_part, diagonal):
        scores = dot_nt(two_heads(q_ref, start, half), keys)
        visible = block_mask(meta_ref, docs, scores.shape, half, q_part, k_part, diagonal)
        weights = jnp.where(visible, jnp.exp2(scores * factor), 0.0).astype(BF16)
        return dot(weights, jnp.concatenate([values, ones], axis=1))

    for e in range(2):
        rows = pl.ds(e * half, half)
        part = own if e == 0 else 2 * count - 1 - own
        acc_ref[e] = block(e * half, k_ref[rows, :], v_ref[rows, :], part, part, True)
    for d in range(count - 1):
        side = meta_ref[docs + 2 * d]
        k_part = meta_ref[docs + 2 * d + 1]
        q_part = jnp.where(side == 0, own, 2 * count - 1 - own)

        @pl.when(any_visible(meta_ref, docs, half, q_part, k_part))
        def _():
            start = pl.multiple_of(side * half, half)
            acc_ref[side] += block(
                start, others[2 * d][...], others[2 * d + 1][...], q_part, k_part, False
            )

    for e in range(2):
        total = acc_ref[e]
        sums = total[:, HEAD:]
        result = total[:, :HEAD] / sums
        lse = jnp.log2(sums)
        for a in range(2):
            part = slice(a * half, (a + 1) * half)
            place = (pl.ds(e * half, half), slice(a * HEAD, (a + 1) * HEAD))
            out_ref[place] = result[part]
            out16_ref[place] = result[part].astype(BF16)
            lse_ref[place] = lse[part]


def backward_kernel(docs, count, meta_ref, q_ref, g_ref, o_ref, lse_ref, k_ref, v_ref, *refs):
    others = refs[: 2 * (count - 1)]
    dq_ref, dkv_ref = refs[2 * (count - 1) : 2 * count]
    given = refs[2 * count : 3 * count - 1]
    acc_ref, stats_ref, delta_ref = refs[3 * count - 1 :]
    half = q_ref.shape[0] // 2
    scale = HEAD**-0.5
    own = meta_ref[0]

    for e in range(2):
        grads = two_heads(g_ref, e * half, half).astype(F32)
        delta = jnp.sum(grads * two_heads(o_ref, e * half, half), axis=1, keepdims=True)
        delta_ref[e] = jnp.broadcast_to(delta, (2 * half, HEAD))
        stats_ref[e] = two_heads(lse_ref, e * half, half)

    def block(side, start, keys, values, q_part, k_part, diagonal):
        queries = two_heads(q_ref, start, half)
        grads = two_heads(g_ref, start, half)
        scores = dot_nt(queries, keys)
        repeat = half // HEAD
        lse = jnp.concatenate([stats_ref[side]] * repeat, axis=1)
        delta = jnp.concatenate([delta_ref[side]] * repeat, axis=1)
        visible = block_mask(meta_ref, docs, scores.shape, half, q_part, k_part, diagonal)
        weights = jnp.where(visible, jnp.exp2(scores * (scale * LOG2E) - lse), 0.0)
        d_weights = dot_nt(grads, values)
        d_scores = (weights * (d_weights - delta)).astype(BF16)
        d_values = dot_tn(weights.astype(BF16), grads)
        d_keys = dot_tn(d_scores, queries) * scale
        return dot(d_scores, keys) * scale, d_keys, d_values

    for e in range(2):
        rows = pl.ds(e * half, half)
        part = own if e == 0 else 2 * count - 1 - own
        d_queries, d_keys, d_values = block(
            e, e * half, k_ref[rows, :], v_ref[rows, :], part, part, True
        )
        acc_ref[e] = d_queries
        dkv_ref[0, rows, :] = d_keys
        dkv_ref[1, rows, :] = d_values
    for d in range(count - 1):
        side = meta_ref[docs + 2 * d]
        k_part = meta_ref[docs + 2 * d + 1]
        q_part = jnp.where(side == 0, own, 2 * count - 1 - own)
        seen = any_visible(meta_ref, docs, half, q_part, k_part)

        @pl.when(seen)
        def _():
            start = pl.multiple_of(side * half, half)
            d_queries, d_keys, d_values = block(
                side, start, others[2 * d][...], others[2 * d + 1][...], q_part, k_part, False
            )
            acc_ref[side] += d_queries
            given[d][0] = d_keys.astype(BF16)
            given[d][1] = d_values.astype(BF16)

        @pl.when(jnp.logical_not(seen))
        def _():
            given[d][...] = jnp.zeros_like(given[d])

    for e in range(2):
        for a in range(2):
            dq_ref[pl.ds(e * half, half), a * HEAD : (a + 1) * HEAD] = acc_ref[
                e, a * half : (a + 1) * half, :
            ]


def key_value_specs(rows, half, kv_heads, count):
    own = [
        pl.BlockSpec((rows, HEAD), lambda h, m: (0, h)),
        pl.BlockSpec((rows, HEAD), lambda h, m: (0, kv_heads + h)),
    ]
    other = [
        pl.BlockSpec((half, HEAD), lambda h, m: (0, h)),
        pl.BlockSpec((half, HEAD), lambda h, m: (0, kv_heads + h)),
    ]
    return own + other * (count - 1)


def twice(arrays):
    return [a for a in arrays for _ in range(2)]


def attend(meta, docs, queries, key_value, others):
    rows, width = queries.shape
    half = rows // 2
    count = len(others) + 1
    kv_heads = key_value.shape[1] // (2 * HEAD)
    column = pl.BlockSpec((rows, 2 * HEAD), lambda h, m: (0, h))
    return pl.pallas_call(
        functools.partial(forward_kernel, docs, count),
        grid_spec=pltpu.PrefetchScalarGridSpec(
            num_scalar_prefetch=1,
            grid=(kv_heads,),
            in_specs=[column] + key_value_specs(rows, half, kv_heads, count),
            out_specs=[column] * 3,
            scratch_shapes=[pltpu.VMEM((2, 2 * half, 2 * HEAD), F32)],
        ),
        out_shape=[
            jax.ShapeDtypeStruct((rows, width), F32),
            jax.ShapeDtypeStruct((rows, width), BF16),
            jax.ShapeDtypeStruct((rows, width), F32),
        ],
        compiler_params=pltpu.CompilerParams(vmem_limit_bytes=VMEM_LIMIT),
        cost_estimate=pl.CostEstimate(
            flops=(count + 1) * half * half * width * 4,
            bytes_accessed=rows * width * 16,
            transcendentals=(count + 1) * half * half * width // HEAD,
        ),
    )(meta, queries, key_value, key_value, *twice(others))


def attend_back(meta, docs, queries, grads, outs, lse, key_value, others):
    rows, width = queries.shape
    half = rows // 2
    count = len(others) + 1
    kv_width = key_value.shape[1] // 2
    kv_heads = kv_width // HEAD
    column = pl.BlockSpec((rows, 2 * HEAD), lambda h, m: (0, h))
    result = pl.pallas_call(
        functools.partial(backward_kernel, docs, count),
        grid_spec=pltpu.PrefetchScalarGridSpec(
            num_scalar_prefetch=1,
            grid=(kv_heads,),
            in_specs=[column] * 4 + key_value_specs(rows, half, kv_heads, count),
            out_specs=[column, pl.BlockSpec((2, rows, HEAD), lambda h, m: (0, 0, h))]
            + [pl.BlockSpec((2, half, HEAD), lambda h, m: (0, 0, h))] * (count - 1),
            scratch_shapes=[pltpu.VMEM((2, 2 * half, HEAD), F32)] * 3,
        ),
        out_shape=[
            jax.ShapeDtypeStruct((rows, width), F32),
            jax.ShapeDtypeStruct((2, rows, kv_width), F32),
        ]
        + [jax.ShapeDtypeStruct((2, half, kv_width), BF16)] * (count - 1),
        compiler_params=pltpu.CompilerParams(vmem_limit_bytes=VMEM_LIMIT),
        cost_estimate=pl.CostEstimate(
            flops=(count + 1) * half * half * width * 10,
            bytes_accessed=rows * width * 24,
            transcendentals=(count + 1) * half * half * width // HEAD,
        ),
    )(meta, queries, grads, outs, lse, key_value, key_value, *twice(others))
    return result[0], result[1], result[2:]


def body(
    tokens,
    cotangent,
    seq_lengths,
    part_order,
    w_query,
    key_weight,
    value_weight,
    w_out,
    w_gate,
    w_up,
    w_down,
    gain_in,
    gain_post,
    gain_q,
    gain_k,
):
    shard_count = lax.axis_size("shard")
    shard = lax.axis_index("shard")
    count = lax.axis_size("ctx")
    ctx = lax.axis_index("ctx")
    rows, model = tokens.shape
    half = rows // 2
    depth = model // shard_count
    docs = seq_lengths.shape[1]
    kv_width = key_weight.shape[1]

    kv_pieces = pieces_of(jnp.concatenate([key_weight, value_weight], axis=1), "shard")
    packed = jnp.concatenate([gain_in, gain_post, gain_q, gain_k])
    gains = lax.all_gather(packed, "shard", axis=0).astype(F32)
    cuts = [0, depth, 2 * depth, 2 * depth + gain_q.shape[0], packed.shape[0]]
    scale_in, scale_post, scale_q, scale_k = (
        gains[:, lo:hi].reshape(1, -1) for lo, hi in zip(cuts[:-1], cuts[1:])
    )

    q_pieces = pieces_of(after(w_query, kv_pieces[-1]), "shard")
    out_pieces = pieces_of(after(w_out, q_pieces[-1]), "shard")
    gate_pieces = pieces_of(after(w_gate, q_pieces[-1]), "shard")
    up_pieces = pieces_of(after(w_up, out_pieces[-1]), "shard")
    down_pieces = pieces_of(after(w_down, out_pieces[-1]), "shard")

    lengths = seq_lengths[0]
    starts = jnp.cumsum(lengths) - lengths
    parts = part_order[:, 0]
    part = parts[ctx]
    other_parts = [parts[ctx ^ d] for d in range(1, count)]
    sides = [jnp.where(p < part, 0, 1).astype(jnp.int32) for p in other_parts]
    held_parts = [jnp.where(p < part, p, 2 * count - 1 - p) for p in other_parts]
    meta = jnp.stack(
        [part]
        + [starts[i] for i in range(1, docs)]
        + [v for pair in zip(sides, held_parts) for v in pair]
    ).astype(jnp.int32)
    places = jnp.concatenate(
        [p * half + jnp.arange(half, dtype=jnp.int32) for p in (part, 2 * count - 1 - part)]
    )
    begins = jnp.zeros_like(places)
    for i in range(1, docs):
        begins = jnp.where(places >= starts[i], starts[i], begins)
    frequency = THETA ** (-jnp.arange(0, HEAD, 2, dtype=F32) / HEAD)
    angles = (places - begins).astype(F32)[:, None] * frequency[None, :]
    cosine, sine = jnp.cos(angles), jnp.sin(angles)
    cosine = jnp.concatenate([cosine, cosine], axis=-1)
    sine = jnp.concatenate([-sine, sine], axis=-1)

    inputs = tokens.astype(F32)
    normal_one, factor_one = rms_parts(inputs)
    normed_input = (normal_one * scale_in).astype(BF16)

    def project(pieces):
        total = None
        for j, piece in enumerate(pieces):
            at = (shard + j) % shard_count * depth
            term = dot(lax.dynamic_slice_in_dim(normed_input, at, depth, 1), piece)
            total = term if total is None else total + term
        return total

    kv_pre = project(kv_pieces)
    key_value = rope(kv_pre, kv_width // HEAD, cosine, sine, scale_k)
    held = []
    for d in range(1, count):
        start = jnp.where(part < other_parts[d - 1], 0, half)
        sent = lax.dynamic_slice_in_dim(key_value, start, half, 0)
        held.append(lax.ppermute(sent, "ctx", [(i, i ^ d) for i in range(count)]))
    q_pre = project(q_pieces)
    queries = rope(q_pre, q_pre.shape[1] // HEAD, cosine, sine, scale_q)
    attended, attn_out, lse = attend(meta, docs, queries, key_value, held)

    full_out = join(out_pieces, 1, shard)
    full_gate = join(gate_pieces, 0, shard)
    full_up = join(up_pieces, 0, shard)
    full_down = join(down_pieces, 1, shard)
    full_kv = join(kv_pieces, 0, shard)
    full_query = join(q_pieces, 0, shard)

    residual = inputs + pair_total(dot(attn_out, full_out))
    normal_two, factor_two = rms_parts(residual)
    normed_two = (normal_two * scale_post).astype(BF16)
    gate_act = dot(normed_two, full_gate)
    upward = dot(normed_two, full_up)
    sigma = jax.nn.sigmoid(gate_act)
    silu_act = gate_act * sigma
    hidden = (silu_act * upward).astype(BF16)
    mixed = (residual + pair_total(dot(hidden, full_down))).astype(BF16)
    grad_down = dot_tn(hidden, cotangent).astype(BF16)
    d_hidden = dot_nt(cotangent, full_down)
    d_gate = (d_hidden * upward * sigma * (1.0 + gate_act * (1.0 - sigma))).astype(BF16)
    d_up = (d_hidden * silu_act).astype(BF16)
    grad_gate = dot_tn(normed_two, d_gate).astype(BF16)
    grad_up = dot_tn(normed_two, d_up).astype(BF16)
    d_normed_two = pair_total(dot_nt(d_gate, full_gate) + dot_nt(d_up, full_up))
    grad_post = jnp.sum(d_normed_two * normal_two, axis=0)
    d_residual = cotangent.astype(F32) + rms_back(
        d_normed_two * scale_post, normal_two, factor_two
    )

    d_branch = d_residual.astype(BF16)
    d_attn = dot_nt(d_branch, full_out).astype(BF16)
    d_queries, d_kv, given = attend_back(
        meta, docs, queries, d_attn, attended, lse, key_value, held
    )
    returned = [
        lax.ppermute(g, "ctx", [(i, i ^ d) for i in range(count)])
        for d, g in zip(range(1, count), given)
    ]
    grad_out = dot_tn(attn_out, d_branch).astype(BF16)
    d_q_pre, gq_part = rope_back(d_queries, q_pre, cosine, sine, scale_q)
    grad_query = dot_tn(normed_input, d_q_pre).astype(BF16)

    first = sum(
        jnp.where(part < p, g.astype(F32), 0.0) for p, g in zip(other_parts, returned)
    )
    second = sum(
        jnp.where(part < p, 0.0, g.astype(F32)) for p, g in zip(other_parts, returned)
    )
    d_kv = d_kv + jnp.concatenate([first, second], axis=1)
    d_k_pre, gk_part = rope_back(d_kv[0], kv_pre, cosine, sine, scale_k)
    d_kv_pre = jnp.concatenate([d_k_pre, d_kv[1].astype(BF16)], axis=1)
    grad_kv = dot_tn(normed_input, d_kv_pre).astype(BF16)
    d_normed = pair_total(dot_nt(d_q_pre, full_query) + dot_nt(d_kv_pre, full_kv))
    grad_in = jnp.sum(d_normed * normal_one, axis=0)
    input_grad = d_residual + rms_back(d_normed * scale_in, normal_one, factor_one)

    once = jnp.where(lax.axis_index("tp") == 0, 1.0, 0.0)
    gain_grads = lax.psum(
        jnp.concatenate([grad_in * once, grad_post * once, gq_part[0], gk_part[0]]),
        ("shard", "ctx", "tp"),
    )
    own_gains = []
    for lo, size in ((0, model), (model, model), (2 * model, HEAD), (2 * model + HEAD, HEAD)):
        size = size // shard_count
        own_gains.append(lax.dynamic_slice_in_dim(gain_grads, lo + shard * size, size, 0))

    owned_down = ctx_total(to_shard_owner(grad_down, 1))
    owned_gate = ctx_total(to_shard_owner(grad_gate, 0))
    owned_up = ctx_total(to_shard_owner(grad_up, 0))
    owned_out = ctx_total(to_shard_owner(grad_out, 1))
    owned_query = ctx_total(to_shard_owner(grad_query, 0))
    owned_kv = ctx_total(to_shard_owner(grad_kv, 0))
    return (
        mixed,
        input_grad,
        owned_query,
        owned_kv[:, :kv_width],
        owned_kv[:, kv_width:],
        owned_out,
        owned_gate,
        owned_up,
        owned_down,
        *own_gains,
    )


def solution(mesh):
    placed = (
        P(("shard", "ctx"), None),
        P(("shard", "ctx"), None),
        P("shard", None),
        P(),
        P("shard", "tp"),
        P("shard", "tp"),
        P("shard", "tp"),
        P("tp", "shard"),
        P("shard", "tp"),
        P("shard", "tp"),
        P("tp", "shard"),
        P("shard"),
        P("shard"),
        P("shard"),
        P("shard"),
    )
    return jax.shard_map(
        body,
        mesh=mesh,
        in_specs=placed,
        out_specs=(
            P(("shard", "ctx"), None),
            P(("shard", "ctx"), None),
            P("shard", "tp"),
            P("shard", "tp"),
            P("shard", "tp"),
            P("tp", "shard"),
            P("shard", "tp"),
            P("shard", "tp"),
            P("tp", "shard"),
            P("shard"),
            P("shard"),
            P("shard"),
            P("shard"),
        ),
        check_vma=False,
    )
```

```python
import functools

import jax
import jax.numpy as jnp
from jax import lax
from jax.experimental import pallas as pl
from jax.experimental.pallas import tpu as pltpu
from jax.sharding import PartitionSpec as P

EPS = 1e-06
THETA = 1000000.0
LOG2E = 1.4426950408889634
HEAD = 128
BF16 = jnp.bfloat16
F32 = jnp.float32
VMEM_LIMIT = 48 * 1024 * 1024


def rms_parts(values):
    factor = lax.rsqrt(jnp.mean(values * values, axis=-1, keepdims=True) + EPS)
    return (values * factor, factor)


def rms_back(grad_hat, normal, factor):
    return factor * (grad_hat - normal * jnp.mean(grad_hat * normal, axis=-1, keepdims=True))


def dot(a, b):
    return jnp.dot(a, b, preferred_element_type=F32)


def dot_nt(a, b):
    return lax.dot_general(a, b, (((1,), (1,)), ((), ())), preferred_element_type=F32)


def dot_tn(a, b):
    return lax.dot_general(a, b, (((0,), (0,)), ((), ())), preferred_element_type=F32)


def after(value, *earlier):
    return lax.optimization_barrier((value,) + earlier)[0]


def pieces_of(own, axis):
    count = lax.axis_size(axis)
    return [own] + [
        lax.ppermute(own, axis, [((i + j) % count, i) for i in range(count)])
        for j in range(1, count)
    ]


def join(pieces, dim, index):
    count = len(pieces)
    if count == 1:
        return pieces[0]
    if count == 2:
        return jnp.where(
            index == 0, jnp.concatenate(pieces, dim), jnp.concatenate(pieces[::-1], dim)
        )
    size = pieces[0].shape[dim]
    shape = list(pieces[0].shape)
    shape[dim] = size * count
    whole = jnp.zeros(shape, pieces[0].dtype)
    for j, piece in enumerate(pieces):
        whole = lax.dynamic_update_slice_in_dim(whole, piece, (index + j) % count * size, dim)
    return whole


def pair_total(partial):
    count = lax.axis_size("tp")
    partial = partial.astype(BF16)
    if count != 2:
        return lax.psum(partial, "tp").astype(F32)
    other = lax.ppermute(partial, "tp", [(0, 1), (1, 0)])
    return partial.astype(F32) + other.astype(F32)


def to_shard_owner(grad, dim):
    count = lax.axis_size("shard")
    index = lax.axis_index("shard")
    if count != 2:
        return lax.psum_scatter(grad, "shard", scatter_dimension=dim, tiled=True).astype(F32)
    size = grad.shape[dim] // 2
    sent = lax.dynamic_slice_in_dim(grad, (1 - index) * size, size, dim)
    kept = lax.dynamic_slice_in_dim(grad, index * size, size, dim)
    other = lax.ppermute(sent, "shard", [(0, 1), (1, 0)])
    return kept.astype(F32) + other.astype(F32)


def ctx_total(value):
    count = lax.axis_size("ctx")
    index = lax.axis_index("ctx")
    levels = [1 << b for b in range(count.bit_length() - 1)]
    for level in levels:
        bit = (index // level) % 2
        size = value.shape[0] // 2
        sent = lax.dynamic_slice_in_dim(value, (1 - bit) * size, size, 0).astype(BF16)
        kept = lax.dynamic_slice_in_dim(value, bit * size, size, 0)
        other = lax.ppermute(sent, "ctx", [(i, i ^ level) for i in range(count)])
        value = kept + other.astype(F32)
    value = value.astype(BF16)
    for level in levels[::-1]:
        bit = (index // level) % 2
        other = lax.ppermute(value, "ctx", [(i, i ^ level) for i in range(count)])
        value = join([value, other], 0, bit)
    return value.astype(F32)


def rope_kernel(roped, pre_ref, cos_ref, sin_ref, gain_ref, out_ref):
    pre = pre_ref[...]

    @pl.when(pl.program_id(0) < roped)
    def _():
        factor = lax.rsqrt(jnp.mean(pre * pre, axis=-1, keepdims=True) + EPS)
        scaled = pre * factor * gain_ref[...]
        turned = pltpu.roll(scaled, HEAD // 2, 1)
        out_ref[...] = (scaled * cos_ref[...] + turned * sin_ref[...]).astype(BF16)

    @pl.when(pl.program_id(0) >= roped)
    def _():
        out_ref[...] = pre.astype(BF16)


def rope(pre, roped, cosine, sine, gain):
    rows, width = pre.shape
    column = pl.BlockSpec((rows, HEAD), lambda h: (0, h))
    table = pl.BlockSpec((rows, HEAD), lambda h: (0, 0))
    return pl.pallas_call(
        functools.partial(rope_kernel, roped),
        grid=(width // HEAD,),
        in_specs=[column, table, table, pl.BlockSpec((1, HEAD), lambda h: (0, 0))],
        out_specs=column,
        out_shape=jax.ShapeDtypeStruct((rows, width), BF16),
        compiler_params=pltpu.CompilerParams(vmem_limit_bytes=VMEM_LIMIT),
    )(pre, cosine, sine, gain)


def rope_back_kernel(grad_ref, pre_ref, cos_ref, sin_ref, gain_ref, out_ref, sum_ref):
    pre = pre_ref[...]
    grad = grad_ref[...]
    factor = lax.rsqrt(jnp.mean(pre * pre, axis=-1, keepdims=True) + EPS)
    hat = pre * factor
    back = grad * cos_ref[...] - pltpu.roll(grad, HEAD // 2, 1) * sin_ref[...]
    terms = jnp.sum(back * hat, axis=0, keepdims=True)

    @pl.when(pl.program_id(0) == 0)
    def _():
        sum_ref[...] = terms

    @pl.when(pl.program_id(0) > 0)
    def _():
        sum_ref[...] += terms

    back = back * gain_ref[...]
    inner = jnp.mean(back * hat, axis=-1, keepdims=True)
    out_ref[...] = (factor * (back - hat * inner)).astype(BF16)


def rope_back(grad, pre, cosine, sine, gain):
    rows, width = grad.shape
    column = pl.BlockSpec((rows, HEAD), lambda h: (0, h))
    table = pl.BlockSpec((rows, HEAD), lambda h: (0, 0))
    one_row = pl.BlockSpec((1, HEAD), lambda h: (0, 0))
    return pl.pallas_call(
        rope_back_kernel,
        grid=(width // HEAD,),
        in_specs=[column, column, table, table, one_row],
        out_specs=[column, one_row],
        out_shape=[
            jax.ShapeDtypeStruct((rows, width), BF16),
            jax.ShapeDtypeStruct((1, HEAD), F32),
        ],
        compiler_params=pltpu.CompilerParams(vmem_limit_bytes=VMEM_LIMIT),
    )(grad, pre, cosine, sine, gain)


def doc_begins(meta_ref, docs, place):
    begin = jnp.zeros_like(place)
    for i in range(1, docs):
        start = meta_ref[i]
        begin = jnp.where(place >= start, start, begin)
    return begin


def block_mask(meta_ref, docs, shape, half, q_part, k_part, diagonal):
    row = lax.broadcasted_iota(jnp.int32, (shape[0], 1), 0)
    q_place = q_part * half + jnp.where(row >= half, row - half, row)
    begin = doc_begins(meta_ref, docs, q_place) - k_part * half
    column = lax.broadcasted_iota(jnp.int32, shape, 1)
    visible = column >= begin
    if diagonal:
        visible = visible & (column <= q_place - k_part * half)
    return visible


def any_visible(meta_ref, docs, half, q_part, k_part):
    return (k_part + 1) * half > doc_begins(meta_ref, docs, q_part * half)


def two_heads(ref, start, half):
    rows = pl.ds(start, half)
    return jnp.concatenate([ref[rows, :HEAD], ref[rows, HEAD:]], axis=0)


def forward_kernel(docs, count, meta_ref, q_ref, k_ref, v_ref, *refs):
    others = refs[: 2 * (count - 1)]
    out_ref, out16_ref, lse_ref, acc_ref = refs[2 * (count - 1) :]
    half = q_ref.shape[0] // 2
    factor = HEAD**-0.5 * LOG2E
    ones = jnp.ones((half, HEAD), BF16)
    own = meta_ref[0]

    def block(start, keys, values, q_part, k_part, diagonal):
        scores = dot_nt(two_heads(q_ref, start, half), keys)
        visible = block_mask(meta_ref, docs, scores.shape, half, q_part, k_part, diagonal)
        weights = jnp.where(visible, jnp.exp2(scores * factor), 0.0).astype(BF16)
        return dot(weights, jnp.concatenate([values, ones], axis=1))

    for e in range(2):
        rows = pl.ds(e * half, half)
        part = own if e == 0 else 2 * count - 1 - own
        acc_ref[e] = block(e * half, k_ref[rows, :], v_ref[rows, :], part, part, True)
    for d in range(count - 1):
        side = meta_ref[docs + 2 * d]
        k_part = meta_ref[docs + 2 * d + 1]
        q_part = jnp.where(side == 0, own, 2 * count - 1 - own)

        @pl.when(any_visible(meta_ref, docs, half, q_part, k_part))
        def _():
            start = pl.multiple_of(side * half, half)
            acc_ref[side] += block(
                start, others[2 * d][...], others[2 * d + 1][...], q_part, k_part, False
            )

    for e in range(2):
        total = acc_ref[e]
        sums = total[:, HEAD:]
        result = total[:, :HEAD] / sums
        lse = jnp.log2(sums)
        for a in range(2):
            part = slice(a * half, (a + 1) * half)
            place = (pl.ds(e * half, half), slice(a * HEAD, (a + 1) * HEAD))
            out_ref[place] = result[part]
            out16_ref[place] = result[part].astype(BF16)
            lse_ref[place] = lse[part]


def backward_kernel(docs, count, meta_ref, q_ref, g_ref, o_ref, lse_ref, k_ref, v_ref, *refs):
    others = refs[: 2 * (count - 1)]
    dq_ref, dkv_ref = refs[2 * (count - 1) : 2 * count]
    given = refs[2 * count : 3 * count - 1]
    acc_ref, stats_ref, delta_ref = refs[3 * count - 1 :]
    half = q_ref.shape[0] // 2
    scale = HEAD**-0.5
    own = meta_ref[0]

    for e in range(2):
        grads = two_heads(g_ref, e * half, half).astype(F32)
        delta = jnp.sum(grads * two_heads(o_ref, e * half, half), axis=1, keepdims=True)
        delta_ref[e] = jnp.broadcast_to(delta, (2 * half, HEAD))
        stats_ref[e] = two_heads(lse_ref, e * half, half)

    def block(side, start, keys, values, q_part, k_part, diagonal):
        queries = two_heads(q_ref, start, half)
        grads = two_heads(g_ref, start, half)
        scores = dot_nt(queries, keys)
        repeat = half // HEAD
        lse = jnp.concatenate([stats_ref[side]] * repeat, axis=1)
        delta = jnp.concatenate([delta_ref[side]] * repeat, axis=1)
        visible = block_mask(meta_ref, docs, scores.shape, half, q_part, k_part, diagonal)
        weights = jnp.where(visible, jnp.exp2(scores * (scale * LOG2E) - lse), 0.0)
        d_weights = dot_nt(grads, values)
        d_scores = (weights * (d_weights - delta)).astype(BF16)
        d_values = dot_tn(weights.astype(BF16), grads)
        d_keys = dot_tn(d_scores, queries) * scale
        return dot(d_scores, keys) * scale, d_keys, d_values

    for e in range(2):
        rows = pl.ds(e * half, half)
        part = own if e == 0 else 2 * count - 1 - own
        d_queries, d_keys, d_values = block(
            e, e * half, k_ref[rows, :], v_ref[rows, :], part, part, True
        )
        acc_ref[e] = d_queries
        dkv_ref[0, rows, :] = d_keys
        dkv_ref[1, rows, :] = d_values
    for d in range(count - 1):
        side = meta_ref[docs + 2 * d]
        k_part = meta_ref[docs + 2 * d + 1]
        q_part = jnp.where(side == 0, own, 2 * count - 1 - own)
        seen = any_visible(meta_ref, docs, half, q_part, k_part)

        @pl.when(seen)
        def _():
            start = pl.multiple_of(side * half, half)
            d_queries, d_keys, d_values = block(
                side, start, others[2 * d][...], others[2 * d + 1][...], q_part, k_part, False
            )
            acc_ref[side] += d_queries
            given[d][0] = d_keys.astype(BF16)
            given[d][1] = d_values.astype(BF16)

        @pl.when(jnp.logical_not(seen))
        def _():
            given[d][...] = jnp.zeros_like(given[d])

    for e in range(2):
        for a in range(2):
            dq_ref[pl.ds(e * half, half), a * HEAD : (a + 1) * HEAD] = acc_ref[
                e, a * half : (a + 1) * half, :
            ]


def key_value_specs(rows, half, kv_heads, count):
    own = [
        pl.BlockSpec((rows, HEAD), lambda h, m: (0, h)),
        pl.BlockSpec((rows, HEAD), lambda h, m: (0, kv_heads + h)),
    ]
    other = [
        pl.BlockSpec((half, HEAD), lambda h, m: (0, h)),
        pl.BlockSpec((half, HEAD), lambda h, m: (0, kv_heads + h)),
    ]
    return own + other * (count - 1)


def twice(arrays):
    return [a for a in arrays for _ in range(2)]


def attend(meta, docs, queries, key_value, others):
    rows, width = queries.shape
    half = rows // 2
    count = len(others) + 1
    kv_heads = key_value.shape[1] // (2 * HEAD)
    column = pl.BlockSpec((rows, 2 * HEAD), lambda h, m: (0, h))
    return pl.pallas_call(
        functools.partial(forward_kernel, docs, count),
        grid_spec=pltpu.PrefetchScalarGridSpec(
            num_scalar_prefetch=1,
            grid=(kv_heads,),
            in_specs=[column] + key_value_specs(rows, half, kv_heads, count),
            out_specs=[column] * 3,
            scratch_shapes=[pltpu.VMEM((2, 2 * half, 2 * HEAD), F32)],
        ),
        out_shape=[
            jax.ShapeDtypeStruct((rows, width), F32),
            jax.ShapeDtypeStruct((rows, width), BF16),
            jax.ShapeDtypeStruct((rows, width), F32),
        ],
        compiler_params=pltpu.CompilerParams(vmem_limit_bytes=VMEM_LIMIT),
        cost_estimate=pl.CostEstimate(
            flops=(count + 1) * half * half * width * 16,
            bytes_accessed=rows * width * 16,
            transcendentals=(count + 1) * half * half * width // HEAD,
        ),
    )(meta, queries, key_value, key_value, *twice(others))


def attend_back(meta, docs, queries, grads, outs, lse, key_value, others):
    rows, width = queries.shape
    half = rows // 2
    count = len(others) + 1
    kv_width = key_value.shape[1] // 2
    kv_heads = kv_width // HEAD
    column = pl.BlockSpec((rows, 2 * HEAD), lambda h, m: (0, h))
    result = pl.pallas_call(
        functools.partial(backward_kernel, docs, count),
        grid_spec=pltpu.PrefetchScalarGridSpec(
            num_scalar_prefetch=1,
            grid=(kv_heads,),
            in_specs=[column] * 4 + key_value_specs(rows, half, kv_heads, count),
            out_specs=[column, pl.BlockSpec((2, rows, HEAD), lambda h, m: (0, 0, h))]
            + [pl.BlockSpec((2, half, HEAD), lambda h, m: (0, 0, h))] * (count - 1),
            scratch_shapes=[pltpu.VMEM((2, 2 * half, HEAD), F32)] * 3,
        ),
        out_shape=[
            jax.ShapeDtypeStruct((rows, width), F32),
            jax.ShapeDtypeStruct((2, rows, kv_width), F32),
        ]
        + [jax.ShapeDtypeStruct((2, half, kv_width), BF16)] * (count - 1),
        compiler_params=pltpu.CompilerParams(vmem_limit_bytes=VMEM_LIMIT),
        cost_estimate=pl.CostEstimate(
            flops=(count + 1) * half * half * width * 40,
            bytes_accessed=rows * width * 24,
            transcendentals=(count + 1) * half * half * width // HEAD,
        ),
    )(meta, queries, grads, outs, lse, key_value, key_value, *twice(others))
    return result[0], result[1], list(result[2:])


def body(
    tokens,
    cotangent,
    seq_lengths,
    part_order,
    w_query,
    key_weight,
    value_weight,
    w_out,
    w_gate,
    w_up,
    w_down,
    gain_in,
    gain_post,
    gain_q,
    gain_k,
):
    shard_count = lax.axis_size("shard")
    shard = lax.axis_index("shard")
    count = lax.axis_size("ctx")
    ctx = lax.axis_index("ctx")
    rows, model = tokens.shape
    half = rows // 2
    depth = model // shard_count
    docs = seq_lengths.shape[1]
    kv_width = key_weight.shape[1]
    units = w_gate.shape[1]

    packed = jnp.concatenate([gain_in, gain_post, gain_q, gain_k])
    lines = -(-packed.shape[0] // (2 * kv_width * 16)) * 16
    packed = jnp.pad(packed, (0, lines * 2 * kv_width - packed.shape[0]))
    kv_own = jnp.concatenate(
        [
            jnp.concatenate([key_weight, value_weight], axis=1),
            packed.reshape(lines, 2 * kv_width),
        ],
        axis=0,
    )
    first_pieces = pieces_of(kv_own, "shard")
    kv_pieces = [piece[:depth] for piece in first_pieces]
    cuts = [0, depth, 2 * depth, 2 * depth + gain_q.shape[0]]
    cuts = cuts + [cuts[-1] + gain_k.shape[0]]
    gain_pieces = [
        [piece[depth:].reshape(-1)[lo:hi].astype(F32) for piece in first_pieces]
        for lo, hi in zip(cuts[:-1], cuts[1:])
    ]
    scale_in, scale_post, scale_q, scale_k = (
        join(pieces, 0, shard).reshape(1, -1) for pieces in gain_pieces
    )

    q_pieces = pieces_of(after(w_query, first_pieces[-1]), "shard")
    gate_up = jnp.concatenate([w_gate, w_up], axis=1)
    full_gate_up = lax.all_gather(
        after(gate_up, first_pieces[-1]), "shard", axis=0, tiled=True
    )
    out_pieces = pieces_of(after(w_out, q_pieces[-1]), "shard")
    down_pieces = pieces_of(after(w_down, q_pieces[-1]), "shard")

    lengths = seq_lengths[0]
    starts = jnp.cumsum(lengths) - lengths
    parts = part_order[:, 0]
    part = parts[ctx]
    other_parts = [parts[ctx ^ d] for d in range(1, count)]
    sides = [jnp.where(p < part, 0, 1).astype(jnp.int32) for p in other_parts]
    held_parts = [jnp.where(p < part, p, 2 * count - 1 - p) for p in other_parts]
    meta = jnp.stack(
        [part]
        + [starts[i] for i in range(1, docs)]
        + [v for pair in zip(sides, held_parts) for v in pair]
    ).astype(jnp.int32)
    places = jnp.concatenate(
        [p * half + jnp.arange(half, dtype=jnp.int32) for p in (part, 2 * count - 1 - part)]
    )
    begins = jnp.zeros_like(places)
    for i in range(1, docs):
        begins = jnp.where(places >= starts[i], starts[i], begins)
    frequency = THETA ** (-jnp.arange(0, HEAD, 2, dtype=F32) / HEAD)
    angles = (places - begins).astype(F32)[:, None] * frequency[None, :]
    cosine, sine = jnp.cos(angles), jnp.sin(angles)
    cosine = jnp.concatenate([cosine, cosine], axis=-1)
    sine = jnp.concatenate([-sine, sine], axis=-1)

    inputs = tokens.astype(F32)
    normal_one, factor_one = rms_parts(inputs)
    normed_input = (normal_one * scale_in).astype(BF16)

    def project(pieces):
        total = None
        for j, piece in enumerate(pieces):
            at = (shard + j) % shard_count * depth
            part_in = lax.dynamic_slice_in_dim(normal_one, at, depth, 1)
            term = dot((part_in * gain_pieces[0][j][None, :]).astype(BF16), piece)
            total = term if total is None else total + term
        return total

    kv_pre = project(kv_pieces)
    key_value = rope(kv_pre, kv_width // HEAD, cosine, sine, scale_k)
    held = []
    for d in range(1, count):
        start = jnp.where(part < other_parts[d - 1], 0, half)
        sent = lax.dynamic_slice_in_dim(key_value, start, half, 0)
        held.append(lax.ppermute(sent, "ctx", [(i, i ^ d) for i in range(count)]))
    q_pre = project(q_pieces)
    queries = rope(q_pre, q_pre.shape[1] // HEAD, cosine, sine, scale_q)
    queries = after(queries, full_gate_up)
    attended, attn_out, lse = attend(meta, docs, queries, key_value, held)

    full_out = join(out_pieces, 1, shard)
    full_down = join(down_pieces, 1, shard)
    full_kv = join(kv_pieces, 0, shard)
    full_query = join(q_pieces, 0, shard)

    residual = inputs + pair_total(dot(attn_out, full_out))
    normal_two, factor_two = rms_parts(residual)
    normed_two = (normal_two * scale_post).astype(BF16)
    gate_upward = dot(normed_two, full_gate_up)
    gate_act = gate_upward[:, :units]
    upward = gate_upward[:, units:]
    sigma = jax.nn.sigmoid(gate_act)
    silu_act = gate_act * sigma
    hidden = (silu_act * upward).astype(BF16)
    mixed = (residual + pair_total(dot(hidden, full_down))).astype(BF16)
    grad_down = dot_tn(hidden, cotangent).astype(BF16)
    d_hidden = dot_nt(cotangent, full_down)
    d_gate = (d_hidden * upward * sigma * (1.0 + gate_act * (1.0 - sigma))).astype(BF16)
    d_up = (d_hidden * silu_act).astype(BF16)
    d_gate_up = jnp.concatenate([d_gate, d_up], axis=1)
    grad_gate_up = dot_tn(normed_two, d_gate_up).astype(BF16)
    d_normed_two = pair_total(dot_nt(d_gate_up, full_gate_up))
    shared_down = to_shard_owner(grad_down, 1).astype(BF16)
    shared_gate_up = to_shard_owner(grad_gate_up, 0).astype(BF16)
    owned_down = lax.psum(shared_down, "ctx")
    owned_gate_up = lax.psum(after(shared_gate_up, owned_down), "ctx")
    grad_post = jnp.sum(d_normed_two * normal_two, axis=0)
    d_residual = cotangent.astype(F32) + rms_back(
        d_normed_two * scale_post, normal_two, factor_two
    )

    d_branch = d_residual.astype(BF16)
    d_attn = after(dot_nt(d_branch, full_out).astype(BF16), shared_down)
    d_queries, d_kv, given = attend_back(
        meta, docs, queries, d_attn, attended, lse, key_value, held
    )
    given = given[:-2] + [after(g, shared_gate_up) for g in given[-2:]]
    returned = [
        lax.ppermute(g, "ctx", [(i, i ^ d) for i in range(count)])
        for d, g in zip(range(1, count), given)
    ]
    grad_out = dot_tn(attn_out, d_branch).astype(BF16)
    d_q_pre, gq_part = rope_back(d_queries, q_pre, cosine, sine, scale_q)
    grad_query = dot_tn(normed_input, d_q_pre).astype(BF16)
    shared_out = to_shard_owner(grad_out, 1).astype(BF16)
    shared_query = to_shard_owner(grad_query, 0).astype(BF16)
    owned_out, owned_query = lax.psum(
        (after(shared_out, owned_gate_up), after(shared_query, owned_gate_up)), "ctx"
    )

    first = sum(
        jnp.where(part < p, g.astype(F32), 0.0) for p, g in zip(other_parts, returned)
    )
    second = sum(
        jnp.where(part < p, 0.0, g.astype(F32)) for p, g in zip(other_parts, returned)
    )
    d_kv = d_kv + jnp.concatenate([first, second], axis=1)
    d_k_pre, gk_part = rope_back(d_kv[0], kv_pre, cosine, sine, scale_k)
    d_kv_pre = jnp.concatenate([d_k_pre, d_kv[1].astype(BF16)], axis=1)
    grad_kv = dot_tn(normed_input, d_kv_pre).astype(BF16)
    d_normed = pair_total(dot_nt(d_q_pre, full_query) + dot_nt(d_kv_pre, full_kv))
    grad_in = jnp.sum(d_normed * normal_one, axis=0)
    input_grad = d_residual + rms_back(d_normed * scale_in, normal_one, factor_one)

    owned_kv = ctx_total(to_shard_owner(grad_kv, 0))

    once = jnp.where(lax.axis_index("tp") == 0, 1.0, 0.0)
    gain_grads = jnp.concatenate([grad_in * once, grad_post * once, gq_part[0], gk_part[0]])
    gain_grads = lax.psum(
        after(gain_grads, owned_query),
        ("shard", "ctx", "tp"),
    )
    own_gains = []
    for lo, size in ((0, model), (model, model), (2 * model, HEAD), (2 * model + HEAD, HEAD)):
        size = size // shard_count
        own_gains.append(lax.dynamic_slice_in_dim(gain_grads, lo + shard * size, size, 0))

    return (
        mixed,
        input_grad,
        owned_query.astype(F32),
        owned_kv[:, :kv_width],
        owned_kv[:, kv_width:],
        owned_out.astype(F32),
        owned_gate_up[:, :units].astype(F32),
        owned_gate_up[:, units:].astype(F32),
        owned_down.astype(F32),
        *own_gains,
    )


def solution(mesh):
    placed = (
        P(("shard", "ctx"), None),
        P(("shard", "ctx"), None),
        P("shard", None),
        P(),
        P("shard", "tp"),
        P("shard", "tp"),
        P("shard", "tp"),
        P("tp", "shard"),
        P("shard", "tp"),
        P("shard", "tp"),
        P("tp", "shard"),
        P("shard"),
        P("shard"),
        P("shard"),
        P("shard"),
    )
    return jax.shard_map(
        body,
        mesh=mesh,
        in_specs=placed,
        out_specs=(
            P(("shard", "ctx"), None),
            P(("shard", "ctx"), None),
            P("shard", "tp"),
            P("shard", "tp"),
            P("shard", "tp"),
            P("tp", "shard"),
            P("shard", "tp"),
            P("shard", "tp"),
            P("tp", "shard"),
            P("shard"),
            P("shard"),
            P("shard"),
            P("shard"),
        ),
        check_vma=False,
    )
```

```python
import functools

import jax
import jax.numpy as jnp
from jax import lax
from jax.experimental import pallas as pl
from jax.experimental.pallas import tpu as pltpu
from jax.sharding import PartitionSpec as P

EPS = 1e-06
THETA = 1000000.0
LOG2E = 1.4426950408889634
HEAD = 128
BF16 = jnp.bfloat16
F32 = jnp.float32
VMEM_LIMIT = 48 * 1024 * 1024


def rms_parts(values):
    factor = lax.rsqrt(jnp.mean(values * values, axis=-1, keepdims=True) + EPS)
    return (values * factor, factor)


def rms_back(grad_hat, normal, factor):
    return factor * (grad_hat - normal * jnp.mean(grad_hat * normal, axis=-1, keepdims=True))


def dot(a, b):
    return jnp.dot(a, b, preferred_element_type=F32)


def dot_nt(a, b):
    return lax.dot_general(a, b, (((1,), (1,)), ((), ())), preferred_element_type=F32)


def dot_tn(a, b):
    return lax.dot_general(a, b, (((0,), (0,)), ((), ())), preferred_element_type=F32)


def tie(*values):
    return lax.optimization_barrier(values)


def pieces_of(own, axis):
    count = lax.axis_size(axis)
    return [own] + [
        lax.ppermute(own, axis, [((i + j) % count, i) for i in range(count)])
        for j in range(1, count)
    ]


def join(pieces, dim, index):
    count = len(pieces)
    if count == 1:
        return pieces[0]
    if count == 2:
        return jnp.where(
            index == 0, jnp.concatenate(pieces, dim), jnp.concatenate(pieces[::-1], dim)
        )
    size = pieces[0].shape[dim]
    shape = list(pieces[0].shape)
    shape[dim] = size * count
    whole = jnp.zeros(shape, pieces[0].dtype)
    for j, piece in enumerate(pieces):
        whole = lax.dynamic_update_slice_in_dim(whole, piece, (index + j) % count * size, dim)
    return whole


def pair_total(partial):
    count = lax.axis_size("tp")
    partial = partial.astype(BF16)
    if count != 2:
        return lax.psum(partial, "tp").astype(F32)
    other = lax.ppermute(partial, "tp", [(0, 1), (1, 0)])
    return partial.astype(F32) + other.astype(F32)


def swap(value, axis, level=1):
    count = lax.axis_size(axis)
    return lax.ppermute(value, axis, [(i, i ^ level) for i in range(count)])


def to_shard_owner(grad):
    count = lax.axis_size("shard")
    index = lax.axis_index("shard")
    if count != 2:
        return lax.psum_scatter(grad, "shard", scatter_dimension=0, tiled=True).astype(F32)
    size = grad.shape[0] // 2
    sent = lax.dynamic_slice_in_dim(grad, (1 - index) * size, size, 0)
    kept = lax.dynamic_slice_in_dim(grad, index * size, size, 0)
    return kept.astype(F32) + swap(sent, "shard").astype(F32)


def bit_of(level):
    return (lax.axis_index("ctx") // level) % 2


def halve(value, level):
    bit = bit_of(level)
    size = value.shape[0] // 2
    sent = lax.dynamic_slice_in_dim(value, (1 - bit) * size, size, 0).astype(BF16)
    kept = lax.dynamic_slice_in_dim(value, bit * size, size, 0)
    return kept + swap(sent, "ctx", level).astype(F32)


def double(value, level):
    value = value.astype(BF16)
    return join([value, swap(value, "ctx", level)], 0, bit_of(level))


def chain_step(value, levels, step):
    if step < len(levels):
        return halve(value, levels[step])
    return double(value, levels[2 * len(levels) - 1 - step])


def rope_kernel(pre_ref, cos_ref, sin_ref, gain_ref, out_ref):
    pre = pre_ref[...]
    factor = lax.rsqrt(jnp.mean(pre * pre, axis=-1, keepdims=True) + EPS)
    scaled = pre * factor * gain_ref[...]
    turned = pltpu.roll(scaled, HEAD // 2, 1)
    out_ref[...] = (scaled * cos_ref[...] + turned * sin_ref[...]).astype(BF16)


def rope_and_copy_kernel(roped, pre_ref, plain_ref, cos_ref, sin_ref, gain_ref, out_ref):
    @pl.when(pl.program_id(0) < roped)
    def _():
        rope_kernel(pre_ref, cos_ref, sin_ref, gain_ref, out_ref)

    @pl.when(pl.program_id(0) >= roped)
    def _():
        out_ref[...] = plain_ref[...].astype(BF16)


def rope(pre, cosine, sine, gain, plain=None):
    rows, width = pre.shape
    heads = width // HEAD
    table = pl.BlockSpec((rows, HEAD), lambda h: (0, 0))
    tables = [table, table, pl.BlockSpec((1, HEAD), lambda h: (0, 0))]
    column = pl.BlockSpec((rows, HEAD), lambda h: (0, h))
    if plain is None:
        kernel, steps, columns, values = rope_kernel, heads, [column], [pre]
    else:
        kernel, steps = functools.partial(rope_and_copy_kernel, heads), 2 * heads
        columns = [
            pl.BlockSpec((rows, HEAD), lambda h: (0, jnp.minimum(h, heads - 1))),
            pl.BlockSpec((rows, HEAD), lambda h: (0, jnp.maximum(h - heads, 0))),
        ]
        values = [pre, plain]
    return pl.pallas_call(
        kernel,
        grid=(steps,),
        in_specs=columns + tables,
        out_specs=column,
        out_shape=jax.ShapeDtypeStruct((rows, steps * HEAD), BF16),
        compiler_params=pltpu.CompilerParams(vmem_limit_bytes=VMEM_LIMIT),
    )(*values, cosine, sine, gain)


def rope_back_kernel(grad_ref, pre_ref, cos_ref, sin_ref, gain_ref, out_ref, sum_ref):
    pre = pre_ref[...]
    grad = grad_ref[...]
    factor = lax.rsqrt(jnp.mean(pre * pre, axis=-1, keepdims=True) + EPS)
    hat = pre * factor
    back = grad * cos_ref[...] - pltpu.roll(grad, HEAD // 2, 1) * sin_ref[...]
    terms = jnp.sum(back * hat, axis=0, keepdims=True)

    @pl.when(pl.program_id(0) == 0)
    def _():
        sum_ref[...] = terms

    @pl.when(pl.program_id(0) > 0)
    def _():
        sum_ref[...] += terms

    back = back * gain_ref[...]
    inner = jnp.mean(back * hat, axis=-1, keepdims=True)
    out_ref[...] = (factor * (back - hat * inner)).astype(BF16)


def rope_back(grad, pre, cosine, sine, gain):
    rows, width = grad.shape
    column = pl.BlockSpec((rows, HEAD), lambda h: (0, h))
    table = pl.BlockSpec((rows, HEAD), lambda h: (0, 0))
    one_row = pl.BlockSpec((1, HEAD), lambda h: (0, 0))
    return pl.pallas_call(
        rope_back_kernel,
        grid=(width // HEAD,),
        in_specs=[column, column, table, table, one_row],
        out_specs=[column, one_row],
        out_shape=[
            jax.ShapeDtypeStruct((rows, width), BF16),
            jax.ShapeDtypeStruct((1, HEAD), F32),
        ],
        compiler_params=pltpu.CompilerParams(vmem_limit_bytes=VMEM_LIMIT),
    )(grad, pre, cosine, sine, gain)


def doc_begins(meta_ref, docs, place):
    begin = jnp.zeros_like(place)
    for i in range(1, docs):
        start = meta_ref[i]
        begin = jnp.where(place >= start, start, begin)
    return begin


def block_mask(meta_ref, docs, shape, half, q_part, k_part, diagonal):
    row = lax.broadcasted_iota(jnp.int32, (shape[0], 1), 0)
    q_place = q_part * half + jnp.where(row >= half, row - half, row)
    begin = doc_begins(meta_ref, docs, q_place) - k_part * half
    column = lax.broadcasted_iota(jnp.int32, shape, 1)
    visible = column >= begin
    if diagonal:
        visible = visible & (column <= q_place - k_part * half)
    return visible


def any_visible(meta_ref, docs, half, q_part, k_part):
    return (k_part + 1) * half > doc_begins(meta_ref, docs, q_part * half)


def all_visible(meta_ref, docs, half, q_part, k_part):
    return k_part * half >= doc_begins(meta_ref, docs, q_part * half + half - 1)


def masked(weights, *mask_args):
    if mask_args[-1] is None:
        return weights
    return jnp.where(block_mask(*mask_args), weights, 0.0)


def two_heads(ref, start, half):
    rows = pl.ds(start, half)
    return jnp.concatenate([ref[rows, :HEAD], ref[rows, HEAD:]], axis=0)


def forward_kernel(docs, count, meta_ref, q_ref, k_ref, v_ref, *refs):
    others = refs[: 2 * (count - 1)]
    out_ref, out16_ref, lse_ref, acc_ref = refs[2 * (count - 1) :]
    half = q_ref.shape[0] // 2
    factor = HEAD**-0.5 * LOG2E
    ones = jnp.ones((half, HEAD), BF16)
    own = meta_ref[0]

    def block(start, keys, values, q_part, k_part, diagonal):
        scores = dot_nt(two_heads(q_ref, start, half), keys)
        weights = jnp.exp2(scores * factor)
        weights = masked(weights, meta_ref, docs, scores.shape, half, q_part, k_part, diagonal)
        weights = weights.astype(BF16)
        return dot(weights, jnp.concatenate([values, ones], axis=1))

    for e in range(2):
        rows = pl.ds(e * half, half)
        part = own if e == 0 else 2 * count - 1 - own
        acc_ref[e] = block(e * half, k_ref[rows, :], v_ref[rows, :], part, part, True)
    for d in range(count - 1):
        side = meta_ref[docs + 2 * d]
        k_part = meta_ref[docs + 2 * d + 1]
        q_part = jnp.where(side == 0, own, 2 * count - 1 - own)

        def add(mask):
            start = pl.multiple_of(side * half, half)
            acc_ref[side] += block(
                start, others[2 * d][...], others[2 * d + 1][...], q_part, k_part, mask
            )

        seen = any_visible(meta_ref, docs, half, q_part, k_part)
        whole = all_visible(meta_ref, docs, half, q_part, k_part)
        pl.when(whole)(functools.partial(add, None))
        pl.when(seen & jnp.logical_not(whole))(functools.partial(add, False))

    for e in range(2):
        total = acc_ref[e]
        sums = total[:, HEAD:]
        result = total[:, :HEAD] / sums
        lse = jnp.log2(sums)
        for a in range(2):
            part = slice(a * half, (a + 1) * half)
            place = (pl.ds(e * half, half), slice(a * HEAD, (a + 1) * HEAD))
            out_ref[place] = result[part]
            out16_ref[place] = result[part].astype(BF16)
            lse_ref[place] = lse[part]


def backward_kernel(docs, count, meta_ref, q_ref, g_ref, o_ref, lse_ref, k_ref, v_ref, *refs):
    others = refs[: 2 * (count - 1)]
    dq_ref, dkv_ref = refs[2 * (count - 1) : 2 * count]
    given = refs[2 * count : 3 * count - 1]
    acc_ref, stats_ref, delta_ref = refs[3 * count - 1 :]
    half = q_ref.shape[0] // 2
    scale = HEAD**-0.5
    own = meta_ref[0]

    for e in range(2):
        grads = two_heads(g_ref, e * half, half).astype(F32)
        delta = jnp.sum(grads * two_heads(o_ref, e * half, half), axis=1, keepdims=True)
        delta_ref[e] = jnp.broadcast_to(delta, (2 * half, HEAD))
        stats_ref[e] = two_heads(lse_ref, e * half, half)

    def block(side, start, keys, values, q_part, k_part, diagonal):
        queries = two_heads(q_ref, start, half)
        grads = two_heads(g_ref, start, half)
        scores = dot_nt(queries, keys)
        repeat = half // HEAD
        lse = jnp.concatenate([stats_ref[side]] * repeat, axis=1)
        delta = jnp.concatenate([delta_ref[side]] * repeat, axis=1)
        weights = jnp.exp2(scores * (scale * LOG2E) - lse)
        weights = masked(weights, meta_ref, docs, scores.shape, half, q_part, k_part, diagonal)
        d_weights = dot_nt(grads, values)
        d_scores = (weights * (d_weights - delta)).astype(BF16)
        d_values = dot_tn(weights.astype(BF16), grads)
        d_keys = dot_tn(d_scores, queries) * scale
        return dot(d_scores, keys) * scale, d_keys, d_values

    for e in range(2):
        rows = pl.ds(e * half, half)
        part = own if e == 0 else 2 * count - 1 - own
        d_queries, d_keys, d_values = block(
            e, e * half, k_ref[rows, :], v_ref[rows, :], part, part, True
        )
        acc_ref[e] = d_queries
        dkv_ref[0, rows, :] = d_keys
        dkv_ref[1, rows, :] = d_values
    for d in range(count - 1):
        side = meta_ref[docs + 2 * d]
        k_part = meta_ref[docs + 2 * d + 1]
        q_part = jnp.where(side == 0, own, 2 * count - 1 - own)
        seen = any_visible(meta_ref, docs, half, q_part, k_part)
        whole = all_visible(meta_ref, docs, half, q_part, k_part)

        def add(mask):
            start = pl.multiple_of(side * half, half)
            d_queries, d_keys, d_values = block(
                side, start, others[2 * d][...], others[2 * d + 1][...], q_part, k_part, mask
            )
            acc_ref[side] += d_queries
            given[d][0] = d_keys.astype(BF16)
            given[d][1] = d_values.astype(BF16)

        pl.when(whole)(functools.partial(add, None))
        pl.when(seen & jnp.logical_not(whole))(functools.partial(add, False))

        @pl.when(jnp.logical_not(seen))
        def _():
            given[d][...] = jnp.zeros_like(given[d])

    for e in range(2):
        for a in range(2):
            dq_ref[pl.ds(e * half, half), a * HEAD : (a + 1) * HEAD] = acc_ref[
                e, a * half : (a + 1) * half, :
            ]


def key_value_specs(rows, half, kv_heads, count):
    own = [
        pl.BlockSpec((rows, HEAD), lambda h, m: (0, h)),
        pl.BlockSpec((rows, HEAD), lambda h, m: (0, kv_heads + h)),
    ]
    other = [
        pl.BlockSpec((half, HEAD), lambda h, m: (0, h)),
        pl.BlockSpec((half, HEAD), lambda h, m: (0, kv_heads + h)),
    ]
    return own + other * (count - 1)


def twice(arrays):
    return [a for a in arrays for _ in range(2)]


def attend(meta, docs, queries, key_value, others):
    rows, width = queries.shape
    half = rows // 2
    count = len(others) + 1
    kv_heads = key_value.shape[1] // (2 * HEAD)
    column = pl.BlockSpec((rows, 2 * HEAD), lambda h, m: (0, h))
    return pl.pallas_call(
        functools.partial(forward_kernel, docs, count),
        grid_spec=pltpu.PrefetchScalarGridSpec(
            num_scalar_prefetch=1,
            grid=(kv_heads,),
            in_specs=[column] + key_value_specs(rows, half, kv_heads, count),
            out_specs=[column] * 3,
            scratch_shapes=[pltpu.VMEM((2, 2 * half, 2 * HEAD), F32)],
        ),
        out_shape=[
            jax.ShapeDtypeStruct((rows, width), F32),
            jax.ShapeDtypeStruct((rows, width), BF16),
            jax.ShapeDtypeStruct((rows, width), F32),
        ],
        compiler_params=pltpu.CompilerParams(vmem_limit_bytes=VMEM_LIMIT),
        cost_estimate=pl.CostEstimate(
            flops=(count + 1) * half * half * width * 16,
            bytes_accessed=rows * width * 16,
            transcendentals=(count + 1) * half * half * width // HEAD,
        ),
    )(meta, queries, key_value, key_value, *twice(others))


def attend_back(meta, docs, queries, grads, outs, lse, key_value, others):
    rows, width = queries.shape
    half = rows // 2
    count = len(others) + 1
    kv_width = key_value.shape[1] // 2
    kv_heads = kv_width // HEAD
    column = pl.BlockSpec((rows, 2 * HEAD), lambda h, m: (0, h))
    result = pl.pallas_call(
        functools.partial(backward_kernel, docs, count),
        grid_spec=pltpu.PrefetchScalarGridSpec(
            num_scalar_prefetch=1,
            grid=(kv_heads,),
            in_specs=[column] * 4 + key_value_specs(rows, half, kv_heads, count),
            out_specs=[column, pl.BlockSpec((2, rows, HEAD), lambda h, m: (0, 0, h))]
            + [pl.BlockSpec((2, half, HEAD), lambda h, m: (0, 0, h))] * (count - 1),
            scratch_shapes=[pltpu.VMEM((2, 2 * half, HEAD), F32)] * 3,
        ),
        out_shape=[
            jax.ShapeDtypeStruct((rows, width), F32),
            jax.ShapeDtypeStruct((2, rows, kv_width), F32),
        ]
        + [jax.ShapeDtypeStruct((2, half, kv_width), BF16)] * (count - 1),
        compiler_params=pltpu.CompilerParams(vmem_limit_bytes=VMEM_LIMIT),
        cost_estimate=pl.CostEstimate(
            flops=(count + 1) * half * half * width * 40,
            bytes_accessed=rows * width * 24,
            transcendentals=(count + 1) * half * half * width // HEAD,
        ),
    )(meta, queries, grads, outs, lse, key_value, key_value, *twice(others))
    return result[0], result[1], list(result[2:])


def body(
    tokens,
    cotangent,
    seq_lengths,
    part_order,
    w_query,
    key_weight,
    value_weight,
    w_out,
    w_gate,
    w_up,
    w_down,
    gain_in,
    gain_post,
    gain_q,
    gain_k,
):
    shard_count = lax.axis_size("shard")
    shard = lax.axis_index("shard")
    count = lax.axis_size("ctx")
    ctx = lax.axis_index("ctx")
    rows, model = tokens.shape
    half = rows // 2
    depth = model // shard_count
    docs = seq_lengths.shape[1]
    kv_width = key_weight.shape[1]
    units = w_gate.shape[1]
    heads_width = w_out.shape[0]

    packed = jnp.concatenate([gain_in, gain_post, gain_q, gain_k])
    packed_pieces = pieces_of(packed, "shard")
    k_pieces = pieces_of(key_weight, "shard")
    v_pieces = pieces_of(value_weight, "shard")
    cuts = [0, depth, 2 * depth, 2 * depth + gain_q.shape[0], packed.shape[0]]
    gain_pieces = [
        [piece[lo:hi].astype(F32) for piece in packed_pieces]
        for lo, hi in zip(cuts[:-1], cuts[1:])
    ]
    scale_in, scale_post, scale_q, scale_k = (
        join(pieces, 0, shard).reshape(1, -1) for pieces in gain_pieces
    )
    own_units = jnp.concatenate([w_gate, w_up, w_down.T], axis=1)
    w_query, own_units, v_pieces[-1] = tie(w_query, own_units, v_pieces[-1])
    q_pieces = pieces_of(w_query, "shard")
    full_units = lax.all_gather(own_units, "shard", axis=0, tiled=True)
    w_out, q_pieces[-1] = tie(w_out, q_pieces[-1])
    out_pieces = pieces_of(w_out, "shard")

    lengths = seq_lengths[0]
    starts = jnp.cumsum(lengths) - lengths
    parts = part_order[:, 0]
    part = parts[ctx]
    other_parts = [parts[ctx ^ d] for d in range(1, count)]
    sides = [jnp.where(p < part, 0, 1).astype(jnp.int32) for p in other_parts]
    held_parts = [jnp.where(p < part, p, 2 * count - 1 - p) for p in other_parts]
    meta = jnp.stack(
        [part]
        + [starts[i] for i in range(1, docs)]
        + [v for pair in zip(sides, held_parts) for v in pair]
    ).astype(jnp.int32)
    places = jnp.concatenate(
        [p * half + jnp.arange(half, dtype=jnp.int32) for p in (part, 2 * count - 1 - part)]
    )
    begins = jnp.zeros_like(places)
    for i in range(1, docs):
        begins = jnp.where(places >= starts[i], starts[i], begins)
    frequency = THETA ** (-jnp.arange(0, HEAD, 2, dtype=F32) / HEAD)
    angles = (places - begins).astype(F32)[:, None] * frequency[None, :]
    cosine, sine = jnp.cos(angles), jnp.sin(angles)
    cosine = jnp.concatenate([cosine, cosine], axis=-1)
    sine = jnp.concatenate([-sine, sine], axis=-1)

    inputs = tokens.astype(F32)
    normal_one, factor_one = rms_parts(inputs)
    normed_input = (normal_one * scale_in).astype(BF16)

    parts_in = []
    for j in range(shard_count):
        at = (shard + j) % shard_count * depth
        part_in = lax.dynamic_slice_in_dim(normal_one, at, depth, 1)
        parts_in.append((part_in * gain_pieces[0][j][None, :]).astype(BF16))

    def project(pieces):
        return sum(dot(part_in, piece) for part_in, piece in zip(parts_in, pieces))

    k_pieces[-1], cosine, sine, meta, parts_in[-1], scale_k = tie(
        k_pieces[-1], cosine, sine, meta, parts_in[-1], scale_k
    )
    k_pre = project(k_pieces)
    key_value = rope(k_pre, cosine, sine, scale_k, project(v_pieces))
    held = []
    for d in range(1, count):
        start = jnp.where(part < other_parts[d - 1], 0, half)
        sent = lax.dynamic_slice_in_dim(key_value, start, half, 0)
        held.append(lax.ppermute(sent, "ctx", [(i, i ^ d) for i in range(count)]))
    q_pre = project(q_pieces)
    queries = rope(q_pre, cosine, sine, scale_q)
    queries, out_pieces[-1] = tie(queries, out_pieces[-1])
    attended, attn_out, lse = attend(meta, docs, queries, key_value, held)

    full_out = join(out_pieces, 1, shard)
    full_gate_up = full_units[:, : 2 * units]
    full_down_t = full_units[:, 2 * units :]
    full_key = join(k_pieces, 0, shard)
    full_value = join(v_pieces, 0, shard)
    full_query = join(q_pieces, 0, shard)

    residual = inputs + pair_total(dot(attn_out, full_out))
    normal_two, factor_two = rms_parts(residual)
    normed_two = (normal_two * scale_post).astype(BF16)
    gate_upward = dot(normed_two, full_gate_up)
    gate_act = gate_upward[:, :units]
    upward = gate_upward[:, units:]
    sigma = jax.nn.sigmoid(gate_act)
    silu_act = gate_act * sigma
    hidden = (silu_act * upward).astype(BF16)
    grad_down = dot_tn(cotangent, hidden).astype(BF16)
    cotangent, grad_down = tie(cotangent, grad_down)
    d_hidden = dot(cotangent, full_down_t)
    d_gate = (d_hidden * upward * sigma * (1.0 + gate_act * (1.0 - sigma))).astype(BF16)
    d_up = (d_hidden * silu_act).astype(BF16)
    d_gate_up = jnp.concatenate([d_gate, d_up], axis=1)
    grad_gate_up = dot_tn(normed_two, d_gate_up).astype(BF16)
    d_gate_up, grad_gate_up = tie(d_gate_up, grad_gate_up)
    d_normed_two = pair_total(dot_nt(d_gate_up, full_gate_up))
    hidden, d_normed_two = tie(hidden, d_normed_two)
    mixed_part = dot_nt(hidden, full_down_t)
    mixed = (residual + pair_total(mixed_part)).astype(BF16)
    shared_down = to_shard_owner(grad_down)
    shared_gate_up = to_shard_owner(grad_gate_up)
    grad_post = jnp.sum(d_normed_two * normal_two, axis=0)
    d_residual = cotangent.astype(F32) + rms_back(
        d_normed_two * scale_post, normal_two, factor_two
    )

    d_branch = d_residual.astype(BF16)
    d_attn, shared_down = tie(dot_nt(d_branch, full_out).astype(BF16), shared_down)
    d_queries, d_kv, given = attend_back(
        meta, docs, queries, d_attn, attended, lse, key_value, held
    )
    levels = [1 << b for b in range(count.bit_length() - 1)]
    turned = levels[1:] + levels[:1]
    half_down = halve(shared_down, levels[0])
    d_queries, half_down, *given = tie(d_queries, half_down, *given)
    returned = {}

    def give_back(turns):
        for d in turns:
            returned[d] = lax.ppermute(given[d - 1], "ctx", [(i, i ^ d) for i in range(count)])

    def settle(turns, *values):
        done = tie(*(returned[d] for d in turns), *values)
        returned.update(zip(turns, done))
        return done[len(turns) :]

    far = [d for d in range(1, count) if d >= count // 2]
    near = [d for d in range(1, count) if d < count // 2]
    early = far[: len(far) // 2] + near[: (len(near) + 1) // 2]
    late = far[len(far) // 2 :] + near[(len(near) + 1) // 2 :]
    give_back(early)
    grad_out = dot_tn(d_branch, attn_out).astype(BF16)
    given = list(given)
    d_queries, shared_gate_up, grad_out, *given = settle(
        early, d_queries, shared_gate_up, grad_out, *given
    )
    give_back(late)
    half_gate_up = halve(shared_gate_up, levels[0])
    d_q_pre, gq_part = rope_back(d_queries, q_pre, cosine, sine, scale_q)
    grad_query = dot_tn(normed_input, d_q_pre).astype(BF16)
    out_query = to_shard_owner(jnp.concatenate([grad_out, grad_query], axis=1))
    (half_gate_up,) = settle(late, half_gate_up)
    returned = [returned[d] for d in range(1, count)]

    first = sum(
        jnp.where(part < p, g.astype(F32), 0.0) for p, g in zip(other_parts, returned)
    )
    second = sum(
        jnp.where(part < p, 0.0, g.astype(F32)) for p, g in zip(other_parts, returned)
    )
    d_kv = d_kv + jnp.concatenate([first, second], axis=1)
    d_k_pre, gk_part = rope_back(d_kv[0], k_pre, cosine, sine, scale_k)
    d_v_pre = d_kv[1].astype(BF16)
    d_kv_pre = jnp.concatenate([d_k_pre, d_v_pre], axis=1)
    grad_kv = dot_tn(normed_input, d_kv_pre).astype(BF16)

    steps = 2 * len(levels)
    unit_chain = jnp.concatenate([half_gate_up, half_down], axis=1)
    (unit_chain,) = tie(unit_chain)
    unit_chain = chain_step(unit_chain, levels, 1)
    rest_chain = jnp.concatenate([out_query, to_shard_owner(grad_kv)], axis=1)
    d_normed = pair_total(
        dot_nt(d_q_pre, full_query) + dot_nt(d_k_pre, full_key) + dot_nt(d_v_pre, full_value)
    )
    grad_in = jnp.sum(d_normed * normal_one, axis=0)
    input_grad = d_residual + rms_back(d_normed * scale_in, normal_one, factor_one)
    once = jnp.where(lax.axis_index("tp") == 0, 1.0, 0.0)
    gain_grads = jnp.concatenate([grad_in * once, grad_post * once, gq_part[0], gk_part[0]])
    gain_grads = gain_grads.reshape(-1, HEAD)
    gain_steps = [("tp", 1)] + [("ctx", level) for level in levels]
    if shard_count == 2:
        gain_steps = gain_steps + [("shard", 1)]
    else:
        gain_grads = lax.psum(gain_grads, "shard")

    for step in range(2, steps):
        unit_chain, rest_chain, gain_grads = tie(unit_chain, rest_chain, gain_grads)
        rest_chain = chain_step(rest_chain, turned, step - 2)
        if step == steps - 1:
            unit_chain, rest_chain = tie(unit_chain, rest_chain)
        unit_chain = chain_step(unit_chain, levels, step)
        if gain_steps:
            gain_grads = gain_grads + swap(gain_grads, *gain_steps.pop(0))
    for step in (steps - 2, steps - 1):
        rest_chain = chain_step(rest_chain, turned, step)
    while gain_steps:
        gain_grads = gain_grads + swap(gain_grads, *gain_steps.pop(0))
    gain_grads = gain_grads.reshape(-1)

    owned_units = unit_chain.astype(F32)
    owned_rest = rest_chain.astype(F32)
    cuts = [0, heads_width, 2 * heads_width, 2 * heads_width + kv_width]
    cuts = cuts + [cuts[-1] + kv_width]
    owned_out, owned_query, owned_key, owned_value = (
        owned_rest[:, lo:hi] for lo, hi in zip(cuts[:-1], cuts[1:])
    )
    own_gains = []
    for lo, size in ((0, model), (model, model), (2 * model, HEAD), (2 * model + HEAD, HEAD)):
        size = size // shard_count
        own_gains.append(lax.dynamic_slice_in_dim(gain_grads, lo + shard * size, size, 0))
    return (
        mixed,
        input_grad,
        owned_query,
        owned_key,
        owned_value,
        owned_out.T,
        owned_units[:, :units],
        owned_units[:, units : 2 * units],
        owned_units[:, 2 * units :].T,
        *own_gains,
    )


def solution(mesh):
    placed = (
        P(("shard", "ctx"), None),
        P(("shard", "ctx"), None),
        P("shard", None),
        P(),
        P("shard", "tp"),
        P("shard", "tp"),
        P("shard", "tp"),
        P("tp", "shard"),
        P("shard", "tp"),
        P("shard", "tp"),
        P("tp", "shard"),
        P("shard"),
        P("shard"),
        P("shard"),
        P("shard"),
    )
    return jax.shard_map(
        body,
        mesh=mesh,
        in_specs=placed,
        out_specs=(
            P(("shard", "ctx"), None),
            P(("shard", "ctx"), None),
            P("shard", "tp"),
            P("shard", "tp"),
            P("shard", "tp"),
            P("tp", "shard"),
            P("shard", "tp"),
            P("shard", "tp"),
            P("tp", "shard"),
            P("shard"),
            P("shard"),
            P("shard"),
            P("shard"),
        ),
        check_vma=False,
    )
```

```python
import functools

import jax
import jax.numpy as jnp
from jax import lax
from jax.experimental import pallas as pl
from jax.experimental.pallas import tpu as pltpu
from jax.sharding import PartitionSpec as P

EPS = 1e-06
THETA = 1000000.0
LOG2E = 1.4426950408889634
HEAD = 128
BF16 = jnp.bfloat16
F32 = jnp.float32
VMEM_LIMIT = 48 * 1024 * 1024
CHEAP = pl.CostEstimate(flops=1000, bytes_accessed=1000, transcendentals=0)


def rms_parts(values):
    factor = lax.rsqrt(jnp.mean(values * values, axis=-1, keepdims=True) + EPS)
    return (values * factor, factor)


def rms_back(grad_hat, normal, factor):
    return factor * (grad_hat - normal * jnp.mean(grad_hat * normal, axis=-1, keepdims=True))


def dot(a, b):
    return jnp.dot(a, b, preferred_element_type=F32)


def dot_nt(a, b):
    return lax.dot_general(a, b, (((1,), (1,)), ((), ())), preferred_element_type=F32)


def dot_tn(a, b):
    return lax.dot_general(a, b, (((0,), (0,)), ((), ())), preferred_element_type=F32)


def tie(*values):
    return lax.optimization_barrier(values)


def pieces_of(own, axis):
    count = lax.axis_size(axis)
    return [own] + [
        lax.ppermute(own, axis, [((i + j) % count, i) for i in range(count)])
        for j in range(1, count)
    ]


def join(pieces, dim, index):
    count = len(pieces)
    if count == 1:
        return pieces[0]
    if count == 2:
        return jnp.where(
            index == 0, jnp.concatenate(pieces, dim), jnp.concatenate(pieces[::-1], dim)
        )
    size = pieces[0].shape[dim]
    shape = list(pieces[0].shape)
    shape[dim] = size * count
    whole = jnp.zeros(shape, pieces[0].dtype)
    for j, piece in enumerate(pieces):
        whole = lax.dynamic_update_slice_in_dim(whole, piece, (index + j) % count * size, dim)
    return whole


def pair_total(partial):
    count = lax.axis_size("tp")
    partial = partial.astype(BF16)
    if count != 2:
        return lax.psum(partial, "tp").astype(F32)
    other = lax.ppermute(partial, "tp", [(0, 1), (1, 0)])
    return partial.astype(F32) + other.astype(F32)


def swap(value, axis, level=1):
    count = lax.axis_size(axis)
    return lax.ppermute(value, axis, [(i, i ^ level) for i in range(count)])


def to_shard_owner(*grads):
    count = lax.axis_size("shard")
    index = lax.axis_index("shard")
    if count != 2:
        grad = jnp.concatenate(grads, axis=1)
        return lax.psum_scatter(grad, "shard", scatter_dimension=0, tiled=True).astype(F32)

    def rows_of(owner):
        size = grads[0].shape[0] // 2
        return jnp.concatenate(
            [lax.dynamic_slice_in_dim(g, owner * size, size, 0) for g in grads], axis=1
        )

    return rows_of(index).astype(F32) + swap(rows_of(1 - index), "shard").astype(F32)


def place_in(masks):
    return (lax.axis_index("ctx") // masks[0]) % (1 << len(masks))


def exchange(values, done, turns):
    count = lax.axis_size("ctx")
    for d in turns:
        done[d] = lax.ppermute(values[d], "ctx", [(i, i ^ d) for i in range(count)])


def settle(done, turns, *values):
    tied = tie(*(done[d] for d in turns), *values)
    done.update(zip(turns, tied))
    return tied[len(turns) :]


def halve(value, masks):
    size = 1 << len(masks)
    rows = value.shape[0] // size
    place = place_in(masks)
    total = lax.dynamic_slice_in_dim(value, place * rows, rows, 0)
    for turn in range(1, size):
        sent = lax.dynamic_slice_in_dim(value, (place ^ turn) * rows, rows, 0)
        total = total + swap(sent.astype(BF16), "ctx", turn * masks[0]).astype(F32)
    return total


def double(value, masks):
    value = value.astype(BF16)
    size = 1 << len(masks)
    place = place_in(masks)
    blocks = [value] + [swap(value, "ctx", turn * masks[0]) for turn in range(1, size)]
    bit = 0
    while len(blocks) > 1:
        pairs = zip(blocks[::2], blocks[1::2])
        blocks = [join(list(pair), 0, (place >> bit) % 2) for pair in pairs]
        bit += 1
    return blocks[0]


def product_kernel(a_ref, b_ref, out_ref):
    out_ref[...] = dot_nt(a_ref[...], b_ref[...]).astype(out_ref.dtype)


def product_nt(a, b, dtype, column=0):
    rows, depth = a.shape
    columns = b.shape[0]
    step = min(columns, 256)
    return pl.pallas_call(
        product_kernel,
        grid=(columns // step,),
        in_specs=[
            pl.BlockSpec((rows, depth), lambda i: (0, 0)),
            pl.BlockSpec((step, depth), lambda i: (i, column)),
        ],
        out_specs=pl.BlockSpec((rows, step), lambda i: (0, i)),
        out_shape=jax.ShapeDtypeStruct((rows, columns), dtype),
        compiler_params=pltpu.CompilerParams(vmem_limit_bytes=VMEM_LIMIT),
        cost_estimate=CHEAP,
    )(a, b)


def rope_kernel(pre_ref, cos_ref, sin_ref, gain_ref, out_ref):
    pre = pre_ref[...]
    factor = lax.rsqrt(jnp.mean(pre * pre, axis=-1, keepdims=True) + EPS)
    scaled = pre * factor * gain_ref[...]
    turned = pltpu.roll(scaled, HEAD // 2, 1)
    out_ref[...] = (scaled * cos_ref[...] + turned * sin_ref[...]).astype(BF16)


def rope_and_copy_kernel(roped, pre_ref, plain_ref, cos_ref, sin_ref, gain_ref, out_ref):
    @pl.when(pl.program_id(0) < roped)
    def _():
        rope_kernel(pre_ref, cos_ref, sin_ref, gain_ref, out_ref)

    @pl.when(pl.program_id(0) >= roped)
    def _():
        out_ref[...] = plain_ref[...].astype(BF16)


def rope(pre, cosine, sine, gain, plain=None):
    rows, width = pre.shape
    heads = width // HEAD
    table = pl.BlockSpec((rows, HEAD), lambda h: (0, 0))
    tables = [table, table, pl.BlockSpec((1, HEAD), lambda h: (0, 0))]
    column = pl.BlockSpec((rows, HEAD), lambda h: (0, h))
    if plain is None:
        kernel, steps, columns, values = rope_kernel, heads, [column], [pre]
    else:
        kernel, steps = functools.partial(rope_and_copy_kernel, heads), 2 * heads
        columns = [
            pl.BlockSpec((rows, HEAD), lambda h: (0, jnp.minimum(h, heads - 1))),
            pl.BlockSpec((rows, HEAD), lambda h: (0, jnp.maximum(h - heads, 0))),
        ]
        values = [pre, plain]
    return pl.pallas_call(
        kernel,
        grid=(steps,),
        in_specs=columns + tables,
        out_specs=column,
        out_shape=jax.ShapeDtypeStruct((rows, steps * HEAD), BF16),
        compiler_params=pltpu.CompilerParams(vmem_limit_bytes=VMEM_LIMIT),
    )(*values, cosine, sine, gain)


def rope_back_kernel(grad_ref, pre_ref, cos_ref, sin_ref, gain_ref, out_ref, sum_ref):
    pre = pre_ref[...]
    grad = grad_ref[...]
    factor = lax.rsqrt(jnp.mean(pre * pre, axis=-1, keepdims=True) + EPS)
    hat = pre * factor
    back = grad * cos_ref[...] - pltpu.roll(grad, HEAD // 2, 1) * sin_ref[...]
    terms = jnp.sum(back * hat, axis=0, keepdims=True)

    @pl.when(pl.program_id(0) == 0)
    def _():
        sum_ref[...] = terms

    @pl.when(pl.program_id(0) > 0)
    def _():
        sum_ref[...] += terms

    back = back * gain_ref[...]
    inner = jnp.mean(back * hat, axis=-1, keepdims=True)
    out_ref[...] = (factor * (back - hat * inner)).astype(BF16)


def rope_back(grad, pre, cosine, sine, gain):
    rows, width = grad.shape
    column = pl.BlockSpec((rows, HEAD), lambda h: (0, h))
    table = pl.BlockSpec((rows, HEAD), lambda h: (0, 0))
    one_row = pl.BlockSpec((1, HEAD), lambda h: (0, 0))
    return pl.pallas_call(
        rope_back_kernel,
        grid=(width // HEAD,),
        in_specs=[column, column, table, table, one_row],
        out_specs=[column, one_row],
        out_shape=[
            jax.ShapeDtypeStruct((rows, width), BF16),
            jax.ShapeDtypeStruct((1, HEAD), F32),
        ],
        compiler_params=pltpu.CompilerParams(vmem_limit_bytes=VMEM_LIMIT),
    )(grad, pre, cosine, sine, gain)


def doc_begins(meta_ref, docs, place):
    begin = jnp.zeros_like(place)
    for i in range(1, docs):
        start = meta_ref[i]
        begin = jnp.where(place >= start, start, begin)
    return begin


def block_mask(meta_ref, docs, shape, half, q_part, k_part, diagonal):
    row = lax.broadcasted_iota(jnp.int32, (shape[0], 1), 0)
    q_place = q_part * half + jnp.where(row >= half, row - half, row)
    begin = doc_begins(meta_ref, docs, q_place) - k_part * half
    column = lax.broadcasted_iota(jnp.int32, shape, 1)
    visible = column >= begin
    if diagonal:
        visible = visible & (column <= q_place - k_part * half)
    return visible


def any_visible(meta_ref, docs, half, q_part, k_part):
    return (k_part + 1) * half > doc_begins(meta_ref, docs, q_part * half)


def all_visible(meta_ref, docs, half, q_part, k_part):
    return k_part * half >= doc_begins(meta_ref, docs, q_part * half + half - 1)


def masked(weights, *mask_args):
    if mask_args[-1] is None:
        return weights
    return jnp.where(block_mask(*mask_args), weights, 0.0)


def two_heads(ref, start, half):
    rows = pl.ds(start, half)
    return jnp.concatenate([ref[rows, :HEAD], ref[rows, HEAD:]], axis=0)


def forward_kernel(docs, count, meta_ref, q_ref, k_ref, v_ref, *refs):
    others = refs[: 2 * (count - 1)]
    out_ref, out16_ref, lse_ref, acc_ref = refs[2 * (count - 1) :]
    half = q_ref.shape[0] // 2
    factor = HEAD**-0.5 * LOG2E
    ones = jnp.ones((half, HEAD), BF16)
    own = meta_ref[0]

    def block(start, keys, values, q_part, k_part, diagonal):
        scores = dot_nt(two_heads(q_ref, start, half), keys)
        weights = jnp.exp2(scores * factor)
        weights = masked(weights, meta_ref, docs, scores.shape, half, q_part, k_part, diagonal)
        weights = weights.astype(BF16)
        return dot(weights, jnp.concatenate([values, ones], axis=1))

    for e in range(2):
        rows = pl.ds(e * half, half)
        part = own if e == 0 else 2 * count - 1 - own
        acc_ref[e] = block(e * half, k_ref[rows, :], v_ref[rows, :], part, part, True)
    for d in range(count - 1):
        side = meta_ref[docs + 2 * d]
        k_part = meta_ref[docs + 2 * d + 1]
        q_part = jnp.where(side == 0, own, 2 * count - 1 - own)

        def add(mask):
            start = pl.multiple_of(side * half, half)
            acc_ref[side] += block(
                start, others[2 * d][...], others[2 * d + 1][...], q_part, k_part, mask
            )

        seen = any_visible(meta_ref, docs, half, q_part, k_part)
        whole = all_visible(meta_ref, docs, half, q_part, k_part)
        pl.when(whole)(functools.partial(add, None))
        pl.when(seen & jnp.logical_not(whole))(functools.partial(add, False))

    for e in range(2):
        total = acc_ref[e]
        sums = total[:, HEAD:]
        result = total[:, :HEAD] / sums
        lse = jnp.log2(sums)
        for a in range(2):
            part = slice(a * half, (a + 1) * half)
            place = (pl.ds(e * half, half), slice(a * HEAD, (a + 1) * HEAD))
            out_ref[place] = result[part]
            out16_ref[place] = result[part].astype(BF16)
            lse_ref[place] = lse[part]


def backward_kernel(docs, count, meta_ref, q_ref, g_ref, o_ref, lse_ref, k_ref, v_ref, *refs):
    others = refs[: 2 * (count - 1)]
    dq_ref, dkv_ref = refs[2 * (count - 1) : 2 * count]
    given = refs[2 * count : 3 * count - 1]
    acc_ref, stats_ref, delta_ref = refs[3 * count - 1 :]
    half = q_ref.shape[0] // 2
    scale = HEAD**-0.5
    own = meta_ref[0]

    for e in range(2):
        grads = two_heads(g_ref, e * half, half).astype(F32)
        delta = jnp.sum(grads * two_heads(o_ref, e * half, half), axis=1, keepdims=True)
        delta_ref[e] = jnp.broadcast_to(delta, (2 * half, HEAD))
        stats_ref[e] = two_heads(lse_ref, e * half, half)

    def block(side, start, keys, values, q_part, k_part, diagonal):
        queries = two_heads(q_ref, start, half)
        grads = two_heads(g_ref, start, half)
        scores = dot_nt(queries, keys)
        repeat = half // HEAD
        lse = jnp.concatenate([stats_ref[side]] * repeat, axis=1)
        delta = jnp.concatenate([delta_ref[side]] * repeat, axis=1)
        weights = jnp.exp2(scores * (scale * LOG2E) - lse)
        weights = masked(weights, meta_ref, docs, scores.shape, half, q_part, k_part, diagonal)
        d_weights = dot_nt(grads, values)
        d_scores = (weights * (d_weights - delta)).astype(BF16)
        d_values = dot_tn(weights.astype(BF16), grads)
        d_keys = dot_tn(d_scores, queries) * scale
        return dot(d_scores, keys) * scale, d_keys, d_values

    for e in range(2):
        rows = pl.ds(e * half, half)
        part = own if e == 0 else 2 * count - 1 - own
        d_queries, d_keys, d_values = block(
            e, e * half, k_ref[rows, :], v_ref[rows, :], part, part, True
        )
        acc_ref[e] = d_queries
        dkv_ref[0, rows, :] = d_keys
        dkv_ref[1, rows, :] = d_values
    for d in range(count - 1):
        side = meta_ref[docs + 2 * d]
        k_part = meta_ref[docs + 2 * d + 1]
        q_part = jnp.where(side == 0, own, 2 * count - 1 - own)
        seen = any_visible(meta_ref, docs, half, q_part, k_part)
        whole = all_visible(meta_ref, docs, half, q_part, k_part)

        def add(mask):
            start = pl.multiple_of(side * half, half)
            d_queries, d_keys, d_values = block(
                side, start, others[2 * d][...], others[2 * d + 1][...], q_part, k_part, mask
            )
            acc_ref[side] += d_queries
            given[d][0] = d_keys.astype(BF16)
            given[d][1] = d_values.astype(BF16)

        pl.when(whole)(functools.partial(add, None))
        pl.when(seen & jnp.logical_not(whole))(functools.partial(add, False))

        @pl.when(jnp.logical_not(seen))
        def _():
            given[d][...] = jnp.zeros_like(given[d])

    for e in range(2):
        for a in range(2):
            dq_ref[pl.ds(e * half, half), a * HEAD : (a + 1) * HEAD] = acc_ref[
                e, a * half : (a + 1) * half, :
            ]


def key_value_specs(rows, half, kv_heads, count):
    own = [
        pl.BlockSpec((rows, HEAD), lambda h, m: (0, h)),
        pl.BlockSpec((rows, HEAD), lambda h, m: (0, kv_heads + h)),
    ]
    other = [
        pl.BlockSpec((half, HEAD), lambda h, m: (0, h)),
        pl.BlockSpec((half, HEAD), lambda h, m: (0, kv_heads + h)),
    ]
    return own + other * (count - 1)


def twice(arrays):
    return [a for a in arrays for _ in range(2)]


def attend(meta, docs, queries, key_value, others):
    rows, width = queries.shape
    half = rows // 2
    count = len(others) + 1
    kv_heads = key_value.shape[1] // (2 * HEAD)
    column = pl.BlockSpec((rows, 2 * HEAD), lambda h, m: (0, h))
    return pl.pallas_call(
        functools.partial(forward_kernel, docs, count),
        grid_spec=pltpu.PrefetchScalarGridSpec(
            num_scalar_prefetch=1,
            grid=(kv_heads,),
            in_specs=[column] + key_value_specs(rows, half, kv_heads, count),
            out_specs=[column] * 3,
            scratch_shapes=[pltpu.VMEM((2, 2 * half, 2 * HEAD), F32)],
        ),
        out_shape=[
            jax.ShapeDtypeStruct((rows, width), F32),
            jax.ShapeDtypeStruct((rows, width), BF16),
            jax.ShapeDtypeStruct((rows, width), F32),
        ],
        compiler_params=pltpu.CompilerParams(vmem_limit_bytes=VMEM_LIMIT),
        cost_estimate=CHEAP,
    )(meta, queries, key_value, key_value, *twice(others))


def attend_back(meta, docs, queries, grads, outs, lse, key_value, others):
    rows, width = queries.shape
    half = rows // 2
    count = len(others) + 1
    kv_width = key_value.shape[1] // 2
    kv_heads = kv_width // HEAD
    column = pl.BlockSpec((rows, 2 * HEAD), lambda h, m: (0, h))
    result = pl.pallas_call(
        functools.partial(backward_kernel, docs, count),
        grid_spec=pltpu.PrefetchScalarGridSpec(
            num_scalar_prefetch=1,
            grid=(kv_heads,),
            in_specs=[column] * 4 + key_value_specs(rows, half, kv_heads, count),
            out_specs=[column, pl.BlockSpec((2, rows, HEAD), lambda h, m: (0, 0, h))]
            + [pl.BlockSpec((2, half, HEAD), lambda h, m: (0, 0, h))] * (count - 1),
            scratch_shapes=[pltpu.VMEM((2, 2 * half, HEAD), F32)] * 3,
        ),
        out_shape=[
            jax.ShapeDtypeStruct((rows, width), F32),
            jax.ShapeDtypeStruct((2, rows, kv_width), F32),
        ]
        + [jax.ShapeDtypeStruct((2, half, kv_width), BF16)] * (count - 1),
        compiler_params=pltpu.CompilerParams(vmem_limit_bytes=VMEM_LIMIT),
        cost_estimate=CHEAP,
    )(meta, queries, grads, outs, lse, key_value, key_value, *twice(others))
    return result[0], result[1], list(result[2:])


def body(
    tokens,
    cotangent,
    seq_lengths,
    part_order,
    w_query,
    key_weight,
    value_weight,
    w_out,
    w_gate,
    w_up,
    w_down,
    gain_in,
    gain_post,
    gain_q,
    gain_k,
):
    shard_count = lax.axis_size("shard")
    shard = lax.axis_index("shard")
    count = lax.axis_size("ctx")
    ctx = lax.axis_index("ctx")
    rows, model = tokens.shape
    half = rows // 2
    depth = model // shard_count
    docs = seq_lengths.shape[1]
    kv_width = key_weight.shape[1]
    units = w_gate.shape[1]
    heads_width = w_out.shape[0]

    packed = jnp.concatenate([gain_in, gain_post, gain_q, gain_k])
    packed_pieces = pieces_of(packed, "shard")
    k_pieces = pieces_of(key_weight, "shard")
    v_pieces = pieces_of(value_weight, "shard")
    own_units = jnp.concatenate([w_gate, w_up, w_down.T], axis=1)

    lengths = seq_lengths[0]
    starts = jnp.cumsum(lengths) - lengths
    parts = part_order[:, 0]
    part = parts[ctx]
    other_parts = [parts[ctx ^ d] for d in range(1, count)]
    sides = [jnp.where(p < part, 0, 1).astype(jnp.int32) for p in other_parts]
    held_parts = [jnp.where(p < part, p, 2 * count - 1 - p) for p in other_parts]
    meta = jnp.stack(
        [part]
        + [starts[i] for i in range(1, docs)]
        + [v for pair in zip(sides, held_parts) for v in pair]
    ).astype(jnp.int32)
    places = jnp.concatenate(
        [p * half + jnp.arange(half, dtype=jnp.int32) for p in (part, 2 * count - 1 - part)]
    )
    begins = jnp.zeros_like(places)
    for i in range(1, docs):
        begins = jnp.where(places >= starts[i], starts[i], begins)
    frequency = THETA ** (-jnp.arange(0, HEAD, 2, dtype=F32) / HEAD)
    angles = (places - begins).astype(F32)[:, None] * frequency[None, :]
    cosine, sine = jnp.cos(angles), jnp.sin(angles)
    cosine = jnp.concatenate([cosine, cosine], axis=-1)
    sine = jnp.concatenate([-sine, sine], axis=-1)

    inputs = tokens.astype(F32)
    normal_one, factor_one = rms_parts(inputs)

    w_query, own_units, packed_pieces[-1], k_pieces[-1], v_pieces[-1] = tie(
        w_query, own_units, packed_pieces[-1], k_pieces[-1], v_pieces[-1]
    )
    cosine, sine, meta, normal_one, k_pieces[-1] = tie(
        cosine, sine, meta, normal_one, k_pieces[-1]
    )
    cuts = [0, depth, 2 * depth, 2 * depth + gain_q.shape[0], packed.shape[0]]
    gain_pieces = [
        [piece[lo:hi].astype(F32) for piece in packed_pieces]
        for lo, hi in zip(cuts[:-1], cuts[1:])
    ]
    scale_in, scale_post, scale_q, scale_k = (
        join(pieces, 0, shard).reshape(1, -1) for pieces in gain_pieces
    )
    parts_in = []
    for j in range(shard_count):
        at = (shard + j) % shard_count * depth
        part_in = lax.dynamic_slice_in_dim(normal_one, at, depth, 1)
        parts_in.append((part_in * gain_pieces[0][j][None, :]).astype(BF16))
    normed_input = (normal_one * scale_in).astype(BF16)

    def project(pieces):
        return sum(dot(part_in, piece) for part_in, piece in zip(parts_in, pieces))

    q_pieces = pieces_of(w_query, "shard")
    full_units = lax.all_gather(own_units, "shard", axis=0, tiled=True)
    k_pre = project(k_pieces)
    key_value = rope(k_pre, cosine, sine, scale_k, project(v_pieces))
    far = [d for d in range(1, count) if d >= count // 2]
    near = [d for d in range(1, count) if d < count // 2]
    early = far[: len(far) // 2] + near[: (len(near) + 1) // 2]
    late = far[len(far) // 2 :] + near[(len(near) + 1) // 2 :]
    sent = {}
    for d in early + late:
        start = jnp.where(part < other_parts[d - 1], 0, half)
        sent[d] = lax.dynamic_slice_in_dim(key_value, start, half, 0)
    held = {}
    exchange(sent, held, early)
    w_out, q_pieces[-1], *rest = settle(held, early, w_out, q_pieces[-1], *(sent[d] for d in late))
    sent.update(zip(late, rest))

    exchange(sent, held, late)
    out_pieces = pieces_of(w_out, "shard")
    q_pre = project(q_pieces)
    queries = rope(q_pre, cosine, sine, scale_q)
    queries, full_out = settle(held, late, queries, join(out_pieces, 1, shard))
    held = [held[d] for d in range(1, count)]
    attended, attn_out, lse = attend(meta, docs, queries, key_value, held)

    full_gate_up = full_units[:, : 2 * units]
    full_down_t = full_units[:, 2 * units :]
    full_key = join(k_pieces, 0, shard)
    full_value = join(v_pieces, 0, shard)
    full_query = join(q_pieces, 0, shard)

    residual = inputs + pair_total(dot(attn_out, full_out))
    normal_two, factor_two = rms_parts(residual)
    normed_two = (normal_two * scale_post).astype(BF16)
    gate_upward = dot(normed_two, full_gate_up)
    gate_act = gate_upward[:, :units]
    upward = gate_upward[:, units:]
    sigma = jax.nn.sigmoid(gate_act)
    silu_act = gate_act * sigma
    hidden = (silu_act * upward).astype(BF16)
    grad_down = dot_tn(cotangent, hidden).astype(BF16)
    cotangent, grad_down = tie(cotangent, grad_down)
    d_hidden = dot(cotangent, full_down_t)
    d_gate = (d_hidden * upward * sigma * (1.0 + gate_act * (1.0 - sigma))).astype(BF16)
    d_up = (d_hidden * silu_act).astype(BF16)
    d_gate_up = jnp.concatenate([d_gate, d_up], axis=1)
    grad_gate_up = dot_tn(normed_two, d_gate_up).astype(BF16)
    d_gate_up, grad_gate_up = tie(d_gate_up, grad_gate_up)
    d_normed_two = pair_total(product_nt(d_gate_up, full_units, BF16))
    hidden, d_normed_two = tie(hidden, d_normed_two)
    mixed_part = product_nt(hidden, full_units, BF16, 2)
    mixed = (residual + pair_total(mixed_part)).astype(BF16)
    shared_units = to_shard_owner(grad_gate_up, grad_down)
    grad_post = jnp.sum(d_normed_two * normal_two, axis=0)
    d_residual = cotangent.astype(F32) + rms_back(
        d_normed_two * scale_post, normal_two, factor_two
    )

    d_branch = d_residual.astype(BF16)
    d_attn = product_nt(d_branch, full_out, BF16)
    d_queries, d_kv, given = attend_back(
        meta, docs, queries, d_attn, attended, lse, key_value, held
    )
    masks = [1 << b for b in range(count.bit_length() - 1)]
    near_axis, far_axis = masks[:1], masks[1:]
    given = dict(zip(range(1, count), given))
    returned = {}
    exchange(given, returned, early)
    grad_out = dot_tn(d_branch, attn_out).astype(BF16)
    d_queries, shared_units, grad_out, *rest = settle(
        returned, early, d_queries, shared_units, grad_out, *(given[d] for d in late)
    )
    given.update(zip(late, rest))
    exchange(given, returned, late)
    unit_chain = halve(shared_units, near_axis)
    d_q_pre, gq_part = rope_back(d_queries, q_pre, cosine, sine, scale_q)
    grad_query = dot_tn(normed_input, d_q_pre).astype(BF16)
    out_query = to_shard_owner(grad_out, grad_query)
    (unit_chain,) = settle(returned, late, unit_chain)
    returned = [returned[d] for d in range(1, count)]

    first = sum(
        jnp.where(part < p, g.astype(F32), 0.0) for p, g in zip(other_parts, returned)
    )
    second = sum(
        jnp.where(part < p, 0.0, g.astype(F32)) for p, g in zip(other_parts, returned)
    )
    d_kv = d_kv + jnp.concatenate([first, second], axis=1)
    d_k_pre, gk_part = rope_back(d_kv[0], k_pre, cosine, sine, scale_k)
    d_v_pre = d_kv[1].astype(BF16)
    d_kv_pre = jnp.concatenate([d_k_pre, d_v_pre], axis=1)
    grad_kv = dot_tn(normed_input, d_kv_pre).astype(BF16)

    unit_chain = halve(unit_chain, far_axis)
    rest_chain = jnp.concatenate([out_query, to_shard_owner(grad_kv)], axis=1)
    unit_chain, rest_chain, d_q_pre, d_k_pre, d_v_pre = tie(
        unit_chain, rest_chain, d_q_pre, d_k_pre, d_v_pre
    )

    unit_chain = double(unit_chain, far_axis)
    rest_chain = halve(rest_chain, near_axis)
    d_normed = pair_total(
        dot_nt(d_q_pre, full_query) + dot_nt(d_k_pre, full_key) + dot_nt(d_v_pre, full_value)
    )
    grad_in = jnp.sum(d_normed * normal_one, axis=0)
    input_grad = d_residual + rms_back(d_normed * scale_in, normal_one, factor_one)
    once = jnp.where(lax.axis_index("tp") == 0, 1.0, 0.0)
    gain_grads = jnp.concatenate([grad_in * once, grad_post * once, gq_part[0], gk_part[0]])
    gain_grads = gain_grads.reshape(-1, HEAD)
    if shard_count != 2:
        gain_grads = lax.psum(gain_grads, "shard")
    unit_chain, rest_chain, gain_grads = tie(unit_chain, rest_chain, gain_grads)

    owned_gate_up = double(unit_chain[:, : 2 * units], near_axis)
    owned_down = unit_chain[:, 2 * units :]
    rest_chain = halve(rest_chain, far_axis)
    gain_grads = gain_grads + swap(gain_grads, "tp")
    gain_grads = gain_grads + swap(gain_grads, "ctx", masks[0])
    owned_gate_up, owned_down, rest_chain, gain_grads = tie(
        owned_gate_up, owned_down, rest_chain, gain_grads
    )

    owned_down = double(owned_down, near_axis)
    rest_chain = double(rest_chain, far_axis)
    for mask in masks[1:]:
        gain_grads = gain_grads + swap(gain_grads, "ctx", mask)
    owned_down, rest_chain, gain_grads = tie(owned_down, rest_chain, gain_grads)

    rest_chain = double(rest_chain, near_axis)
    if shard_count == 2:
        gain_grads = gain_grads + swap(gain_grads, "shard")
    gain_grads = gain_grads.reshape(-1)
    owned_gate_up = owned_gate_up.astype(F32)
    owned_down = owned_down.astype(F32)
    owned_rest = rest_chain.astype(F32)
    cuts = [0, heads_width, 2 * heads_width, 2 * heads_width + kv_width]
    cuts = cuts + [cuts[-1] + kv_width]
    owned_out, owned_query, owned_key, owned_value = (
        owned_rest[:, lo:hi] for lo, hi in zip(cuts[:-1], cuts[1:])
    )
    own_gains = []
    for lo, size in ((0, model), (model, model), (2 * model, HEAD), (2 * model + HEAD, HEAD)):
        size = size // shard_count
        own_gains.append(lax.dynamic_slice_in_dim(gain_grads, lo + shard * size, size, 0))
    return (
        mixed,
        input_grad,
        owned_query,
        owned_key,
        owned_value,
        owned_out.T,
        owned_gate_up[:, :units],
        owned_gate_up[:, units:],
        owned_down.T,
        *own_gains,
    )


def solution(mesh):
    placed = (
        P(("shard", "ctx"), None),
        P(("shard", "ctx"), None),
        P("shard", None),
        P(),
        P("shard", "tp"),
        P("shard", "tp"),
        P("shard", "tp"),
        P("tp", "shard"),
        P("shard", "tp"),
        P("shard", "tp"),
        P("tp", "shard"),
        P("shard"),
        P("shard"),
        P("shard"),
        P("shard"),
    )
    return jax.shard_map(
        body,
        mesh=mesh,
        in_specs=placed,
        out_specs=(
            P(("shard", "ctx"), None),
            P(("shard", "ctx"), None),
            P("shard", "tp"),
            P("shard", "tp"),
            P("shard", "tp"),
            P("tp", "shard"),
            P("shard", "tp"),
            P("shard", "tp"),
            P("tp", "shard"),
            P("shard"),
            P("shard"),
            P("shard"),
            P("shard"),
        ),
        check_vma=False,
    )
```

```python
import functools

import jax
import jax.numpy as jnp
from jax import lax
from jax.experimental import pallas as pl
from jax.experimental.pallas import tpu as pltpu
from jax.sharding import PartitionSpec as P

EPS = 1e-06
THETA = 1000000.0
LOG2E = 1.4426950408889634
HEAD = 128
BF16 = jnp.bfloat16
F32 = jnp.float32
VMEM_LIMIT = 48 * 1024 * 1024
CHEAP = pl.CostEstimate(flops=1000, bytes_accessed=1000, transcendentals=0)


def rms_parts(values):
    factor = lax.rsqrt(jnp.mean(values * values, axis=-1, keepdims=True) + EPS)
    return (values * factor, factor)


def rms_back(grad_hat, normal, factor):
    return factor * (grad_hat - normal * jnp.mean(grad_hat * normal, axis=-1, keepdims=True))


def dot(a, b):
    return jnp.dot(a, b, preferred_element_type=F32)


def dot_nt(a, b):
    return lax.dot_general(a, b, (((1,), (1,)), ((), ())), preferred_element_type=F32)


def dot_tn(a, b):
    return lax.dot_general(a, b, (((0,), (0,)), ((), ())), preferred_element_type=F32)


def tie(*values):
    return lax.optimization_barrier(values)


def pieces_of(own, axis):
    count = lax.axis_size(axis)
    return [own] + [
        lax.ppermute(own, axis, [((i + j) % count, i) for i in range(count)])
        for j in range(1, count)
    ]


def join(pieces, dim, index):
    count = len(pieces)
    if count == 1:
        return pieces[0]
    if count == 2:
        return jnp.where(
            index == 0, jnp.concatenate(pieces, dim), jnp.concatenate(pieces[::-1], dim)
        )
    size = pieces[0].shape[dim]
    shape = list(pieces[0].shape)
    shape[dim] = size * count
    whole = jnp.zeros(shape, pieces[0].dtype)
    for j, piece in enumerate(pieces):
        whole = lax.dynamic_update_slice_in_dim(whole, piece, (index + j) % count * size, dim)
    return whole


def pair_total(partial):
    count = lax.axis_size("tp")
    partial = partial.astype(BF16)
    if count != 2:
        return lax.psum(partial, "tp").astype(F32)
    other = lax.ppermute(partial, "tp", [(0, 1), (1, 0)])
    return partial.astype(F32) + other.astype(F32)


def swap(value, axis, level=1):
    count = lax.axis_size(axis)
    return lax.ppermute(value, axis, [(i, i ^ level) for i in range(count)])


def place_in(masks):
    return (lax.axis_index("ctx") // masks[0]) % (1 << len(masks))


def exchange(values, done, turns):
    count = lax.axis_size("ctx")
    for d in turns:
        done[d] = lax.ppermute(values[d], "ctx", [(i, i ^ d) for i in range(count)])


def settle(done, turns, *values):
    tied = tie(*(done[d] for d in turns), *values)
    done.update(zip(turns, tied))
    return tied[len(turns) :]


def total(addends):
    return sum(a.astype(F32) for a in addends).astype(BF16)


def rows_at(addends, block, rows):
    return [lax.dynamic_slice_in_dim(a, block * rows, rows, 0) for a in addends]


def halve(addends, masks):
    size = 1 << len(masks)
    rows = addends[0].shape[0] // size
    place = place_in(masks)
    kept = rows_at(addends, place, rows)
    for turn in range(1, size):
        sent = total(rows_at(addends, place ^ turn, rows))
        kept = kept + [swap(sent, "ctx", turn * masks[0])]
    return kept


def over_shard(pairs):
    count = lax.axis_size("shard")
    index = lax.axis_index("shard")
    if count != 2:
        grads = [dot_tn(a, b[:, lo:hi]).astype(BF16) for a, b, lo, hi in pairs]
        grad = jnp.concatenate(grads, axis=1)
        return [lax.psum_scatter(grad, "shard", scatter_dimension=0, tiled=True)]
    away, home = 2 * (1 - index), 2 * index
    sent = split_product((away, away + 1), pairs)
    return [split_product((home, home + 1), pairs), swap(sent, "shard")]


def over_near_then_shard(pairs, near_axis):
    count = lax.axis_size("shard")
    index = lax.axis_index("shard")
    bit = place_in(near_axis)
    if count != 2:
        return halve(over_shard(pairs), near_axis), None
    sent = split_product((1 - bit, 3 - bit), pairs)
    addends = [split_product((bit, 2 + bit), pairs), swap(sent, "ctx", near_axis[0])]
    rows = addends[0].shape[0] // 2
    return rows_at(addends, index, rows), lambda: rows_at(addends, 1 - index, rows)


def double(value, masks):
    size = 1 << len(masks)
    place = place_in(masks)
    blocks = [value] + [swap(value, "ctx", turn * masks[0]) for turn in range(1, size)]
    bit = 0
    while len(blocks) > 1:
        pairs = zip(blocks[::2], blocks[1::2])
        blocks = [join(list(pair), 0, (place >> bit) % 2) for pair in pairs]
        bit += 1
    return blocks[0]


def product_kernel(count, *refs):
    products = [dot_nt(refs[2 * i][...], refs[2 * i + 1][...]) for i in range(count)]
    refs[-1][...] = sum(products).astype(BF16)


def product_nt(*terms):
    rows = terms[0][0].shape[0]
    columns = terms[0][1].shape[0]
    step = min(columns, 256)
    specs, values = [], []
    for a, b, column in terms:
        depth = a.shape[1]
        specs.append(pl.BlockSpec((rows, depth), lambda i: (0, 0)))
        specs.append(pl.BlockSpec((step, depth), lambda i, column=column: (i, column)))
        values += [a, b]
    return pl.pallas_call(
        functools.partial(product_kernel, len(terms)),
        grid=(columns // step,),
        in_specs=specs,
        out_specs=pl.BlockSpec((rows, step), lambda i: (0, i)),
        out_shape=jax.ShapeDtypeStruct((rows, columns), BF16),
        compiler_params=pltpu.CompilerParams(vmem_limit_bytes=VMEM_LIMIT),
        cost_estimate=CHEAP,
    )(*values)


def split_product_kernel(spans, which_ref, *refs):
    j = pl.program_id(1)
    for i, (lo, hi) in enumerate(spans):

        @pl.when((j >= lo) & (j < hi))
        def _():
            refs[-1][...] = dot_tn(refs[2 * i][...], refs[2 * i + 1][...]).astype(BF16)


def split_product(which, pairs):
    tokens, model = pairs[0][0].shape
    rows = model // 4
    step = min(hi - lo for a, b, lo, hi in pairs)
    specs, values, spans, done = [], [], [], 0
    for a, b, lo, hi in pairs:
        blocks = (hi - lo) // step

        def column(i, j, w, first=done, base=lo // step, blocks=blocks):
            return (0, base + jnp.clip(j - first, 0, blocks - 1))

        specs.append(pl.BlockSpec((tokens, rows), lambda i, j, w: (0, w[i])))
        specs.append(pl.BlockSpec((tokens, step), column))
        values += [a, b]
        spans.append((done, done + blocks))
        done += blocks
    return pl.pallas_call(
        functools.partial(split_product_kernel, spans),
        grid_spec=pltpu.PrefetchScalarGridSpec(
            num_scalar_prefetch=1,
            grid=(2, done),
            in_specs=specs,
            out_specs=pl.BlockSpec((rows, step), lambda i, j, w: (i, j)),
        ),
        out_shape=jax.ShapeDtypeStruct((2 * rows, done * step), BF16),
        compiler_params=pltpu.CompilerParams(vmem_limit_bytes=VMEM_LIMIT),
        cost_estimate=CHEAP,
    )(jnp.stack(which).astype(jnp.int32), *values)


def rope_kernel(pre_ref, cos_ref, sin_ref, gain_ref, out_ref):
    pre = pre_ref[...]
    factor = lax.rsqrt(jnp.mean(pre * pre, axis=-1, keepdims=True) + EPS)
    scaled = pre * factor * gain_ref[...]
    turned = pltpu.roll(scaled, HEAD // 2, 1)
    out_ref[...] = (scaled * cos_ref[...] + turned * sin_ref[...]).astype(BF16)


def rope(pre, cosine, sine, gain):
    rows, width = pre.shape
    table = pl.BlockSpec((rows, HEAD), lambda h: (0, 0))
    column = pl.BlockSpec((rows, HEAD), lambda h: (0, h))
    return pl.pallas_call(
        rope_kernel,
        grid=(width // HEAD,),
        in_specs=[column, table, table, pl.BlockSpec((1, HEAD), lambda h: (0, 0))],
        out_specs=column,
        out_shape=jax.ShapeDtypeStruct((rows, width), BF16),
        compiler_params=pltpu.CompilerParams(vmem_limit_bytes=VMEM_LIMIT),
        cost_estimate=CHEAP,
    )(pre, cosine, sine, gain)


def part_start(meta_ref, docs, d, half):
    return pl.multiple_of((1 - meta_ref[docs + d]) * half, half)


def key_value_kernel(heads, docs, count, meta_ref, key_ref, value_ref, *refs):
    cos_ref, sin_ref, gain_ref, out_ref = refs[:4]
    half = out_ref.shape[0] // 2

    @pl.when(pl.program_id(0) < heads)
    def _():
        rope_kernel(key_ref, cos_ref, sin_ref, gain_ref, out_ref)

    @pl.when(pl.program_id(0) >= heads)
    def _():
        out_ref[...] = value_ref[...].astype(BF16)

    for d, sent_ref in enumerate(refs[4:]):
        sent_ref[...] = out_ref[pl.ds(part_start(meta_ref, docs, d, half), half), :]


def key_value_and_parts(meta, docs, count, key, value, cosine, sine, gain):
    rows, width = key.shape
    heads = width // HEAD
    table = pl.BlockSpec((rows, HEAD), lambda h, m: (0, 0))
    column = pl.BlockSpec((rows, HEAD), lambda h, m: (0, h))
    part = pl.BlockSpec((rows // 2, HEAD), lambda h, m: (0, h))
    result = pl.pallas_call(
        functools.partial(key_value_kernel, heads, docs, count),
        grid_spec=pltpu.PrefetchScalarGridSpec(
            num_scalar_prefetch=1,
            grid=(2 * heads,),
            in_specs=[
                pl.BlockSpec((rows, HEAD), lambda h, m: (0, jnp.minimum(h, heads - 1))),
                pl.BlockSpec((rows, HEAD), lambda h, m: (0, jnp.maximum(h - heads, 0))),
                table,
                table,
                pl.BlockSpec((1, HEAD), lambda h, m: (0, 0)),
            ],
            out_specs=[column] + [part] * (count - 1),
        ),
        out_shape=[jax.ShapeDtypeStruct((rows, 2 * width), BF16)]
        + [jax.ShapeDtypeStruct((rows // 2, 2 * width), BF16)] * (count - 1),
        compiler_params=pltpu.CompilerParams(vmem_limit_bytes=VMEM_LIMIT),
        cost_estimate=CHEAP,
    )(meta, key, value, cosine, sine, gain)
    return result[0], dict(zip(range(1, count), result[1:]))


def turn_back(grad, pre_ref, cos_ref, sin_ref, gain_ref, out_ref, sum_ref):
    pre = pre_ref[...]
    factor = lax.rsqrt(jnp.mean(pre * pre, axis=-1, keepdims=True) + EPS)
    hat = pre * factor
    back = grad * cos_ref[...] - pltpu.roll(grad, HEAD // 2, 1) * sin_ref[...]
    terms = jnp.sum(back * hat, axis=0, keepdims=True)

    @pl.when(pl.program_id(0) == 0)
    def _():
        sum_ref[...] = terms

    @pl.when(pl.program_id(0) > 0)
    def _():
        sum_ref[...] += terms

    back = back * gain_ref[...]
    inner = jnp.mean(back * hat, axis=-1, keepdims=True)
    out_ref[...] = (factor * (back - hat * inner)).astype(BF16)


def rope_back_kernel(grad_ref, *refs):
    turn_back(grad_ref[...], *refs)


def key_value_back_kernel(docs, meta_ref, own_ref, *refs):
    returned = refs[:-8]
    key_ref, cos_ref, sin_ref, gain_ref, d_key_ref, d_value_ref, sum_ref, acc_ref = refs[-8:]
    half = key_ref.shape[0] // 2
    acc_ref[...] = own_ref[...]
    for d, given_ref in enumerate(returned):
        rows = pl.ds(part_start(meta_ref, docs, d, half), half)
        acc_ref[:, rows, :] += given_ref[...].astype(F32)
    d_value_ref[...] = acc_ref[1].astype(BF16)
    turn_back(acc_ref[0], key_ref, cos_ref, sin_ref, gain_ref, d_key_ref, sum_ref)


def key_value_back(meta, docs, own, returned, key, cosine, sine, gain):
    rows, width = key.shape
    table = pl.BlockSpec((rows, HEAD), lambda h, m: (0, 0))
    column = pl.BlockSpec((rows, HEAD), lambda h, m: (0, h))
    one_row = pl.BlockSpec((1, HEAD), lambda h, m: (0, 0))
    return pl.pallas_call(
        functools.partial(key_value_back_kernel, docs),
        grid_spec=pltpu.PrefetchScalarGridSpec(
            num_scalar_prefetch=1,
            grid=(width // HEAD,),
            in_specs=[pl.BlockSpec((2, rows, HEAD), lambda h, m: (0, 0, h))]
            + [pl.BlockSpec((2, rows // 2, HEAD), lambda h, m: (0, 0, h))] * len(returned)
            + [column, table, table, one_row],
            out_specs=[column, column, one_row],
            scratch_shapes=[pltpu.VMEM((2, rows, HEAD), F32)],
        ),
        out_shape=[
            jax.ShapeDtypeStruct((rows, width), BF16),
            jax.ShapeDtypeStruct((rows, width), BF16),
            jax.ShapeDtypeStruct((1, HEAD), F32),
        ],
        compiler_params=pltpu.CompilerParams(vmem_limit_bytes=VMEM_LIMIT),
        cost_estimate=CHEAP,
    )(meta, own, *returned, key, cosine, sine, gain)


def rope_back(grad, pre, cosine, sine, gain):
    rows, width = grad.shape
    column = pl.BlockSpec((rows, HEAD), lambda h: (0, h))
    table = pl.BlockSpec((rows, HEAD), lambda h: (0, 0))
    one_row = pl.BlockSpec((1, HEAD), lambda h: (0, 0))
    return pl.pallas_call(
        rope_back_kernel,
        grid=(width // HEAD,),
        in_specs=[column, column, table, table, one_row],
        out_specs=[column, one_row],
        out_shape=[
            jax.ShapeDtypeStruct((rows, width), BF16),
            jax.ShapeDtypeStruct((1, HEAD), F32),
        ],
        compiler_params=pltpu.CompilerParams(vmem_limit_bytes=VMEM_LIMIT),
    )(grad, pre, cosine, sine, gain)


def doc_begins(meta_ref, docs, place):
    begin = jnp.zeros_like(place)
    for i in range(1, docs):
        start = meta_ref[i]
        begin = jnp.where(place >= start, start, begin)
    return begin


def block_mask(meta_ref, docs, shape, half, q_part, k_part, diagonal):
    row = lax.broadcasted_iota(jnp.int32, (shape[0], 1), 0)
    q_place = q_part * half + jnp.where(row >= half, row - half, row)
    begin = doc_begins(meta_ref, docs, q_place) - k_part * half
    column = lax.broadcasted_iota(jnp.int32, shape, 1)
    visible = column >= begin
    if diagonal:
        visible = visible & (column <= q_place - k_part * half)
    return visible


def any_visible(meta_ref, docs, half, q_part, k_part):
    return (k_part + 1) * half > doc_begins(meta_ref, docs, q_part * half)


def all_visible(meta_ref, docs, half, q_part, k_part):
    return k_part * half >= doc_begins(meta_ref, docs, q_part * half + half - 1)


def masked(weights, *mask_args):
    if mask_args[-1] is None:
        return weights
    return jnp.where(block_mask(*mask_args), weights, 0.0)


def two_heads(ref, start, half):
    rows = pl.ds(start, half)
    return jnp.concatenate([ref[rows, :HEAD], ref[rows, HEAD:]], axis=0)


def forward_kernel(docs, count, meta_ref, q_ref, k_ref, v_ref, *refs):
    others = refs[: 2 * (count - 1)]
    out_ref, out16_ref, lse_ref, acc_ref = refs[2 * (count - 1) :]
    half = q_ref.shape[0] // 2
    factor = HEAD**-0.5 * LOG2E
    ones = jnp.ones((half, HEAD), BF16)
    own = meta_ref[0]

    def block(start, keys, values, q_part, k_part, diagonal):
        scores = dot_nt(two_heads(q_ref, start, half), keys)
        weights = jnp.exp2(scores * factor)
        weights = masked(weights, meta_ref, docs, scores.shape, half, q_part, k_part, diagonal)
        weights = weights.astype(BF16)
        return dot(weights, jnp.concatenate([values, ones], axis=1))

    for e in range(2):
        rows = pl.ds(e * half, half)
        part = own if e == 0 else 2 * count - 1 - own
        acc_ref[e] = block(e * half, k_ref[rows, :], v_ref[rows, :], part, part, True)
    for d in range(count - 1):
        side = meta_ref[docs + d]
        k_part = meta_ref[docs + count - 1 + d]
        q_part = jnp.where(side == 0, own, 2 * count - 1 - own)

        def add(mask):
            start = pl.multiple_of(side * half, half)
            acc_ref[side] += block(
                start, others[2 * d][...], others[2 * d + 1][...], q_part, k_part, mask
            )

        seen = any_visible(meta_ref, docs, half, q_part, k_part)
        whole = all_visible(meta_ref, docs, half, q_part, k_part)
        pl.when(whole)(functools.partial(add, None))
        pl.when(seen & jnp.logical_not(whole))(functools.partial(add, False))

    for e in range(2):
        total = acc_ref[e]
        sums = total[:, HEAD:]
        result = total[:, :HEAD] / sums
        lse = jnp.log2(sums)
        for a in range(2):
            part = slice(a * half, (a + 1) * half)
            place = (pl.ds(e * half, half), slice(a * HEAD, (a + 1) * HEAD))
            out_ref[place] = result[part]
            out16_ref[place] = result[part].astype(BF16)
            lse_ref[place] = lse[part]


def backward_kernel(docs, count, meta_ref, q_ref, g_ref, o_ref, lse_ref, k_ref, v_ref, *refs):
    others = refs[: 2 * (count - 1)]
    dq_ref, dkv_ref = refs[2 * (count - 1) : 2 * count]
    given = refs[2 * count : 3 * count - 1]
    acc_ref, stats_ref, delta_ref = refs[3 * count - 1 :]
    half = q_ref.shape[0] // 2
    scale = HEAD**-0.5
    own = meta_ref[0]

    for e in range(2):
        grads = two_heads(g_ref, e * half, half).astype(F32)
        delta = jnp.sum(grads * two_heads(o_ref, e * half, half), axis=1, keepdims=True)
        delta_ref[e] = jnp.broadcast_to(delta, (2 * half, HEAD))
        stats_ref[e] = two_heads(lse_ref, e * half, half)

    def block(side, start, keys, values, q_part, k_part, diagonal):
        queries = two_heads(q_ref, start, half)
        grads = two_heads(g_ref, start, half)
        scores = dot_nt(queries, keys)
        repeat = half // HEAD
        lse = jnp.concatenate([stats_ref[side]] * repeat, axis=1)
        delta = jnp.concatenate([delta_ref[side]] * repeat, axis=1)
        weights = jnp.exp2(scores * (scale * LOG2E) - lse)
        weights = masked(weights, meta_ref, docs, scores.shape, half, q_part, k_part, diagonal)
        d_weights = dot_nt(grads, values)
        d_scores = (weights * (d_weights - delta)).astype(BF16)
        d_values = dot_tn(weights.astype(BF16), grads)
        d_keys = dot_tn(d_scores, queries) * scale
        return dot(d_scores, keys) * scale, d_keys, d_values

    for e in range(2):
        rows = pl.ds(e * half, half)
        part = own if e == 0 else 2 * count - 1 - own
        d_queries, d_keys, d_values = block(
            e, e * half, k_ref[rows, :], v_ref[rows, :], part, part, True
        )
        acc_ref[e] = d_queries
        dkv_ref[0, rows, :] = d_keys
        dkv_ref[1, rows, :] = d_values
    for d in range(count - 1):
        side = meta_ref[docs + d]
        k_part = meta_ref[docs + count - 1 + d]
        q_part = jnp.where(side == 0, own, 2 * count - 1 - own)
        seen = any_visible(meta_ref, docs, half, q_part, k_part)
        whole = all_visible(meta_ref, docs, half, q_part, k_part)

        def add(mask):
            start = pl.multiple_of(side * half, half)
            d_queries, d_keys, d_values = block(
                side, start, others[2 * d][...], others[2 * d + 1][...], q_part, k_part, mask
            )
            acc_ref[side] += d_queries
            given[d][0] = d_keys.astype(BF16)
            given[d][1] = d_values.astype(BF16)

        pl.when(whole)(functools.partial(add, None))
        pl.when(seen & jnp.logical_not(whole))(functools.partial(add, False))

        @pl.when(jnp.logical_not(seen))
        def _():
            given[d][...] = jnp.zeros_like(given[d])

    for e in range(2):
        for a in range(2):
            dq_ref[pl.ds(e * half, half), a * HEAD : (a + 1) * HEAD] = acc_ref[
                e, a * half : (a + 1) * half, :
            ]


def key_value_specs(rows, half, kv_heads, count):
    own = [
        pl.BlockSpec((rows, HEAD), lambda h, m: (0, h)),
        pl.BlockSpec((rows, HEAD), lambda h, m: (0, kv_heads + h)),
    ]
    other = [
        pl.BlockSpec((half, HEAD), lambda h, m: (0, h)),
        pl.BlockSpec((half, HEAD), lambda h, m: (0, kv_heads + h)),
    ]
    return own + other * (count - 1)


def twice(arrays):
    return [a for a in arrays for _ in range(2)]


def attend(meta, docs, queries, key_value, others):
    rows, width = queries.shape
    half = rows // 2
    count = len(others) + 1
    kv_heads = key_value.shape[1] // (2 * HEAD)
    column = pl.BlockSpec((rows, 2 * HEAD), lambda h, m: (0, h))
    return pl.pallas_call(
        functools.partial(forward_kernel, docs, count),
        grid_spec=pltpu.PrefetchScalarGridSpec(
            num_scalar_prefetch=1,
            grid=(kv_heads,),
            in_specs=[column] + key_value_specs(rows, half, kv_heads, count),
            out_specs=[column] * 3,
            scratch_shapes=[pltpu.VMEM((2, 2 * half, 2 * HEAD), F32)],
        ),
        out_shape=[
            jax.ShapeDtypeStruct((rows, width), F32),
            jax.ShapeDtypeStruct((rows, width), BF16),
            jax.ShapeDtypeStruct((rows, width), F32),
        ],
        compiler_params=pltpu.CompilerParams(vmem_limit_bytes=VMEM_LIMIT),
        cost_estimate=CHEAP,
    )(meta, queries, key_value, key_value, *twice(others))


def attend_back(meta, docs, queries, grads, outs, lse, key_value, others):
    rows, width = queries.shape
    half = rows // 2
    count = len(others) + 1
    kv_width = key_value.shape[1] // 2
    kv_heads = kv_width // HEAD
    column = pl.BlockSpec((rows, 2 * HEAD), lambda h, m: (0, h))
    result = pl.pallas_call(
        functools.partial(backward_kernel, docs, count),
        grid_spec=pltpu.PrefetchScalarGridSpec(
            num_scalar_prefetch=1,
            grid=(kv_heads,),
            in_specs=[column] * 4 + key_value_specs(rows, half, kv_heads, count),
            out_specs=[column, pl.BlockSpec((2, rows, HEAD), lambda h, m: (0, 0, h))]
            + [pl.BlockSpec((2, half, HEAD), lambda h, m: (0, 0, h))] * (count - 1),
            scratch_shapes=[pltpu.VMEM((2, 2 * half, HEAD), F32)] * 3,
        ),
        out_shape=[
            jax.ShapeDtypeStruct((rows, width), F32),
            jax.ShapeDtypeStruct((2, rows, kv_width), F32),
        ]
        + [jax.ShapeDtypeStruct((2, half, kv_width), BF16)] * (count - 1),
        compiler_params=pltpu.CompilerParams(vmem_limit_bytes=VMEM_LIMIT),
        cost_estimate=CHEAP,
    )(meta, queries, grads, outs, lse, key_value, key_value, *twice(others))
    return result[0], result[1], list(result[2:])


def body(
    tokens,
    cotangent,
    seq_lengths,
    part_order,
    w_query,
    key_weight,
    value_weight,
    w_out,
    w_gate,
    w_up,
    w_down,
    gain_in,
    gain_post,
    gain_q,
    gain_k,
):
    shard_count = lax.axis_size("shard")
    shard = lax.axis_index("shard")
    count = lax.axis_size("ctx")
    ctx = lax.axis_index("ctx")
    rows, model = tokens.shape
    half = rows // 2
    depth = model // shard_count
    docs = seq_lengths.shape[1]
    kv_width = key_weight.shape[1]
    units = w_gate.shape[1]
    heads_width = w_out.shape[0]

    masks = [1 << b for b in range(count.bit_length() - 1)]
    near_axis, far_axis = masks[:1], masks[1:]
    far = [d for d in range(1, count) if d >= count // 2]
    near = [d for d in range(1, count) if d < count // 2]
    crossing = [d for d in far + near if d % 2 == 1]
    straight = [d for d in far + near if d % 2 == 0]

    packed = jnp.concatenate([gain_in, gain_post, gain_q, gain_k])
    k_pieces = pieces_of(key_weight, "shard")
    v_pieces = pieces_of(value_weight, "shard")
    packed_pieces = pieces_of(packed, "shard")
    own_rest = jnp.concatenate([w_query, w_out.T, w_down.T], axis=1)
    own_gate_up = jnp.concatenate([w_gate, w_up], axis=1)

    turns = jnp.arange(count, dtype=jnp.int32)
    partner = jnp.bitwise_xor(ctx.astype(jnp.int32), turns)
    parts = jnp.sum(
        jnp.where(partner[:, None] == turns[None, :], part_order[:, 0][None, :], 0), axis=1
    )
    part = parts[:1]
    lengths = seq_lengths[0]
    order = jnp.arange(docs, dtype=jnp.int32)
    starts = jnp.sum(jnp.where(order[None, :] < order[:, None], lengths[None, :], 0), axis=1)
    meta = jnp.concatenate(
        [
            part,
            starts[1:],
            (parts[1:] >= part).astype(jnp.int32),
            jnp.where(parts[1:] < part, parts[1:], 2 * count - 1 - parts[1:]),
        ]
    ).astype(jnp.int32)
    row = jnp.arange(rows, dtype=jnp.int32)
    places = jnp.where(row < half, part * half + row, (2 * count - 2 - part) * half + row)
    reached = places[:, None] >= starts[None, :]
    begins = jnp.max(jnp.where(reached, starts[None, :], 0), axis=1)
    frequency = THETA ** (-jnp.arange(0, HEAD, 2, dtype=F32) / HEAD)
    angles = (places - begins).astype(F32)[:, None] * frequency[None, :]
    cosine, sine = jnp.cos(angles), jnp.sin(angles)
    cosine = jnp.concatenate([cosine, cosine], axis=-1)
    sine = jnp.concatenate([-sine, sine], axis=-1)

    inputs = tokens.astype(F32)
    normal_one, factor_one = rms_parts(inputs)

    own_rest, own_gate_up, packed_pieces[-1], k_pieces[-1], v_pieces[-1] = tie(
        own_rest, own_gate_up, packed_pieces[-1], k_pieces[-1], v_pieces[-1]
    )
    cosine, sine, meta, normal_one, k_pieces[-1] = tie(
        cosine, sine, meta, normal_one, k_pieces[-1]
    )
    cuts = [0, depth, 2 * depth, 2 * depth + gain_q.shape[0], packed.shape[0]]
    scale_in, scale_post, scale_q, scale_k = (
        join([piece[lo:hi] for piece in packed_pieces], 0, shard).astype(F32).reshape(1, -1)
        for lo, hi in zip(cuts[:-1], cuts[1:])
    )
    normed_input = (normal_one * scale_in).astype(BF16)
    full_key = join(k_pieces, 0, shard)
    full_value = join(v_pieces, 0, shard)

    full_gate_up = lax.all_gather(own_gate_up, "shard", axis=0, tiled=True)
    if shard_count == 2:
        bit = place_in(near_axis)
        half_rest = lax.dynamic_slice_in_dim(own_rest, bit * (depth // 2), depth // 2, 0)
        half_rest = swap(half_rest, "shard")
    else:
        half_rest = own_rest
    k_pre = dot(normed_input, full_key)
    key_value, sent = key_value_and_parts(
        meta, docs, count, k_pre, dot(normed_input, full_value), cosine, sine, scale_k
    )
    held = {}
    exchange(sent, held, crossing)
    half_rest, *rest = settle(held, crossing, half_rest, *(sent[d] for d in straight))
    sent.update(zip(straight, rest))

    exchange(sent, held, straight)
    if shard_count == 2:
        other_rest = join([half_rest, swap(half_rest, "ctx", near_axis[0])], 0, bit)
        full_rest = join([own_rest, other_rest], 0, shard)
    else:
        full_rest = lax.all_gather(half_rest, "shard", axis=0, tiled=True)
    full_query = full_rest[:, :heads_width]
    full_out_t = full_rest[:, heads_width : 2 * heads_width]
    full_down_t = full_rest[:, 2 * heads_width :]
    q_pre = dot(normed_input, full_query)
    queries = rope(q_pre, cosine, sine, scale_q)
    queries, full_out_t = settle(held, straight, queries, full_out_t)
    held = [held[d] for d in range(1, count)]
    attended, attn_out, lse = attend(meta, docs, queries, key_value, held)

    residual = inputs + pair_total(dot_nt(attn_out, full_out_t))
    normal_two, factor_two = rms_parts(residual)
    normed_two = (normal_two * scale_post).astype(BF16)
    gate_upward = dot(normed_two, full_gate_up)
    gate_act = gate_upward[:, :units]
    upward = gate_upward[:, units:]
    sigma = jax.nn.sigmoid(gate_act)
    silu_act = gate_act * sigma
    hidden = (silu_act * upward).astype(BF16)
    d_hidden = dot(cotangent, full_down_t)
    d_gate = (d_hidden * upward * sigma * (1.0 + gate_act * (1.0 - sigma))).astype(BF16)
    d_up = (d_hidden * silu_act).astype(BF16)
    middle = units // 2
    units_a = over_shard([(normed_two, d_gate, 0, units), (normed_two, d_up, 0, middle)])
    units_b, units_b_away = over_near_then_shard(
        [(normed_two, d_up, middle, units), (cotangent, hidden, 0, units)], near_axis
    )
    d_normed_two = pair_total(
        product_nt((d_gate, full_gate_up, 0), (d_up, full_gate_up, 1))
    )
    hidden, d_normed_two = tie(hidden, d_normed_two)
    mixed_part = product_nt((hidden, full_down_t, 0))
    mixed = (residual + pair_total(mixed_part)).astype(BF16)
    grad_post = jnp.sum(d_normed_two * normal_two, axis=0)
    d_residual = cotangent.astype(F32) + rms_back(
        d_normed_two * scale_post, normal_two, factor_two
    )

    d_branch = d_residual.astype(BF16)
    d_attn = dot(d_branch, full_out_t).astype(BF16)
    d_queries, d_kv, given = attend_back(
        meta, docs, queries, d_attn, attended, lse, key_value, held
    )
    given = dict(zip(range(1, count), given))
    returned = {}
    exchange(given, returned, straight)
    units_a = halve(units_a, near_axis)
    if units_b_away is not None:
        units_b = units_b + [swap(total(units_b_away()), "shard")]
    d_q_pre, gq_part = rope_back(d_queries, q_pre, cosine, sine, scale_q)
    out_query = over_shard(
        [(d_branch, attn_out, 0, heads_width), (normed_input, d_q_pre, 0, heads_width)]
    )
    units_a[-1], units_b[-1], out_query[0], *rest = settle(
        returned, straight, units_a[-1], units_b[-1], out_query[0], *(given[d] for d in crossing)
    )
    given.update(zip(crossing, rest))
    exchange(given, returned, crossing)
    out_query[-1], d_kv = settle(returned, crossing, out_query[-1], d_kv)
    returned = [returned[d] for d in range(1, count)]

    units_a = halve(units_a, far_axis)
    units_b = halve(units_b, far_axis)
    out_query = halve(out_query, near_axis)
    d_k_pre, d_v_pre, gk_part = key_value_back(
        meta, docs, d_kv, returned, k_pre, cosine, sine, scale_k
    )
    key_value_grad = over_shard(
        [(normed_input, d_k_pre, 0, kv_width), (normed_input, d_v_pre, 0, kv_width)]
    )
    units_a, units_b = total(units_a), total(units_b)
    units_a, units_b, out_query[-1], key_value_grad[-1], d_q_pre, d_k_pre, d_v_pre = tie(
        units_a, units_b, out_query[-1], key_value_grad[-1], d_q_pre, d_k_pre, d_v_pre
    )

    units_chain = double(jnp.concatenate([units_a, units_b], axis=1), far_axis)
    key_value_grad = halve(key_value_grad, near_axis)
    d_normed = pair_total(
        dot_nt(d_q_pre, full_query) + dot_nt(d_k_pre, full_key) + dot_nt(d_v_pre, full_value)
    )
    grad_in = jnp.sum(d_normed * normal_one, axis=0)
    input_grad = d_residual + rms_back(d_normed * scale_in, normal_one, factor_one)
    once = jnp.where(lax.axis_index("tp") == 0, 1.0, 0.0)
    gain_grads = jnp.concatenate([grad_in * once, grad_post * once, gq_part[0], gk_part[0]])
    gain_grads = gain_grads.reshape(-1, HEAD)
    if shard_count != 2:
        gain_grads = lax.psum(gain_grads, "shard")
    units_chain, key_value_grad[-1], gain_grads = tie(
        units_chain, key_value_grad[-1], gain_grads
    )

    cut = units_chain.shape[1] // 2
    owned_a = double(units_chain[:, :cut], near_axis)
    owned_b = units_chain[:, cut:]
    rest_chain = jnp.concatenate([total(out_query), total(key_value_grad)], axis=1)
    rest_chain = total(halve([rest_chain], far_axis))
    gain_grads = gain_grads + swap(gain_grads, "tp")
    gain_grads = gain_grads + swap(gain_grads, "ctx", masks[0])
    owned_a, owned_b, rest_chain, gain_grads = tie(owned_a, owned_b, rest_chain, gain_grads)

    owned_b = double(owned_b, near_axis)
    rest_chain = double(rest_chain, far_axis)
    for mask in masks[1:]:
        gain_grads = gain_grads + swap(gain_grads, "ctx", mask)
    owned_b, rest_chain, gain_grads = tie(owned_b, rest_chain, gain_grads)

    owned_rest = double(rest_chain, near_axis).astype(F32)
    if shard_count == 2:
        gain_grads = gain_grads + swap(gain_grads, "shard")
    gain_grads = gain_grads.reshape(-1)
    cuts = [0, heads_width, 2 * heads_width, 2 * heads_width + kv_width]
    cuts = cuts + [cuts[-1] + kv_width]
    owned_out, owned_query, owned_key, owned_value = (
        owned_rest[:, lo:hi] for lo, hi in zip(cuts[:-1], cuts[1:])
    )
    owned_up = jnp.concatenate([owned_a[:, units:], owned_b[:, :middle]], axis=1)
    own_gains = []
    for lo, size in ((0, model), (model, model), (2 * model, HEAD), (2 * model + HEAD, HEAD)):
        size = size // shard_count
        own_gains.append(lax.dynamic_slice_in_dim(gain_grads, lo + shard * size, size, 0))
    return (
        mixed,
        input_grad,
        owned_query,
        owned_key,
        owned_value,
        owned_out.T,
        owned_a[:, :units].astype(F32),
        owned_up.astype(F32),
        owned_b[:, middle:].astype(F32).T,
        *own_gains,
    )


def solution(mesh):
    placed = (
        P(("shard", "ctx"), None),
        P(("shard", "ctx"), None),
        P("shard", None),
        P(),
        P("shard", "tp"),
        P("shard", "tp"),
        P("shard", "tp"),
        P("tp", "shard"),
        P("shard", "tp"),
        P("shard", "tp"),
        P("tp", "shard"),
        P("shard"),
        P("shard"),
        P("shard"),
        P("shard"),
    )
    return jax.shard_map(
        body,
        mesh=mesh,
        in_specs=placed,
        out_specs=(
            P(("shard", "ctx"), None),
            P(("shard", "ctx"), None),
            P("shard", "tp"),
            P("shard", "tp"),
            P("shard", "tp"),
            P("tp", "shard"),
            P("shard", "tp"),
            P("shard", "tp"),
            P("tp", "shard"),
            P("shard"),
            P("shard"),
            P("shard"),
            P("shard"),
        ),
        check_vma=False,
    )
```

```python
import functools

import jax
import jax.numpy as jnp
from jax import lax
from jax.experimental import pallas as pl
from jax.experimental.pallas import tpu as pltpu
from jax.sharding import PartitionSpec as P

EPS = 1e-06
THETA = 1000000.0
LOG2E = 1.4426950408889634
HEAD = 128
BF16 = jnp.bfloat16
F32 = jnp.float32
VMEM_LIMIT = 48 * 1024 * 1024
CHEAP = pl.CostEstimate(flops=1000, bytes_accessed=1000, transcendentals=0)


def rms_parts(values):
    factor = lax.rsqrt(jnp.mean(values * values, axis=-1, keepdims=True) + EPS)
    return (values * factor, factor)


def rms_back(grad_hat, normal, factor):
    return factor * (grad_hat - normal * jnp.mean(grad_hat * normal, axis=-1, keepdims=True))


def dot(a, b):
    return jnp.dot(a, b, preferred_element_type=F32)


def dot_nt(a, b):
    return lax.dot_general(a, b, (((1,), (1,)), ((), ())), preferred_element_type=F32)


def dot_tn(a, b):
    return lax.dot_general(a, b, (((0,), (0,)), ((), ())), preferred_element_type=F32)


def tie(*values):
    return lax.optimization_barrier(values)


def pieces_of(own, axis):
    count = lax.axis_size(axis)
    return [own] + [
        lax.ppermute(own, axis, [((i + j) % count, i) for i in range(count)])
        for j in range(1, count)
    ]


def join(pieces, dim, index):
    count = len(pieces)
    if count == 1:
        return pieces[0]
    if count == 2:
        return jnp.where(
            index == 0, jnp.concatenate(pieces, dim), jnp.concatenate(pieces[::-1], dim)
        )
    size = pieces[0].shape[dim]
    shape = list(pieces[0].shape)
    shape[dim] = size * count
    whole = jnp.zeros(shape, pieces[0].dtype)
    for j, piece in enumerate(pieces):
        whole = lax.dynamic_update_slice_in_dim(whole, piece, (index + j) % count * size, dim)
    return whole


def pair_total(partial):
    count = lax.axis_size("tp")
    partial = partial.astype(BF16)
    if count != 2:
        return lax.psum(partial, "tp").astype(F32)
    other = lax.ppermute(partial, "tp", [(0, 1), (1, 0)])
    return partial.astype(F32) + other.astype(F32)


def swap(value, axis, level=1):
    count = lax.axis_size(axis)
    return lax.ppermute(value, axis, [(i, i ^ level) for i in range(count)])


def place_in(masks):
    return (lax.axis_index("ctx") // masks[0]) % (1 << len(masks))


def exchange(values, done, turns):
    count = lax.axis_size("ctx")
    for d in turns:
        done[d] = lax.ppermute(values[d], "ctx", [(i, i ^ d) for i in range(count)])


def settle(done, turns, *values):
    tied = tie(*(done[d] for d in turns), *values)
    done.update(zip(turns, tied))
    return tied[len(turns) :]


def total(addends):
    return sum(a.astype(F32) for a in addends).astype(BF16)


def rows_at(addends, block, rows):
    return [lax.dynamic_slice_in_dim(a, block * rows, rows, 0) for a in addends]


def halve(addends, masks):
    size = 1 << len(masks)
    rows = addends[0].shape[0] // size
    place = place_in(masks)
    kept = rows_at(addends, place, rows)
    for turn in range(1, size):
        sent = total(rows_at(addends, place ^ turn, rows))
        kept = kept + [swap(sent, "ctx", turn * masks[0])]
    return kept


def scattered(pairs):
    grads = [dot_tn(a, b[:, lo:hi]).astype(BF16) for a, b, lo, hi in pairs]
    grad = jnp.concatenate(grads, axis=1)
    return [lax.psum_scatter(grad, "shard", scatter_dimension=0, tiled=True)]


def double(value, masks):
    size = 1 << len(masks)
    place = place_in(masks)
    blocks = [value] + [swap(value, "ctx", turn * masks[0]) for turn in range(1, size)]
    bit = 0
    while len(blocks) > 1:
        pairs = zip(blocks[::2], blocks[1::2])
        blocks = [join(list(pair), 0, (place >> bit) % 2) for pair in pairs]
        bit += 1
    return blocks[0]


def product_kernel(count, *refs):
    products = [dot_nt(refs[2 * i][...], refs[2 * i + 1][...]) for i in range(count)]
    refs[-1][...] = sum(products).astype(BF16)


def product_nt(*terms):
    rows = terms[0][0].shape[0]
    columns = terms[0][1].shape[0]
    step = min(columns, 256)
    specs, values = [], []
    for a, b, column in terms:
        depth = a.shape[1]
        specs.append(pl.BlockSpec((rows, depth), lambda i: (0, 0)))
        specs.append(pl.BlockSpec((step, depth), lambda i, column=column: (i, column)))
        values += [a, b]
    return pl.pallas_call(
        functools.partial(product_kernel, len(terms)),
        grid=(columns // step,),
        in_specs=specs,
        out_specs=pl.BlockSpec((rows, step), lambda i: (0, i)),
        out_shape=jax.ShapeDtypeStruct((rows, columns), BF16),
        compiler_params=pltpu.CompilerParams(vmem_limit_bytes=VMEM_LIMIT),
        cost_estimate=CHEAP,
    )(*values)


def split_product_kernel(spans, which_ref, *refs):
    j = pl.program_id(1)
    for i, (lo, hi) in enumerate(spans):

        @pl.when((j >= lo) & (j < hi))
        def _():
            refs[-1][...] = dot_tn(refs[2 * i][...], refs[2 * i + 1][...]).astype(BF16)


def split_product(which, pairs):
    tokens, model = pairs[0][0].shape
    rows = model // 4
    step = min(hi - lo for a, b, lo, hi in pairs)
    specs, values, spans, done = [], [], [], 0
    for a, b, lo, hi in pairs:
        blocks = (hi - lo) // step

        def column(i, j, w, first=done, base=lo // step, blocks=blocks):
            return (0, base + jnp.clip(j - first, 0, blocks - 1))

        specs.append(pl.BlockSpec((tokens, rows), lambda i, j, w: (0, w[i])))
        specs.append(pl.BlockSpec((tokens, step), column))
        values += [a, b]
        spans.append((done, done + blocks))
        done += blocks
    return pl.pallas_call(
        functools.partial(split_product_kernel, spans),
        grid_spec=pltpu.PrefetchScalarGridSpec(
            num_scalar_prefetch=1,
            grid=(2, done),
            in_specs=specs,
            out_specs=pl.BlockSpec((rows, step), lambda i, j, w: (i, j)),
        ),
        out_shape=jax.ShapeDtypeStruct((2 * rows, done * step), BF16),
        compiler_params=pltpu.CompilerParams(vmem_limit_bytes=VMEM_LIMIT),
        cost_estimate=CHEAP,
    )(jnp.stack(which).astype(jnp.int32), *values)


def rope_kernel(pre_ref, cos_ref, sin_ref, gain_ref, out_ref):
    pre = pre_ref[...]
    factor = lax.rsqrt(jnp.mean(pre * pre, axis=-1, keepdims=True) + EPS)
    scaled = pre * factor * gain_ref[...]
    turned = pltpu.roll(scaled, HEAD // 2, 1)
    out_ref[...] = (scaled * cos_ref[...] + turned * sin_ref[...]).astype(BF16)


def rope(pre, cosine, sine, gain):
    rows, width = pre.shape
    table = pl.BlockSpec((rows, HEAD), lambda h: (0, 0))
    column = pl.BlockSpec((rows, HEAD), lambda h: (0, h))
    return pl.pallas_call(
        rope_kernel,
        grid=(width // HEAD,),
        in_specs=[column, table, table, pl.BlockSpec((1, HEAD), lambda h: (0, 0))],
        out_specs=column,
        out_shape=jax.ShapeDtypeStruct((rows, width), BF16),
        compiler_params=pltpu.CompilerParams(vmem_limit_bytes=VMEM_LIMIT),
        cost_estimate=CHEAP,
    )(pre, cosine, sine, gain)


def part_start(meta_ref, docs, d, half):
    return pl.multiple_of((1 - meta_ref[docs + d]) * half, half)


def key_value_kernel(heads, docs, count, pieces, meta_ref, normal_ref, scale_ref, *refs):
    weights = refs[: 2 * pieces]
    cos_ref, sin_ref, gain_ref = refs[2 * pieces : 2 * pieces + 3]
    key_ref, out_ref, normed_ref = refs[2 * pieces + 3 : 2 * pieces + 6]
    sent = refs[2 * pieces + 6 :]
    half = out_ref.shape[0] // 2
    depth = normal_ref.shape[1] // pieces
    step = pl.program_id(0)

    @pl.when(step == 0)
    def _():
        normed_ref[...] = (normal_ref[...] * scale_ref[...]).astype(BF16)

    def product(parts):
        result = None
        for j, part in enumerate(parts):
            at = pl.multiple_of(meta_ref[docs + 2 * (count - 1) + j] * depth, HEAD)
            term = dot(normed_ref[:, pl.ds(at, depth)], part[...])
            result = term if result is None else result + term
        return result

    @pl.when(step < heads // 2)
    def _():
        key_ref[...] = product(weights[:pieces])
        for a in range(2):
            lanes = slice(a * HEAD, (a + 1) * HEAD)
            pre = key_ref[:, lanes]
            factor = lax.rsqrt(jnp.mean(pre * pre, axis=-1, keepdims=True) + EPS)
            scaled = pre * factor * gain_ref[...]
            turned = pltpu.roll(scaled, HEAD // 2, 1)
            out_ref[:, lanes] = (scaled * cos_ref[...] + turned * sin_ref[...]).astype(BF16)

    @pl.when(step >= heads // 2)
    def _():
        out_ref[...] = product(weights[pieces:]).astype(BF16)

    for d, sent_ref in enumerate(sent):
        sent_ref[...] = out_ref[pl.ds(part_start(meta_ref, docs, d, half), half), :]


def key_value_and_parts(meta, docs, count, normal, scale, keys, values, cosine, sine, gain):
    rows, model = normal.shape
    depth, width = keys[0].shape
    heads = width // HEAD
    half_steps = heads // 2
    whole = lambda shape: pl.BlockSpec(shape, lambda h, m: (0, 0))
    column = pl.BlockSpec((rows, 2 * HEAD), lambda h, m: (0, h))
    key_spec = pl.BlockSpec((depth, 2 * HEAD), lambda h, m: (0, jnp.minimum(h, half_steps - 1)))
    value_spec = pl.BlockSpec((depth, 2 * HEAD), lambda h, m: (0, jnp.maximum(h - half_steps, 0)))
    part = pl.BlockSpec((rows // 2, 2 * HEAD), lambda h, m: (0, h))
    result = pl.pallas_call(
        functools.partial(key_value_kernel, heads, docs, count, len(keys)),
        grid_spec=pltpu.PrefetchScalarGridSpec(
            num_scalar_prefetch=1,
            grid=(heads,),
            in_specs=[whole((rows, model)), whole((1, model))]
            + [key_spec] * len(keys)
            + [value_spec] * len(values)
            + [whole((rows, HEAD)), whole((rows, HEAD)), whole((1, HEAD))],
            out_specs=[
                pl.BlockSpec((rows, 2 * HEAD), lambda h, m: (0, jnp.minimum(h, half_steps - 1))),
                column,
                whole((rows, model)),
            ]
            + [part] * (count - 1),
        ),
        out_shape=[
            jax.ShapeDtypeStruct((rows, width), F32),
            jax.ShapeDtypeStruct((rows, 2 * width), BF16),
            jax.ShapeDtypeStruct((rows, model), BF16),
        ]
        + [jax.ShapeDtypeStruct((rows // 2, 2 * width), BF16)] * (count - 1),
        compiler_params=pltpu.CompilerParams(vmem_limit_bytes=VMEM_LIMIT),
        cost_estimate=CHEAP,
    )(meta, normal, scale, *keys, *values, cosine, sine, gain)
    return result[0], result[1], result[2], dict(zip(range(1, count), result[3:]))


def turn_back(grad, pre_ref, cos_ref, sin_ref, gain_ref, out_ref, sum_ref):
    pre = pre_ref[...]
    factor = lax.rsqrt(jnp.mean(pre * pre, axis=-1, keepdims=True) + EPS)
    hat = pre * factor
    back = grad * cos_ref[...] - pltpu.roll(grad, HEAD // 2, 1) * sin_ref[...]
    terms = jnp.sum(back * hat, axis=0, keepdims=True)

    @pl.when(pl.program_id(0) == 0)
    def _():
        sum_ref[...] = terms

    @pl.when(pl.program_id(0) > 0)
    def _():
        sum_ref[...] += terms

    back = back * gain_ref[...]
    inner = jnp.mean(back * hat, axis=-1, keepdims=True)
    out_ref[...] = (factor * (back - hat * inner)).astype(BF16)


def rope_back_kernel(grad_ref, *refs):
    turn_back(grad_ref[...], *refs)


def key_value_back_kernel(docs, meta_ref, own_ref, *refs):
    returned = refs[:-8]
    key_ref, cos_ref, sin_ref, gain_ref, d_key_ref, d_value_ref, sum_ref, acc_ref = refs[-8:]
    half = key_ref.shape[0] // 2
    acc_ref[...] = own_ref[...]
    for d, given_ref in enumerate(returned):
        rows = pl.ds(part_start(meta_ref, docs, d, half), half)
        acc_ref[:, rows, :] += given_ref[...].astype(F32)
    d_value_ref[...] = acc_ref[1].astype(BF16)
    turn_back(acc_ref[0], key_ref, cos_ref, sin_ref, gain_ref, d_key_ref, sum_ref)


def key_value_back(meta, docs, own, returned, key, cosine, sine, gain):
    rows, width = key.shape
    table = pl.BlockSpec((rows, HEAD), lambda h, m: (0, 0))
    column = pl.BlockSpec((rows, HEAD), lambda h, m: (0, h))
    one_row = pl.BlockSpec((1, HEAD), lambda h, m: (0, 0))
    return pl.pallas_call(
        functools.partial(key_value_back_kernel, docs),
        grid_spec=pltpu.PrefetchScalarGridSpec(
            num_scalar_prefetch=1,
            grid=(width // HEAD,),
            in_specs=[pl.BlockSpec((2, rows, HEAD), lambda h, m: (0, 0, h))]
            + [pl.BlockSpec((2, rows // 2, HEAD), lambda h, m: (0, 0, h))] * len(returned)
            + [column, table, table, one_row],
            out_specs=[column, column, one_row],
            scratch_shapes=[pltpu.VMEM((2, rows, HEAD), F32)],
        ),
        out_shape=[
            jax.ShapeDtypeStruct((rows, width), BF16),
            jax.ShapeDtypeStruct((rows, width), BF16),
            jax.ShapeDtypeStruct((1, HEAD), F32),
        ],
        compiler_params=pltpu.CompilerParams(vmem_limit_bytes=VMEM_LIMIT),
        cost_estimate=CHEAP,
    )(meta, own, *returned, key, cosine, sine, gain)


def rope_back(grad, pre, cosine, sine, gain):
    rows, width = grad.shape
    column = pl.BlockSpec((rows, HEAD), lambda h: (0, h))
    table = pl.BlockSpec((rows, HEAD), lambda h: (0, 0))
    one_row = pl.BlockSpec((1, HEAD), lambda h: (0, 0))
    return pl.pallas_call(
        rope_back_kernel,
        grid=(width // HEAD,),
        in_specs=[column, column, table, table, one_row],
        out_specs=[column, one_row],
        out_shape=[
            jax.ShapeDtypeStruct((rows, width), BF16),
            jax.ShapeDtypeStruct((1, HEAD), F32),
        ],
        compiler_params=pltpu.CompilerParams(vmem_limit_bytes=VMEM_LIMIT),
    )(grad, pre, cosine, sine, gain)


def doc_begins(meta_ref, docs, place):
    begin = jnp.zeros_like(place)
    for i in range(1, docs):
        start = meta_ref[i]
        begin = jnp.where(place >= start, start, begin)
    return begin


def block_mask(meta_ref, docs, shape, half, q_part, k_part, diagonal):
    row = lax.broadcasted_iota(jnp.int32, (shape[0], 1), 0)
    q_place = q_part * half + jnp.where(row >= half, row - half, row)
    begin = doc_begins(meta_ref, docs, q_place) - k_part * half
    column = lax.broadcasted_iota(jnp.int32, shape, 1)
    visible = column >= begin
    if diagonal:
        visible = visible & (column <= q_place - k_part * half)
    return visible


def mask_across(meta_ref, docs, shape, half, q_part, k_part, diagonal):
    column = lax.broadcasted_iota(jnp.int32, (1, shape[1]), 1)
    q_place = q_part * half + jnp.where(column >= half, column - half, column)
    begin = doc_begins(meta_ref, docs, q_place) - k_part * half
    row = lax.broadcasted_iota(jnp.int32, shape, 0)
    visible = row >= begin
    if diagonal:
        visible = visible & (row <= q_place - k_part * half)
    return visible


def any_visible(meta_ref, docs, half, q_part, k_part):
    return (k_part + 1) * half > doc_begins(meta_ref, docs, q_part * half)


def all_visible(meta_ref, docs, half, q_part, k_part):
    return k_part * half >= doc_begins(meta_ref, docs, q_part * half + half - 1)


def masked(weights, *mask_args):
    if mask_args[-1] is None:
        return weights
    return jnp.where(block_mask(*mask_args), weights, 0.0)


def two_heads(ref, start, half):
    rows = pl.ds(start, half)
    return jnp.concatenate([ref[rows, :HEAD], ref[rows, HEAD:]], axis=0)


def forward_kernel(docs, count, meta_ref, q_ref, k_ref, v_ref, *refs):
    others = refs[: 2 * (count - 1)]
    out_ref, out16_ref, lse_ref, acc_ref = refs[2 * (count - 1) :]
    half = q_ref.shape[0] // 2
    factor = HEAD**-0.5 * LOG2E
    ones = jnp.ones((half, HEAD), BF16)
    own = meta_ref[0]

    def block(start, keys, values, q_part, k_part, diagonal):
        scores = dot_nt(two_heads(q_ref, start, half), keys)
        weights = jnp.exp2(scores * factor)
        weights = masked(weights, meta_ref, docs, scores.shape, half, q_part, k_part, diagonal)
        weights = weights.astype(BF16)
        return dot(weights, jnp.concatenate([values, ones], axis=1))

    for e in range(2):
        rows = pl.ds(e * half, half)
        part = own if e == 0 else 2 * count - 1 - own
        acc_ref[e] = block(e * half, k_ref[rows, :], v_ref[rows, :], part, part, True)
    for d in range(count - 1):
        side = meta_ref[docs + d]
        k_part = meta_ref[docs + count - 1 + d]
        q_part = jnp.where(side == 0, own, 2 * count - 1 - own)

        def add(mask):
            start = pl.multiple_of(side * half, half)
            acc_ref[side] += block(
                start, others[2 * d][...], others[2 * d + 1][...], q_part, k_part, mask
            )

        seen = any_visible(meta_ref, docs, half, q_part, k_part)
        whole = all_visible(meta_ref, docs, half, q_part, k_part)
        pl.when(whole)(functools.partial(add, None))
        pl.when(seen & jnp.logical_not(whole))(functools.partial(add, False))

    for e in range(2):
        total = acc_ref[e]
        sums = total[:, HEAD:]
        result = total[:, :HEAD] / sums
        lse = jnp.log2(sums)
        for a in range(2):
            part = slice(a * half, (a + 1) * half)
            place = (pl.ds(e * half, half), slice(a * HEAD, (a + 1) * HEAD))
            out_ref[place] = result[part]
            out16_ref[place] = result[part].astype(BF16)
            lse_ref[place] = lse[part]


def backward_kernel(docs, count, meta_ref, q_ref, g_ref, o_ref, lse_ref, k_ref, v_ref, *refs):
    others = refs[: 2 * (count - 1)]
    dq_ref, dkv_ref = refs[2 * (count - 1) : 2 * count]
    given = refs[2 * count : 3 * count - 1]
    acc_ref, stats_ref, delta_ref = refs[3 * count - 1 :]
    half = q_ref.shape[0] // 2
    scale = HEAD**-0.5
    own = meta_ref[0]

    for e in range(2):
        grads = two_heads(g_ref, e * half, half).astype(F32)
        delta = jnp.sum(grads * two_heads(o_ref, e * half, half), axis=1, keepdims=True)
        delta = jnp.broadcast_to(delta, (2 * half, HEAD))
        delta_ref[e] = jnp.transpose(delta)[:8]
        stats_ref[e] = jnp.transpose(two_heads(lse_ref, e * half, half))[:8]

    def block(side, start, keys, values, q_part, k_part, diagonal):
        queries = two_heads(q_ref, start, half)
        grads = two_heads(g_ref, start, half)
        scores = dot_nt(keys, queries)
        lse = stats_ref[side][:1]
        delta = delta_ref[side][:1]
        weights = jnp.exp2(scores * (scale * LOG2E) - lse)
        if diagonal is not None:
            visible = mask_across(
                meta_ref, docs, scores.shape, half, q_part, k_part, diagonal
            )
            weights = jnp.where(visible, weights, 0.0)
        d_weights = dot_nt(values, grads)
        d_scores = (weights * (d_weights - delta)).astype(BF16)
        d_values = dot(weights.astype(BF16), grads)
        d_keys = dot(d_scores, queries) * scale
        return dot_tn(d_scores, keys) * scale, d_keys, d_values

    for e in range(2):
        rows = pl.ds(e * half, half)
        part = own if e == 0 else 2 * count - 1 - own
        d_queries, d_keys, d_values = block(
            e, e * half, k_ref[rows, :], v_ref[rows, :], part, part, True
        )
        acc_ref[e] = d_queries
        dkv_ref[0, rows, :] = d_keys
        dkv_ref[1, rows, :] = d_values
    for d in range(count - 1):
        side = meta_ref[docs + d]
        k_part = meta_ref[docs + count - 1 + d]
        q_part = jnp.where(side == 0, own, 2 * count - 1 - own)
        seen = any_visible(meta_ref, docs, half, q_part, k_part)
        whole = all_visible(meta_ref, docs, half, q_part, k_part)

        def add(mask):
            start = pl.multiple_of(side * half, half)
            d_queries, d_keys, d_values = block(
                side, start, others[2 * d][...], others[2 * d + 1][...], q_part, k_part, mask
            )
            acc_ref[side] += d_queries
            given[d][0] = d_keys.astype(BF16)
            given[d][1] = d_values.astype(BF16)

        pl.when(whole)(functools.partial(add, None))
        pl.when(seen & jnp.logical_not(whole))(functools.partial(add, False))

        @pl.when(jnp.logical_not(seen))
        def _():
            given[d][...] = jnp.zeros_like(given[d])

    for e in range(2):
        for a in range(2):
            dq_ref[pl.ds(e * half, half), a * HEAD : (a + 1) * HEAD] = acc_ref[
                e, a * half : (a + 1) * half, :
            ]


def key_value_specs(rows, half, kv_heads, count):
    own = [
        pl.BlockSpec((rows, HEAD), lambda h, m: (0, h)),
        pl.BlockSpec((rows, HEAD), lambda h, m: (0, kv_heads + h)),
    ]
    other = [
        pl.BlockSpec((half, HEAD), lambda h, m: (0, h)),
        pl.BlockSpec((half, HEAD), lambda h, m: (0, kv_heads + h)),
    ]
    return own + other * (count - 1)


def twice(arrays):
    return [a for a in arrays for _ in range(2)]


def attend(meta, docs, queries, key_value, others):
    rows, width = queries.shape
    half = rows // 2
    count = len(others) + 1
    kv_heads = key_value.shape[1] // (2 * HEAD)
    column = pl.BlockSpec((rows, 2 * HEAD), lambda h, m: (0, h))
    return pl.pallas_call(
        functools.partial(forward_kernel, docs, count),
        grid_spec=pltpu.PrefetchScalarGridSpec(
            num_scalar_prefetch=1,
            grid=(kv_heads,),
            in_specs=[column] + key_value_specs(rows, half, kv_heads, count),
            out_specs=[column] * 3,
            scratch_shapes=[pltpu.VMEM((2, 2 * half, 2 * HEAD), F32)],
        ),
        out_shape=[
            jax.ShapeDtypeStruct((rows, width), F32),
            jax.ShapeDtypeStruct((rows, width), BF16),
            jax.ShapeDtypeStruct((rows, width), F32),
        ],
        compiler_params=pltpu.CompilerParams(vmem_limit_bytes=VMEM_LIMIT),
        cost_estimate=CHEAP,
    )(meta, queries, key_value, key_value, *twice(others))


def attend_back(meta, docs, queries, grads, outs, lse, key_value, others):
    rows, width = queries.shape
    half = rows // 2
    count = len(others) + 1
    kv_width = key_value.shape[1] // 2
    kv_heads = kv_width // HEAD
    column = pl.BlockSpec((rows, 2 * HEAD), lambda h, m: (0, h))
    result = pl.pallas_call(
        functools.partial(backward_kernel, docs, count),
        grid_spec=pltpu.PrefetchScalarGridSpec(
            num_scalar_prefetch=1,
            grid=(kv_heads,),
            in_specs=[column] * 4 + key_value_specs(rows, half, kv_heads, count),
            out_specs=[column, pl.BlockSpec((2, rows, HEAD), lambda h, m: (0, 0, h))]
            + [pl.BlockSpec((2, half, HEAD), lambda h, m: (0, 0, h))] * (count - 1),
            scratch_shapes=[
                pltpu.VMEM((2, 2 * half, HEAD), F32),
                pltpu.VMEM((2, 8, 2 * half), F32),
                pltpu.VMEM((2, 8, 2 * half), F32),
            ],
        ),
        out_shape=[
            jax.ShapeDtypeStruct((rows, width), F32),
            jax.ShapeDtypeStruct((2, rows, kv_width), F32),
        ]
        + [jax.ShapeDtypeStruct((2, half, kv_width), BF16)] * (count - 1),
        compiler_params=pltpu.CompilerParams(vmem_limit_bytes=VMEM_LIMIT),
        cost_estimate=CHEAP,
    )(meta, queries, grads, outs, lse, key_value, key_value, *twice(others))
    return result[0], result[1], list(result[2:])


def body(
    tokens,
    cotangent,
    seq_lengths,
    part_order,
    w_query,
    key_weight,
    value_weight,
    w_out,
    w_gate,
    w_up,
    w_down,
    gain_in,
    gain_post,
    gain_q,
    gain_k,
):
    shard_count = lax.axis_size("shard")
    shard = lax.axis_index("shard")
    count = lax.axis_size("ctx")
    ctx = lax.axis_index("ctx")
    rows, model = tokens.shape
    half = rows // 2
    depth = model // shard_count
    docs = seq_lengths.shape[1]
    kv_width = key_weight.shape[1]
    units = w_gate.shape[1]
    heads_width = w_out.shape[0]

    masks = [1 << b for b in range(count.bit_length() - 1)]
    near_axis, far_axis = masks[:1], masks[1:]
    far = [d for d in range(1, count) if d >= count // 2]
    near = [d for d in range(1, count) if d < count // 2]
    crossing = [d for d in far + near if d % 2 == 1]
    straight = [d for d in far + near if d % 2 == 0]

    packed = jnp.concatenate([gain_in, gain_post, gain_q, gain_k])
    k_pieces = pieces_of(key_weight, "shard")
    v_pieces = pieces_of(value_weight, "shard")
    packed_pieces = pieces_of(packed, "shard")
    own_rest = jnp.concatenate([w_query, w_out.T, w_down.T], axis=1)
    own_gate_up = jnp.concatenate([w_gate, w_up], axis=1)

    turns = jnp.arange(count, dtype=jnp.int32)
    partner = jnp.bitwise_xor(ctx.astype(jnp.int32), turns)
    parts = jnp.sum(
        jnp.where(partner[:, None] == turns[None, :], part_order[:, 0][None, :], 0), axis=1
    )
    part = parts[:1]
    lengths = seq_lengths[0]
    order = jnp.arange(docs, dtype=jnp.int32)
    starts = jnp.sum(jnp.where(order[None, :] < order[:, None], lengths[None, :], 0), axis=1)
    meta = jnp.concatenate(
        [
            part,
            starts[1:],
            (parts[1:] >= part).astype(jnp.int32),
            jnp.where(parts[1:] < part, parts[1:], 2 * count - 1 - parts[1:]),
            (shard + jnp.arange(shard_count, dtype=jnp.int32)) % shard_count,
        ]
    ).astype(jnp.int32)
    row = jnp.arange(rows, dtype=jnp.int32)
    places = jnp.where(row < half, part * half + row, (2 * count - 2 - part) * half + row)
    reached = places[:, None] >= starts[None, :]
    begins = jnp.max(jnp.where(reached, starts[None, :], 0), axis=1)
    frequency = THETA ** (-jnp.arange(0, HEAD, 2, dtype=F32) / HEAD)
    angles = (places - begins).astype(F32)[:, None] * frequency[None, :]
    cosine, sine = jnp.cos(angles), jnp.sin(angles)
    cosine = jnp.concatenate([cosine, cosine], axis=-1)
    sine = jnp.concatenate([-sine, sine], axis=-1)

    inputs = tokens.astype(F32)
    normal_one, factor_one = rms_parts(inputs)

    own_rest, own_gate_up, packed_pieces[-1], k_pieces[-1], v_pieces[-1] = tie(
        own_rest, own_gate_up, packed_pieces[-1], k_pieces[-1], v_pieces[-1]
    )
    cosine, sine, meta, normal_one, k_pieces[-1] = tie(
        cosine, sine, meta, normal_one, k_pieces[-1]
    )
    cuts = [0, depth, 2 * depth, 2 * depth + gain_q.shape[0], packed.shape[0]]
    scale_in, scale_post, scale_q, scale_k = (
        join([piece[lo:hi] for piece in packed_pieces], 0, shard).astype(F32).reshape(1, -1)
        for lo, hi in zip(cuts[:-1], cuts[1:])
    )
    full_key = join(k_pieces, 0, shard)
    full_value = join(v_pieces, 0, shard)

    full_gate_up = lax.all_gather(own_gate_up, "shard", axis=0, tiled=True)
    if shard_count == 2:
        bit = place_in(near_axis)
        half_rest = lax.dynamic_slice_in_dim(own_rest, bit * (depth // 2), depth // 2, 0)
        half_rest = swap(half_rest, "shard")
    else:
        half_rest = own_rest
    k_pre, key_value, normed_input, sent = key_value_and_parts(
        meta, docs, count, normal_one, scale_in, k_pieces, v_pieces, cosine, sine, scale_k
    )
    held = {}
    exchange(sent, held, crossing)
    half_rest, *rest = settle(held, crossing, half_rest, *(sent[d] for d in straight))
    sent.update(zip(straight, rest))

    exchange(sent, held, straight)
    if shard_count == 2:
        other_rest = join([half_rest, swap(half_rest, "ctx", near_axis[0])], 0, bit)
        full_rest = join([own_rest, other_rest], 0, shard)
    else:
        full_rest = lax.all_gather(half_rest, "shard", axis=0, tiled=True)
    full_query = full_rest[:, :heads_width]
    full_out_t = full_rest[:, heads_width : 2 * heads_width]
    full_down_t = full_rest[:, 2 * heads_width :]
    q_pre = dot(normed_input, full_query)
    queries = rope(q_pre, cosine, sine, scale_q)
    queries, full_out_t = settle(held, straight, queries, full_out_t)
    held = [held[d] for d in range(1, count)]
    attended, attn_out, lse = attend(meta, docs, queries, key_value, held)

    residual = inputs + pair_total(dot_nt(attn_out, full_out_t))
    normal_two, factor_two = rms_parts(residual)
    normed_two = (normal_two * scale_post).astype(BF16)
    gate_upward = dot(normed_two, full_gate_up)
    gate_act = gate_upward[:, :units]
    upward = gate_upward[:, units:]
    sigma = jax.nn.sigmoid(gate_act)
    silu_act = gate_act * sigma
    hidden = (silu_act * upward).astype(BF16)
    d_hidden = dot(cotangent, full_down_t)
    d_gate = (d_hidden * upward * sigma * (1.0 + gate_act * (1.0 - sigma))).astype(BF16)
    d_up = (d_hidden * silu_act).astype(BF16)
    middle = units // 2
    away, home = (2 - 2 * shard, 3 - 2 * shard), (2 * shard, 2 * shard + 1)
    bit = place_in(near_axis)

    def pairs_a(normed):
        return [(normed, d_gate, 0, units), (normed, d_up, 0, middle)]

    def pairs_b(normed, upstream):
        return [(normed, d_up, middle, units), (upstream, hidden, 0, units)]

    if shard_count == 2:
        sent_a = split_product(away, pairs_a(normed_two))
        sent_b = split_product((1 - bit, 3 - bit), pairs_b(normed_two, cotangent))
        d_gate, d_up, sent_a, sent_b = tie(d_gate, d_up, sent_a, sent_b)
        got_a, got_b = swap(sent_a, "shard"), swap(sent_b, "ctx", near_axis[0])
    d_normed_two = pair_total(
        product_nt((d_gate, full_gate_up, 0), (d_up, full_gate_up, 1))
    )
    hidden, d_normed_two = tie(hidden, d_normed_two)
    mixed_part = product_nt((hidden, full_down_t, 0))
    mixed = (residual + pair_total(mixed_part)).astype(BF16)
    grad_post = jnp.sum(d_normed_two * normal_two, axis=0)
    d_residual = cotangent.astype(F32) + rms_back(
        d_normed_two * scale_post, normal_two, factor_two
    )

    d_branch = d_residual.astype(BF16)
    d_attn = dot(d_branch, full_out_t).astype(BF16)
    d_queries, d_kv, given = attend_back(
        meta, docs, queries, d_attn, attended, lse, key_value, held
    )
    given = dict(zip(range(1, count), given))
    returned = {}
    exchange(given, returned, straight)
    if shard_count == 2:
        first, second = straight[-1], straight[0]
        normed_late, returned[first] = tie(normed_two, returned[first])
        units_a = [split_product(home, pairs_a(normed_late)), got_a]
        units_a = halve(units_a, near_axis)
        normed_late, upstream_late, returned[second] = tie(
            normed_two, cotangent, returned[second]
        )
        kept_b = split_product((bit, 2 + bit), pairs_b(normed_late, upstream_late))
        units_b = [kept_b, got_b]
        units_b_away = total(rows_at(units_b, 1 - shard, depth // 2))
        units_b = rows_at(units_b, shard, depth // 2) + [swap(units_b_away, "shard")]
    else:
        units_a = halve(scattered(pairs_a(normed_two)), near_axis)
        units_b = halve(scattered(pairs_b(normed_two, cotangent)), near_axis)
    d_q_pre, gq_part = rope_back(d_queries, q_pre, cosine, sine, scale_q)
    out_pairs = [(d_branch, attn_out, 0, heads_width), (normed_input, d_q_pre, 0, heads_width)]
    if shard_count == 2:
        out_query = [split_product(home, out_pairs), split_product(away, out_pairs)]
    else:
        out_query = scattered(out_pairs)
    units_a[-1], units_b[-1], out_query[0], out_query[-1], *rest = settle(
        returned,
        straight,
        units_a[-1],
        units_b[-1],
        out_query[0],
        out_query[-1],
        *(given[d] for d in crossing),
    )
    if shard_count == 2:
        out_query[-1] = swap(out_query[-1], "shard")
    given.update(zip(crossing, rest))
    exchange(given, returned, crossing)
    out_query[-1], d_kv = settle(returned, crossing, out_query[-1], d_kv)
    returned = [returned[d] for d in range(1, count)]

    units_a = halve(units_a, far_axis)
    units_b = halve(units_b, far_axis)
    out_query = halve(out_query, near_axis)
    d_k_pre, d_v_pre, gk_part = key_value_back(
        meta, docs, d_kv, returned, k_pre, cosine, sine, scale_k
    )
    kv_pairs = [(normed_input, d_k_pre, 0, kv_width), (normed_input, d_v_pre, 0, kv_width)]
    if shard_count == 2:
        sent_kv = swap(split_product(away, kv_pairs), "shard")
        key_value_grad = [split_product(home, kv_pairs), sent_kv]
    else:
        key_value_grad = scattered(kv_pairs)
    units_a, units_b = total(units_a), total(units_b)
    units_a, units_b, out_query[-1], key_value_grad[-1], d_q_pre, d_k_pre, d_v_pre = tie(
        units_a, units_b, out_query[-1], key_value_grad[-1], d_q_pre, d_k_pre, d_v_pre
    )

    units_a = double(units_a, far_axis)
    key_value_grad = halve(key_value_grad, near_axis)
    units_a, units_b, key_value_grad[-1], out_query[-1] = tie(
        units_a, units_b, key_value_grad[-1], out_query[-1]
    )

    units_b = double(units_b, far_axis)
    owned_a = double(units_a, near_axis)
    d_normed = pair_total(
        dot_nt(d_q_pre, full_query) + dot_nt(d_k_pre, full_key) + dot_nt(d_v_pre, full_value)
    )
    grad_in = jnp.sum(d_normed * normal_one, axis=0)
    input_grad = d_residual + rms_back(d_normed * scale_in, normal_one, factor_one)
    once = jnp.where(lax.axis_index("tp") == 0, 1.0, 0.0)
    gain_grads = jnp.concatenate([grad_in * once, grad_post * once, gq_part[0], gk_part[0]])
    gain_grads = gain_grads.reshape(-1, HEAD)
    if shard_count != 2:
        gain_grads = lax.psum(gain_grads, "shard")
    rest_chain = [jnp.concatenate([total(out_query), total(key_value_grad)], axis=1)]
    units_b, owned_a, rest_chain[0], gain_grads = tie(
        units_b, owned_a, rest_chain[0], gain_grads
    )

    owned_b = double(units_b, near_axis)
    rest_chain = total(halve(rest_chain, far_axis))
    gain_grads = gain_grads + swap(gain_grads, "tp")
    gain_grads = gain_grads + swap(gain_grads, "ctx", masks[0])
    owned_b, rest_chain, gain_grads = tie(owned_b, rest_chain, gain_grads)

    cut = rest_chain.shape[1] // 2
    rest_a, rest_b = rest_chain[:, :cut], rest_chain[:, cut:]
    rest_a = double(rest_a, far_axis)
    gain_grads = gain_grads + swap(gain_grads, "ctx", masks[1])
    rest_a, rest_b, gain_grads = tie(rest_a, rest_b, gain_grads)

    rest_b = double(rest_b, far_axis)
    rest_a = double(rest_a, near_axis)
    for mask in masks[2:]:
        gain_grads = gain_grads + swap(gain_grads, "ctx", mask)
    rest_a, rest_b, gain_grads = tie(rest_a, rest_b, gain_grads)

    rest_b = double(rest_b, near_axis)
    if shard_count == 2:
        gain_grads = gain_grads + swap(gain_grads, "shard")
    gain_grads = gain_grads.reshape(-1)
    owned_rest = jnp.concatenate([rest_a, rest_b], axis=1).astype(F32)
    cuts = [0, heads_width, 2 * heads_width, 2 * heads_width + kv_width]
    cuts = cuts + [cuts[-1] + kv_width]
    owned_out, owned_query, owned_key, owned_value = (
        owned_rest[:, lo:hi] for lo, hi in zip(cuts[:-1], cuts[1:])
    )
    owned_up = jnp.concatenate([owned_a[:, units:], owned_b[:, :middle]], axis=1)
    own_gains = []
    for lo, size in ((0, model), (model, model), (2 * model, HEAD), (2 * model + HEAD, HEAD)):
        size = size // shard_count
        own_gains.append(lax.dynamic_slice_in_dim(gain_grads, lo + shard * size, size, 0))
    return (
        mixed,
        input_grad,
        owned_query,
        owned_key,
        owned_value,
        owned_out.T,
        owned_a[:, :units].astype(F32),
        owned_up.astype(F32),
        owned_b[:, middle:].astype(F32).T,
        *own_gains,
    )


def solution(mesh):
    placed = (
        P(("shard", "ctx"), None),
        P(("shard", "ctx"), None),
        P("shard", None),
        P(),
        P("shard", "tp"),
        P("shard", "tp"),
        P("shard", "tp"),
        P("tp", "shard"),
        P("shard", "tp"),
        P("shard", "tp"),
        P("tp", "shard"),
        P("shard"),
        P("shard"),
        P("shard"),
        P("shard"),
    )
    return jax.shard_map(
        body,
        mesh=mesh,
        in_specs=placed,
        out_specs=(
            P(("shard", "ctx"), None),
            P(("shard", "ctx"), None),
            P("shard", "tp"),
            P("shard", "tp"),
            P("shard", "tp"),
            P("tp", "shard"),
            P("shard", "tp"),
            P("shard", "tp"),
            P("tp", "shard"),
            P("shard"),
            P("shard"),
            P("shard"),
            P("shard"),
        ),
        check_vma=False,
    )
```

```python
import functools

import jax
import jax.numpy as jnp
from jax import lax
from jax.experimental import pallas as pl
from jax.experimental.pallas import tpu as pltpu
from jax.sharding import PartitionSpec as P

EPS = 1e-06
THETA = 1000000.0
LOG2E = 1.4426950408889634
HEAD = 128
BF16 = jnp.bfloat16
F32 = jnp.float32
VMEM_LIMIT = 48 * 1024 * 1024
CHEAP = pl.CostEstimate(flops=1000, bytes_accessed=1000, transcendentals=0)


def rms_parts(values):
    factor = lax.rsqrt(jnp.mean(values * values, axis=-1, keepdims=True) + EPS)
    return (values * factor, factor)


def rms_back(grad_hat, normal, factor):
    return factor * (grad_hat - normal * jnp.mean(grad_hat * normal, axis=-1, keepdims=True))


def dot(a, b):
    return jnp.dot(a, b, preferred_element_type=F32)


def dot_nt(a, b):
    return lax.dot_general(a, b, (((1,), (1,)), ((), ())), preferred_element_type=F32)


def dot_tn(a, b):
    return lax.dot_general(a, b, (((0,), (0,)), ((), ())), preferred_element_type=F32)


def tie(*values):
    return lax.optimization_barrier(values)


def pieces_of(own, axis):
    count = lax.axis_size(axis)
    return [own] + [
        lax.ppermute(own, axis, [((i + j) % count, i) for i in range(count)])
        for j in range(1, count)
    ]


def join(pieces, dim, index):
    count = len(pieces)
    if count == 1:
        return pieces[0]
    if count == 2:
        return jnp.where(
            index == 0, jnp.concatenate(pieces, dim), jnp.concatenate(pieces[::-1], dim)
        )
    size = pieces[0].shape[dim]
    shape = list(pieces[0].shape)
    shape[dim] = size * count
    whole = jnp.zeros(shape, pieces[0].dtype)
    for j, piece in enumerate(pieces):
        whole = lax.dynamic_update_slice_in_dim(whole, piece, (index + j) % count * size, dim)
    return whole


def pair_total(partial):
    count = lax.axis_size("tp")
    partial = partial.astype(BF16)
    if count != 2:
        return lax.psum(partial, "tp").astype(F32)
    other = lax.ppermute(partial, "tp", [(0, 1), (1, 0)])
    return partial.astype(F32) + other.astype(F32)


def swap(value, axis, level=1):
    count = lax.axis_size(axis)
    return lax.ppermute(value, axis, [(i, i ^ level) for i in range(count)])


def place_in(masks):
    return (lax.axis_index("ctx") // masks[0]) % (1 << len(masks))


def exchange(values, done, turns):
    count = lax.axis_size("ctx")
    for d in turns:
        done[d] = lax.ppermute(values[d], "ctx", [(i, i ^ d) for i in range(count)])


def settle(done, turns, *values):
    tied = tie(*(done[d] for d in turns), *values)
    done.update(zip(turns, tied))
    return tied[len(turns) :]


def total(addends):
    return sum(a.astype(F32) for a in addends).astype(BF16)


def rows_at(addends, block, rows):
    return [lax.dynamic_slice_in_dim(a, block * rows, rows, 0) for a in addends]


def halve(addends, masks):
    size = 1 << len(masks)
    rows = addends[0].shape[0] // size
    place = place_in(masks)
    kept = rows_at(addends, place, rows)
    for turn in range(1, size):
        sent = total(rows_at(addends, place ^ turn, rows))
        kept = kept + [swap(sent, "ctx", turn * masks[0])]
    return kept


def scattered(pairs):
    grads = [dot_tn(a, b[:, lo:hi]).astype(BF16) for a, b, lo, hi in pairs]
    grad = jnp.concatenate(grads, axis=1)
    return [lax.psum_scatter(grad, "shard", scatter_dimension=0, tiled=True)]


def double(value, masks):
    size = 1 << len(masks)
    place = place_in(masks)
    blocks = [value] + [swap(value, "ctx", turn * masks[0]) for turn in range(1, size)]
    bit = 0
    while len(blocks) > 1:
        pairs = zip(blocks[::2], blocks[1::2])
        blocks = [join(list(pair), 0, (place >> bit) % 2) for pair in pairs]
        bit += 1
    return blocks[0]


def product_kernel(count, *refs):
    products = [dot_nt(refs[2 * i][...], refs[2 * i + 1][...]) for i in range(count)]
    refs[-1][...] = sum(products).astype(BF16)


def product_nt(*terms):
    rows = terms[0][0].shape[0]
    columns = terms[0][1].shape[0]
    step = min(columns, 256)
    specs, values = [], []
    for a, b, column in terms:
        depth = a.shape[1]
        specs.append(pl.BlockSpec((rows, depth), lambda i: (0, 0)))
        specs.append(pl.BlockSpec((step, depth), lambda i, column=column: (i, column)))
        values += [a, b]
    return pl.pallas_call(
        functools.partial(product_kernel, len(terms)),
        grid=(columns // step,),
        in_specs=specs,
        out_specs=pl.BlockSpec((rows, step), lambda i: (0, i)),
        out_shape=jax.ShapeDtypeStruct((rows, columns), BF16),
        compiler_params=pltpu.CompilerParams(vmem_limit_bytes=VMEM_LIMIT),
        cost_estimate=CHEAP,
    )(*values)


def split_product_kernel(spans, which_ref, *refs):
    j = pl.program_id(1)
    for i, (lo, hi) in enumerate(spans):

        @pl.when((j >= lo) & (j < hi))
        def _():
            refs[-1][...] = dot_tn(refs[2 * i][...], refs[2 * i + 1][...]).astype(BF16)


def split_product(which, pairs):
    tokens, model = pairs[0][0].shape
    rows = model // 4
    step = min(hi - lo for a, b, lo, hi in pairs)
    specs, values, spans, done = [], [], [], 0
    for a, b, lo, hi in pairs:
        blocks = (hi - lo) // step

        def column(i, j, w, first=done, base=lo // step, blocks=blocks):
            return (0, base + jnp.clip(j - first, 0, blocks - 1))

        specs.append(pl.BlockSpec((tokens, rows), lambda i, j, w: (0, w[i])))
        specs.append(pl.BlockSpec((tokens, step), column))
        values += [a, b]
        spans.append((done, done + blocks))
        done += blocks
    return pl.pallas_call(
        functools.partial(split_product_kernel, spans),
        grid_spec=pltpu.PrefetchScalarGridSpec(
            num_scalar_prefetch=1,
            grid=(2, done),
            in_specs=specs,
            out_specs=pl.BlockSpec((rows, step), lambda i, j, w: (i, j)),
        ),
        out_shape=jax.ShapeDtypeStruct((2 * rows, done * step), BF16),
        compiler_params=pltpu.CompilerParams(vmem_limit_bytes=VMEM_LIMIT),
        cost_estimate=CHEAP,
    )(jnp.stack(which).astype(jnp.int32), *values)


def rope_kernel(pre_ref, cos_ref, sin_ref, gain_ref, out_ref):
    pre = pre_ref[...]
    factor = lax.rsqrt(jnp.mean(pre * pre, axis=-1, keepdims=True) + EPS)
    scaled = pre * factor * gain_ref[...]
    turned = pltpu.roll(scaled, HEAD // 2, 1)
    out_ref[...] = (scaled * cos_ref[...] + turned * sin_ref[...]).astype(BF16)


def rope(pre, cosine, sine, gain):
    rows, width = pre.shape
    table = pl.BlockSpec((rows, HEAD), lambda h: (0, 0))
    column = pl.BlockSpec((rows, HEAD), lambda h: (0, h))
    return pl.pallas_call(
        rope_kernel,
        grid=(width // HEAD,),
        in_specs=[column, table, table, pl.BlockSpec((1, HEAD), lambda h: (0, 0))],
        out_specs=column,
        out_shape=jax.ShapeDtypeStruct((rows, width), BF16),
        compiler_params=pltpu.CompilerParams(vmem_limit_bytes=VMEM_LIMIT),
        cost_estimate=CHEAP,
    )(pre, cosine, sine, gain)


def part_start(meta_ref, docs, d, half):
    return pl.multiple_of((1 - meta_ref[docs + d]) * half, half)


def key_value_kernel(
    heads, docs, count, pieces, meta_ref, tokens_ref, factor_ref, scale_ref, *refs
):
    weights = refs[: 2 * pieces]
    cos_ref, sin_ref, gain_ref = refs[2 * pieces : 2 * pieces + 3]
    key_ref, out_ref, normed_ref = refs[2 * pieces + 3 : 2 * pieces + 6]
    sent = refs[2 * pieces + 6 :]
    half = out_ref.shape[0] // 2
    depth = tokens_ref.shape[1] // pieces
    step = pl.program_id(0)

    @pl.when(step == 0)
    def _():
        normal = tokens_ref[...].astype(F32) * factor_ref[...]
        normed_ref[...] = (normal * scale_ref[...]).astype(BF16)

    def product(parts):
        result = None
        for j, part in enumerate(parts):
            at = pl.multiple_of(meta_ref[docs + 2 * (count - 1) + j] * depth, HEAD)
            term = dot(normed_ref[:, pl.ds(at, depth)], part[...])
            result = term if result is None else result + term
        return result

    @pl.when(step < heads // 2)
    def _():
        key_ref[...] = product(weights[:pieces])
        for a in range(2):
            lanes = slice(a * HEAD, (a + 1) * HEAD)
            pre = key_ref[:, lanes]
            factor = lax.rsqrt(jnp.mean(pre * pre, axis=-1, keepdims=True) + EPS)
            scaled = pre * factor * gain_ref[...]
            turned = pltpu.roll(scaled, HEAD // 2, 1)
            out_ref[:, lanes] = (scaled * cos_ref[...] + turned * sin_ref[...]).astype(BF16)

    @pl.when(step >= heads // 2)
    def _():
        out_ref[...] = product(weights[pieces:]).astype(BF16)

    for d, sent_ref in enumerate(sent):
        sent_ref[...] = out_ref[pl.ds(part_start(meta_ref, docs, d, half), half), :]


def key_value_and_parts(
    meta, docs, count, tokens, factor, scale, keys, values, cosine, sine, gain
):
    rows, model = tokens.shape
    depth, width = keys[0].shape
    heads = width // HEAD
    half_steps = heads // 2
    whole = lambda shape: pl.BlockSpec(shape, lambda h, m: (0, 0))
    column = pl.BlockSpec((rows, 2 * HEAD), lambda h, m: (0, h))
    key_spec = pl.BlockSpec((depth, 2 * HEAD), lambda h, m: (0, jnp.minimum(h, half_steps - 1)))
    value_spec = pl.BlockSpec((depth, 2 * HEAD), lambda h, m: (0, jnp.maximum(h - half_steps, 0)))
    part = pl.BlockSpec((rows // 2, 2 * HEAD), lambda h, m: (0, h))
    result = pl.pallas_call(
        functools.partial(key_value_kernel, heads, docs, count, len(keys)),
        grid_spec=pltpu.PrefetchScalarGridSpec(
            num_scalar_prefetch=1,
            grid=(heads,),
            in_specs=[whole((rows, model)), whole((rows, 1)), whole((1, model))]
            + [key_spec] * len(keys)
            + [value_spec] * len(values)
            + [whole((rows, HEAD)), whole((rows, HEAD)), whole((1, HEAD))],
            out_specs=[
                pl.BlockSpec((rows, 2 * HEAD), lambda h, m: (0, jnp.minimum(h, half_steps - 1))),
                column,
                whole((rows, model)),
            ]
            + [part] * (count - 1),
        ),
        out_shape=[
            jax.ShapeDtypeStruct((rows, width), F32),
            jax.ShapeDtypeStruct((rows, 2 * width), BF16),
            jax.ShapeDtypeStruct((rows, model), BF16),
        ]
        + [jax.ShapeDtypeStruct((rows // 2, 2 * width), BF16)] * (count - 1),
        compiler_params=pltpu.CompilerParams(vmem_limit_bytes=VMEM_LIMIT),
        cost_estimate=CHEAP,
    )(meta, tokens, factor, scale, *keys, *values, cosine, sine, gain)
    return result[0], result[1], result[2], dict(zip(range(1, count), result[3:]))


def turn_back(grad, pre_ref, cos_ref, sin_ref, gain_ref, out_ref, sum_ref):
    pre = pre_ref[...]
    factor = lax.rsqrt(jnp.mean(pre * pre, axis=-1, keepdims=True) + EPS)
    hat = pre * factor
    back = grad * cos_ref[...] - pltpu.roll(grad, HEAD // 2, 1) * sin_ref[...]
    terms = jnp.sum(back * hat, axis=0, keepdims=True)

    @pl.when(pl.program_id(0) == 0)
    def _():
        sum_ref[...] = terms

    @pl.when(pl.program_id(0) > 0)
    def _():
        sum_ref[...] += terms

    back = back * gain_ref[...]
    inner = jnp.mean(back * hat, axis=-1, keepdims=True)
    out_ref[...] = (factor * (back - hat * inner)).astype(BF16)


def rope_back_kernel(grad_ref, *refs):
    turn_back(grad_ref[...], *refs)


def key_value_back_kernel(docs, meta_ref, own_ref, *refs):
    returned = refs[:-8]
    key_ref, cos_ref, sin_ref, gain_ref, d_key_ref, d_value_ref, sum_ref, acc_ref = refs[-8:]
    half = key_ref.shape[0] // 2
    acc_ref[...] = own_ref[...]
    for d, given_ref in enumerate(returned):
        rows = pl.ds(part_start(meta_ref, docs, d, half), half)
        acc_ref[:, rows, :] += given_ref[...].astype(F32)
    d_value_ref[...] = acc_ref[1].astype(BF16)
    turn_back(acc_ref[0], key_ref, cos_ref, sin_ref, gain_ref, d_key_ref, sum_ref)


def key_value_back(meta, docs, own, returned, key, cosine, sine, gain):
    rows, width = key.shape
    table = pl.BlockSpec((rows, HEAD), lambda h, m: (0, 0))
    column = pl.BlockSpec((rows, HEAD), lambda h, m: (0, h))
    one_row = pl.BlockSpec((1, HEAD), lambda h, m: (0, 0))
    return pl.pallas_call(
        functools.partial(key_value_back_kernel, docs),
        grid_spec=pltpu.PrefetchScalarGridSpec(
            num_scalar_prefetch=1,
            grid=(width // HEAD,),
            in_specs=[pl.BlockSpec((2, rows, HEAD), lambda h, m: (0, 0, h))]
            + [pl.BlockSpec((2, rows // 2, HEAD), lambda h, m: (0, 0, h))] * len(returned)
            + [column, table, table, one_row],
            out_specs=[column, column, one_row],
            scratch_shapes=[pltpu.VMEM((2, rows, HEAD), F32)],
        ),
        out_shape=[
            jax.ShapeDtypeStruct((rows, width), BF16),
            jax.ShapeDtypeStruct((rows, width), BF16),
            jax.ShapeDtypeStruct((1, HEAD), F32),
        ],
        compiler_params=pltpu.CompilerParams(vmem_limit_bytes=VMEM_LIMIT),
        cost_estimate=CHEAP,
    )(meta, own, *returned, key, cosine, sine, gain)


def rope_back(grad, pre, cosine, sine, gain):
    rows, width = grad.shape
    column = pl.BlockSpec((rows, HEAD), lambda h: (0, h))
    table = pl.BlockSpec((rows, HEAD), lambda h: (0, 0))
    one_row = pl.BlockSpec((1, HEAD), lambda h: (0, 0))
    return pl.pallas_call(
        rope_back_kernel,
        grid=(width // HEAD,),
        in_specs=[column, column, table, table, one_row],
        out_specs=[column, one_row],
        out_shape=[
            jax.ShapeDtypeStruct((rows, width), BF16),
            jax.ShapeDtypeStruct((1, HEAD), F32),
        ],
        compiler_params=pltpu.CompilerParams(vmem_limit_bytes=VMEM_LIMIT),
    )(grad, pre, cosine, sine, gain)


def doc_begins(meta_ref, docs, place):
    begin = jnp.zeros_like(place)
    for i in range(1, docs):
        start = meta_ref[i]
        begin = jnp.where(place >= start, start, begin)
    return begin


def block_mask(meta_ref, docs, shape, half, q_part, k_part, diagonal):
    row = lax.broadcasted_iota(jnp.int32, (shape[0], 1), 0)
    q_place = q_part * half + jnp.where(row >= half, row - half, row)
    begin = doc_begins(meta_ref, docs, q_place) - k_part * half
    column = lax.broadcasted_iota(jnp.int32, shape, 1)
    visible = column >= begin
    if diagonal:
        visible = visible & (column <= q_place - k_part * half)
    return visible


def mask_across(meta_ref, docs, shape, half, q_part, k_part, diagonal):
    column = lax.broadcasted_iota(jnp.int32, (1, shape[1]), 1)
    q_place = q_part * half + jnp.where(column >= half, column - half, column)
    begin = doc_begins(meta_ref, docs, q_place) - k_part * half
    row = lax.broadcasted_iota(jnp.int32, shape, 0)
    visible = row >= begin
    if diagonal:
        visible = visible & (row <= q_place - k_part * half)
    return visible


def any_visible(meta_ref, docs, half, q_part, k_part):
    return (k_part + 1) * half > doc_begins(meta_ref, docs, q_part * half)


def all_visible(meta_ref, docs, half, q_part, k_part):
    return k_part * half >= doc_begins(meta_ref, docs, q_part * half + half - 1)


def masked(weights, *mask_args):
    if mask_args[-1] is None:
        return weights
    return jnp.where(block_mask(*mask_args), weights, 0.0)


def two_heads(ref, start, half):
    rows = pl.ds(start, half)
    return jnp.concatenate([ref[rows, :HEAD], ref[rows, HEAD:]], axis=0)


def forward_kernel(docs, count, meta_ref, q_ref, k_ref, v_ref, *refs):
    others = refs[: 2 * (count - 1)]
    out_ref, out16_ref, lse_ref, acc_ref = refs[2 * (count - 1) :]
    half = q_ref.shape[0] // 2
    factor = HEAD**-0.5 * LOG2E
    ones = jnp.ones((half, HEAD), BF16)
    own = meta_ref[0]

    def block(start, keys, values, q_part, k_part, diagonal):
        scores = dot_nt(two_heads(q_ref, start, half), keys)
        weights = jnp.exp2(scores * factor)
        weights = masked(weights, meta_ref, docs, scores.shape, half, q_part, k_part, diagonal)
        weights = weights.astype(BF16)
        return dot(weights, jnp.concatenate([values, ones], axis=1))

    for e in range(2):
        rows = pl.ds(e * half, half)
        part = own if e == 0 else 2 * count - 1 - own
        acc_ref[e] = block(e * half, k_ref[rows, :], v_ref[rows, :], part, part, True)
    for d in range(count - 1):
        side = meta_ref[docs + d]
        k_part = meta_ref[docs + count - 1 + d]
        q_part = jnp.where(side == 0, own, 2 * count - 1 - own)

        def add(mask):
            start = pl.multiple_of(side * half, half)
            acc_ref[side] += block(
                start, others[2 * d][...], others[2 * d + 1][...], q_part, k_part, mask
            )

        seen = any_visible(meta_ref, docs, half, q_part, k_part)
        whole = all_visible(meta_ref, docs, half, q_part, k_part)
        pl.when(whole)(functools.partial(add, None))
        pl.when(seen & jnp.logical_not(whole))(functools.partial(add, False))

    for e in range(2):
        total = acc_ref[e]
        sums = total[:, HEAD:]
        result = total[:, :HEAD] / sums
        lse = jnp.log2(sums)
        for a in range(2):
            part = slice(a * half, (a + 1) * half)
            place = (pl.ds(e * half, half), slice(a * HEAD, (a + 1) * HEAD))
            out_ref[place] = result[part]
            out16_ref[place] = result[part].astype(BF16)
            lse_ref[place] = lse[part]


def backward_kernel(docs, count, meta_ref, q_ref, g_ref, o_ref, lse_ref, k_ref, v_ref, *refs):
    others = refs[: 2 * (count - 1)]
    dq_ref, dkv_ref = refs[2 * (count - 1) : 2 * count]
    given = refs[2 * count : 3 * count - 1]
    acc_ref, stats_ref, delta_ref = refs[3 * count - 1 :]
    half = q_ref.shape[0] // 2
    scale = HEAD**-0.5
    own = meta_ref[0]

    for e in range(2):
        grads = two_heads(g_ref, e * half, half).astype(F32)
        delta = jnp.sum(grads * two_heads(o_ref, e * half, half), axis=1, keepdims=True)
        delta = jnp.broadcast_to(delta, (2 * half, HEAD))
        delta_ref[e] = jnp.transpose(delta)[:8]
        stats_ref[e] = jnp.transpose(two_heads(lse_ref, e * half, half))[:8]

    def block(side, start, keys, values, q_part, k_part, diagonal):
        queries = two_heads(q_ref, start, half)
        grads = two_heads(g_ref, start, half)
        scores = dot_nt(keys, queries)
        lse = stats_ref[side][:1]
        delta = delta_ref[side][:1]
        weights = jnp.exp2(scores * (scale * LOG2E) - lse)
        if diagonal is not None:
            visible = mask_across(
                meta_ref, docs, scores.shape, half, q_part, k_part, diagonal
            )
            weights = jnp.where(visible, weights, 0.0)
        d_weights = dot_nt(values, grads)
        d_scores = (weights * (d_weights - delta)).astype(BF16)
        d_values = dot(weights.astype(BF16), grads)
        d_keys = dot(d_scores, queries) * scale
        return dot_tn(d_scores, keys) * scale, d_keys, d_values

    for e in range(2):
        rows = pl.ds(e * half, half)
        part = own if e == 0 else 2 * count - 1 - own
        d_queries, d_keys, d_values = block(
            e, e * half, k_ref[rows, :], v_ref[rows, :], part, part, True
        )
        acc_ref[e] = d_queries
        dkv_ref[0, rows, :] = d_keys
        dkv_ref[1, rows, :] = d_values
    for d in range(count - 1):
        side = meta_ref[docs + d]
        k_part = meta_ref[docs + count - 1 + d]
        q_part = jnp.where(side == 0, own, 2 * count - 1 - own)
        seen = any_visible(meta_ref, docs, half, q_part, k_part)
        whole = all_visible(meta_ref, docs, half, q_part, k_part)

        def add(mask):
            start = pl.multiple_of(side * half, half)
            d_queries, d_keys, d_values = block(
                side, start, others[2 * d][...], others[2 * d + 1][...], q_part, k_part, mask
            )
            acc_ref[side] += d_queries
            given[d][0] = d_keys.astype(BF16)
            given[d][1] = d_values.astype(BF16)

        pl.when(whole)(functools.partial(add, None))
        pl.when(seen & jnp.logical_not(whole))(functools.partial(add, False))

        @pl.when(jnp.logical_not(seen))
        def _():
            given[d][...] = jnp.zeros_like(given[d])

    for e in range(2):
        for a in range(2):
            dq_ref[pl.ds(e * half, half), a * HEAD : (a + 1) * HEAD] = acc_ref[
                e, a * half : (a + 1) * half, :
            ]


def key_value_specs(rows, half, kv_heads, count):
    own = [
        pl.BlockSpec((rows, HEAD), lambda h, m: (0, h)),
        pl.BlockSpec((rows, HEAD), lambda h, m: (0, kv_heads + h)),
    ]
    other = [
        pl.BlockSpec((half, HEAD), lambda h, m: (0, h)),
        pl.BlockSpec((half, HEAD), lambda h, m: (0, kv_heads + h)),
    ]
    return own + other * (count - 1)


def twice(arrays):
    return [a for a in arrays for _ in range(2)]


def attend(meta, docs, queries, key_value, others):
    rows, width = queries.shape
    half = rows // 2
    count = len(others) + 1
    kv_heads = key_value.shape[1] // (2 * HEAD)
    column = pl.BlockSpec((rows, 2 * HEAD), lambda h, m: (0, h))
    return pl.pallas_call(
        functools.partial(forward_kernel, docs, count),
        grid_spec=pltpu.PrefetchScalarGridSpec(
            num_scalar_prefetch=1,
            grid=(kv_heads,),
            in_specs=[column] + key_value_specs(rows, half, kv_heads, count),
            out_specs=[column] * 3,
            scratch_shapes=[pltpu.VMEM((2, 2 * half, 2 * HEAD), F32)],
        ),
        out_shape=[
            jax.ShapeDtypeStruct((rows, width), F32),
            jax.ShapeDtypeStruct((rows, width), BF16),
            jax.ShapeDtypeStruct((rows, width), F32),
        ],
        compiler_params=pltpu.CompilerParams(vmem_limit_bytes=VMEM_LIMIT),
        cost_estimate=CHEAP,
    )(meta, queries, key_value, key_value, *twice(others))


def attend_back(meta, docs, queries, grads, outs, lse, key_value, others):
    rows, width = queries.shape
    half = rows // 2
    count = len(others) + 1
    kv_width = key_value.shape[1] // 2
    kv_heads = kv_width // HEAD
    column = pl.BlockSpec((rows, 2 * HEAD), lambda h, m: (0, h))
    result = pl.pallas_call(
        functools.partial(backward_kernel, docs, count),
        grid_spec=pltpu.PrefetchScalarGridSpec(
            num_scalar_prefetch=1,
            grid=(kv_heads,),
            in_specs=[column] * 4 + key_value_specs(rows, half, kv_heads, count),
            out_specs=[column, pl.BlockSpec((2, rows, HEAD), lambda h, m: (0, 0, h))]
            + [pl.BlockSpec((2, half, HEAD), lambda h, m: (0, 0, h))] * (count - 1),
            scratch_shapes=[
                pltpu.VMEM((2, 2 * half, HEAD), F32),
                pltpu.VMEM((2, 8, 2 * half), F32),
                pltpu.VMEM((2, 8, 2 * half), F32),
            ],
        ),
        out_shape=[
            jax.ShapeDtypeStruct((rows, width), F32),
            jax.ShapeDtypeStruct((2, rows, kv_width), F32),
        ]
        + [jax.ShapeDtypeStruct((2, half, kv_width), BF16)] * (count - 1),
        compiler_params=pltpu.CompilerParams(vmem_limit_bytes=VMEM_LIMIT),
        cost_estimate=CHEAP,
    )(meta, queries, grads, outs, lse, key_value, key_value, *twice(others))
    return result[0], result[1], list(result[2:])


def body(
    tokens,
    cotangent,
    seq_lengths,
    part_order,
    w_query,
    key_weight,
    value_weight,
    w_out,
    w_gate,
    w_up,
    w_down,
    gain_in,
    gain_post,
    gain_q,
    gain_k,
):
    shard_count = lax.axis_size("shard")
    shard = lax.axis_index("shard")
    count = lax.axis_size("ctx")
    ctx = lax.axis_index("ctx")
    rows, model = tokens.shape
    half = rows // 2
    depth = model // shard_count
    docs = seq_lengths.shape[1]
    kv_width = key_weight.shape[1]
    units = w_gate.shape[1]
    heads_width = w_out.shape[0]

    masks = [1 << b for b in range(count.bit_length() - 1)]
    near_axis, far_axis = masks[:1], masks[1:]
    far = [d for d in range(1, count) if d >= count // 2]
    near = [d for d in range(1, count) if d < count // 2]
    crossing = [d for d in far + near if d % 2 == 1]
    straight = [d for d in far + near if d % 2 == 0]

    packed = jnp.concatenate([gain_in, gain_post, gain_q, gain_k])
    k_pieces = pieces_of(key_weight, "shard")
    v_pieces = pieces_of(value_weight, "shard")
    packed_pieces = pieces_of(packed, "shard")
    own_rest = jnp.concatenate([w_query, w_out.T, w_down.T], axis=1)
    own_gate_up = jnp.concatenate([w_gate, w_up], axis=1)

    turns = jnp.arange(count, dtype=jnp.int32)
    partner = jnp.bitwise_xor(ctx.astype(jnp.int32), turns)
    parts = jnp.sum(
        jnp.where(partner[:, None] == turns[None, :], part_order[:, 0][None, :], 0), axis=1
    )
    part = parts[:1]
    lengths = seq_lengths[0]
    order = jnp.arange(docs, dtype=jnp.int32)
    starts = jnp.sum(jnp.where(order[None, :] < order[:, None], lengths[None, :], 0), axis=1)
    meta = jnp.concatenate(
        [
            part,
            starts[1:],
            (parts[1:] >= part).astype(jnp.int32),
            jnp.where(parts[1:] < part, parts[1:], 2 * count - 1 - parts[1:]),
            (shard + jnp.arange(shard_count, dtype=jnp.int32)) % shard_count,
        ]
    ).astype(jnp.int32)
    row = jnp.arange(rows, dtype=jnp.int32)
    places = jnp.where(row < half, part * half + row, (2 * count - 2 - part) * half + row)
    reached = places[:, None] >= starts[None, :]
    begins = jnp.max(jnp.where(reached, starts[None, :], 0), axis=1)
    frequency = THETA ** (-jnp.arange(0, HEAD, 2, dtype=F32) / HEAD)
    angles = (places - begins).astype(F32)[:, None] * frequency[None, :]
    cosine, sine = jnp.cos(angles), jnp.sin(angles)
    cosine = jnp.concatenate([cosine, cosine], axis=-1)
    sine = jnp.concatenate([-sine, sine], axis=-1)

    inputs = tokens.astype(F32)
    normal_one, factor_one = rms_parts(inputs)

    bit = place_in(near_axis)
    half_rest = own_rest
    if shard_count == 2:
        half_rest = lax.dynamic_slice_in_dim(own_rest, bit * (depth // 2), depth // 2, 0)
    half_rest, own_gate_up, packed_pieces[-1], k_pieces[-1], v_pieces[-1] = tie(
        half_rest, own_gate_up, packed_pieces[-1], k_pieces[-1], v_pieces[-1]
    )
    cosine, sine, meta, factor_one, k_pieces[-1] = tie(
        cosine, sine, meta, factor_one, k_pieces[-1]
    )
    cuts = [0, depth, 2 * depth, 2 * depth + gain_q.shape[0], packed.shape[0]]
    scale_in, scale_post, scale_q, scale_k = (
        join([piece[lo:hi] for piece in packed_pieces], 0, shard).astype(F32).reshape(1, -1)
        for lo, hi in zip(cuts[:-1], cuts[1:])
    )
    full_key = join(k_pieces, 0, shard)
    full_value = join(v_pieces, 0, shard)

    full_gate_up = lax.all_gather(own_gate_up, "shard", axis=0, tiled=True)
    if shard_count == 2:
        half_rest = swap(half_rest, "shard")
    k_pre, key_value, normed_input, sent = key_value_and_parts(
        meta,
        docs,
        count,
        tokens,
        factor_one,
        scale_in,
        k_pieces,
        v_pieces,
        cosine,
        sine,
        scale_k,
    )
    held = {}
    exchange(sent, held, crossing)
    half_rest, *rest = settle(held, crossing, half_rest, *(sent[d] for d in straight))
    sent.update(zip(straight, rest))

    exchange(sent, held, straight)
    if shard_count == 2:
        query_half, rest_half = half_rest[:, :heads_width], half_rest[:, heads_width:]
        query_got = swap(query_half, "ctx", near_axis[0])
        query_got, rest_half = tie(query_got, rest_half)
        other_query = join([query_half, query_got], 0, bit)
        other_rest = join([rest_half, swap(rest_half, "ctx", near_axis[0])], 0, bit)
        full_query = join([own_rest[:, :heads_width], other_query], 0, shard)
        full_rest = join([own_rest[:, heads_width:], other_rest], 0, shard)
    else:
        full_rest = lax.all_gather(half_rest, "shard", axis=0, tiled=True)
        full_query, full_rest = full_rest[:, :heads_width], full_rest[:, heads_width:]
    full_out_t = full_rest[:, :heads_width]
    full_down_t = full_rest[:, heads_width:]
    q_pre = dot(normed_input, full_query)
    queries = rope(q_pre, cosine, sine, scale_q)
    queries, full_out_t = settle(held, straight, queries, full_out_t)
    held = [held[d] for d in range(1, count)]
    attended, attn_out, lse = attend(meta, docs, queries, key_value, held)

    residual = inputs + pair_total(dot_nt(attn_out, full_out_t))
    normal_two, factor_two = rms_parts(residual)
    normed_two = (normal_two * scale_post).astype(BF16)
    gate_upward = dot(normed_two, full_gate_up)
    gate_act = gate_upward[:, :units]
    upward = gate_upward[:, units:]
    sigma = jax.nn.sigmoid(gate_act)
    silu_act = gate_act * sigma
    hidden = (silu_act * upward).astype(BF16)
    d_hidden = dot(cotangent, full_down_t)
    d_gate = (d_hidden * upward * sigma * (1.0 + gate_act * (1.0 - sigma))).astype(BF16)
    d_up = (d_hidden * silu_act).astype(BF16)
    middle = units // 2
    away, home = (2 - 2 * shard, 3 - 2 * shard), (2 * shard, 2 * shard + 1)

    def pairs_a(normed):
        return [(normed, d_gate, 0, units), (normed, d_up, 0, middle)]

    def pairs_b(normed, upstream):
        return [(normed, d_up, middle, units), (upstream, hidden, 0, units)]

    if shard_count == 2:
        sent_a = split_product(away, pairs_a(normed_two))
        sent_b = split_product((1 - bit, 3 - bit), pairs_b(normed_two, cotangent))
        d_gate, d_up, sent_a, sent_b = tie(d_gate, d_up, sent_a, sent_b)
        got_a, got_b = swap(sent_a, "shard"), swap(sent_b, "ctx", near_axis[0])
    d_normed_two = pair_total(
        product_nt((d_gate, full_gate_up, 0), (d_up, full_gate_up, 1))
    )
    hidden, d_normed_two = tie(hidden, d_normed_two)
    mixed_part = product_nt((hidden, full_down_t, 0))
    mixed = (residual + pair_total(mixed_part)).astype(BF16)
    grad_post = jnp.sum(d_normed_two * normal_two, axis=0)
    d_residual = cotangent.astype(F32) + rms_back(
        d_normed_two * scale_post, normal_two, factor_two
    )

    d_branch = d_residual.astype(BF16)
    d_attn = dot(d_branch, full_out_t).astype(BF16)
    d_queries, d_kv, given = attend_back(
        meta, docs, queries, d_attn, attended, lse, key_value, held
    )
    given = dict(zip(range(1, count), given))
    returned = {}
    exchange(given, returned, crossing)
    normed_late, d_queries = tie(normed_two, d_queries)
    gates = crossing[:4]
    if shard_count == 2:
        normed_b, upstream_b, returned[gates[0]] = tie(
            normed_late, cotangent, returned[gates[0]]
        )
        kept_b = split_product((bit, 2 + bit), pairs_b(normed_b, upstream_b))
        normed_a, kept_b, returned[gates[1]] = tie(normed_late, kept_b, returned[gates[1]])
        kept_a = split_product(home, pairs_a(normed_a))
        d_queries, kept_a = tie(d_queries, kept_a)
    d_queries, returned[gates[2]] = tie(d_queries, returned[gates[2]])
    d_q_pre, gq_part = rope_back(d_queries, q_pre, cosine, sine, scale_q)
    d_q_pre, returned[gates[3]] = tie(d_q_pre, returned[gates[3]])
    out_pairs = [(d_branch, attn_out, 0, heads_width), (normed_input, d_q_pre, 0, heads_width)]
    if shard_count == 2:
        kept_out, sent_out = split_product(home, out_pairs), split_product(away, out_pairs)
        kept_a, kept_b, kept_out, sent_out, got_a, got_b, *rest = settle(
            returned,
            crossing,
            kept_a,
            kept_b,
            kept_out,
            sent_out,
            got_a,
            got_b,
            *(given[d] for d in straight),
        )
        given.update(zip(straight, rest))
    exchange(given, returned, straight)
    if shard_count == 2:
        units_a = halve([kept_a, got_a], near_axis)
        units_b = [kept_b, got_b]
        units_b_away = total(rows_at(units_b, 1 - shard, depth // 2))
        units_b = rows_at(units_b, shard, depth // 2) + [swap(units_b_away, "shard")]
        out_query = [kept_out, swap(sent_out, "shard")]
    else:
        units_a = halve(scattered(pairs_a(normed_two)), near_axis)
        units_b = halve(scattered(pairs_b(normed_two, cotangent)), near_axis)
        out_query = scattered(out_pairs)
    units_a[-1], units_b[-1], d_kv = settle(
        returned, straight, units_a[-1], units_b[-1], d_kv
    )
    returned = [returned[d] for d in range(1, count)]

    units_sum = halve([jnp.concatenate([total(units_a), total(units_b)], axis=1)], far_axis)
    d_k_pre, d_v_pre, gk_part = key_value_back(
        meta, docs, d_kv, returned, k_pre, cosine, sine, scale_k
    )
    d_k_pre, d_v_pre, out_query[-1] = tie(d_k_pre, d_v_pre, out_query[-1])
    out_query = halve(out_query, near_axis)
    kv_pairs = [(normed_input, d_k_pre, 0, kv_width), (normed_input, d_v_pre, 0, kv_width)]
    if shard_count == 2:
        sent_kv = swap(split_product(away, kv_pairs), "shard")
        key_value_grad = [split_product(home, kv_pairs), sent_kv]
    else:
        key_value_grad = scattered(kv_pairs)
    units_sum = total(units_sum)
    cut = units_sum.shape[1] // 2
    units_a, units_b = units_sum[:, :cut], units_sum[:, cut:]
    units_a, units_b, out_query[-1], key_value_grad[-1], d_q_pre, d_k_pre, d_v_pre = tie(
        units_a, units_b, out_query[-1], key_value_grad[-1], d_q_pre, d_k_pre, d_v_pre
    )

    units_a = double(units_a, far_axis)
    key_value_grad = halve(key_value_grad, near_axis)
    units_a, units_b, key_value_grad[-1], out_query[-1] = tie(
        units_a, units_b, key_value_grad[-1], out_query[-1]
    )

    units_b = double(units_b, far_axis)
    owned_a = double(units_a, near_axis)
    d_normed = pair_total(
        dot_nt(d_q_pre, full_query) + dot_nt(d_k_pre, full_key) + dot_nt(d_v_pre, full_value)
    )
    grad_in = jnp.sum(d_normed * normal_one, axis=0)
    input_grad = d_residual + rms_back(d_normed * scale_in, normal_one, factor_one)
    once = jnp.where(lax.axis_index("tp") == 0, 1.0, 0.0)
    gain_grads = jnp.concatenate([grad_in * once, grad_post * once, gq_part[0], gk_part[0]])
    gain_grads = gain_grads.reshape(-1, HEAD)
    if shard_count != 2:
        gain_grads = lax.psum(gain_grads, "shard")
    out_query, key_value_grad = total(out_query), total(key_value_grad)
    rest_chain = [
        jnp.concatenate(
            [
                out_query[:, :heads_width],
                key_value_grad[:, :kv_width],
                out_query[:, heads_width:],
                key_value_grad[:, kv_width:],
            ],
            axis=1,
        )
    ]
    units_b, owned_a, rest_chain[0], gain_grads = tie(
        units_b, owned_a, rest_chain[0], gain_grads
    )

    owned_b = double(units_b, near_axis)
    rest_chain = total(halve(rest_chain, far_axis))
    gain_grads = gain_grads + swap(gain_grads, "tp")
    gain_grads = gain_grads + swap(gain_grads, "ctx", masks[0])
    owned_b, rest_chain, gain_grads = tie(owned_b, rest_chain, gain_grads)

    cut = rest_chain.shape[1] // 2
    rest_a, rest_b = rest_chain[:, :cut], rest_chain[:, cut:]
    rest_a = double(rest_a, far_axis)
    gain_grads = gain_grads + swap(gain_grads, "ctx", masks[1])
    rest_a, rest_b, gain_grads = tie(rest_a, rest_b, gain_grads)

    rest_b = double(rest_b, far_axis)
    rest_a = double(rest_a, near_axis)
    for mask in masks[2:]:
        gain_grads = gain_grads + swap(gain_grads, "ctx", mask)
    rest_a, rest_b, gain_grads = tie(rest_a, rest_b, gain_grads)

    rest_b = double(rest_b, near_axis)
    if shard_count == 2:
        gain_grads = gain_grads + swap(gain_grads, "shard")
    gain_grads = gain_grads.reshape(-1)
    owned_up = jnp.concatenate([owned_a[:, units:], owned_b[:, :middle]], axis=1)
    own_gains = []
    for lo, size in ((0, model), (model, model), (2 * model, HEAD), (2 * model + HEAD, HEAD)):
        size = size // shard_count
        own_gains.append(lax.dynamic_slice_in_dim(gain_grads, lo + shard * size, size, 0))
    return (
        mixed,
        input_grad,
        rest_b[:, :heads_width].astype(F32),
        rest_a[:, heads_width:].astype(F32),
        rest_b[:, heads_width:].astype(F32),
        rest_a[:, :heads_width].astype(F32).T,
        owned_a[:, :units].astype(F32),
        owned_up.astype(F32),
        owned_b[:, middle:].astype(F32).T,
        *own_gains,
    )


def solution(mesh):
    placed = (
        P(("shard", "ctx"), None),
        P(("shard", "ctx"), None),
        P("shard", None),
        P(),
        P("shard", "tp"),
        P("shard", "tp"),
        P("shard", "tp"),
        P("tp", "shard"),
        P("shard", "tp"),
        P("shard", "tp"),
        P("tp", "shard"),
        P("shard"),
        P("shard"),
        P("shard"),
        P("shard"),
    )
    return jax.shard_map(
        body,
        mesh=mesh,
        in_specs=placed,
        out_specs=(
            P(("shard", "ctx"), None),
            P(("shard", "ctx"), None),
            P("shard", "tp"),
            P("shard", "tp"),
            P("shard", "tp"),
            P("tp", "shard"),
            P("shard", "tp"),
            P("shard", "tp"),
            P("tp", "shard"),
            P("shard"),
            P("shard"),
            P("shard"),
            P("shard"),
        ),
        check_vma=False,
    )
```

```python
import functools

import jax
import jax.numpy as jnp
from jax import lax
from jax.experimental import pallas as pl
from jax.experimental.pallas import tpu as pltpu
from jax.sharding import PartitionSpec as P

EPS = 1e-06
THETA = 1000000.0
LOG2E = 1.4426950408889634
HEAD = 128
BF16 = jnp.bfloat16
F32 = jnp.float32
VMEM_LIMIT = 48 * 1024 * 1024
CHEAP = pl.CostEstimate(flops=1000, bytes_accessed=1000, transcendentals=0)


def rms_parts(values):
    factor = lax.rsqrt(jnp.mean(values * values, axis=-1, keepdims=True) + EPS)
    return (values * factor, factor)


def rms_back(grad_hat, normal, factor):
    return factor * (grad_hat - normal * jnp.mean(grad_hat * normal, axis=-1, keepdims=True))


def dot(a, b):
    return jnp.dot(a, b, preferred_element_type=F32)


def dot_nt(a, b):
    return lax.dot_general(a, b, (((1,), (1,)), ((), ())), preferred_element_type=F32)


def dot_tn(a, b):
    return lax.dot_general(a, b, (((0,), (0,)), ((), ())), preferred_element_type=F32)


def tie(*values):
    return lax.optimization_barrier(values)


def pieces_of(own, axis):
    count = lax.axis_size(axis)
    return [own] + [
        lax.ppermute(own, axis, [((i + j) % count, i) for i in range(count)])
        for j in range(1, count)
    ]


def join(pieces, dim, index):
    count = len(pieces)
    if count == 1:
        return pieces[0]
    if count == 2:
        return jnp.where(
            index == 0, jnp.concatenate(pieces, dim), jnp.concatenate(pieces[::-1], dim)
        )
    size = pieces[0].shape[dim]
    shape = list(pieces[0].shape)
    shape[dim] = size * count
    whole = jnp.zeros(shape, pieces[0].dtype)
    for j, piece in enumerate(pieces):
        whole = lax.dynamic_update_slice_in_dim(whole, piece, (index + j) % count * size, dim)
    return whole


def pair_total(partial):
    count = lax.axis_size("tp")
    partial = partial.astype(BF16)
    if count != 2:
        return lax.psum(partial, "tp").astype(F32)
    other = lax.ppermute(partial, "tp", [(0, 1), (1, 0)])
    return partial.astype(F32) + other.astype(F32)


def swap(value, axis, level=1):
    count = lax.axis_size(axis)
    return lax.ppermute(value, axis, [(i, i ^ level) for i in range(count)])


def place_in(masks):
    return (lax.axis_index("ctx") // masks[0]) % (1 << len(masks))


def exchange(values, done, turns):
    count = lax.axis_size("ctx")
    for d in turns:
        done[d] = lax.ppermute(values[d], "ctx", [(i, i ^ d) for i in range(count)])


def settle(done, turns, *values):
    tied = tie(*(done[d] for d in turns), *values)
    done.update(zip(turns, tied))
    return tied[len(turns) :]


def total(addends):
    return sum(a.astype(F32) for a in addends).astype(BF16)


def rows_at(addends, block, rows):
    return [lax.dynamic_slice_in_dim(a, block * rows, rows, 0) for a in addends]


def halve(addends, masks):
    size = 1 << len(masks)
    rows = addends[0].shape[0] // size
    place = place_in(masks)
    kept = rows_at(addends, place, rows)
    for turn in range(1, size):
        sent = total(rows_at(addends, place ^ turn, rows))
        kept = kept + [swap(sent, "ctx", turn * masks[0])]
    return kept


def scattered(pairs):
    grads = [dot_tn(a, b[:, lo:hi]).astype(BF16) for a, b, lo, hi in pairs]
    grad = jnp.concatenate(grads, axis=1)
    return [lax.psum_scatter(grad, "shard", scatter_dimension=0, tiled=True)]


def double(value, masks):
    size = 1 << len(masks)
    place = place_in(masks)
    blocks = [value] + [swap(value, "ctx", turn * masks[0]) for turn in range(1, size)]
    bit = 0
    while len(blocks) > 1:
        pairs = zip(blocks[::2], blocks[1::2])
        blocks = [join(list(pair), 0, (place >> bit) % 2) for pair in pairs]
        bit += 1
    return blocks[0]


def product_kernel(count, *refs):
    products = [dot_nt(refs[2 * i][...], refs[2 * i + 1][...]) for i in range(count)]
    refs[-1][...] = sum(products).astype(BF16)


def product_nt(*terms):
    rows = terms[0][0].shape[0]
    columns = terms[0][1].shape[0]
    step = min(columns, 256)
    specs, values = [], []
    for a, b, column in terms:
        depth = a.shape[1]
        specs.append(pl.BlockSpec((rows, depth), lambda i: (0, 0)))
        specs.append(pl.BlockSpec((step, depth), lambda i, column=column: (i, column)))
        values += [a, b]
    return pl.pallas_call(
        functools.partial(product_kernel, len(terms)),
        grid=(columns // step,),
        in_specs=specs,
        out_specs=pl.BlockSpec((rows, step), lambda i: (0, i)),
        out_shape=jax.ShapeDtypeStruct((rows, columns), BF16),
        compiler_params=pltpu.CompilerParams(vmem_limit_bytes=VMEM_LIMIT),
        cost_estimate=CHEAP,
    )(*values)


def split_product_kernel(spans, which_ref, *refs):
    j = pl.program_id(1)
    for i, (lo, hi) in enumerate(spans):

        @pl.when((j >= lo) & (j < hi))
        def _():
            refs[-1][...] = dot_tn(refs[2 * i][...], refs[2 * i + 1][...]).astype(BF16)


def split_product(which, pairs):
    tokens, model = pairs[0][0].shape
    rows = model // 4
    step = min(hi - lo for a, b, lo, hi in pairs)
    specs, values, spans, done = [], [], [], 0
    for a, b, lo, hi in pairs:
        blocks = (hi - lo) // step

        def column(i, j, w, first=done, base=lo // step, blocks=blocks):
            return (0, base + jnp.clip(j - first, 0, blocks - 1))

        specs.append(pl.BlockSpec((tokens, rows), lambda i, j, w: (0, w[i])))
        specs.append(pl.BlockSpec((tokens, step), column))
        values += [a, b]
        spans.append((done, done + blocks))
        done += blocks
    return pl.pallas_call(
        functools.partial(split_product_kernel, spans),
        grid_spec=pltpu.PrefetchScalarGridSpec(
            num_scalar_prefetch=1,
            grid=(2, done),
            in_specs=specs,
            out_specs=pl.BlockSpec((rows, step), lambda i, j, w: (i, j)),
        ),
        out_shape=jax.ShapeDtypeStruct((2 * rows, done * step), BF16),
        compiler_params=pltpu.CompilerParams(vmem_limit_bytes=VMEM_LIMIT),
        cost_estimate=CHEAP,
    )(jnp.stack(which).astype(jnp.int32), *values)


def rope_kernel(pre_ref, cos_ref, sin_ref, gain_ref, out_ref):
    pre = pre_ref[...]
    factor = lax.rsqrt(jnp.mean(pre * pre, axis=-1, keepdims=True) + EPS)
    scaled = pre * factor * gain_ref[...]
    turned = pltpu.roll(scaled, HEAD // 2, 1)
    out_ref[...] = (scaled * cos_ref[...] + turned * sin_ref[...]).astype(BF16)


def rope(pre, cosine, sine, gain):
    rows, width = pre.shape
    table = pl.BlockSpec((rows, HEAD), lambda h: (0, 0))
    column = pl.BlockSpec((rows, HEAD), lambda h: (0, h))
    return pl.pallas_call(
        rope_kernel,
        grid=(width // HEAD,),
        in_specs=[column, table, table, pl.BlockSpec((1, HEAD), lambda h: (0, 0))],
        out_specs=column,
        out_shape=jax.ShapeDtypeStruct((rows, width), BF16),
        compiler_params=pltpu.CompilerParams(vmem_limit_bytes=VMEM_LIMIT),
        cost_estimate=CHEAP,
    )(pre, cosine, sine, gain)


def part_start(meta_ref, docs, d, half):
    return pl.multiple_of((1 - meta_ref[docs + d]) * half, half)


def key_value_kernel(
    heads, docs, count, pieces, meta_ref, tokens_ref, factor_ref, scale_ref, *refs
):
    weights = refs[: 2 * pieces]
    cos_ref, sin_ref, gain_ref = refs[2 * pieces : 2 * pieces + 3]
    key_ref, out_ref, normed_ref = refs[2 * pieces + 3 : 2 * pieces + 6]
    sent = refs[2 * pieces + 6 :]
    half = out_ref.shape[0] // 2
    depth = tokens_ref.shape[1] // pieces
    step = pl.program_id(0)

    @pl.when(step == 0)
    def _():
        normal = tokens_ref[...].astype(F32) * factor_ref[...]
        normed_ref[...] = (normal * scale_ref[...]).astype(BF16)

    def product(parts):
        result = None
        for j, part in enumerate(parts):
            at = pl.multiple_of(meta_ref[docs + 2 * (count - 1) + j] * depth, HEAD)
            term = dot(normed_ref[:, pl.ds(at, depth)], part[...])
            result = term if result is None else result + term
        return result

    @pl.when(step < heads // 2)
    def _():
        key_ref[...] = product(weights[:pieces])
        for a in range(2):
            lanes = slice(a * HEAD, (a + 1) * HEAD)
            pre = key_ref[:, lanes]
            factor = lax.rsqrt(jnp.mean(pre * pre, axis=-1, keepdims=True) + EPS)
            scaled = pre * factor * gain_ref[...]
            turned = pltpu.roll(scaled, HEAD // 2, 1)
            out_ref[:, lanes] = (scaled * cos_ref[...] + turned * sin_ref[...]).astype(BF16)

    @pl.when(step >= heads // 2)
    def _():
        out_ref[...] = product(weights[pieces:]).astype(BF16)

    for d, sent_ref in enumerate(sent):
        sent_ref[...] = out_ref[pl.ds(part_start(meta_ref, docs, d, half), half), :]


def key_value_and_parts(
    meta, docs, count, tokens, factor, scale, keys, values, cosine, sine, gain
):
    rows, model = tokens.shape
    depth, width = keys[0].shape
    heads = width // HEAD
    half_steps = heads // 2
    whole = lambda shape: pl.BlockSpec(shape, lambda h, m: (0, 0))
    column = pl.BlockSpec((rows, 2 * HEAD), lambda h, m: (0, h))
    key_spec = pl.BlockSpec((depth, 2 * HEAD), lambda h, m: (0, jnp.minimum(h, half_steps - 1)))
    value_spec = pl.BlockSpec((depth, 2 * HEAD), lambda h, m: (0, jnp.maximum(h - half_steps, 0)))
    part = pl.BlockSpec((rows // 2, 2 * HEAD), lambda h, m: (0, h))
    result = pl.pallas_call(
        functools.partial(key_value_kernel, heads, docs, count, len(keys)),
        grid_spec=pltpu.PrefetchScalarGridSpec(
            num_scalar_prefetch=1,
            grid=(heads,),
            in_specs=[whole((rows, model)), whole((rows, 1)), whole((1, model))]
            + [key_spec] * len(keys)
            + [value_spec] * len(values)
            + [whole((rows, HEAD)), whole((rows, HEAD)), whole((1, HEAD))],
            out_specs=[
                pl.BlockSpec((rows, 2 * HEAD), lambda h, m: (0, jnp.minimum(h, half_steps - 1))),
                column,
                whole((rows, model)),
            ]
            + [part] * (count - 1),
        ),
        out_shape=[
            jax.ShapeDtypeStruct((rows, width), F32),
            jax.ShapeDtypeStruct((rows, 2 * width), BF16),
            jax.ShapeDtypeStruct((rows, model), BF16),
        ]
        + [jax.ShapeDtypeStruct((rows // 2, 2 * width), BF16)] * (count - 1),
        compiler_params=pltpu.CompilerParams(vmem_limit_bytes=VMEM_LIMIT),
        cost_estimate=CHEAP,
    )(meta, tokens, factor, scale, *keys, *values, cosine, sine, gain)
    return result[0], result[1], result[2], dict(zip(range(1, count), result[3:]))


def turn_back(grad, pre_ref, cos_ref, sin_ref, gain_ref, out_ref, sum_ref):
    pre = pre_ref[...]
    factor = lax.rsqrt(jnp.mean(pre * pre, axis=-1, keepdims=True) + EPS)
    hat = pre * factor
    back = grad * cos_ref[...] - pltpu.roll(grad, HEAD // 2, 1) * sin_ref[...]
    terms = jnp.sum(back * hat, axis=0, keepdims=True)

    @pl.when(pl.program_id(0) == 0)
    def _():
        sum_ref[...] = terms

    @pl.when(pl.program_id(0) > 0)
    def _():
        sum_ref[...] += terms

    back = back * gain_ref[...]
    inner = jnp.mean(back * hat, axis=-1, keepdims=True)
    out_ref[...] = (factor * (back - hat * inner)).astype(BF16)


def rope_back_kernel(grad_ref, *refs):
    turn_back(grad_ref[...], *refs)


def key_value_back_kernel(docs, meta_ref, own_ref, *refs):
    returned = refs[:-8]
    key_ref, cos_ref, sin_ref, gain_ref, d_key_ref, d_value_ref, sum_ref, acc_ref = refs[-8:]
    half = key_ref.shape[0] // 2
    acc_ref[...] = own_ref[...]
    for d, given_ref in enumerate(returned):
        rows = pl.ds(part_start(meta_ref, docs, d, half), half)
        acc_ref[:, rows, :] += given_ref[...].astype(F32)
    d_value_ref[...] = acc_ref[1].astype(BF16)
    turn_back(acc_ref[0], key_ref, cos_ref, sin_ref, gain_ref, d_key_ref, sum_ref)


def key_value_back(meta, docs, own, returned, key, cosine, sine, gain):
    rows, width = key.shape
    table = pl.BlockSpec((rows, HEAD), lambda h, m: (0, 0))
    column = pl.BlockSpec((rows, HEAD), lambda h, m: (0, h))
    one_row = pl.BlockSpec((1, HEAD), lambda h, m: (0, 0))
    return pl.pallas_call(
        functools.partial(key_value_back_kernel, docs),
        grid_spec=pltpu.PrefetchScalarGridSpec(
            num_scalar_prefetch=1,
            grid=(width // HEAD,),
            in_specs=[pl.BlockSpec((2, rows, HEAD), lambda h, m: (0, 0, h))]
            + [pl.BlockSpec((2, rows // 2, HEAD), lambda h, m: (0, 0, h))] * len(returned)
            + [column, table, table, one_row],
            out_specs=[column, column, one_row],
            scratch_shapes=[pltpu.VMEM((2, rows, HEAD), F32)],
        ),
        out_shape=[
            jax.ShapeDtypeStruct((rows, width), BF16),
            jax.ShapeDtypeStruct((rows, width), BF16),
            jax.ShapeDtypeStruct((1, HEAD), F32),
        ],
        compiler_params=pltpu.CompilerParams(vmem_limit_bytes=VMEM_LIMIT),
        cost_estimate=CHEAP,
    )(meta, own, *returned, key, cosine, sine, gain)


def rope_back(grad, pre, cosine, sine, gain):
    rows, width = grad.shape
    column = pl.BlockSpec((rows, HEAD), lambda h: (0, h))
    table = pl.BlockSpec((rows, HEAD), lambda h: (0, 0))
    one_row = pl.BlockSpec((1, HEAD), lambda h: (0, 0))
    return pl.pallas_call(
        rope_back_kernel,
        grid=(width // HEAD,),
        in_specs=[column, column, table, table, one_row],
        out_specs=[column, one_row],
        out_shape=[
            jax.ShapeDtypeStruct((rows, width), BF16),
            jax.ShapeDtypeStruct((1, HEAD), F32),
        ],
        compiler_params=pltpu.CompilerParams(vmem_limit_bytes=VMEM_LIMIT),
    )(grad, pre, cosine, sine, gain)


def doc_begins(meta_ref, docs, place):
    begin = jnp.zeros_like(place)
    for i in range(1, docs):
        start = meta_ref[i]
        begin = jnp.where(place >= start, start, begin)
    return begin


def mask_across(meta_ref, docs, shape, half, q_part, k_part, diagonal):
    column = lax.broadcasted_iota(jnp.int32, (1, shape[1]), 1)
    q_place = q_part * half + jnp.where(column >= half, column - half, column)
    begin = doc_begins(meta_ref, docs, q_place) - k_part * half
    row = lax.broadcasted_iota(jnp.int32, shape, 0)
    visible = row >= begin
    if diagonal:
        visible = visible & (row <= q_place - k_part * half)
    return visible


def two_heads(ref, start, half):
    rows = pl.ds(start, half)
    return jnp.concatenate([ref[rows, :HEAD], ref[rows, HEAD:]], axis=0)


def forward_kernel(docs, count, meta_ref, q_ref, k_ref, v_ref, *refs):
    others = refs[: 2 * (count - 1)]
    out_ref, out16_ref, lse_ref, acc_ref, begin_ref = refs[2 * (count - 1) :]
    half = q_ref.shape[0] // 2
    factor = HEAD**-0.5 * LOG2E
    ones = jnp.ones((half, HEAD), BF16)
    own = meta_ref[0]
    parts = (own, 2 * count - 1 - own)

    @pl.when(pl.program_id(0) == 0)
    def _():
        row = lax.broadcasted_iota(jnp.int32, (2 * half, HEAD), 0)
        for e in range(2):
            place = parts[e] * half + jnp.where(row >= half, row - half, row)
            begin_ref[e] = doc_begins(meta_ref, docs, place)

    def block(side, start, keys, values, k_part, diagonal):
        scores = dot_nt(two_heads(q_ref, start, half), keys)
        column = lax.broadcasted_iota(jnp.int32, scores.shape, 1)
        begin = begin_ref[side] - k_part * half
        visible = column >= jnp.concatenate([begin] * (half // HEAD), axis=1)
        if diagonal:
            row = lax.broadcasted_iota(jnp.int32, scores.shape, 0)
            visible = visible & (column <= jnp.where(row >= half, row - half, row))
        weights = jnp.where(visible, jnp.exp2(scores * factor), 0.0).astype(BF16)
        return dot(weights, jnp.concatenate([values, ones], axis=1))

    for e in range(2):
        rows = pl.ds(e * half, half)
        acc_ref[e] = block(e, e * half, k_ref[rows, :], v_ref[rows, :], parts[e], True)
    for d in range(count - 1):
        side = meta_ref[docs + d]
        k_part = meta_ref[docs + count - 1 + d]
        start = pl.multiple_of(side * half, half)
        acc_ref[side] += block(
            side, start, others[2 * d][...], others[2 * d + 1][...], k_part, False
        )

    for e in range(2):
        total = acc_ref[e]
        sums = total[:, HEAD:]
        result = total[:, :HEAD] / sums
        lse = jnp.log2(sums)
        for a in range(2):
            part = slice(a * half, (a + 1) * half)
            place = (pl.ds(e * half, half), slice(a * HEAD, (a + 1) * HEAD))
            out_ref[place] = result[part]
            out16_ref[place] = result[part].astype(BF16)
            lse_ref[place] = lse[part]


def backward_kernel(docs, count, meta_ref, q_ref, g_ref, o_ref, lse_ref, k_ref, v_ref, *refs):
    others = refs[: 2 * (count - 1)]
    dq_ref, dkv_ref = refs[2 * (count - 1) : 2 * count]
    given = refs[2 * count : 3 * count - 1]
    acc_ref, stats_ref, delta_ref = refs[3 * count - 1 :]
    half = q_ref.shape[0] // 2
    scale = HEAD**-0.5
    own = meta_ref[0]

    for e in range(2):
        grads = two_heads(g_ref, e * half, half).astype(F32)
        delta = jnp.sum(grads * two_heads(o_ref, e * half, half), axis=1, keepdims=True)
        delta = jnp.broadcast_to(delta, (2 * half, HEAD))
        delta_ref[e] = jnp.transpose(delta)[:8]
        stats_ref[e] = jnp.transpose(two_heads(lse_ref, e * half, half))[:8]

    def block(side, start, keys, values, q_part, k_part, diagonal):
        queries = two_heads(q_ref, start, half)
        grads = two_heads(g_ref, start, half)
        scores = dot_nt(keys, queries)
        lse = stats_ref[side][:1]
        delta = delta_ref[side][:1]
        weights = jnp.exp2(scores * (scale * LOG2E) - lse)
        visible = mask_across(meta_ref, docs, scores.shape, half, q_part, k_part, diagonal)
        weights = jnp.where(visible, weights, 0.0)
        d_weights = dot_nt(values, grads)
        d_scores = (weights * (d_weights - delta)).astype(BF16)
        d_values = dot(weights.astype(BF16), grads)
        d_keys = dot(d_scores, queries) * scale
        return dot_tn(d_scores, keys) * scale, d_keys, d_values

    for e in range(2):
        rows = pl.ds(e * half, half)
        part = own if e == 0 else 2 * count - 1 - own
        d_queries, d_keys, d_values = block(
            e, e * half, k_ref[rows, :], v_ref[rows, :], part, part, True
        )
        acc_ref[e] = d_queries
        dkv_ref[0, rows, :] = d_keys
        dkv_ref[1, rows, :] = d_values
    for d in range(count - 1):
        side = meta_ref[docs + d]
        k_part = meta_ref[docs + count - 1 + d]
        q_part = jnp.where(side == 0, own, 2 * count - 1 - own)
        start = pl.multiple_of(side * half, half)
        d_queries, d_keys, d_values = block(
            side, start, others[2 * d][...], others[2 * d + 1][...], q_part, k_part, False
        )
        acc_ref[side] += d_queries
        given[d][0] = d_keys.astype(BF16)
        given[d][1] = d_values.astype(BF16)

    for e in range(2):
        for a in range(2):
            dq_ref[pl.ds(e * half, half), a * HEAD : (a + 1) * HEAD] = acc_ref[
                e, a * half : (a + 1) * half, :
            ]


def key_value_specs(rows, half, kv_heads, count):
    own = [
        pl.BlockSpec((rows, HEAD), lambda h, m: (0, h)),
        pl.BlockSpec((rows, HEAD), lambda h, m: (0, kv_heads + h)),
    ]
    other = [
        pl.BlockSpec((half, HEAD), lambda h, m: (0, h)),
        pl.BlockSpec((half, HEAD), lambda h, m: (0, kv_heads + h)),
    ]
    return own + other * (count - 1)


def twice(arrays):
    return [a for a in arrays for _ in range(2)]


def attend(meta, docs, queries, key_value, others):
    rows, width = queries.shape
    half = rows // 2
    count = len(others) + 1
    kv_heads = key_value.shape[1] // (2 * HEAD)
    column = pl.BlockSpec((rows, 2 * HEAD), lambda h, m: (0, h))
    return pl.pallas_call(
        functools.partial(forward_kernel, docs, count),
        grid_spec=pltpu.PrefetchScalarGridSpec(
            num_scalar_prefetch=1,
            grid=(kv_heads,),
            in_specs=[column] + key_value_specs(rows, half, kv_heads, count),
            out_specs=[column] * 3,
            scratch_shapes=[
                pltpu.VMEM((2, 2 * half, 2 * HEAD), F32),
                pltpu.VMEM((2, 2 * half, HEAD), jnp.int32),
            ],
        ),
        out_shape=[
            jax.ShapeDtypeStruct((rows, width), F32),
            jax.ShapeDtypeStruct((rows, width), BF16),
            jax.ShapeDtypeStruct((rows, width), F32),
        ],
        compiler_params=pltpu.CompilerParams(vmem_limit_bytes=VMEM_LIMIT),
        cost_estimate=CHEAP,
    )(meta, queries, key_value, key_value, *twice(others))


def attend_back(meta, docs, queries, grads, outs, lse, key_value, others):
    rows, width = queries.shape
    half = rows // 2
    count = len(others) + 1
    kv_width = key_value.shape[1] // 2
    kv_heads = kv_width // HEAD
    column = pl.BlockSpec((rows, 2 * HEAD), lambda h, m: (0, h))
    result = pl.pallas_call(
        functools.partial(backward_kernel, docs, count),
        grid_spec=pltpu.PrefetchScalarGridSpec(
            num_scalar_prefetch=1,
            grid=(kv_heads,),
            in_specs=[column] * 4 + key_value_specs(rows, half, kv_heads, count),
            out_specs=[column, pl.BlockSpec((2, rows, HEAD), lambda h, m: (0, 0, h))]
            + [pl.BlockSpec((2, half, HEAD), lambda h, m: (0, 0, h))] * (count - 1),
            scratch_shapes=[
                pltpu.VMEM((2, 2 * half, HEAD), F32),
                pltpu.VMEM((2, 8, 2 * half), F32),
                pltpu.VMEM((2, 8, 2 * half), F32),
            ],
        ),
        out_shape=[
            jax.ShapeDtypeStruct((rows, width), F32),
            jax.ShapeDtypeStruct((2, rows, kv_width), F32),
        ]
        + [jax.ShapeDtypeStruct((2, half, kv_width), BF16)] * (count - 1),
        compiler_params=pltpu.CompilerParams(vmem_limit_bytes=VMEM_LIMIT),
        cost_estimate=CHEAP,
    )(meta, queries, grads, outs, lse, key_value, key_value, *twice(others))
    return result[0], result[1], list(result[2:])


def body(
    tokens,
    cotangent,
    seq_lengths,
    part_order,
    w_query,
    key_weight,
    value_weight,
    w_out,
    w_gate,
    w_up,
    w_down,
    gain_in,
    gain_post,
    gain_q,
    gain_k,
):
    shard_count = lax.axis_size("shard")
    shard = lax.axis_index("shard")
    count = lax.axis_size("ctx")
    ctx = lax.axis_index("ctx")
    rows, model = tokens.shape
    half = rows // 2
    depth = model // shard_count
    docs = seq_lengths.shape[1]
    kv_width = key_weight.shape[1]
    units = w_gate.shape[1]
    heads_width = w_out.shape[0]

    masks = [1 << b for b in range(count.bit_length() - 1)]
    near_axis, far_axis = masks[:1], masks[1:]
    far = [d for d in range(1, count) if d >= count // 2]
    near = [d for d in range(1, count) if d < count // 2]
    crossing = [d for d in far + near if d % 2 == 1]
    straight = [d for d in far + near if d % 2 == 0]

    packed = jnp.concatenate([gain_in, gain_post, gain_q, gain_k])
    k_pieces = pieces_of(key_weight, "shard")
    v_pieces = pieces_of(value_weight, "shard")
    packed_pieces = pieces_of(packed, "shard")
    own_rest = jnp.concatenate([w_query, w_out.T, w_down.T], axis=1)
    own_gate_up = jnp.concatenate([w_gate, w_up], axis=1)

    turns = jnp.arange(count, dtype=jnp.int32)
    partner = jnp.bitwise_xor(ctx.astype(jnp.int32), turns)
    parts = jnp.sum(
        jnp.where(partner[:, None] == turns[None, :], part_order[:, 0][None, :], 0), axis=1
    )
    part = parts[:1]
    lengths = seq_lengths[0]
    order = jnp.arange(docs, dtype=jnp.int32)
    starts = jnp.sum(jnp.where(order[None, :] < order[:, None], lengths[None, :], 0), axis=1)
    meta = jnp.concatenate(
        [
            part,
            starts[1:],
            (parts[1:] >= part).astype(jnp.int32),
            jnp.where(parts[1:] < part, parts[1:], 2 * count - 1 - parts[1:]),
            (shard + jnp.arange(shard_count, dtype=jnp.int32)) % shard_count,
        ]
    ).astype(jnp.int32)
    row = jnp.arange(rows, dtype=jnp.int32)
    places = jnp.where(row < half, part * half + row, (2 * count - 2 - part) * half + row)
    reached = places[:, None] >= starts[None, :]
    begins = jnp.max(jnp.where(reached, starts[None, :], 0), axis=1)
    frequency = THETA ** (-jnp.arange(0, HEAD, 2, dtype=F32) / HEAD)
    angles = (places - begins).astype(F32)[:, None] * frequency[None, :]
    cosine, sine = jnp.cos(angles), jnp.sin(angles)
    cosine = jnp.concatenate([cosine, cosine], axis=-1)
    sine = jnp.concatenate([-sine, sine], axis=-1)

    inputs = tokens.astype(F32)
    normal_one, factor_one = rms_parts(inputs)

    bit = place_in(near_axis)
    half_rest = own_rest
    if shard_count == 2:
        half_rest = lax.dynamic_slice_in_dim(own_rest, bit * (depth // 2), depth // 2, 0)
    half_rest, own_gate_up, packed_pieces[-1], k_pieces[-1], v_pieces[-1] = tie(
        half_rest, own_gate_up, packed_pieces[-1], k_pieces[-1], v_pieces[-1]
    )
    cosine, sine, meta, factor_one, k_pieces[-1] = tie(
        cosine, sine, meta, factor_one, k_pieces[-1]
    )
    cuts = [0, depth, 2 * depth, 2 * depth + gain_q.shape[0], packed.shape[0]]
    scale_in, scale_post, scale_q, scale_k = (
        join([piece[lo:hi] for piece in packed_pieces], 0, shard).astype(F32).reshape(1, -1)
        for lo, hi in zip(cuts[:-1], cuts[1:])
    )
    full_key = join(k_pieces, 0, shard)
    full_value = join(v_pieces, 0, shard)

    full_gate_up = lax.all_gather(own_gate_up, "shard", axis=0, tiled=True)
    if shard_count == 2:
        half_rest = swap(half_rest, "shard")
    k_pre, key_value, normed_input, sent = key_value_and_parts(
        meta,
        docs,
        count,
        tokens,
        factor_one,
        scale_in,
        k_pieces,
        v_pieces,
        cosine,
        sine,
        scale_k,
    )
    held = {}
    exchange(sent, held, crossing)
    half_rest, *rest = settle(held, crossing, half_rest, *(sent[d] for d in straight))
    sent.update(zip(straight, rest))

    exchange(sent, held, straight)
    if shard_count == 2:
        other_rest = join([half_rest, swap(half_rest, "ctx", near_axis[0])], 0, bit)
        full_rest = join([own_rest, other_rest], 0, shard)
    else:
        full_rest = lax.all_gather(half_rest, "shard", axis=0, tiled=True)
    full_query = full_rest[:, :heads_width]
    full_out_t = full_rest[:, heads_width : 2 * heads_width]
    full_down_t = full_rest[:, 2 * heads_width :]
    q_pre = dot(normed_input, full_query)
    queries = rope(q_pre, cosine, sine, scale_q)
    queries, full_out_t = settle(held, straight, queries, full_out_t)
    held = [held[d] for d in range(1, count)]
    attended, attn_out, lse = attend(meta, docs, queries, key_value, held)

    residual = inputs + pair_total(dot_nt(attn_out, full_out_t))
    normal_two, factor_two = rms_parts(residual)
    normed_two = (normal_two * scale_post).astype(BF16)
    gate_upward = dot(normed_two, full_gate_up)
    gate_act = gate_upward[:, :units]
    upward = gate_upward[:, units:]
    sigma = jax.nn.sigmoid(gate_act)
    silu_act = gate_act * sigma
    hidden = (silu_act * upward).astype(BF16)
    d_hidden = dot(cotangent, full_down_t)
    d_gate = (d_hidden * upward * sigma * (1.0 + gate_act * (1.0 - sigma))).astype(BF16)
    d_up = (d_hidden * silu_act).astype(BF16)
    middle = units // 2
    away, home = (2 - 2 * shard, 3 - 2 * shard), (2 * shard, 2 * shard + 1)

    def pairs_a(normed):
        return [(normed, d_gate, 0, units), (normed, d_up, 0, middle)]

    def pairs_b(normed, upstream):
        return [(normed, d_up, middle, units), (upstream, hidden, 0, units)]

    if shard_count == 2:
        sent_a = split_product(away, pairs_a(normed_two))
        sent_b = split_product((1 - bit, 3 - bit), pairs_b(normed_two, cotangent))
        d_gate, d_up, sent_a, sent_b = tie(d_gate, d_up, sent_a, sent_b)
        got_a, got_b = swap(sent_a, "shard"), swap(sent_b, "ctx", near_axis[0])
    d_normed_two = pair_total(
        product_nt((d_gate, full_gate_up, 0), (d_up, full_gate_up, 1))
    )
    hidden, d_normed_two = tie(hidden, d_normed_two)
    mixed_part = product_nt((hidden, full_down_t, 0))
    mixed = (residual + pair_total(mixed_part)).astype(BF16)
    grad_post = jnp.sum(d_normed_two * normal_two, axis=0)
    d_residual = cotangent.astype(F32) + rms_back(
        d_normed_two * scale_post, normal_two, factor_two
    )

    d_branch = d_residual.astype(BF16)
    d_attn = dot(d_branch, full_out_t).astype(BF16)
    d_queries, d_kv, given = attend_back(
        meta, docs, queries, d_attn, attended, lse, key_value, held
    )
    given = dict(zip(range(1, count), given))
    returned = {}
    exchange(given, returned, straight)
    if shard_count == 2:
        first, second = straight[-1], straight[0]
        normed_late, returned[first] = tie(normed_two, returned[first])
        units_a = [split_product(home, pairs_a(normed_late)), got_a]
        units_a = halve(units_a, near_axis)
        normed_late, upstream_late, returned[second] = tie(
            normed_two, cotangent, returned[second]
        )
        kept_b = split_product((bit, 2 + bit), pairs_b(normed_late, upstream_late))
        units_b = [kept_b, got_b]
        units_b_away = total(rows_at(units_b, 1 - shard, depth // 2))
        units_b = rows_at(units_b, shard, depth // 2) + [swap(units_b_away, "shard")]
    else:
        units_a = halve(scattered(pairs_a(normed_two)), near_axis)
        units_b = halve(scattered(pairs_b(normed_two, cotangent)), near_axis)
    d_q_pre, gq_part = rope_back(d_queries, q_pre, cosine, sine, scale_q)
    out_pairs = [(d_branch, attn_out, 0, heads_width), (normed_input, d_q_pre, 0, heads_width)]
    if shard_count == 2:
        out_query = [split_product(home, out_pairs), split_product(away, out_pairs)]
    else:
        out_query = scattered(out_pairs)
    units_a[-1], units_b[-1], out_query[0], out_query[-1], *rest = settle(
        returned,
        straight,
        units_a[-1],
        units_b[-1],
        out_query[0],
        out_query[-1],
        *(given[d] for d in crossing),
    )
    if shard_count == 2:
        out_query[-1] = swap(out_query[-1], "shard")
    given.update(zip(crossing, rest))
    exchange(given, returned, crossing)
    units_sum = jnp.concatenate([total(units_a), total(units_b)], axis=1)
    units_sum, d_kv = settle(returned, crossing, units_sum, d_kv)
    returned = [returned[d] for d in range(1, count)]

    units_sum = halve([units_sum], far_axis)
    d_k_pre, d_v_pre, gk_part = key_value_back(
        meta, docs, d_kv, returned, k_pre, cosine, sine, scale_k
    )
    d_k_pre, d_v_pre, out_query[-1] = tie(d_k_pre, d_v_pre, out_query[-1])
    out_query = halve(out_query, near_axis)
    kv_pairs = [(normed_input, d_k_pre, 0, kv_width), (normed_input, d_v_pre, 0, kv_width)]
    if shard_count == 2:
        sent_kv = swap(split_product(away, kv_pairs), "shard")
        key_value_grad = [split_product(home, kv_pairs), sent_kv]
    else:
        key_value_grad = scattered(kv_pairs)
    units_sum = total(units_sum)
    cut = units_sum.shape[1] // 2
    units_a, units_b = units_sum[:, :cut], units_sum[:, cut:]
    units_a, units_b, out_query[-1], key_value_grad[-1], d_q_pre, d_k_pre, d_v_pre = tie(
        units_a, units_b, out_query[-1], key_value_grad[-1], d_q_pre, d_k_pre, d_v_pre
    )

    units_a = double(units_a, far_axis)
    key_value_grad = halve(key_value_grad, near_axis)
    units_a, units_b, key_value_grad[-1], out_query[-1] = tie(
        units_a, units_b, key_value_grad[-1], out_query[-1]
    )

    units_b = double(units_b, far_axis)
    owned_a = double(units_a, near_axis)
    d_normed = pair_total(
        dot_nt(d_q_pre, full_query) + dot_nt(d_k_pre, full_key) + dot_nt(d_v_pre, full_value)
    )
    grad_in = jnp.sum(d_normed * normal_one, axis=0)
    input_grad = d_residual + rms_back(d_normed * scale_in, normal_one, factor_one)
    once = jnp.where(lax.axis_index("tp") == 0, 1.0, 0.0)
    gain_grads = jnp.concatenate([grad_in * once, grad_post * once, gq_part[0], gk_part[0]])
    gain_grads = gain_grads.reshape(-1, HEAD)
    if shard_count != 2:
        gain_grads = lax.psum(gain_grads, "shard")
    out_query, key_value_grad = total(out_query), total(key_value_grad)
    rest_chain = [
        jnp.concatenate(
            [
                out_query[:, :heads_width],
                key_value_grad[:, :kv_width],
                out_query[:, heads_width:],
                key_value_grad[:, kv_width:],
            ],
            axis=1,
        )
    ]
    units_b, owned_a, rest_chain[0], gain_grads = tie(
        units_b, owned_a, rest_chain[0], gain_grads
    )

    owned_b = double(units_b, near_axis)
    rest_chain = total(halve(rest_chain, far_axis))
    gain_grads = gain_grads + swap(gain_grads, "tp")
    gain_grads = gain_grads + swap(gain_grads, "ctx", masks[0])
    owned_b, rest_chain, gain_grads = tie(owned_b, rest_chain, gain_grads)

    cut = rest_chain.shape[1] // 2
    rest_a, rest_b = rest_chain[:, :cut], rest_chain[:, cut:]
    rest_a = double(rest_a, far_axis)
    gain_grads = gain_grads + swap(gain_grads, "ctx", masks[1])
    rest_a, rest_b, gain_grads = tie(rest_a, rest_b, gain_grads)

    rest_b = double(rest_b, far_axis)
    rest_a = double(rest_a, near_axis)
    for mask in masks[2:]:
        gain_grads = gain_grads + swap(gain_grads, "ctx", mask)
    rest_a, rest_b, gain_grads = tie(rest_a, rest_b, gain_grads)

    rest_b = double(rest_b, near_axis)
    if shard_count == 2:
        gain_grads = gain_grads + swap(gain_grads, "shard")
    gain_grads = gain_grads.reshape(-1)
    owned_up = jnp.concatenate([owned_a[:, units:], owned_b[:, :middle]], axis=1)
    own_gains = []
    for lo, size in ((0, model), (model, model), (2 * model, HEAD), (2 * model + HEAD, HEAD)):
        size = size // shard_count
        own_gains.append(lax.dynamic_slice_in_dim(gain_grads, lo + shard * size, size, 0))
    return (
        mixed,
        input_grad,
        rest_b[:, :heads_width].astype(F32),
        rest_a[:, heads_width:].astype(F32),
        rest_b[:, heads_width:].astype(F32),
        rest_a[:, :heads_width].astype(F32).T,
        owned_a[:, :units].astype(F32),
        owned_up.astype(F32),
        owned_b[:, middle:].astype(F32).T,
        *own_gains,
    )


def solution(mesh):
    placed = (
        P(("shard", "ctx"), None),
        P(("shard", "ctx"), None),
        P("shard", None),
        P(),
        P("shard", "tp"),
        P("shard", "tp"),
        P("shard", "tp"),
        P("tp", "shard"),
        P("shard", "tp"),
        P("shard", "tp"),
        P("tp", "shard"),
        P("shard"),
        P("shard"),
        P("shard"),
        P("shard"),
    )
    return jax.shard_map(
        body,
        mesh=mesh,
        in_specs=placed,
        out_specs=(
            P(("shard", "ctx"), None),
            P(("shard", "ctx"), None),
            P("shard", "tp"),
            P("shard", "tp"),
            P("shard", "tp"),
            P("tp", "shard"),
            P("shard", "tp"),
            P("shard", "tp"),
            P("tp", "shard"),
            P("shard"),
            P("shard"),
            P("shard"),
            P("shard"),
        ),
        check_vma=False,
    )
```

```python
import functools

import jax
import jax.numpy as jnp
from jax import lax
from jax.experimental import pallas as pl
from jax.experimental.pallas import tpu as pltpu
from jax.sharding import PartitionSpec as P

EPS = 1e-06
THETA = 1000000.0
LOG2E = 1.4426950408889634
HEAD = 128
BF16 = jnp.bfloat16
F32 = jnp.float32
VMEM_LIMIT = 48 * 1024 * 1024
CHEAP = pl.CostEstimate(flops=1000, bytes_accessed=1000, transcendentals=0)


def rms_parts(values):
    factor = lax.rsqrt(jnp.mean(values * values, axis=-1, keepdims=True) + EPS)
    return (values * factor, factor)


def rms_back(grad_hat, normal, factor):
    return factor * (grad_hat - normal * jnp.mean(grad_hat * normal, axis=-1, keepdims=True))


def dot(a, b):
    return jnp.dot(a, b, preferred_element_type=F32)


def dot_nt(a, b):
    return lax.dot_general(a, b, (((1,), (1,)), ((), ())), preferred_element_type=F32)


def dot_tn(a, b):
    return lax.dot_general(a, b, (((0,), (0,)), ((), ())), preferred_element_type=F32)


def tie(*values):
    return lax.optimization_barrier(values)


def pieces_of(own, axis):
    count = lax.axis_size(axis)
    return [own] + [
        lax.ppermute(own, axis, [((i + j) % count, i) for i in range(count)])
        for j in range(1, count)
    ]


def join(pieces, dim, index):
    count = len(pieces)
    if count == 1:
        return pieces[0]
    if count == 2:
        return jnp.where(
            index == 0, jnp.concatenate(pieces, dim), jnp.concatenate(pieces[::-1], dim)
        )
    size = pieces[0].shape[dim]
    shape = list(pieces[0].shape)
    shape[dim] = size * count
    whole = jnp.zeros(shape, pieces[0].dtype)
    for j, piece in enumerate(pieces):
        whole = lax.dynamic_update_slice_in_dim(whole, piece, (index + j) % count * size, dim)
    return whole


def pair_total(partial):
    count = lax.axis_size("tp")
    partial = partial.astype(BF16)
    if count != 2:
        return lax.psum(partial, "tp").astype(F32)
    other = lax.ppermute(partial, "tp", [(0, 1), (1, 0)])
    return partial.astype(F32) + other.astype(F32)


def swap(value, axis, level=1):
    count = lax.axis_size(axis)
    return lax.ppermute(value, axis, [(i, i ^ level) for i in range(count)])


def place_in(masks):
    return (lax.axis_index("ctx") // masks[0]) % (1 << len(masks))


def exchange(values, done, turns):
    count = lax.axis_size("ctx")
    for d in turns:
        done[d] = lax.ppermute(values[d], "ctx", [(i, i ^ d) for i in range(count)])


def settle(done, turns, *values):
    tied = tie(*(done[d] for d in turns), *values)
    done.update(zip(turns, tied))
    return tied[len(turns) :]


def total(addends):
    return sum(a.astype(F32) for a in addends).astype(BF16)


def rows_at(addends, block, rows):
    return [lax.dynamic_slice_in_dim(a, block * rows, rows, 0) for a in addends]


def halve(addends, masks):
    size = 1 << len(masks)
    rows = addends[0].shape[0] // size
    place = place_in(masks)
    kept = rows_at(addends, place, rows)
    for turn in range(1, size):
        sent = picked_sum(addends, place ^ turn, rows)
        kept = kept + [swap(sent, "ctx", turn * masks[0])]
    return kept


def scattered(pairs):
    grads = [dot_tn(a, b[:, lo:hi]).astype(BF16) for a, b, lo, hi in pairs]
    grad = jnp.concatenate(grads, axis=1)
    return [lax.psum_scatter(grad, "shard", scatter_dimension=0, tiled=True)]


def double(value, masks):
    size = 1 << len(masks)
    place = place_in(masks)
    blocks = [value] + [swap(value, "ctx", turn * masks[0]) for turn in range(1, size)]
    bit = 0
    while len(blocks) > 1:
        pairs = zip(blocks[::2], blocks[1::2])
        blocks = [join(list(pair), 0, (place >> bit) % 2) for pair in pairs]
        bit += 1
    return blocks[0]


def picked_sum_kernel(which_ref, *refs):
    refs[-1][...] = sum(ref[...].astype(F32) for ref in refs[:-1]).astype(BF16)


def picked_sum(addends, block, rows):
    if rows % 16 != 0:
        return total(rows_at(addends, block, rows))
    width = addends[0].shape[1]
    step = width // 4 if width % 512 == 0 else width // 2
    picked = pl.BlockSpec((rows, step), lambda i, w: (w[0], i))
    return pl.pallas_call(
        picked_sum_kernel,
        grid_spec=pltpu.PrefetchScalarGridSpec(
            num_scalar_prefetch=1,
            grid=(width // step,),
            in_specs=[picked] * len(addends),
            out_specs=pl.BlockSpec((rows, step), lambda i, w: (0, i)),
        ),
        out_shape=jax.ShapeDtypeStruct((rows, width), BF16),
        compiler_params=pltpu.CompilerParams(vmem_limit_bytes=VMEM_LIMIT),
        cost_estimate=CHEAP,
    )(jnp.reshape(block, (1,)).astype(jnp.int32), *addends)


def product_kernel(count, *refs):
    products = [dot_nt(refs[2 * i][...], refs[2 * i + 1][...]) for i in range(count)]
    refs[-1][...] = sum(products).astype(BF16)


def product_nt(*terms):
    rows = terms[0][0].shape[0]
    columns = terms[0][1].shape[0]
    step = min(columns, 256)
    specs, values = [], []
    for a, b, column in terms:
        depth = a.shape[1]
        specs.append(pl.BlockSpec((rows, depth), lambda i: (0, 0)))
        specs.append(pl.BlockSpec((step, depth), lambda i, column=column: (i, column)))
        values += [a, b]
    return pl.pallas_call(
        functools.partial(product_kernel, len(terms)),
        grid=(columns // step,),
        in_specs=specs,
        out_specs=pl.BlockSpec((rows, step), lambda i: (0, i)),
        out_shape=jax.ShapeDtypeStruct((rows, columns), BF16),
        compiler_params=pltpu.CompilerParams(vmem_limit_bytes=VMEM_LIMIT),
        cost_estimate=CHEAP,
    )(*values)


def split_product_kernel(spans, which_ref, *refs):
    j = pl.program_id(1)
    for i, (lo, hi) in enumerate(spans):

        @pl.when((j >= lo) & (j < hi))
        def _():
            refs[-1][...] = dot_tn(refs[2 * i][...], refs[2 * i + 1][...]).astype(BF16)


def split_product(which, pairs):
    tokens, model = pairs[0][0].shape
    rows = model // 4
    step = min(hi - lo for a, b, lo, hi in pairs)
    specs, values, spans, done = [], [], [], 0
    for a, b, lo, hi in pairs:
        blocks = (hi - lo) // step

        def column(i, j, w, first=done, base=lo // step, blocks=blocks):
            return (0, base + jnp.clip(j - first, 0, blocks - 1))

        specs.append(pl.BlockSpec((tokens, rows), lambda i, j, w: (0, w[i])))
        specs.append(pl.BlockSpec((tokens, step), column))
        values += [a, b]
        spans.append((done, done + blocks))
        done += blocks
    return pl.pallas_call(
        functools.partial(split_product_kernel, spans),
        grid_spec=pltpu.PrefetchScalarGridSpec(
            num_scalar_prefetch=1,
            grid=(2, done),
            in_specs=specs,
            out_specs=pl.BlockSpec((rows, step), lambda i, j, w: (i, j)),
        ),
        out_shape=jax.ShapeDtypeStruct((2 * rows, done * step), BF16),
        compiler_params=pltpu.CompilerParams(vmem_limit_bytes=VMEM_LIMIT),
        cost_estimate=CHEAP,
    )(jnp.stack(which).astype(jnp.int32), *values)


def rope_kernel(pre_ref, cos_ref, sin_ref, gain_ref, out_ref):
    pre = pre_ref[...]
    factor = lax.rsqrt(jnp.mean(pre * pre, axis=-1, keepdims=True) + EPS)
    scaled = pre * factor * gain_ref[...]
    turned = pltpu.roll(scaled, HEAD // 2, 1)
    out_ref[...] = (scaled * cos_ref[...] + turned * sin_ref[...]).astype(BF16)


def rope(pre, cosine, sine, gain):
    rows, width = pre.shape
    table = pl.BlockSpec((rows, HEAD), lambda h: (0, 0))
    column = pl.BlockSpec((rows, HEAD), lambda h: (0, h))
    return pl.pallas_call(
        rope_kernel,
        grid=(width // HEAD,),
        in_specs=[column, table, table, pl.BlockSpec((1, HEAD), lambda h: (0, 0))],
        out_specs=column,
        out_shape=jax.ShapeDtypeStruct((rows, width), BF16),
        compiler_params=pltpu.CompilerParams(vmem_limit_bytes=VMEM_LIMIT),
        cost_estimate=CHEAP,
    )(pre, cosine, sine, gain)


def part_start(meta_ref, docs, d, half):
    return pl.multiple_of((1 - meta_ref[docs + d]) * half, half)


def key_value_kernel(
    heads, docs, count, pieces, meta_ref, tokens_ref, factor_ref, scale_ref, *refs
):
    weights = refs[: 2 * pieces]
    cos_ref, sin_ref, gain_ref = refs[2 * pieces : 2 * pieces + 3]
    key_ref, out_ref, normed_ref = refs[2 * pieces + 3 : 2 * pieces + 6]
    sent = refs[2 * pieces + 6 :]
    half = out_ref.shape[0] // 2
    depth = tokens_ref.shape[1] // pieces
    step = pl.program_id(0)

    @pl.when(step == 0)
    def _():
        normal = tokens_ref[...].astype(F32) * factor_ref[...]
        normed_ref[...] = (normal * scale_ref[...]).astype(BF16)

    def product(parts):
        result = None
        for j, part in enumerate(parts):
            at = pl.multiple_of(meta_ref[docs + 2 * (count - 1) + j] * depth, HEAD)
            term = dot(normed_ref[:, pl.ds(at, depth)], part[...])
            result = term if result is None else result + term
        return result

    @pl.when(step < heads // 2)
    def _():
        key_ref[...] = product(weights[:pieces])
        for a in range(2):
            lanes = slice(a * HEAD, (a + 1) * HEAD)
            pre = key_ref[:, lanes]
            factor = lax.rsqrt(jnp.mean(pre * pre, axis=-1, keepdims=True) + EPS)
            scaled = pre * factor * gain_ref[...]
            turned = pltpu.roll(scaled, HEAD // 2, 1)
            out_ref[:, lanes] = (scaled * cos_ref[...] + turned * sin_ref[...]).astype(BF16)

    @pl.when(step >= heads // 2)
    def _():
        out_ref[...] = product(weights[pieces:]).astype(BF16)

    for d, sent_ref in enumerate(sent):
        sent_ref[...] = out_ref[pl.ds(part_start(meta_ref, docs, d, half), half), :]


def key_value_and_parts(
    meta, docs, count, tokens, factor, scale, keys, values, cosine, sine, gain
):
    rows, model = tokens.shape
    depth, width = keys[0].shape
    heads = width // HEAD
    half_steps = heads // 2
    whole = lambda shape: pl.BlockSpec(shape, lambda h, m: (0, 0))
    column = pl.BlockSpec((rows, 2 * HEAD), lambda h, m: (0, h))
    key_spec = pl.BlockSpec((depth, 2 * HEAD), lambda h, m: (0, jnp.minimum(h, half_steps - 1)))
    value_spec = pl.BlockSpec((depth, 2 * HEAD), lambda h, m: (0, jnp.maximum(h - half_steps, 0)))
    part = pl.BlockSpec((rows // 2, 2 * HEAD), lambda h, m: (0, h))
    result = pl.pallas_call(
        functools.partial(key_value_kernel, heads, docs, count, len(keys)),
        grid_spec=pltpu.PrefetchScalarGridSpec(
            num_scalar_prefetch=1,
            grid=(heads,),
            in_specs=[whole((rows, model)), whole((rows, 1)), whole((1, model))]
            + [key_spec] * len(keys)
            + [value_spec] * len(values)
            + [whole((rows, HEAD)), whole((rows, HEAD)), whole((1, HEAD))],
            out_specs=[
                pl.BlockSpec((rows, 2 * HEAD), lambda h, m: (0, jnp.minimum(h, half_steps - 1))),
                column,
                whole((rows, model)),
            ]
            + [part] * (count - 1),
        ),
        out_shape=[
            jax.ShapeDtypeStruct((rows, width), F32),
            jax.ShapeDtypeStruct((rows, 2 * width), BF16),
            jax.ShapeDtypeStruct((rows, model), BF16),
        ]
        + [jax.ShapeDtypeStruct((rows // 2, 2 * width), BF16)] * (count - 1),
        compiler_params=pltpu.CompilerParams(vmem_limit_bytes=VMEM_LIMIT),
        cost_estimate=CHEAP,
    )(meta, tokens, factor, scale, *keys, *values, cosine, sine, gain)
    return result[0], result[1], result[2], dict(zip(range(1, count), result[3:]))


def turn_back(grad, pre_ref, cos_ref, sin_ref, gain_ref, out_ref, sum_ref):
    pre = pre_ref[...]
    factor = lax.rsqrt(jnp.mean(pre * pre, axis=-1, keepdims=True) + EPS)
    hat = pre * factor
    back = grad * cos_ref[...] - pltpu.roll(grad, HEAD // 2, 1) * sin_ref[...]
    terms = jnp.sum(back * hat, axis=0, keepdims=True)

    @pl.when(pl.program_id(0) == 0)
    def _():
        sum_ref[...] = terms

    @pl.when(pl.program_id(0) > 0)
    def _():
        sum_ref[...] += terms

    back = back * gain_ref[...]
    inner = jnp.mean(back * hat, axis=-1, keepdims=True)
    out_ref[...] = (factor * (back - hat * inner)).astype(BF16)


def rope_back_kernel(grad_ref, *refs):
    turn_back(grad_ref[...], *refs)


def key_value_back_kernel(docs, meta_ref, own_ref, *refs):
    returned = refs[:-8]
    key_ref, cos_ref, sin_ref, gain_ref, d_key_ref, d_value_ref, sum_ref, acc_ref = refs[-8:]
    half = key_ref.shape[0] // 2
    acc_ref[...] = own_ref[...]
    for d, given_ref in enumerate(returned):
        rows = pl.ds(part_start(meta_ref, docs, d, half), half)
        acc_ref[:, rows, :] += given_ref[...].astype(F32)
    d_value_ref[...] = acc_ref[1].astype(BF16)
    turn_back(acc_ref[0], key_ref, cos_ref, sin_ref, gain_ref, d_key_ref, sum_ref)


def key_value_back(meta, docs, own, returned, key, cosine, sine, gain):
    rows, width = key.shape
    table = pl.BlockSpec((rows, HEAD), lambda h, m: (0, 0))
    column = pl.BlockSpec((rows, HEAD), lambda h, m: (0, h))
    one_row = pl.BlockSpec((1, HEAD), lambda h, m: (0, 0))
    return pl.pallas_call(
        functools.partial(key_value_back_kernel, docs),
        grid_spec=pltpu.PrefetchScalarGridSpec(
            num_scalar_prefetch=1,
            grid=(width // HEAD,),
            in_specs=[pl.BlockSpec((2, rows, HEAD), lambda h, m: (0, 0, h))]
            + [pl.BlockSpec((2, rows // 2, HEAD), lambda h, m: (0, 0, h))] * len(returned)
            + [column, table, table, one_row],
            out_specs=[column, column, one_row],
            scratch_shapes=[pltpu.VMEM((2, rows, HEAD), F32)],
        ),
        out_shape=[
            jax.ShapeDtypeStruct((rows, width), BF16),
            jax.ShapeDtypeStruct((rows, width), BF16),
            jax.ShapeDtypeStruct((1, HEAD), F32),
        ],
        compiler_params=pltpu.CompilerParams(vmem_limit_bytes=VMEM_LIMIT),
        cost_estimate=CHEAP,
    )(meta, own, *returned, key, cosine, sine, gain)


def rope_back(grad, pre, cosine, sine, gain):
    rows, width = grad.shape
    column = pl.BlockSpec((rows, HEAD), lambda h: (0, h))
    table = pl.BlockSpec((rows, HEAD), lambda h: (0, 0))
    one_row = pl.BlockSpec((1, HEAD), lambda h: (0, 0))
    return pl.pallas_call(
        rope_back_kernel,
        grid=(width // HEAD,),
        in_specs=[column, column, table, table, one_row],
        out_specs=[column, one_row],
        out_shape=[
            jax.ShapeDtypeStruct((rows, width), BF16),
            jax.ShapeDtypeStruct((1, HEAD), F32),
        ],
        compiler_params=pltpu.CompilerParams(vmem_limit_bytes=VMEM_LIMIT),
    )(grad, pre, cosine, sine, gain)


def doc_begins(meta_ref, docs, place):
    begin = jnp.zeros_like(place)
    for i in range(1, docs):
        start = meta_ref[i]
        begin = jnp.where(place >= start, start, begin)
    return begin


def mask_across(meta_ref, docs, shape, half, q_part, k_part, diagonal):
    column = lax.broadcasted_iota(jnp.int32, (1, shape[1]), 1)
    q_place = q_part * half + jnp.where(column >= half, column - half, column)
    begin = doc_begins(meta_ref, docs, q_place) - k_part * half
    row = lax.broadcasted_iota(jnp.int32, shape, 0)
    visible = row >= begin
    if diagonal:
        visible = visible & (row <= q_place - k_part * half)
    return visible


def two_heads(ref, start, half):
    rows = pl.ds(start, half)
    return jnp.concatenate([ref[rows, :HEAD], ref[rows, HEAD:]], axis=0)


def forward_kernel(docs, count, meta_ref, q_ref, k_ref, v_ref, *refs):
    others = refs[: 2 * (count - 1)]
    out_ref, out16_ref, lse_ref, acc_ref, begin_ref = refs[2 * (count - 1) :]
    half = q_ref.shape[0] // 2
    factor = HEAD**-0.5 * LOG2E
    ones = jnp.ones((half, HEAD), BF16)
    own = meta_ref[0]
    parts = (own, 2 * count - 1 - own)

    @pl.when(pl.program_id(0) == 0)
    def _():
        row = lax.broadcasted_iota(jnp.int32, (2 * half, HEAD), 0)
        for e in range(2):
            place = parts[e] * half + jnp.where(row >= half, row - half, row)
            begin_ref[e] = doc_begins(meta_ref, docs, place)

    def block(side, start, keys, values, k_part, diagonal):
        scores = dot_nt(two_heads(q_ref, start, half), keys)
        column = lax.broadcasted_iota(jnp.int32, scores.shape, 1)
        begin = begin_ref[side] - k_part * half
        visible = column >= jnp.concatenate([begin] * (half // HEAD), axis=1)
        if diagonal:
            row = lax.broadcasted_iota(jnp.int32, scores.shape, 0)
            visible = visible & (column <= jnp.where(row >= half, row - half, row))
        weights = jnp.where(visible, jnp.exp2(scores * factor), 0.0).astype(BF16)
        return dot(weights, jnp.concatenate([values, ones], axis=1))

    for e in range(2):
        rows = pl.ds(e * half, half)
        acc_ref[e] = block(e, e * half, k_ref[rows, :], v_ref[rows, :], parts[e], True)
    for d in range(count - 1):
        side = meta_ref[docs + d]
        k_part = meta_ref[docs + count - 1 + d]
        start = pl.multiple_of(side * half, half)
        acc_ref[side] += block(
            side, start, others[2 * d][...], others[2 * d + 1][...], k_part, False
        )

    for e in range(2):
        total = acc_ref[e]
        sums = total[:, HEAD:]
        result = total[:, :HEAD] / sums
        lse = jnp.log2(sums)
        for a in range(2):
            part = slice(a * half, (a + 1) * half)
            place = (pl.ds(e * half, half), slice(a * HEAD, (a + 1) * HEAD))
            out_ref[place] = result[part]
            out16_ref[place] = result[part].astype(BF16)
            lse_ref[place] = lse[part]


def backward_kernel(docs, count, meta_ref, q_ref, g_ref, o_ref, lse_ref, k_ref, v_ref, *refs):
    others = refs[: 2 * (count - 1)]
    dq_ref, dkv_ref = refs[2 * (count - 1) : 2 * count]
    given = refs[2 * count : 3 * count - 1]
    acc_ref, stats_ref, delta_ref = refs[3 * count - 1 :]
    half = q_ref.shape[0] // 2
    scale = HEAD**-0.5
    own = meta_ref[0]

    for e in range(2):
        grads = two_heads(g_ref, e * half, half).astype(F32)
        delta = jnp.sum(grads * two_heads(o_ref, e * half, half), axis=1, keepdims=True)
        delta = jnp.broadcast_to(delta, (2 * half, HEAD))
        delta_ref[e] = jnp.transpose(delta)[:8]
        stats_ref[e] = jnp.transpose(two_heads(lse_ref, e * half, half))[:8]

    def block(side, start, keys, values, q_part, k_part, diagonal):
        queries = two_heads(q_ref, start, half)
        grads = two_heads(g_ref, start, half)
        scores = dot_nt(keys, queries)
        lse = stats_ref[side][:1]
        delta = delta_ref[side][:1]
        weights = jnp.exp2(scores * (scale * LOG2E) - lse)
        visible = mask_across(meta_ref, docs, scores.shape, half, q_part, k_part, diagonal)
        weights = jnp.where(visible, weights, 0.0)
        d_weights = dot_nt(values, grads)
        d_scores = (weights * (d_weights - delta)).astype(BF16)
        d_values = dot(weights.astype(BF16), grads)
        d_keys = dot(d_scores, queries) * scale
        return dot_tn(d_scores, keys) * scale, d_keys, d_values

    for e in range(2):
        rows = pl.ds(e * half, half)
        part = own if e == 0 else 2 * count - 1 - own
        d_queries, d_keys, d_values = block(
            e, e * half, k_ref[rows, :], v_ref[rows, :], part, part, True
        )
        acc_ref[e] = d_queries
        dkv_ref[0, rows, :] = d_keys
        dkv_ref[1, rows, :] = d_values
    for d in range(count - 1):
        side = meta_ref[docs + d]
        k_part = meta_ref[docs + count - 1 + d]
        q_part = jnp.where(side == 0, own, 2 * count - 1 - own)
        start = pl.multiple_of(side * half, half)
        d_queries, d_keys, d_values = block(
            side, start, others[2 * d][...], others[2 * d + 1][...], q_part, k_part, False
        )
        acc_ref[side] += d_queries
        given[d][0] = d_keys.astype(BF16)
        given[d][1] = d_values.astype(BF16)

    for e in range(2):
        for a in range(2):
            dq_ref[pl.ds(e * half, half), a * HEAD : (a + 1) * HEAD] = acc_ref[
                e, a * half : (a + 1) * half, :
            ]


def key_value_specs(rows, half, kv_heads, count):
    own = [
        pl.BlockSpec((rows, HEAD), lambda h, m: (0, h)),
        pl.BlockSpec((rows, HEAD), lambda h, m: (0, kv_heads + h)),
    ]
    other = [
        pl.BlockSpec((half, HEAD), lambda h, m: (0, h)),
        pl.BlockSpec((half, HEAD), lambda h, m: (0, kv_heads + h)),
    ]
    return own + other * (count - 1)


def twice(arrays):
    return [a for a in arrays for _ in range(2)]


def attend(meta, docs, queries, key_value, others):
    rows, width = queries.shape
    half = rows // 2
    count = len(others) + 1
    kv_heads = key_value.shape[1] // (2 * HEAD)
    column = pl.BlockSpec((rows, 2 * HEAD), lambda h, m: (0, h))
    return pl.pallas_call(
        functools.partial(forward_kernel, docs, count),
        grid_spec=pltpu.PrefetchScalarGridSpec(
            num_scalar_prefetch=1,
            grid=(kv_heads,),
            in_specs=[column] + key_value_specs(rows, half, kv_heads, count),
            out_specs=[column] * 3,
            scratch_shapes=[
                pltpu.VMEM((2, 2 * half, 2 * HEAD), F32),
                pltpu.VMEM((2, 2 * half, HEAD), jnp.int32),
            ],
        ),
        out_shape=[
            jax.ShapeDtypeStruct((rows, width), F32),
            jax.ShapeDtypeStruct((rows, width), BF16),
            jax.ShapeDtypeStruct((rows, width), F32),
        ],
        compiler_params=pltpu.CompilerParams(vmem_limit_bytes=VMEM_LIMIT),
        cost_estimate=CHEAP,
    )(meta, queries, key_value, key_value, *twice(others))


def attend_back(meta, docs, queries, grads, outs, lse, key_value, others):
    rows, width = queries.shape
    half = rows // 2
    count = len(others) + 1
    kv_width = key_value.shape[1] // 2
    kv_heads = kv_width // HEAD
    column = pl.BlockSpec((rows, 2 * HEAD), lambda h, m: (0, h))
    result = pl.pallas_call(
        functools.partial(backward_kernel, docs, count),
        grid_spec=pltpu.PrefetchScalarGridSpec(
            num_scalar_prefetch=1,
            grid=(kv_heads,),
            in_specs=[column] * 4 + key_value_specs(rows, half, kv_heads, count),
            out_specs=[column, pl.BlockSpec((2, rows, HEAD), lambda h, m: (0, 0, h))]
            + [pl.BlockSpec((2, half, HEAD), lambda h, m: (0, 0, h))] * (count - 1),
            scratch_shapes=[
                pltpu.VMEM((2, 2 * half, HEAD), F32),
                pltpu.VMEM((2, 8, 2 * half), F32),
                pltpu.VMEM((2, 8, 2 * half), F32),
            ],
        ),
        out_shape=[
            jax.ShapeDtypeStruct((rows, width), F32),
            jax.ShapeDtypeStruct((2, rows, kv_width), F32),
        ]
        + [jax.ShapeDtypeStruct((2, half, kv_width), BF16)] * (count - 1),
        compiler_params=pltpu.CompilerParams(vmem_limit_bytes=VMEM_LIMIT),
        cost_estimate=CHEAP,
    )(meta, queries, grads, outs, lse, key_value, key_value, *twice(others))
    return result[0], result[1], list(result[2:])


def body(
    tokens,
    cotangent,
    seq_lengths,
    part_order,
    w_query,
    key_weight,
    value_weight,
    w_out,
    w_gate,
    w_up,
    w_down,
    gain_in,
    gain_post,
    gain_q,
    gain_k,
):
    shard_count = lax.axis_size("shard")
    shard = lax.axis_index("shard")
    count = lax.axis_size("ctx")
    ctx = lax.axis_index("ctx")
    rows, model = tokens.shape
    half = rows // 2
    depth = model // shard_count
    docs = seq_lengths.shape[1]
    kv_width = key_weight.shape[1]
    units = w_gate.shape[1]
    heads_width = w_out.shape[0]

    masks = [1 << b for b in range(count.bit_length() - 1)]
    near_axis, far_axis = masks[:1], masks[1:]
    far = [d for d in range(1, count) if d >= count // 2]
    near = [d for d in range(1, count) if d < count // 2]
    crossing = [d for d in far + near if d % 2 == 1]
    straight = [d for d in far + near if d % 2 == 0]

    packed = jnp.concatenate([gain_in, gain_post, gain_q, gain_k])
    k_pieces = pieces_of(key_weight, "shard")
    v_pieces = pieces_of(value_weight, "shard")
    packed_pieces = pieces_of(packed, "shard")
    (own_rest,) = tie(jnp.concatenate([w_query, w_out.T, w_down.T], axis=1))
    own_gate_up = jnp.concatenate([w_gate, w_up], axis=1)

    turns = jnp.arange(count, dtype=jnp.int32)
    partner = jnp.bitwise_xor(ctx.astype(jnp.int32), turns)
    parts = jnp.sum(
        jnp.where(partner[:, None] == turns[None, :], part_order[:, 0][None, :], 0), axis=1
    )
    part = parts[:1]
    lengths = seq_lengths[0]
    order = jnp.arange(docs, dtype=jnp.int32)
    starts = jnp.sum(jnp.where(order[None, :] < order[:, None], lengths[None, :], 0), axis=1)
    meta = jnp.concatenate(
        [
            part,
            starts[1:],
            (parts[1:] >= part).astype(jnp.int32),
            jnp.where(parts[1:] < part, parts[1:], 2 * count - 1 - parts[1:]),
            (shard + jnp.arange(shard_count, dtype=jnp.int32)) % shard_count,
        ]
    ).astype(jnp.int32)
    row = jnp.arange(rows, dtype=jnp.int32)
    places = jnp.where(row < half, part * half + row, (2 * count - 2 - part) * half + row)
    reached = places[:, None] >= starts[None, :]
    begins = jnp.max(jnp.where(reached, starts[None, :], 0), axis=1)
    frequency = THETA ** (-jnp.arange(0, HEAD, 2, dtype=F32) / HEAD)
    angles = (places - begins).astype(F32)[:, None] * frequency[None, :]
    cosine, sine = jnp.cos(angles), jnp.sin(angles)
    cosine = jnp.concatenate([cosine, cosine], axis=-1)
    sine = jnp.concatenate([-sine, sine], axis=-1)

    inputs = tokens.astype(F32)
    normal_one, factor_one = rms_parts(inputs)

    bit = place_in(near_axis)
    half_rest = own_rest
    if shard_count == 2:
        half_rest = lax.dynamic_slice_in_dim(own_rest, bit * (depth // 2), depth // 2, 0)
    half_rest, own_rest, own_gate_up, packed_pieces[-1], k_pieces[-1], v_pieces[-1] = tie(
        half_rest, own_rest, own_gate_up, packed_pieces[-1], k_pieces[-1], v_pieces[-1]
    )
    cosine, sine, meta, factor_one, k_pieces[-1] = tie(
        cosine, sine, meta, factor_one, k_pieces[-1]
    )
    cuts = [0, depth, 2 * depth, 2 * depth + gain_q.shape[0], packed.shape[0]]
    scale_in, scale_post, scale_q, scale_k = (
        join([piece[lo:hi] for piece in packed_pieces], 0, shard).astype(F32).reshape(1, -1)
        for lo, hi in zip(cuts[:-1], cuts[1:])
    )
    full_key = join(k_pieces, 0, shard)
    full_value = join(v_pieces, 0, shard)

    full_gate_up = lax.all_gather(own_gate_up, "shard", axis=0, tiled=True)
    if shard_count == 2:
        half_rest = swap(half_rest, "shard")
    k_pre, key_value, normed_input, sent = key_value_and_parts(
        meta,
        docs,
        count,
        tokens,
        factor_one,
        scale_in,
        k_pieces,
        v_pieces,
        cosine,
        sine,
        scale_k,
    )
    held = {}
    exchange(sent, held, crossing)
    half_rest, *rest = settle(held, crossing, half_rest, *(sent[d] for d in straight))
    sent.update(zip(straight, rest))

    exchange(sent, held, straight)
    if shard_count == 2:
        other_rest = join([half_rest, swap(half_rest, "ctx", near_axis[0])], 0, bit)
        full_rest = join([own_rest, other_rest], 0, shard)
    else:
        full_rest = lax.all_gather(half_rest, "shard", axis=0, tiled=True)
    full_query = full_rest[:, :heads_width]
    full_out_t = full_rest[:, heads_width : 2 * heads_width]
    full_down_t = full_rest[:, 2 * heads_width :]
    q_pre = dot(normed_input, full_query)
    queries = rope(q_pre, cosine, sine, scale_q)
    queries, full_out_t = settle(held, straight, queries, full_out_t)
    held = [held[d] for d in range(1, count)]
    attended, attn_out, lse = attend(meta, docs, queries, key_value, held)

    residual = inputs + pair_total(dot_nt(attn_out, full_out_t))
    normal_two, factor_two = rms_parts(residual)
    normed_two = (normal_two * scale_post).astype(BF16)
    gate_upward = dot(normed_two, full_gate_up)
    gate_act = gate_upward[:, :units]
    upward = gate_upward[:, units:]
    sigma = jax.nn.sigmoid(gate_act)
    silu_act = gate_act * sigma
    hidden = (silu_act * upward).astype(BF16)
    d_hidden = dot(cotangent, full_down_t)
    d_gate = (d_hidden * upward * sigma * (1.0 + gate_act * (1.0 - sigma))).astype(BF16)
    d_up = (d_hidden * silu_act).astype(BF16)
    middle = units // 2
    away, home = (2 - 2 * shard, 3 - 2 * shard), (2 * shard, 2 * shard + 1)

    def pairs_a(normed):
        return [(normed, d_gate, 0, units), (normed, d_up, 0, middle)]

    def pairs_b(normed, upstream):
        return [(normed, d_up, middle, units), (upstream, hidden, 0, units)]

    if shard_count == 2:
        sent_a = split_product(away, pairs_a(normed_two))
        sent_b = split_product((1 - bit, 3 - bit), pairs_b(normed_two, cotangent))
        d_gate, d_up, sent_a, sent_b = tie(d_gate, d_up, sent_a, sent_b)
        got_a, got_b = swap(sent_a, "shard"), swap(sent_b, "ctx", near_axis[0])
    d_normed_two = pair_total(
        product_nt((d_gate, full_gate_up, 0), (d_up, full_gate_up, 1))
    )
    hidden, d_normed_two = tie(hidden, d_normed_two)
    mixed_part = product_nt((hidden, full_down_t, 0))
    mixed = (residual + pair_total(mixed_part)).astype(BF16)
    grad_post = jnp.sum(d_normed_two * normal_two, axis=0)
    d_residual = cotangent.astype(F32) + rms_back(
        d_normed_two * scale_post, normal_two, factor_two
    )

    d_branch = d_residual.astype(BF16)
    d_attn = dot(d_branch, full_out_t).astype(BF16)
    d_queries, d_kv, given = attend_back(
        meta, docs, queries, d_attn, attended, lse, key_value, held
    )
    given = dict(zip(range(1, count), given))
    returned = {}
    exchange(given, returned, straight)
    if shard_count == 2:
        first, second = straight[-1], straight[0]
        normed_late, returned[first] = tie(normed_two, returned[first])
        kept_a = split_product(home, pairs_a(normed_late))
        normed_late, upstream_late, kept_a, returned[second] = tie(
            normed_two, cotangent, kept_a, returned[second]
        )
        kept_b = split_product((bit, 2 + bit), pairs_b(normed_late, upstream_late))
        units_a = halve([kept_a, got_a], near_axis)
        d_queries, kept_b = tie(d_queries, kept_b)
        units_b = [kept_b, got_b]
        units_b_away = picked_sum(units_b, 1 - shard, depth // 2)
        units_b = rows_at(units_b, shard, depth // 2) + [swap(units_b_away, "shard")]
    else:
        units_a = halve(scattered(pairs_a(normed_two)), near_axis)
        units_b = halve(scattered(pairs_b(normed_two, cotangent)), near_axis)
    d_q_pre, gq_part = rope_back(d_queries, q_pre, cosine, sine, scale_q)
    out_pairs = [(d_branch, attn_out, 0, heads_width), (normed_input, d_q_pre, 0, heads_width)]
    if shard_count == 2:
        out_query = [split_product(home, out_pairs), split_product(away, out_pairs)]
    else:
        out_query = scattered(out_pairs)
    units_a[-1], units_b[-1], out_query[0], out_query[-1], *rest = settle(
        returned,
        straight,
        units_a[-1],
        units_b[-1],
        out_query[0],
        out_query[-1],
        *(given[d] for d in crossing),
    )
    if shard_count == 2:
        out_query[-1] = swap(out_query[-1], "shard")
    given.update(zip(crossing, rest))
    exchange(given, returned, crossing)
    units_sum = jnp.concatenate([total(units_a), total(units_b)], axis=1)
    units_sum, d_kv = settle(returned, crossing, units_sum, d_kv)
    returned = [returned[d] for d in range(1, count)]

    units_sum = halve([units_sum], far_axis)
    d_k_pre, d_v_pre, gk_part = key_value_back(
        meta, docs, d_kv, returned, k_pre, cosine, sine, scale_k
    )
    d_k_pre, d_v_pre, out_query[-1] = tie(d_k_pre, d_v_pre, out_query[-1])
    out_query = halve(out_query, near_axis)
    kv_pairs = [(normed_input, d_k_pre, 0, kv_width), (normed_input, d_v_pre, 0, kv_width)]
    if shard_count == 2:
        sent_kv = swap(split_product(away, kv_pairs), "shard")
        key_value_grad = [split_product(home, kv_pairs), sent_kv]
    else:
        key_value_grad = scattered(kv_pairs)
    units_sum = total(units_sum)
    cut = units_sum.shape[1] // 2
    units_a, units_b = units_sum[:, :cut], units_sum[:, cut:]
    units_a, units_b, out_query[-1], key_value_grad[-1], d_q_pre, d_k_pre, d_v_pre = tie(
        units_a, units_b, out_query[-1], key_value_grad[-1], d_q_pre, d_k_pre, d_v_pre
    )

    units_a = double(units_a, far_axis)
    key_value_grad = halve(key_value_grad, near_axis)
    units_a, units_b, key_value_grad[-1], out_query[-1] = tie(
        units_a, units_b, key_value_grad[-1], out_query[-1]
    )

    units_b = double(units_b, far_axis)
    owned_a = double(units_a, near_axis)
    d_normed = pair_total(
        dot_nt(d_q_pre, full_query) + dot_nt(d_k_pre, full_key) + dot_nt(d_v_pre, full_value)
    )
    grad_in = jnp.sum(d_normed * normal_one, axis=0)
    input_grad = d_residual + rms_back(d_normed * scale_in, normal_one, factor_one)
    once = jnp.where(lax.axis_index("tp") == 0, 1.0, 0.0)
    gain_grads = jnp.concatenate([grad_in * once, grad_post * once, gq_part[0], gk_part[0]])
    gain_grads = gain_grads.reshape(-1, HEAD)
    if shard_count != 2:
        gain_grads = lax.psum(gain_grads, "shard")
    out_query, key_value_grad = total(out_query), total(key_value_grad)
    rest_chain = [
        jnp.concatenate(
            [
                out_query[:, :heads_width],
                key_value_grad[:, :kv_width],
                out_query[:, heads_width:],
                key_value_grad[:, kv_width:],
            ],
            axis=1,
        )
    ]
    units_b, owned_a, rest_chain[0], gain_grads = tie(
        units_b, owned_a, rest_chain[0], gain_grads
    )

    owned_b = double(units_b, near_axis)
    rest_chain = total(halve(rest_chain, far_axis))
    gain_grads = gain_grads + swap(gain_grads, "tp")
    gain_grads = gain_grads + swap(gain_grads, "ctx", masks[0])
    owned_b, rest_chain, gain_grads = tie(owned_b, rest_chain, gain_grads)

    cut = rest_chain.shape[1] // 2
    rest_a, rest_b = rest_chain[:, :cut], rest_chain[:, cut:]
    rest_a = double(rest_a, far_axis)
    gain_grads = gain_grads + swap(gain_grads, "ctx", masks[1])
    rest_a, rest_b, gain_grads = tie(rest_a, rest_b, gain_grads)

    rest_b = double(rest_b, far_axis)
    rest_a = double(rest_a, near_axis)
    for mask in masks[2:]:
        gain_grads = gain_grads + swap(gain_grads, "ctx", mask)
    rest_a, rest_b, gain_grads = tie(rest_a, rest_b, gain_grads)

    rest_b = double(rest_b, near_axis)
    if shard_count == 2:
        gain_grads = gain_grads + swap(gain_grads, "shard")
    gain_grads = gain_grads.reshape(-1)
    owned_up = jnp.concatenate([owned_a[:, units:], owned_b[:, :middle]], axis=1)
    own_gains = []
    for lo, size in ((0, model), (model, model), (2 * model, HEAD), (2 * model + HEAD, HEAD)):
        size = size // shard_count
        own_gains.append(lax.dynamic_slice_in_dim(gain_grads, lo + shard * size, size, 0))
    return (
        mixed,
        input_grad,
        rest_b[:, :heads_width].astype(F32),
        rest_a[:, heads_width:].astype(F32),
        rest_b[:, heads_width:].astype(F32),
        rest_a[:, :heads_width].astype(F32).T,
        owned_a[:, :units].astype(F32),
        owned_up.astype(F32),
        owned_b[:, middle:].astype(F32).T,
        *own_gains,
    )


def solution(mesh):
    placed = (
        P(("shard", "ctx"), None),
        P(("shard", "ctx"), None),
        P("shard", None),
        P(),
        P("shard", "tp"),
        P("shard", "tp"),
        P("shard", "tp"),
        P("tp", "shard"),
        P("shard", "tp"),
        P("shard", "tp"),
        P("tp", "shard"),
        P("shard"),
        P("shard"),
        P("shard"),
        P("shard"),
    )
    return jax.shard_map(
        body,
        mesh=mesh,
        in_specs=placed,
        out_specs=(
            P(("shard", "ctx"), None),
            P(("shard", "ctx"), None),
            P("shard", "tp"),
            P("shard", "tp"),
            P("shard", "tp"),
            P("tp", "shard"),
            P("shard", "tp"),
            P("shard", "tp"),
            P("tp", "shard"),
            P("shard"),
            P("shard"),
            P("shard"),
            P("shard"),
        ),
        check_vma=False,
    )
```

```python
import functools

import jax
import jax.numpy as jnp
from jax import lax
from jax.experimental import pallas as pl
from jax.experimental.pallas import tpu as pltpu
from jax.sharding import PartitionSpec as P

EPS = 1e-06
THETA = 1000000.0
LOG2E = 1.4426950408889634
HEAD = 128
BF16 = jnp.bfloat16
F32 = jnp.float32
VMEM_LIMIT = 48 * 1024 * 1024
CHEAP = pl.CostEstimate(flops=1000, bytes_accessed=1000, transcendentals=0)


def rms_parts(values):
    factor = lax.rsqrt(jnp.mean(values * values, axis=-1, keepdims=True) + EPS)
    return (values * factor, factor)


def rms_back(grad_hat, normal, factor):
    return factor * (grad_hat - normal * jnp.mean(grad_hat * normal, axis=-1, keepdims=True))


def dot(a, b):
    return jnp.dot(a, b, preferred_element_type=F32)


def dot_nt(a, b):
    return lax.dot_general(a, b, (((1,), (1,)), ((), ())), preferred_element_type=F32)


def dot_tn(a, b):
    return lax.dot_general(a, b, (((0,), (0,)), ((), ())), preferred_element_type=F32)


def tie(*values):
    return lax.optimization_barrier(values)


def pieces_of(own, axis):
    count = lax.axis_size(axis)
    return [own] + [
        lax.ppermute(own, axis, [((i + j) % count, i) for i in range(count)])
        for j in range(1, count)
    ]


def join(pieces, dim, index):
    count = len(pieces)
    if count == 1:
        return pieces[0]
    if count == 2:
        return jnp.where(
            index == 0, jnp.concatenate(pieces, dim), jnp.concatenate(pieces[::-1], dim)
        )
    size = pieces[0].shape[dim]
    shape = list(pieces[0].shape)
    shape[dim] = size * count
    whole = jnp.zeros(shape, pieces[0].dtype)
    for j, piece in enumerate(pieces):
        whole = lax.dynamic_update_slice_in_dim(whole, piece, (index + j) % count * size, dim)
    return whole


def pair_total(partial):
    count = lax.axis_size("tp")
    partial = partial.astype(BF16)
    if count != 2:
        return lax.psum(partial, "tp").astype(F32)
    other = lax.ppermute(partial, "tp", [(0, 1), (1, 0)])
    return partial.astype(F32) + other.astype(F32)


def swap(value, axis, level=1):
    count = lax.axis_size(axis)
    return lax.ppermute(value, axis, [(i, i ^ level) for i in range(count)])


def place_in(masks):
    return (lax.axis_index("ctx") // masks[0]) % (1 << len(masks))


def exchange(values, done, turns):
    count = lax.axis_size("ctx")
    for d in turns:
        done[d] = lax.ppermute(values[d], "ctx", [(i, i ^ d) for i in range(count)])


def settle(done, turns, *values):
    tied = tie(*(done[d] for d in turns), *values)
    done.update(zip(turns, tied))
    return tied[len(turns) :]


def total(addends):
    return sum(a.astype(F32) for a in addends).astype(BF16)


def rows_at(addends, block, rows):
    return [lax.dynamic_slice_in_dim(a, block * rows, rows, 0) for a in addends]


def halve(addends, masks):
    size = 1 << len(masks)
    rows = addends[0].shape[0] // size
    place = place_in(masks)
    kept = rows_at(addends, place, rows)
    for turn in range(1, size):
        sent = picked_sum(addends, place ^ turn, rows)
        kept = kept + [swap(sent, "ctx", turn * masks[0])]
    return kept


def scattered(pairs):
    grads = [dot_tn(a, b[:, lo:hi]).astype(BF16) for a, b, lo, hi in pairs]
    grad = jnp.concatenate(grads, axis=1)
    return [lax.psum_scatter(grad, "shard", scatter_dimension=0, tiled=True)]


def double(value, masks):
    size = 1 << len(masks)
    place = place_in(masks)
    blocks = [value] + [swap(value, "ctx", turn * masks[0]) for turn in range(1, size)]
    bit = 0
    while len(blocks) > 1:
        pairs = zip(blocks[::2], blocks[1::2])
        blocks = [join(list(pair), 0, (place >> bit) % 2) for pair in pairs]
        bit += 1
    return blocks[0]


def picked_sum_kernel(which_ref, *refs):
    refs[-1][...] = sum(ref[...].astype(F32) for ref in refs[:-1]).astype(BF16)


def picked_sum(addends, block, rows):
    if rows % 16 != 0:
        return total(rows_at(addends, block, rows))
    width = addends[0].shape[1]
    step = width // 4 if width % 512 == 0 else width // 2
    picked = pl.BlockSpec((rows, step), lambda i, w: (w[0], i))
    return pl.pallas_call(
        picked_sum_kernel,
        grid_spec=pltpu.PrefetchScalarGridSpec(
            num_scalar_prefetch=1,
            grid=(width // step,),
            in_specs=[picked] * len(addends),
            out_specs=pl.BlockSpec((rows, step), lambda i, w: (0, i)),
        ),
        out_shape=jax.ShapeDtypeStruct((rows, width), BF16),
        compiler_params=pltpu.CompilerParams(vmem_limit_bytes=VMEM_LIMIT),
        cost_estimate=CHEAP,
    )(jnp.reshape(block, (1,)).astype(jnp.int32), *addends)


def product_kernel(count, *refs):
    products = [dot_nt(refs[2 * i][...], refs[2 * i + 1][...]) for i in range(count)]
    refs[-1][...] = sum(products).astype(BF16)


def product_nt(*terms):
    rows = terms[0][0].shape[0]
    columns = terms[0][1].shape[0]
    step = min(columns, 256)
    specs, values = [], []
    for a, b, column in terms:
        depth = a.shape[1]
        specs.append(pl.BlockSpec((rows, depth), lambda i: (0, 0)))
        specs.append(pl.BlockSpec((step, depth), lambda i, column=column: (i, column)))
        values += [a, b]
    return pl.pallas_call(
        functools.partial(product_kernel, len(terms)),
        grid=(columns // step,),
        in_specs=specs,
        out_specs=pl.BlockSpec((rows, step), lambda i: (0, i)),
        out_shape=jax.ShapeDtypeStruct((rows, columns), BF16),
        compiler_params=pltpu.CompilerParams(vmem_limit_bytes=VMEM_LIMIT),
        cost_estimate=CHEAP,
    )(*values)


def split_product_kernel(spans, which_ref, *refs):
    j = pl.program_id(1)
    for i, (lo, hi) in enumerate(spans):

        @pl.when((j >= lo) & (j < hi))
        def _():
            refs[-1][...] = dot_tn(refs[2 * i][...], refs[2 * i + 1][...]).astype(BF16)


def split_product(which, pairs):
    tokens, model = pairs[0][0].shape
    rows = model // 4
    step = min(hi - lo for a, b, lo, hi in pairs)
    specs, values, spans, done = [], [], [], 0
    for a, b, lo, hi in pairs:
        blocks = (hi - lo) // step

        def column(i, j, w, first=done, base=lo // step, blocks=blocks):
            return (0, base + jnp.clip(j - first, 0, blocks - 1))

        specs.append(pl.BlockSpec((tokens, rows), lambda i, j, w: (0, w[i])))
        specs.append(pl.BlockSpec((tokens, step), column))
        values += [a, b]
        spans.append((done, done + blocks))
        done += blocks
    return pl.pallas_call(
        functools.partial(split_product_kernel, spans),
        grid_spec=pltpu.PrefetchScalarGridSpec(
            num_scalar_prefetch=1,
            grid=(2, done),
            in_specs=specs,
            out_specs=pl.BlockSpec((rows, step), lambda i, j, w: (i, j)),
        ),
        out_shape=jax.ShapeDtypeStruct((2 * rows, done * step), BF16),
        compiler_params=pltpu.CompilerParams(vmem_limit_bytes=VMEM_LIMIT),
        cost_estimate=CHEAP,
    )(jnp.stack(which).astype(jnp.int32), *values)


def rope_kernel(pre_ref, cos_ref, sin_ref, gain_ref, out_ref):
    pre = pre_ref[...]
    factor = lax.rsqrt(jnp.mean(pre * pre, axis=-1, keepdims=True) + EPS)
    scaled = pre * factor * gain_ref[...]
    turned = pltpu.roll(scaled, HEAD // 2, 1)
    out_ref[...] = (scaled * cos_ref[...] + turned * sin_ref[...]).astype(BF16)


def rope(pre, cosine, sine, gain):
    rows, width = pre.shape
    table = pl.BlockSpec((rows, HEAD), lambda h: (0, 0))
    column = pl.BlockSpec((rows, HEAD), lambda h: (0, h))
    return pl.pallas_call(
        rope_kernel,
        grid=(width // HEAD,),
        in_specs=[column, table, table, pl.BlockSpec((1, HEAD), lambda h: (0, 0))],
        out_specs=column,
        out_shape=jax.ShapeDtypeStruct((rows, width), BF16),
        compiler_params=pltpu.CompilerParams(vmem_limit_bytes=VMEM_LIMIT),
        cost_estimate=CHEAP,
    )(pre, cosine, sine, gain)


def part_start(meta_ref, docs, d, half):
    return pl.multiple_of((1 - meta_ref[docs + d]) * half, half)


def key_value_kernel(
    heads, docs, count, pieces, meta_ref, tokens_ref, factor_ref, scale_ref, *refs
):
    weights = refs[: 2 * pieces]
    cos_ref, sin_ref, gain_ref = refs[2 * pieces : 2 * pieces + 3]
    key_ref, out_ref, normed_ref = refs[2 * pieces + 3 : 2 * pieces + 6]
    sent = refs[2 * pieces + 6 :]
    half = out_ref.shape[0] // 2
    depth = tokens_ref.shape[1] // pieces
    step = pl.program_id(0)

    @pl.when(step == 0)
    def _():
        normal = tokens_ref[...].astype(F32) * factor_ref[...]
        normed_ref[...] = (normal * scale_ref[...]).astype(BF16)

    def product(parts):
        result = None
        for j, part in enumerate(parts):
            at = pl.multiple_of(meta_ref[docs + 2 * (count - 1) + j] * depth, HEAD)
            term = dot(normed_ref[:, pl.ds(at, depth)], part[...])
            result = term if result is None else result + term
        return result

    @pl.when(step < heads // 2)
    def _():
        key_ref[...] = product(weights[:pieces])
        for a in range(2):
            lanes = slice(a * HEAD, (a + 1) * HEAD)
            pre = key_ref[:, lanes]
            factor = lax.rsqrt(jnp.mean(pre * pre, axis=-1, keepdims=True) + EPS)
            scaled = pre * factor * gain_ref[...]
            turned = pltpu.roll(scaled, HEAD // 2, 1)
            out_ref[:, lanes] = (scaled * cos_ref[...] + turned * sin_ref[...]).astype(BF16)

    @pl.when(step >= heads // 2)
    def _():
        out_ref[...] = product(weights[pieces:]).astype(BF16)

    for d, sent_ref in enumerate(sent):
        sent_ref[...] = out_ref[pl.ds(part_start(meta_ref, docs, d, half), half), :]


def key_value_and_parts(
    meta, docs, count, tokens, factor, scale, keys, values, cosine, sine, gain
):
    rows, model = tokens.shape
    depth, width = keys[0].shape
    heads = width // HEAD
    half_steps = heads // 2
    whole = lambda shape: pl.BlockSpec(shape, lambda h, m: (0, 0))
    column = pl.BlockSpec((rows, 2 * HEAD), lambda h, m: (0, h))
    key_spec = pl.BlockSpec((depth, 2 * HEAD), lambda h, m: (0, jnp.minimum(h, half_steps - 1)))
    value_spec = pl.BlockSpec((depth, 2 * HEAD), lambda h, m: (0, jnp.maximum(h - half_steps, 0)))
    part = pl.BlockSpec((rows // 2, 2 * HEAD), lambda h, m: (0, h))
    result = pl.pallas_call(
        functools.partial(key_value_kernel, heads, docs, count, len(keys)),
        grid_spec=pltpu.PrefetchScalarGridSpec(
            num_scalar_prefetch=1,
            grid=(heads,),
            in_specs=[whole((rows, model)), whole((rows, 1)), whole((1, model))]
            + [key_spec] * len(keys)
            + [value_spec] * len(values)
            + [whole((rows, HEAD)), whole((rows, HEAD)), whole((1, HEAD))],
            out_specs=[
                pl.BlockSpec((rows, 2 * HEAD), lambda h, m: (0, jnp.minimum(h, half_steps - 1))),
                column,
                whole((rows, model)),
            ]
            + [part] * (count - 1),
        ),
        out_shape=[
            jax.ShapeDtypeStruct((rows, width), F32),
            jax.ShapeDtypeStruct((rows, 2 * width), BF16),
            jax.ShapeDtypeStruct((rows, model), BF16),
        ]
        + [jax.ShapeDtypeStruct((rows // 2, 2 * width), BF16)] * (count - 1),
        compiler_params=pltpu.CompilerParams(vmem_limit_bytes=VMEM_LIMIT),
        cost_estimate=CHEAP,
    )(meta, tokens, factor, scale, *keys, *values, cosine, sine, gain)
    return result[0], result[1], result[2], dict(zip(range(1, count), result[3:]))


def turn_back(grad, pre_ref, cos_ref, sin_ref, gain_ref, out_ref, sum_ref):
    pre = pre_ref[...]
    factor = lax.rsqrt(jnp.mean(pre * pre, axis=-1, keepdims=True) + EPS)
    hat = pre * factor
    back = grad * cos_ref[...] - pltpu.roll(grad, HEAD // 2, 1) * sin_ref[...]
    terms = jnp.sum(back * hat, axis=0, keepdims=True)

    @pl.when(pl.program_id(0) == 0)
    def _():
        sum_ref[...] = terms

    @pl.when(pl.program_id(0) > 0)
    def _():
        sum_ref[...] += terms

    back = back * gain_ref[...]
    inner = jnp.mean(back * hat, axis=-1, keepdims=True)
    out_ref[...] = (factor * (back - hat * inner)).astype(BF16)


def rope_back_kernel(grad_ref, *refs):
    turn_back(grad_ref[...], *refs)


def key_value_back_kernel(docs, meta_ref, own_ref, *refs):
    returned = refs[:-8]
    key_ref, cos_ref, sin_ref, gain_ref, d_key_ref, d_value_ref, sum_ref, acc_ref = refs[-8:]
    half = key_ref.shape[0] // 2
    acc_ref[...] = own_ref[...]
    for d, given_ref in enumerate(returned):
        rows = pl.ds(part_start(meta_ref, docs, d, half), half)
        acc_ref[:, rows, :] += given_ref[...].astype(F32)
    d_value_ref[...] = acc_ref[1].astype(BF16)
    turn_back(acc_ref[0], key_ref, cos_ref, sin_ref, gain_ref, d_key_ref, sum_ref)


def key_value_back(meta, docs, own, returned, key, cosine, sine, gain):
    rows, width = key.shape
    table = pl.BlockSpec((rows, HEAD), lambda h, m: (0, 0))
    column = pl.BlockSpec((rows, HEAD), lambda h, m: (0, h))
    one_row = pl.BlockSpec((1, HEAD), lambda h, m: (0, 0))
    return pl.pallas_call(
        functools.partial(key_value_back_kernel, docs),
        grid_spec=pltpu.PrefetchScalarGridSpec(
            num_scalar_prefetch=1,
            grid=(width // HEAD,),
            in_specs=[pl.BlockSpec((2, rows, HEAD), lambda h, m: (0, 0, h))]
            + [pl.BlockSpec((2, rows // 2, HEAD), lambda h, m: (0, 0, h))] * len(returned)
            + [column, table, table, one_row],
            out_specs=[column, column, one_row],
            scratch_shapes=[pltpu.VMEM((2, rows, HEAD), F32)],
        ),
        out_shape=[
            jax.ShapeDtypeStruct((rows, width), BF16),
            jax.ShapeDtypeStruct((rows, width), BF16),
            jax.ShapeDtypeStruct((1, HEAD), F32),
        ],
        compiler_params=pltpu.CompilerParams(vmem_limit_bytes=VMEM_LIMIT),
        cost_estimate=CHEAP,
    )(meta, own, *returned, key, cosine, sine, gain)


def rope_back(grad, pre, cosine, sine, gain):
    rows, width = grad.shape
    column = pl.BlockSpec((rows, HEAD), lambda h: (0, h))
    table = pl.BlockSpec((rows, HEAD), lambda h: (0, 0))
    one_row = pl.BlockSpec((1, HEAD), lambda h: (0, 0))
    return pl.pallas_call(
        rope_back_kernel,
        grid=(width // HEAD,),
        in_specs=[column, column, table, table, one_row],
        out_specs=[column, one_row],
        out_shape=[
            jax.ShapeDtypeStruct((rows, width), BF16),
            jax.ShapeDtypeStruct((1, HEAD), F32),
        ],
        compiler_params=pltpu.CompilerParams(vmem_limit_bytes=VMEM_LIMIT),
    )(grad, pre, cosine, sine, gain)


def doc_begins(meta_ref, docs, place):
    begin = jnp.zeros_like(place)
    for i in range(1, docs):
        start = meta_ref[i]
        begin = jnp.where(place >= start, start, begin)
    return begin


def mask_across(meta_ref, docs, shape, half, q_part, k_part, diagonal):
    column = lax.broadcasted_iota(jnp.int32, (1, shape[1]), 1)
    q_place = q_part * half + jnp.where(column >= half, column - half, column)
    begin = doc_begins(meta_ref, docs, q_place) - k_part * half
    row = lax.broadcasted_iota(jnp.int32, shape, 0)
    visible = row >= begin
    if diagonal:
        visible = visible & (row <= q_place - k_part * half)
    return visible


def two_heads(ref, start, half):
    rows = pl.ds(start, half)
    return jnp.concatenate([ref[rows, :HEAD], ref[rows, HEAD:]], axis=0)


def forward_kernel(docs, count, meta_ref, q_ref, k_ref, v_ref, *refs):
    others = refs[: 2 * (count - 1)]
    out_ref, out16_ref, lse_ref, acc_ref, begin_ref = refs[2 * (count - 1) :]
    half = q_ref.shape[0] // 2
    factor = HEAD**-0.5 * LOG2E
    ones = jnp.ones((half, HEAD), BF16)
    own = meta_ref[0]
    parts = (own, 2 * count - 1 - own)

    @pl.when(pl.program_id(0) == 0)
    def _():
        row = lax.broadcasted_iota(jnp.int32, (2 * half, HEAD), 0)
        for e in range(2):
            place = parts[e] * half + jnp.where(row >= half, row - half, row)
            begin_ref[e] = doc_begins(meta_ref, docs, place)

    def block(side, start, keys, values, k_part, diagonal):
        scores = dot_nt(two_heads(q_ref, start, half), keys)
        column = lax.broadcasted_iota(jnp.int32, scores.shape, 1)
        begin = begin_ref[side] - k_part * half
        visible = column >= jnp.concatenate([begin] * (half // HEAD), axis=1)
        if diagonal:
            row = lax.broadcasted_iota(jnp.int32, scores.shape, 0)
            visible = visible & (column <= jnp.where(row >= half, row - half, row))
        weights = jnp.where(visible, jnp.exp2(scores * factor), 0.0).astype(BF16)
        return dot(weights, jnp.concatenate([values, ones], axis=1))

    for e in range(2):
        rows = pl.ds(e * half, half)
        acc_ref[e] = block(e, e * half, k_ref[rows, :], v_ref[rows, :], parts[e], True)
    for d in range(count - 1):
        side = meta_ref[docs + d]
        k_part = meta_ref[docs + count - 1 + d]
        start = pl.multiple_of(side * half, half)
        acc_ref[side] += block(
            side, start, others[2 * d][...], others[2 * d + 1][...], k_part, False
        )

    for e in range(2):
        total = acc_ref[e]
        sums = total[:, HEAD:]
        result = total[:, :HEAD] / sums
        lse = jnp.log2(sums)
        for a in range(2):
            part = slice(a * half, (a + 1) * half)
            place = (pl.ds(e * half, half), slice(a * HEAD, (a + 1) * HEAD))
            out_ref[place] = result[part]
            out16_ref[place] = result[part].astype(BF16)
            lse_ref[place] = lse[part]


def backward_kernel(docs, count, meta_ref, q_ref, g_ref, o_ref, lse_ref, k_ref, v_ref, *refs):
    others = refs[: 2 * (count - 1)]
    dq_ref, dkv_ref = refs[2 * (count - 1) : 2 * count]
    given = refs[2 * count : 3 * count - 1]
    acc_ref, stats_ref, delta_ref = refs[3 * count - 1 :]
    half = q_ref.shape[0] // 2
    scale = HEAD**-0.5
    own = meta_ref[0]

    for e in range(2):
        grads = two_heads(g_ref, e * half, half).astype(F32)
        delta = jnp.sum(grads * two_heads(o_ref, e * half, half), axis=1, keepdims=True)
        delta = jnp.broadcast_to(delta, (2 * half, HEAD))
        delta_ref[e] = jnp.transpose(delta)[:8]
        stats_ref[e] = jnp.transpose(two_heads(lse_ref, e * half, half))[:8]

    def block(side, start, keys, values, q_part, k_part, diagonal):
        queries = two_heads(q_ref, start, half)
        grads = two_heads(g_ref, start, half)
        scores = dot_nt(keys, queries)
        lse = stats_ref[side][:1]
        delta = delta_ref[side][:1]
        weights = jnp.exp2(scores * (scale * LOG2E) - lse)
        visible = mask_across(meta_ref, docs, scores.shape, half, q_part, k_part, diagonal)
        weights = jnp.where(visible, weights, 0.0)
        d_weights = dot_nt(values, grads)
        d_scores = (weights * (d_weights - delta)).astype(BF16)
        d_values = dot(weights.astype(BF16), grads)
        d_keys = dot(d_scores, queries) * scale
        return dot_tn(d_scores, keys) * scale, d_keys, d_values

    for e in range(2):
        rows = pl.ds(e * half, half)
        part = own if e == 0 else 2 * count - 1 - own
        d_queries, d_keys, d_values = block(
            e, e * half, k_ref[rows, :], v_ref[rows, :], part, part, True
        )
        acc_ref[e] = d_queries
        dkv_ref[0, rows, :] = d_keys
        dkv_ref[1, rows, :] = d_values
    for d in range(count - 1):
        side = meta_ref[docs + d]
        k_part = meta_ref[docs + count - 1 + d]
        q_part = jnp.where(side == 0, own, 2 * count - 1 - own)
        start = pl.multiple_of(side * half, half)
        d_queries, d_keys, d_values = block(
            side, start, others[2 * d][...], others[2 * d + 1][...], q_part, k_part, False
        )
        acc_ref[side] += d_queries
        given[d][0] = d_keys.astype(BF16)
        given[d][1] = d_values.astype(BF16)

    for e in range(2):
        for a in range(2):
            dq_ref[pl.ds(e * half, half), a * HEAD : (a + 1) * HEAD] = acc_ref[
                e, a * half : (a + 1) * half, :
            ]


def key_value_specs(rows, half, kv_heads, count):
    own = [
        pl.BlockSpec((rows, HEAD), lambda h, m: (0, h)),
        pl.BlockSpec((rows, HEAD), lambda h, m: (0, kv_heads + h)),
    ]
    other = [
        pl.BlockSpec((half, HEAD), lambda h, m: (0, h)),
        pl.BlockSpec((half, HEAD), lambda h, m: (0, kv_heads + h)),
    ]
    return own + other * (count - 1)


def twice(arrays):
    return [a for a in arrays for _ in range(2)]


def attend(meta, docs, queries, key_value, others):
    rows, width = queries.shape
    half = rows // 2
    count = len(others) + 1
    kv_heads = key_value.shape[1] // (2 * HEAD)
    column = pl.BlockSpec((rows, 2 * HEAD), lambda h, m: (0, h))
    return pl.pallas_call(
        functools.partial(forward_kernel, docs, count),
        grid_spec=pltpu.PrefetchScalarGridSpec(
            num_scalar_prefetch=1,
            grid=(kv_heads,),
            in_specs=[column] + key_value_specs(rows, half, kv_heads, count),
            out_specs=[column] * 3,
            scratch_shapes=[
                pltpu.VMEM((2, 2 * half, 2 * HEAD), F32),
                pltpu.VMEM((2, 2 * half, HEAD), jnp.int32),
            ],
        ),
        out_shape=[
            jax.ShapeDtypeStruct((rows, width), F32),
            jax.ShapeDtypeStruct((rows, width), BF16),
            jax.ShapeDtypeStruct((rows, width), F32),
        ],
        compiler_params=pltpu.CompilerParams(vmem_limit_bytes=VMEM_LIMIT),
        cost_estimate=CHEAP,
    )(meta, queries, key_value, key_value, *twice(others))


def attend_back(meta, docs, queries, grads, outs, lse, key_value, others):
    rows, width = queries.shape
    half = rows // 2
    count = len(others) + 1
    kv_width = key_value.shape[1] // 2
    kv_heads = kv_width // HEAD
    column = pl.BlockSpec((rows, 2 * HEAD), lambda h, m: (0, h))
    result = pl.pallas_call(
        functools.partial(backward_kernel, docs, count),
        grid_spec=pltpu.PrefetchScalarGridSpec(
            num_scalar_prefetch=1,
            grid=(kv_heads,),
            in_specs=[column] * 4 + key_value_specs(rows, half, kv_heads, count),
            out_specs=[column, pl.BlockSpec((2, rows, HEAD), lambda h, m: (0, 0, h))]
            + [pl.BlockSpec((2, half, HEAD), lambda h, m: (0, 0, h))] * (count - 1),
            scratch_shapes=[
                pltpu.VMEM((2, 2 * half, HEAD), F32),
                pltpu.VMEM((2, 8, 2 * half), F32),
                pltpu.VMEM((2, 8, 2 * half), F32),
            ],
        ),
        out_shape=[
            jax.ShapeDtypeStruct((rows, width), F32),
            jax.ShapeDtypeStruct((2, rows, kv_width), F32),
        ]
        + [jax.ShapeDtypeStruct((2, half, kv_width), BF16)] * (count - 1),
        compiler_params=pltpu.CompilerParams(vmem_limit_bytes=VMEM_LIMIT),
        cost_estimate=CHEAP,
    )(meta, queries, grads, outs, lse, key_value, key_value, *twice(others))
    return result[0], result[1], list(result[2:])


def body(
    tokens,
    cotangent,
    seq_lengths,
    part_order,
    w_query,
    key_weight,
    value_weight,
    w_out,
    w_gate,
    w_up,
    w_down,
    gain_in,
    gain_post,
    gain_q,
    gain_k,
):
    shard_count = lax.axis_size("shard")
    shard = lax.axis_index("shard")
    count = lax.axis_size("ctx")
    ctx = lax.axis_index("ctx")
    rows, model = tokens.shape
    half = rows // 2
    depth = model // shard_count
    docs = seq_lengths.shape[1]
    kv_width = key_weight.shape[1]
    units = w_gate.shape[1]
    heads_width = w_out.shape[0]

    masks = [1 << b for b in range(count.bit_length() - 1)]
    near_axis, far_axis = masks[:1], masks[1:]
    far = [d for d in range(1, count) if d >= count // 2]
    near = [d for d in range(1, count) if d < count // 2]
    crossing = [d for d in far + near if d % 2 == 1]
    straight = [d for d in far + near if d % 2 == 0]

    k_pieces = pieces_of(key_weight, "shard")
    v_pieces = pieces_of(value_weight, "shard")
    (own_rest,) = tie(jnp.concatenate([w_query, w_out.T, w_down.T], axis=1))
    own_gate_up = jnp.concatenate([w_gate, w_up], axis=1)

    turns = jnp.arange(count, dtype=jnp.int32)
    partner = jnp.bitwise_xor(ctx.astype(jnp.int32), turns)
    parts = jnp.sum(
        jnp.where(partner[:, None] == turns[None, :], part_order[:, 0][None, :], 0), axis=1
    )
    part = parts[:1]
    lengths = seq_lengths[0]
    order = jnp.arange(docs, dtype=jnp.int32)
    starts = jnp.sum(jnp.where(order[None, :] < order[:, None], lengths[None, :], 0), axis=1)
    meta = jnp.concatenate(
        [
            part,
            starts[1:],
            (parts[1:] >= part).astype(jnp.int32),
            jnp.where(parts[1:] < part, parts[1:], 2 * count - 1 - parts[1:]),
            (shard + jnp.arange(shard_count, dtype=jnp.int32)) % shard_count,
        ]
    ).astype(jnp.int32)
    row = jnp.arange(rows, dtype=jnp.int32)
    places = jnp.where(row < half, part * half + row, (2 * count - 2 - part) * half + row)
    reached = places[:, None] >= starts[None, :]
    begins = jnp.max(jnp.where(reached, starts[None, :], 0), axis=1)
    frequency = THETA ** (-jnp.arange(0, HEAD, 2, dtype=F32) / HEAD)
    angles = (places - begins).astype(F32)[:, None] * frequency[None, :]
    cosine, sine = jnp.cos(angles), jnp.sin(angles)
    cosine = jnp.concatenate([cosine, cosine], axis=-1)
    sine = jnp.concatenate([-sine, sine], axis=-1)

    inputs = tokens.astype(F32)
    normal_one, factor_one = rms_parts(inputs)
    factor_one, gain_in = tie(factor_one, gain_in)
    packed = jnp.concatenate([gain_in, gain_post, gain_q, gain_k])
    packed_pieces = pieces_of(packed, "shard")

    bit = place_in(near_axis)
    half_rest = own_rest
    if shard_count == 2:
        half_rest = lax.dynamic_slice_in_dim(own_rest, bit * (depth // 2), depth // 2, 0)
    half_rest, own_rest, own_gate_up, packed_pieces[-1], k_pieces[-1], v_pieces[-1] = tie(
        half_rest, own_rest, own_gate_up, packed_pieces[-1], k_pieces[-1], v_pieces[-1]
    )
    cosine, sine, meta, factor_one, k_pieces[-1] = tie(
        cosine, sine, meta, factor_one, k_pieces[-1]
    )
    cuts = [0, depth, 2 * depth, 2 * depth + gain_q.shape[0], packed.shape[0]]
    scale_in, scale_post, scale_q, scale_k = (
        join([piece[lo:hi] for piece in packed_pieces], 0, shard).astype(F32).reshape(1, -1)
        for lo, hi in zip(cuts[:-1], cuts[1:])
    )
    full_key = join(k_pieces, 0, shard)
    full_value = join(v_pieces, 0, shard)

    full_gate_up = lax.all_gather(own_gate_up, "shard", axis=0, tiled=True)
    if shard_count == 2:
        half_rest = swap(half_rest, "shard")
    k_pre, key_value, normed_input, sent = key_value_and_parts(
        meta,
        docs,
        count,
        tokens,
        factor_one,
        scale_in,
        k_pieces,
        v_pieces,
        cosine,
        sine,
        scale_k,
    )
    held = {}
    exchange(sent, held, crossing)
    half_rest, *rest = settle(held, crossing, half_rest, *(sent[d] for d in straight))
    sent.update(zip(straight, rest))

    exchange(sent, held, straight)
    if shard_count == 2:
        other_rest = join([half_rest, swap(half_rest, "ctx", near_axis[0])], 0, bit)
        full_rest = join([own_rest, other_rest], 0, shard)
    else:
        full_rest = lax.all_gather(half_rest, "shard", axis=0, tiled=True)
    full_query = full_rest[:, :heads_width]
    full_out_t = full_rest[:, heads_width : 2 * heads_width]
    full_down_t = full_rest[:, 2 * heads_width :]
    q_pre = dot(normed_input, full_query)
    queries = rope(q_pre, cosine, sine, scale_q)
    queries, full_out_t = settle(held, straight, queries, full_out_t)
    held = [held[d] for d in range(1, count)]
    attended, attn_out, lse = attend(meta, docs, queries, key_value, held)

    residual = inputs + pair_total(dot_nt(attn_out, full_out_t))
    normal_two, factor_two = rms_parts(residual)
    normed_two = (normal_two * scale_post).astype(BF16)
    gate_upward = dot(normed_two, full_gate_up)
    gate_act = gate_upward[:, :units]
    upward = gate_upward[:, units:]
    sigma = jax.nn.sigmoid(gate_act)
    silu_act = gate_act * sigma
    hidden = (silu_act * upward).astype(BF16)
    d_hidden = dot(cotangent, full_down_t)
    d_gate = (d_hidden * upward * sigma * (1.0 + gate_act * (1.0 - sigma))).astype(BF16)
    d_up = (d_hidden * silu_act).astype(BF16)
    middle = units // 2
    away, home = (2 - 2 * shard, 3 - 2 * shard), (2 * shard, 2 * shard + 1)

    def pairs_a(normed):
        return [(normed, d_gate, 0, units), (normed, d_up, 0, middle)]

    def pairs_b(normed, upstream):
        return [(normed, d_up, middle, units), (upstream, hidden, 0, units)]

    if shard_count == 2:
        sent_a = split_product(away, pairs_a(normed_two))
        sent_b = split_product((1 - bit, 3 - bit), pairs_b(normed_two, cotangent))
        d_gate, d_up, sent_a, sent_b = tie(d_gate, d_up, sent_a, sent_b)
        got_a, got_b = swap(sent_a, "shard"), swap(sent_b, "ctx", near_axis[0])
    d_normed_two = pair_total(
        product_nt((d_gate, full_gate_up, 0), (d_up, full_gate_up, 1))
    )
    grad_post = jnp.sum(d_normed_two * normal_two, axis=0)
    d_residual = cotangent.astype(F32) + rms_back(
        d_normed_two * scale_post, normal_two, factor_two
    )

    d_branch = d_residual.astype(BF16)
    d_attn = dot(d_branch, full_out_t).astype(BF16)
    d_queries, d_kv, given = attend_back(
        meta, docs, queries, d_attn, attended, lse, key_value, held
    )
    given = dict(zip(range(1, count), given))
    returned = {}
    exchange(given, returned, straight)
    if shard_count == 2:
        first, second = straight[-1], straight[0]
        normed_late, returned[first] = tie(normed_two, returned[first])
        kept_a = split_product(home, pairs_a(normed_late))
        normed_late, upstream_late, kept_a, returned[second] = tie(
            normed_two, cotangent, kept_a, returned[second]
        )
        kept_b = split_product((bit, 2 + bit), pairs_b(normed_late, upstream_late))
        units_a = halve([kept_a, got_a], near_axis)
        d_queries, kept_b = tie(d_queries, kept_b)
        units_b = [kept_b, got_b]
        units_b_away = picked_sum(units_b, 1 - shard, depth // 2)
        units_b = rows_at(units_b, shard, depth // 2) + [swap(units_b_away, "shard")]
    else:
        units_a = halve(scattered(pairs_a(normed_two)), near_axis)
        units_b = halve(scattered(pairs_b(normed_two, cotangent)), near_axis)
    d_q_pre, gq_part = rope_back(d_queries, q_pre, cosine, sine, scale_q)
    out_pairs = [(d_branch, attn_out, 0, heads_width), (normed_input, d_q_pre, 0, heads_width)]
    if shard_count == 2:
        out_query = [split_product(home, out_pairs), split_product(away, out_pairs)]
    else:
        out_query = scattered(out_pairs)
    units_a[-1], units_b[-1], out_query[0], out_query[-1], *rest = settle(
        returned,
        straight,
        units_a[-1],
        units_b[-1],
        out_query[0],
        out_query[-1],
        *(given[d] for d in crossing),
    )
    if shard_count == 2:
        out_query[-1] = swap(out_query[-1], "shard")
    given.update(zip(crossing, rest))
    exchange(given, returned, crossing)
    units_sum = jnp.concatenate([total(units_a), total(units_b)], axis=1)
    units_sum, d_kv = settle(returned, crossing, units_sum, d_kv)
    returned = [returned[d] for d in range(1, count)]

    units_sum = halve([units_sum], far_axis)
    d_k_pre, d_v_pre, gk_part = key_value_back(
        meta, docs, d_kv, returned, k_pre, cosine, sine, scale_k
    )
    d_k_pre, d_v_pre, out_query[-1] = tie(d_k_pre, d_v_pre, out_query[-1])
    out_query = halve(out_query, near_axis)
    kv_pairs = [(normed_input, d_k_pre, 0, kv_width), (normed_input, d_v_pre, 0, kv_width)]
    if shard_count == 2:
        sent_kv = swap(split_product(away, kv_pairs), "shard")
        key_value_grad = [split_product(home, kv_pairs), sent_kv]
    else:
        key_value_grad = scattered(kv_pairs)
    units_sum = total(units_sum)
    cut = units_sum.shape[1] // 2
    units_a, units_b = units_sum[:, :cut], units_sum[:, cut:]
    units_a, units_b, out_query[-1], key_value_grad[-1], d_q_pre, d_k_pre, d_v_pre = tie(
        units_a, units_b, out_query[-1], key_value_grad[-1], d_q_pre, d_k_pre, d_v_pre
    )

    units_a = double(units_a, far_axis)
    key_value_grad = halve(key_value_grad, near_axis)
    d_normed = pair_total(
        dot_nt(d_q_pre, full_query) + dot_nt(d_k_pre, full_key) + dot_nt(d_v_pre, full_value)
    )
    units_a, units_b, key_value_grad[-1], out_query[-1], d_normed = tie(
        units_a, units_b, key_value_grad[-1], out_query[-1], d_normed
    )

    units_b = double(units_b, far_axis)
    owned_a = double(units_a, near_axis)
    grad_in = jnp.sum(d_normed * normal_one, axis=0)
    input_grad = d_residual + rms_back(d_normed * scale_in, normal_one, factor_one)
    once = jnp.where(lax.axis_index("tp") == 0, 1.0, 0.0)
    gain_grads = jnp.concatenate([grad_in * once, grad_post * once, gq_part[0], gk_part[0]])
    gain_grads = gain_grads.reshape(-1, HEAD)
    if shard_count != 2:
        gain_grads = lax.psum(gain_grads, "shard")
    out_query, key_value_grad = total(out_query), total(key_value_grad)
    rest_chain = [
        jnp.concatenate(
            [
                out_query[:, :heads_width],
                key_value_grad[:, :kv_width],
                out_query[:, heads_width:],
                key_value_grad[:, kv_width:],
            ],
            axis=1,
        )
    ]
    units_b, owned_a, rest_chain[0], gain_grads = tie(
        units_b, owned_a, rest_chain[0], gain_grads
    )

    owned_b = double(units_b, near_axis)
    rest_chain = total(halve(rest_chain, far_axis))
    gain_grads = gain_grads + swap(gain_grads, "tp")
    gain_grads = gain_grads + swap(gain_grads, "ctx", masks[0])
    owned_b, rest_chain, gain_grads, hidden = tie(owned_b, rest_chain, gain_grads, hidden)

    cut = rest_chain.shape[1] // 2
    rest_a, rest_b = rest_chain[:, :cut], rest_chain[:, cut:]
    rest_a = double(rest_a, far_axis)
    gain_grads = gain_grads + swap(gain_grads, "ctx", masks[1])
    mixed_part = product_nt((hidden, full_down_t, 0))
    mixed = (residual + pair_total(mixed_part)).astype(BF16)
    rest_a, rest_b, gain_grads, mixed = tie(rest_a, rest_b, gain_grads, mixed)

    rest_b = double(rest_b, far_axis)
    rest_a = double(rest_a, near_axis)
    for mask in masks[2:]:
        gain_grads = gain_grads + swap(gain_grads, "ctx", mask)
    rest_a, rest_b, gain_grads = tie(rest_a, rest_b, gain_grads)

    rest_b = double(rest_b, near_axis)
    if shard_count == 2:
        gain_grads = gain_grads + swap(gain_grads, "shard")
    gain_grads = gain_grads.reshape(-1)
    owned_up = jnp.concatenate([owned_a[:, units:], owned_b[:, :middle]], axis=1)
    own_gains = []
    for lo, size in ((0, model), (model, model), (2 * model, HEAD), (2 * model + HEAD, HEAD)):
        size = size // shard_count
        own_gains.append(lax.dynamic_slice_in_dim(gain_grads, lo + shard * size, size, 0))
    return (
        mixed,
        input_grad,
        rest_b[:, :heads_width].astype(F32),
        rest_a[:, heads_width:].astype(F32),
        rest_b[:, heads_width:].astype(F32),
        rest_a[:, :heads_width].astype(F32).T,
        owned_a[:, :units].astype(F32),
        owned_up.astype(F32),
        owned_b[:, middle:].astype(F32).T,
        *own_gains,
    )


def solution(mesh):
    placed = (
        P(("shard", "ctx"), None),
        P(("shard", "ctx"), None),
        P("shard", None),
        P(),
        P("shard", "tp"),
        P("shard", "tp"),
        P("shard", "tp"),
        P("tp", "shard"),
        P("shard", "tp"),
        P("shard", "tp"),
        P("tp", "shard"),
        P("shard"),
        P("shard"),
        P("shard"),
        P("shard"),
    )
    return jax.shard_map(
        body,
        mesh=mesh,
        in_specs=placed,
        out_specs=(
            P(("shard", "ctx"), None),
            P(("shard", "ctx"), None),
            P("shard", "tp"),
            P("shard", "tp"),
            P("shard", "tp"),
            P("tp", "shard"),
            P("shard", "tp"),
            P("shard", "tp"),
            P("tp", "shard"),
            P("shard"),
            P("shard"),
            P("shard"),
            P("shard"),
        ),
        check_vma=False,
    )
```

```python
import functools

import jax
import jax.numpy as jnp
from jax import lax
from jax.experimental import pallas as pl
from jax.experimental.pallas import tpu as pltpu
from jax.sharding import PartitionSpec as P

EPS = 1e-06
THETA = 1000000.0
LOG2E = 1.4426950408889634
HEAD = 128
BF16 = jnp.bfloat16
F32 = jnp.float32
VMEM_LIMIT = 48 * 1024 * 1024
CHEAP = pl.CostEstimate(flops=1000, bytes_accessed=1000, transcendentals=0)


def rms_parts(values):
    factor = lax.rsqrt(jnp.mean(values * values, axis=-1, keepdims=True) + EPS)
    return (values * factor, factor)


def rms_back(grad_hat, normal, factor):
    return factor * (grad_hat - normal * jnp.mean(grad_hat * normal, axis=-1, keepdims=True))


def dot(a, b):
    return jnp.dot(a, b, preferred_element_type=F32)


def dot_nt(a, b):
    return lax.dot_general(a, b, (((1,), (1,)), ((), ())), preferred_element_type=F32)


def dot_tn(a, b):
    return lax.dot_general(a, b, (((0,), (0,)), ((), ())), preferred_element_type=F32)


def tie(*values):
    return lax.optimization_barrier(values)


def pieces_of(own, axis):
    count = lax.axis_size(axis)
    return [own] + [
        lax.ppermute(own, axis, [((i + j) % count, i) for i in range(count)])
        for j in range(1, count)
    ]


def join(pieces, dim, index):
    count = len(pieces)
    if count == 1:
        return pieces[0]
    if count == 2:
        return jnp.where(
            index == 0, jnp.concatenate(pieces, dim), jnp.concatenate(pieces[::-1], dim)
        )
    size = pieces[0].shape[dim]
    shape = list(pieces[0].shape)
    shape[dim] = size * count
    whole = jnp.zeros(shape, pieces[0].dtype)
    for j, piece in enumerate(pieces):
        whole = lax.dynamic_update_slice_in_dim(whole, piece, (index + j) % count * size, dim)
    return whole


def pair_total(partial):
    count = lax.axis_size("tp")
    partial = partial.astype(BF16)
    if count != 2:
        return lax.psum(partial, "tp").astype(F32)
    other = lax.ppermute(partial, "tp", [(0, 1), (1, 0)])
    return partial.astype(F32) + other.astype(F32)


def swap(value, axis, level=1):
    count = lax.axis_size(axis)
    return lax.ppermute(value, axis, [(i, i ^ level) for i in range(count)])


def place_in(masks):
    return (lax.axis_index("ctx") // masks[0]) % (1 << len(masks))


def exchange(values, done, turns):
    count = lax.axis_size("ctx")
    for d in turns:
        done[d] = lax.ppermute(values[d], "ctx", [(i, i ^ d) for i in range(count)])


def settle(done, turns, *values):
    tied = tie(*(done[d] for d in turns), *values)
    done.update(zip(turns, tied))
    return tied[len(turns) :]


def total(addends):
    return sum(a.astype(F32) for a in addends).astype(BF16)


def rows_at(addends, block, rows):
    return [lax.dynamic_slice_in_dim(a, block * rows, rows, 0) for a in addends]


def halve(addends, masks):
    size = 1 << len(masks)
    rows = addends[0].shape[0] // size
    place = place_in(masks)
    kept = rows_at(addends, place, rows)
    for turn in range(1, size):
        sent = picked_sum(addends, place ^ turn, rows)
        kept = kept + [swap(sent, "ctx", turn * masks[0])]
    return kept


def scattered(pairs):
    grads = [dot_tn(a, b[:, lo:hi]).astype(BF16) for a, b, lo, hi in pairs]
    grad = jnp.concatenate(grads, axis=1)
    return [lax.psum_scatter(grad, "shard", scatter_dimension=0, tiled=True)]


def double(value, masks):
    size = 1 << len(masks)
    place = place_in(masks)
    blocks = [value] + [swap(value, "ctx", turn * masks[0]) for turn in range(1, size)]
    bit = 0
    while len(blocks) > 1:
        pairs = zip(blocks[::2], blocks[1::2])
        blocks = [join(list(pair), 0, (place >> bit) % 2) for pair in pairs]
        bit += 1
    return blocks[0]


def picked_sum_kernel(which_ref, *refs):
    refs[-1][...] = sum(ref[...].astype(F32) for ref in refs[:-1]).astype(BF16)


def picked_sum(addends, block, rows):
    if rows % 16 != 0:
        return total(rows_at(addends, block, rows))
    width = addends[0].shape[1]
    step = width // 4 if width % 512 == 0 else width // 2
    picked = pl.BlockSpec((rows, step), lambda i, w: (w[0], i))
    return pl.pallas_call(
        picked_sum_kernel,
        grid_spec=pltpu.PrefetchScalarGridSpec(
            num_scalar_prefetch=1,
            grid=(width // step,),
            in_specs=[picked] * len(addends),
            out_specs=pl.BlockSpec((rows, step), lambda i, w: (0, i)),
        ),
        out_shape=jax.ShapeDtypeStruct((rows, width), BF16),
        compiler_params=pltpu.CompilerParams(vmem_limit_bytes=VMEM_LIMIT),
        cost_estimate=CHEAP,
    )(jnp.reshape(block, (1,)).astype(jnp.int32), *addends)


def product_kernel(count, *refs):
    products = [dot_nt(refs[2 * i][...], refs[2 * i + 1][...]) for i in range(count)]
    refs[-1][...] = sum(products).astype(BF16)


def product_nt(*terms):
    rows = terms[0][0].shape[0]
    columns = terms[0][1].shape[0]
    step = min(columns, 256)
    specs, values = [], []
    for a, b, column in terms:
        depth = a.shape[1]
        specs.append(pl.BlockSpec((rows, depth), lambda i: (0, 0)))
        specs.append(pl.BlockSpec((step, depth), lambda i, column=column: (i, column)))
        values += [a, b]
    return pl.pallas_call(
        functools.partial(product_kernel, len(terms)),
        grid=(columns // step,),
        in_specs=specs,
        out_specs=pl.BlockSpec((rows, step), lambda i: (0, i)),
        out_shape=jax.ShapeDtypeStruct((rows, columns), BF16),
        compiler_params=pltpu.CompilerParams(vmem_limit_bytes=VMEM_LIMIT),
        cost_estimate=CHEAP,
    )(*values)


def split_product_kernel(spans, which_ref, *refs):
    j = pl.program_id(1)
    for i, (lo, hi) in enumerate(spans):

        @pl.when((j >= lo) & (j < hi))
        def _():
            refs[-1][...] = dot_tn(refs[2 * i][...], refs[2 * i + 1][...]).astype(BF16)


def split_product(which, pairs):
    tokens, model = pairs[0][0].shape
    rows = model // 4
    step = min(hi - lo for a, b, lo, hi in pairs)
    specs, values, spans, done = [], [], [], 0
    for a, b, lo, hi in pairs:
        blocks = (hi - lo) // step

        def column(i, j, w, first=done, base=lo // step, blocks=blocks):
            return (0, base + jnp.clip(j - first, 0, blocks - 1))

        specs.append(pl.BlockSpec((tokens, rows), lambda i, j, w: (0, w[i])))
        specs.append(pl.BlockSpec((tokens, step), column))
        values += [a, b]
        spans.append((done, done + blocks))
        done += blocks
    return pl.pallas_call(
        functools.partial(split_product_kernel, spans),
        grid_spec=pltpu.PrefetchScalarGridSpec(
            num_scalar_prefetch=1,
            grid=(2, done),
            in_specs=specs,
            out_specs=pl.BlockSpec((rows, step), lambda i, j, w: (i, j)),
        ),
        out_shape=jax.ShapeDtypeStruct((2 * rows, done * step), BF16),
        compiler_params=pltpu.CompilerParams(vmem_limit_bytes=VMEM_LIMIT),
        cost_estimate=CHEAP,
    )(jnp.stack(which).astype(jnp.int32), *values)


def rope_kernel(pre_ref, cos_ref, sin_ref, gain_ref, out_ref):
    pre = pre_ref[...]
    factor = lax.rsqrt(jnp.mean(pre * pre, axis=-1, keepdims=True) + EPS)
    scaled = pre * factor * gain_ref[...]
    turned = pltpu.roll(scaled, HEAD // 2, 1)
    out_ref[...] = (scaled * cos_ref[...] + turned * sin_ref[...]).astype(BF16)


def rope(pre, cosine, sine, gain):
    rows, width = pre.shape
    table = pl.BlockSpec((rows, HEAD), lambda h: (0, 0))
    column = pl.BlockSpec((rows, HEAD), lambda h: (0, h))
    return pl.pallas_call(
        rope_kernel,
        grid=(width // HEAD,),
        in_specs=[column, table, table, pl.BlockSpec((1, HEAD), lambda h: (0, 0))],
        out_specs=column,
        out_shape=jax.ShapeDtypeStruct((rows, width), BF16),
        compiler_params=pltpu.CompilerParams(vmem_limit_bytes=VMEM_LIMIT),
        cost_estimate=CHEAP,
    )(pre, cosine, sine, gain)


def part_start(meta_ref, docs, d, half):
    return pl.multiple_of((1 - meta_ref[docs + d]) * half, half)


def key_value_kernel(
    heads, docs, count, pieces, meta_ref, tokens_ref, factor_ref, scale_ref, *refs
):
    weights = refs[: 2 * pieces]
    cos_ref, sin_ref, gain_ref = refs[2 * pieces : 2 * pieces + 3]
    key_ref, out_ref, normed_ref = refs[2 * pieces + 3 : 2 * pieces + 6]
    sent = refs[2 * pieces + 6 :]
    half = out_ref.shape[0] // 2
    depth = tokens_ref.shape[1] // pieces
    step = pl.program_id(0)

    @pl.when(step == 0)
    def _():
        normal = tokens_ref[...].astype(F32) * factor_ref[...]
        normed_ref[...] = (normal * scale_ref[...]).astype(BF16)

    def product(parts):
        result = None
        for j, part in enumerate(parts):
            at = pl.multiple_of(meta_ref[docs + 2 * (count - 1) + j] * depth, HEAD)
            term = dot(normed_ref[:, pl.ds(at, depth)], part[...])
            result = term if result is None else result + term
        return result

    @pl.when(step < heads // 2)
    def _():
        key_ref[...] = product(weights[:pieces])
        for a in range(2):
            lanes = slice(a * HEAD, (a + 1) * HEAD)
            pre = key_ref[:, lanes]
            factor = lax.rsqrt(jnp.mean(pre * pre, axis=-1, keepdims=True) + EPS)
            scaled = pre * factor * gain_ref[...]
            turned = pltpu.roll(scaled, HEAD // 2, 1)
            out_ref[:, lanes] = (scaled * cos_ref[...] + turned * sin_ref[...]).astype(BF16)

    @pl.when(step >= heads // 2)
    def _():
        out_ref[...] = product(weights[pieces:]).astype(BF16)

    for d, sent_ref in enumerate(sent):
        sent_ref[...] = out_ref[pl.ds(part_start(meta_ref, docs, d, half), half), :]


def key_value_and_parts(
    meta, docs, count, tokens, factor, scale, keys, values, cosine, sine, gain
):
    rows, model = tokens.shape
    depth, width = keys[0].shape
    heads = width // HEAD
    half_steps = heads // 2
    whole = lambda shape: pl.BlockSpec(shape, lambda h, m: (0, 0))
    column = pl.BlockSpec((rows, 2 * HEAD), lambda h, m: (0, h))
    key_spec = pl.BlockSpec((depth, 2 * HEAD), lambda h, m: (0, jnp.minimum(h, half_steps - 1)))
    value_spec = pl.BlockSpec((depth, 2 * HEAD), lambda h, m: (0, jnp.maximum(h - half_steps, 0)))
    part = pl.BlockSpec((rows // 2, 2 * HEAD), lambda h, m: (0, h))
    result = pl.pallas_call(
        functools.partial(key_value_kernel, heads, docs, count, len(keys)),
        grid_spec=pltpu.PrefetchScalarGridSpec(
            num_scalar_prefetch=1,
            grid=(heads,),
            in_specs=[whole((rows, model)), whole((rows, 1)), whole((1, model))]
            + [key_spec] * len(keys)
            + [value_spec] * len(values)
            + [whole((rows, HEAD)), whole((rows, HEAD)), whole((1, HEAD))],
            out_specs=[
                pl.BlockSpec((rows, 2 * HEAD), lambda h, m: (0, jnp.minimum(h, half_steps - 1))),
                column,
                whole((rows, model)),
            ]
            + [part] * (count - 1),
        ),
        out_shape=[
            jax.ShapeDtypeStruct((rows, width), F32),
            jax.ShapeDtypeStruct((rows, 2 * width), BF16),
            jax.ShapeDtypeStruct((rows, model), BF16),
        ]
        + [jax.ShapeDtypeStruct((rows // 2, 2 * width), BF16)] * (count - 1),
        compiler_params=pltpu.CompilerParams(vmem_limit_bytes=VMEM_LIMIT),
        cost_estimate=CHEAP,
    )(meta, tokens, factor, scale, *keys, *values, cosine, sine, gain)
    return result[0], result[1], result[2], dict(zip(range(1, count), result[3:]))


def turn_back(grad, pre_ref, cos_ref, sin_ref, gain_ref, out_ref, sum_ref):
    pre = pre_ref[...]
    factor = lax.rsqrt(jnp.mean(pre * pre, axis=-1, keepdims=True) + EPS)
    hat = pre * factor
    back = grad * cos_ref[...] - pltpu.roll(grad, HEAD // 2, 1) * sin_ref[...]
    terms = jnp.sum(back * hat, axis=0, keepdims=True)

    @pl.when(pl.program_id(0) == 0)
    def _():
        sum_ref[...] = terms

    @pl.when(pl.program_id(0) > 0)
    def _():
        sum_ref[...] += terms

    back = back * gain_ref[...]
    inner = jnp.mean(back * hat, axis=-1, keepdims=True)
    out_ref[...] = (factor * (back - hat * inner)).astype(BF16)


def rope_back_kernel(grad_ref, *refs):
    turn_back(grad_ref[...], *refs)


def key_value_back_kernel(docs, meta_ref, own_ref, *refs):
    returned = refs[:-8]
    key_ref, cos_ref, sin_ref, gain_ref, d_key_ref, d_value_ref, sum_ref, acc_ref = refs[-8:]
    half = key_ref.shape[0] // 2
    acc_ref[...] = own_ref[...]
    for d, given_ref in enumerate(returned):
        rows = pl.ds(part_start(meta_ref, docs, d, half), half)
        acc_ref[:, rows, :] += given_ref[...].astype(F32)
    d_value_ref[...] = acc_ref[1].astype(BF16)
    turn_back(acc_ref[0], key_ref, cos_ref, sin_ref, gain_ref, d_key_ref, sum_ref)


def key_value_back(meta, docs, own, returned, key, cosine, sine, gain):
    rows, width = key.shape
    table = pl.BlockSpec((rows, HEAD), lambda h, m: (0, 0))
    column = pl.BlockSpec((rows, HEAD), lambda h, m: (0, h))
    one_row = pl.BlockSpec((1, HEAD), lambda h, m: (0, 0))
    return pl.pallas_call(
        functools.partial(key_value_back_kernel, docs),
        grid_spec=pltpu.PrefetchScalarGridSpec(
            num_scalar_prefetch=1,
            grid=(width // HEAD,),
            in_specs=[pl.BlockSpec((2, rows, HEAD), lambda h, m: (0, 0, h))]
            + [pl.BlockSpec((2, rows // 2, HEAD), lambda h, m: (0, 0, h))] * len(returned)
            + [column, table, table, one_row],
            out_specs=[column, column, one_row],
            scratch_shapes=[pltpu.VMEM((2, rows, HEAD), F32)],
        ),
        out_shape=[
            jax.ShapeDtypeStruct((rows, width), BF16),
            jax.ShapeDtypeStruct((rows, width), BF16),
            jax.ShapeDtypeStruct((1, HEAD), F32),
        ],
        compiler_params=pltpu.CompilerParams(vmem_limit_bytes=VMEM_LIMIT),
        cost_estimate=CHEAP,
    )(meta, own, *returned, key, cosine, sine, gain)


def rope_back(grad, pre, cosine, sine, gain):
    rows, width = grad.shape
    column = pl.BlockSpec((rows, HEAD), lambda h: (0, h))
    table = pl.BlockSpec((rows, HEAD), lambda h: (0, 0))
    one_row = pl.BlockSpec((1, HEAD), lambda h: (0, 0))
    return pl.pallas_call(
        rope_back_kernel,
        grid=(width // HEAD,),
        in_specs=[column, column, table, table, one_row],
        out_specs=[column, one_row],
        out_shape=[
            jax.ShapeDtypeStruct((rows, width), BF16),
            jax.ShapeDtypeStruct((1, HEAD), F32),
        ],
        compiler_params=pltpu.CompilerParams(vmem_limit_bytes=VMEM_LIMIT),
    )(grad, pre, cosine, sine, gain)


def doc_begins(meta_ref, docs, place):
    begin = jnp.zeros_like(place)
    for i in range(1, docs):
        start = meta_ref[i]
        begin = jnp.where(place >= start, start, begin)
    return begin


def mask_across(meta_ref, docs, shape, half, q_part, k_part, diagonal):
    column = lax.broadcasted_iota(jnp.int32, (1, shape[1]), 1)
    q_place = q_part * half + jnp.where(column >= half, column - half, column)
    begin = doc_begins(meta_ref, docs, q_place) - k_part * half
    row = lax.broadcasted_iota(jnp.int32, shape, 0)
    visible = row >= begin
    if diagonal:
        visible = visible & (row <= q_place - k_part * half)
    return visible


def two_heads(ref, start, half):
    rows = pl.ds(start, half)
    return jnp.concatenate([ref[rows, :HEAD], ref[rows, HEAD:]], axis=0)


def forward_kernel(docs, count, meta_ref, q_ref, k_ref, v_ref, *refs):
    others = refs[: 2 * (count - 1)]
    out_ref, out16_ref, lse_ref, acc_ref, begin_ref = refs[2 * (count - 1) :]
    half = q_ref.shape[0] // 2
    factor = HEAD**-0.5 * LOG2E
    ones = jnp.ones((half, HEAD), BF16)
    own = meta_ref[0]
    parts = (own, 2 * count - 1 - own)

    @pl.when(pl.program_id(0) == 0)
    def _():
        row = lax.broadcasted_iota(jnp.int32, (2 * half, HEAD), 0)
        for e in range(2):
            place = parts[e] * half + jnp.where(row >= half, row - half, row)
            begin_ref[e] = doc_begins(meta_ref, docs, place)

    def block(side, start, keys, values, k_part, diagonal):
        scores = dot_nt(two_heads(q_ref, start, half), keys)
        column = lax.broadcasted_iota(jnp.int32, scores.shape, 1)
        begin = begin_ref[side] - k_part * half
        visible = column >= jnp.concatenate([begin] * (half // HEAD), axis=1)
        if diagonal:
            row = lax.broadcasted_iota(jnp.int32, scores.shape, 0)
            visible = visible & (column <= jnp.where(row >= half, row - half, row))
        weights = jnp.where(visible, jnp.exp2(scores * factor), 0.0).astype(BF16)
        return dot(weights, jnp.concatenate([values, ones], axis=1))

    for e in range(2):
        rows = pl.ds(e * half, half)
        acc_ref[e] = block(e, e * half, k_ref[rows, :], v_ref[rows, :], parts[e], True)
    for d in range(count - 1):
        side = meta_ref[docs + d]
        k_part = meta_ref[docs + count - 1 + d]
        start = pl.multiple_of(side * half, half)
        acc_ref[side] += block(
            side, start, others[2 * d][...], others[2 * d + 1][...], k_part, False
        )

    for e in range(2):
        total = acc_ref[e]
        sums = total[:, HEAD:]
        result = total[:, :HEAD] / sums
        lse = jnp.log2(sums)
        for a in range(2):
            part = slice(a * half, (a + 1) * half)
            place = (pl.ds(e * half, half), slice(a * HEAD, (a + 1) * HEAD))
            out_ref[place] = result[part]
            out16_ref[place] = result[part].astype(BF16)
            lse_ref[place] = lse[part]


def backward_kernel(docs, count, meta_ref, q_ref, g_ref, o_ref, lse_ref, k_ref, v_ref, *refs):
    others = refs[: 2 * (count - 1)]
    dq_ref, dkv_ref = refs[2 * (count - 1) : 2 * count]
    given = refs[2 * count : 3 * count - 1]
    acc_ref, stats_ref, delta_ref = refs[3 * count - 1 :]
    half = q_ref.shape[0] // 2
    scale = HEAD**-0.5
    own = meta_ref[0]

    for e in range(2):
        grads = two_heads(g_ref, e * half, half).astype(F32)
        delta = jnp.sum(grads * two_heads(o_ref, e * half, half), axis=1, keepdims=True)
        delta = jnp.broadcast_to(delta, (2 * half, HEAD))
        delta_ref[e] = jnp.transpose(delta)[:8]
        stats_ref[e] = jnp.transpose(two_heads(lse_ref, e * half, half))[:8]

    def block(side, start, keys, values, q_part, k_part, diagonal):
        queries = two_heads(q_ref, start, half)
        grads = two_heads(g_ref, start, half)
        scores = dot_nt(keys, queries)
        lse = stats_ref[side][:1]
        delta = delta_ref[side][:1]
        weights = jnp.exp2(scores * (scale * LOG2E) - lse)
        visible = mask_across(meta_ref, docs, scores.shape, half, q_part, k_part, diagonal)
        weights = jnp.where(visible, weights, 0.0)
        d_weights = dot_nt(values, grads)
        d_scores = (weights * (d_weights - delta)).astype(BF16)
        d_values = dot(weights.astype(BF16), grads)
        d_keys = dot(d_scores, queries) * scale
        return dot_tn(d_scores, keys) * scale, d_keys, d_values

    for e in range(2):
        rows = pl.ds(e * half, half)
        part = own if e == 0 else 2 * count - 1 - own
        d_queries, d_keys, d_values = block(
            e, e * half, k_ref[rows, :], v_ref[rows, :], part, part, True
        )
        acc_ref[e] = d_queries
        dkv_ref[0, rows, :] = d_keys
        dkv_ref[1, rows, :] = d_values
    for d in range(count - 1):
        side = meta_ref[docs + d]
        k_part = meta_ref[docs + count - 1 + d]
        q_part = jnp.where(side == 0, own, 2 * count - 1 - own)
        start = pl.multiple_of(side * half, half)
        d_queries, d_keys, d_values = block(
            side, start, others[2 * d][...], others[2 * d + 1][...], q_part, k_part, False
        )
        acc_ref[side] += d_queries
        given[d][0] = d_keys.astype(BF16)
        given[d][1] = d_values.astype(BF16)

    for e in range(2):
        for a in range(2):
            dq_ref[pl.ds(e * half, half), a * HEAD : (a + 1) * HEAD] = acc_ref[
                e, a * half : (a + 1) * half, :
            ]


def key_value_specs(rows, half, kv_heads, count):
    own = [
        pl.BlockSpec((rows, HEAD), lambda h, m: (0, h)),
        pl.BlockSpec((rows, HEAD), lambda h, m: (0, kv_heads + h)),
    ]
    other = [
        pl.BlockSpec((half, HEAD), lambda h, m: (0, h)),
        pl.BlockSpec((half, HEAD), lambda h, m: (0, kv_heads + h)),
    ]
    return own + other * (count - 1)


def twice(arrays):
    return [a for a in arrays for _ in range(2)]


def attend(meta, docs, queries, key_value, others):
    rows, width = queries.shape
    half = rows // 2
    count = len(others) + 1
    kv_heads = key_value.shape[1] // (2 * HEAD)
    column = pl.BlockSpec((rows, 2 * HEAD), lambda h, m: (0, h))
    return pl.pallas_call(
        functools.partial(forward_kernel, docs, count),
        grid_spec=pltpu.PrefetchScalarGridSpec(
            num_scalar_prefetch=1,
            grid=(kv_heads,),
            in_specs=[column] + key_value_specs(rows, half, kv_heads, count),
            out_specs=[column] * 3,
            scratch_shapes=[
                pltpu.VMEM((2, 2 * half, 2 * HEAD), F32),
                pltpu.VMEM((2, 2 * half, HEAD), jnp.int32),
            ],
        ),
        out_shape=[
            jax.ShapeDtypeStruct((rows, width), F32),
            jax.ShapeDtypeStruct((rows, width), BF16),
            jax.ShapeDtypeStruct((rows, width), F32),
        ],
        compiler_params=pltpu.CompilerParams(vmem_limit_bytes=VMEM_LIMIT),
        cost_estimate=CHEAP,
    )(meta, queries, key_value, key_value, *twice(others))


def attend_back(meta, docs, queries, grads, outs, lse, key_value, others):
    rows, width = queries.shape
    half = rows // 2
    count = len(others) + 1
    kv_width = key_value.shape[1] // 2
    kv_heads = kv_width // HEAD
    column = pl.BlockSpec((rows, 2 * HEAD), lambda h, m: (0, h))
    result = pl.pallas_call(
        functools.partial(backward_kernel, docs, count),
        grid_spec=pltpu.PrefetchScalarGridSpec(
            num_scalar_prefetch=1,
            grid=(kv_heads,),
            in_specs=[column] * 4 + key_value_specs(rows, half, kv_heads, count),
            out_specs=[column, pl.BlockSpec((2, rows, HEAD), lambda h, m: (0, 0, h))]
            + [pl.BlockSpec((2, half, HEAD), lambda h, m: (0, 0, h))] * (count - 1),
            scratch_shapes=[
                pltpu.VMEM((2, 2 * half, HEAD), F32),
                pltpu.VMEM((2, 8, 2 * half), F32),
                pltpu.VMEM((2, 8, 2 * half), F32),
            ],
        ),
        out_shape=[
            jax.ShapeDtypeStruct((rows, width), F32),
            jax.ShapeDtypeStruct((2, rows, kv_width), F32),
        ]
        + [jax.ShapeDtypeStruct((2, half, kv_width), BF16)] * (count - 1),
        compiler_params=pltpu.CompilerParams(vmem_limit_bytes=VMEM_LIMIT),
        cost_estimate=CHEAP,
    )(meta, queries, grads, outs, lse, key_value, key_value, *twice(others))
    return result[0], result[1], list(result[2:])


def body(
    tokens,
    cotangent,
    seq_lengths,
    part_order,
    w_query,
    key_weight,
    value_weight,
    w_out,
    w_gate,
    w_up,
    w_down,
    gain_in,
    gain_post,
    gain_q,
    gain_k,
):
    shard_count = lax.axis_size("shard")
    shard = lax.axis_index("shard")
    count = lax.axis_size("ctx")
    ctx = lax.axis_index("ctx")
    rows, model = tokens.shape
    half = rows // 2
    depth = model // shard_count
    docs = seq_lengths.shape[1]
    kv_width = key_weight.shape[1]
    units = w_gate.shape[1]
    heads_width = w_out.shape[0]

    masks = [1 << b for b in range(count.bit_length() - 1)]
    near_axis, far_axis = masks[:1], masks[1:]
    far = [d for d in range(1, count) if d >= count // 2]
    near = [d for d in range(1, count) if d < count // 2]
    crossing = [d for d in far + near if d % 2 == 1]
    straight = [d for d in far + near if d % 2 == 0]

    k_pieces = pieces_of(key_weight, "shard")
    v_pieces = pieces_of(value_weight, "shard")
    (own_rest,) = tie(jnp.concatenate([w_down.T, w_query, w_out.T], axis=1))
    own_gate_up = jnp.concatenate([w_gate, w_up], axis=1)

    turns = jnp.arange(count, dtype=jnp.int32)
    partner = jnp.bitwise_xor(ctx.astype(jnp.int32), turns)
    parts = jnp.sum(
        jnp.where(partner[:, None] == turns[None, :], part_order[:, 0][None, :], 0), axis=1
    )
    part = parts[:1]
    lengths = seq_lengths[0]
    order = jnp.arange(docs, dtype=jnp.int32)
    starts = jnp.sum(jnp.where(order[None, :] < order[:, None], lengths[None, :], 0), axis=1)
    meta = jnp.concatenate(
        [
            part,
            starts[1:],
            (parts[1:] >= part).astype(jnp.int32),
            jnp.where(parts[1:] < part, parts[1:], 2 * count - 1 - parts[1:]),
            (shard + jnp.arange(shard_count, dtype=jnp.int32)) % shard_count,
        ]
    ).astype(jnp.int32)
    row = jnp.arange(rows, dtype=jnp.int32)
    places = jnp.where(row < half, part * half + row, (2 * count - 2 - part) * half + row)
    reached = places[:, None] >= starts[None, :]
    begins = jnp.max(jnp.where(reached, starts[None, :], 0), axis=1)
    frequency = THETA ** (-jnp.arange(0, HEAD, 2, dtype=F32) / HEAD)
    angles = (places - begins).astype(F32)[:, None] * frequency[None, :]
    cosine, sine = jnp.cos(angles), jnp.sin(angles)
    cosine = jnp.concatenate([cosine, cosine], axis=-1)
    sine = jnp.concatenate([-sine, sine], axis=-1)

    inputs = tokens.astype(F32)
    normal_one, factor_one = rms_parts(inputs)
    factor_one, gain_in = tie(factor_one, gain_in)
    packed = jnp.concatenate([gain_in, gain_post, gain_q, gain_k])
    packed_pieces = pieces_of(packed, "shard")

    bit = place_in(near_axis)
    half_rest = own_rest
    if shard_count == 2:
        half_rest = lax.dynamic_slice_in_dim(own_rest, bit * (depth // 2), depth // 2, 0)
    half_rest, own_rest, own_gate_up, packed_pieces[-1], k_pieces[-1], v_pieces[-1] = tie(
        half_rest, own_rest, own_gate_up, packed_pieces[-1], k_pieces[-1], v_pieces[-1]
    )
    cosine, sine, meta, factor_one, k_pieces[-1] = tie(
        cosine, sine, meta, factor_one, k_pieces[-1]
    )
    cuts = [0, depth, 2 * depth, 2 * depth + gain_q.shape[0], packed.shape[0]]
    scale_in, scale_post, scale_q, scale_k = (
        join([piece[lo:hi] for piece in packed_pieces], 0, shard).astype(F32).reshape(1, -1)
        for lo, hi in zip(cuts[:-1], cuts[1:])
    )
    full_key = join(k_pieces, 0, shard)
    full_value = join(v_pieces, 0, shard)

    full_gate_up = lax.all_gather(own_gate_up, "shard", axis=0, tiled=True)
    if shard_count == 2:
        half_rest = swap(half_rest, "shard")
    k_pre, key_value, normed_input, sent = key_value_and_parts(
        meta,
        docs,
        count,
        tokens,
        factor_one,
        scale_in,
        k_pieces,
        v_pieces,
        cosine,
        sine,
        scale_k,
    )
    held = {}
    exchange(sent, held, crossing)
    half_rest, *rest = settle(held, crossing, half_rest, *(sent[d] for d in straight))
    sent.update(zip(straight, rest))

    exchange(sent, held, straight)
    if shard_count == 2:
        other_rest = join([half_rest, swap(half_rest, "ctx", near_axis[0])], 0, bit)
        full_rest = join([own_rest, other_rest], 0, shard)
    else:
        full_rest = lax.all_gather(half_rest, "shard", axis=0, tiled=True)
    full_query = full_rest[:, units : units + heads_width]
    q_pre = dot(normed_input, full_query)
    queries = rope(q_pre, cosine, sine, scale_q)
    queries, full_rest = settle(held, straight, queries, full_rest)
    full_down_t = full_rest[:, :units]
    full_query = full_rest[:, units : units + heads_width]
    full_out_t = full_rest[:, units + heads_width :]
    held = [held[d] for d in range(1, count)]
    attended, attn_out, lse = attend(meta, docs, queries, key_value, held)

    residual = inputs + pair_total(dot_nt(attn_out, full_out_t))
    normal_two, factor_two = rms_parts(residual)
    normed_two = (normal_two * scale_post).astype(BF16)
    gate_upward = dot(normed_two, full_gate_up)
    gate_act = gate_upward[:, :units]
    upward = gate_upward[:, units:]
    sigma = jax.nn.sigmoid(gate_act)
    silu_act = gate_act * sigma
    hidden = (silu_act * upward).astype(BF16)
    d_hidden = dot(cotangent, full_down_t)
    d_gate = (d_hidden * upward * sigma * (1.0 + gate_act * (1.0 - sigma))).astype(BF16)
    d_up = (d_hidden * silu_act).astype(BF16)
    middle = units // 2
    away, home = (2 - 2 * shard, 3 - 2 * shard), (2 * shard, 2 * shard + 1)

    def pairs_a(normed):
        return [(normed, d_gate, 0, units), (normed, d_up, 0, middle)]

    def pairs_b(normed, upstream):
        return [(normed, d_up, middle, units), (upstream, hidden, 0, units)]

    if shard_count == 2:
        sent_a = split_product(away, pairs_a(normed_two))
        sent_b = split_product((1 - bit, 3 - bit), pairs_b(normed_two, cotangent))
        d_gate, d_up, sent_a, sent_b = tie(d_gate, d_up, sent_a, sent_b)
        got_a, got_b = swap(sent_a, "shard"), swap(sent_b, "ctx", near_axis[0])
    d_normed_two = pair_total(
        product_nt((d_gate, full_gate_up, 0), (d_up, full_gate_up, 1))
    )
    grad_post = jnp.sum(d_normed_two * normal_two, axis=0)
    d_residual = cotangent.astype(F32) + rms_back(
        d_normed_two * scale_post, normal_two, factor_two
    )

    d_branch = d_residual.astype(BF16)
    d_attn = dot(d_branch, full_out_t).astype(BF16)
    d_queries, d_kv, given = attend_back(
        meta, docs, queries, d_attn, attended, lse, key_value, held
    )
    given = dict(zip(range(1, count), given))
    returned = {}
    exchange(given, returned, straight)
    if shard_count == 2:
        first, second = straight[-1], straight[0]
        normed_late, d_queries = tie(normed_two, d_queries)
        kept_a = split_product(home, pairs_a(normed_late))
        normed_late, upstream_late, kept_a, returned[first] = tie(
            normed_late, cotangent, kept_a, returned[first]
        )
        kept_b = split_product((bit, 2 + bit), pairs_b(normed_late, upstream_late))
        kept_a, kept_b, returned[second] = tie(kept_a, kept_b, returned[second])
        units_a = halve([kept_a, got_a], near_axis)
        d_queries, kept_b = tie(d_queries, kept_b)
        units_b = [kept_b, got_b]
        units_b_away = picked_sum(units_b, 1 - shard, depth // 2)
        units_b = rows_at(units_b, shard, depth // 2) + [swap(units_b_away, "shard")]
    else:
        units_a = halve(scattered(pairs_a(normed_two)), near_axis)
        units_b = halve(scattered(pairs_b(normed_two, cotangent)), near_axis)
    d_q_pre, gq_part = rope_back(d_queries, q_pre, cosine, sine, scale_q)
    out_pairs = [(d_branch, attn_out, 0, heads_width), (normed_input, d_q_pre, 0, heads_width)]
    if shard_count == 2:
        out_query = [split_product(home, out_pairs), split_product(away, out_pairs)]
    else:
        out_query = scattered(out_pairs)
    units_a[-1], units_b[-1], out_query[0], out_query[-1], *rest = settle(
        returned,
        straight,
        units_a[-1],
        units_b[-1],
        out_query[0],
        out_query[-1],
        *(given[d] for d in crossing),
    )
    if shard_count == 2:
        out_query[-1] = swap(out_query[-1], "shard")
    given.update(zip(crossing, rest))
    exchange(given, returned, crossing)
    units_sum = jnp.concatenate([total(units_a), total(units_b)], axis=1)
    units_sum, d_kv = settle(returned, crossing, units_sum, d_kv)
    returned = [returned[d] for d in range(1, count)]

    units_sum = halve([units_sum], far_axis)
    d_k_pre, d_v_pre, gk_part = key_value_back(
        meta, docs, d_kv, returned, k_pre, cosine, sine, scale_k
    )
    d_k_pre, d_v_pre, out_query[-1] = tie(d_k_pre, d_v_pre, out_query[-1])
    out_query = halve(out_query, near_axis)
    kv_pairs = [(normed_input, d_k_pre, 0, kv_width), (normed_input, d_v_pre, 0, kv_width)]
    if shard_count == 2:
        sent_kv = swap(split_product(away, kv_pairs), "shard")
        key_value_grad = [split_product(home, kv_pairs), sent_kv]
    else:
        key_value_grad = scattered(kv_pairs)
    units_sum = total(units_sum)
    cut = units_sum.shape[1] // 2
    units_a, units_b = units_sum[:, :cut], units_sum[:, cut:]
    units_a, units_b, out_query[-1], key_value_grad[-1], d_q_pre, d_k_pre, d_v_pre = tie(
        units_a, units_b, out_query[-1], key_value_grad[-1], d_q_pre, d_k_pre, d_v_pre
    )

    units_a = double(units_a, far_axis)
    key_value_grad = halve(key_value_grad, near_axis)
    d_normed = pair_total(
        dot_nt(d_q_pre, full_query) + dot_nt(d_k_pre, full_key) + dot_nt(d_v_pre, full_value)
    )
    units_a, units_b, key_value_grad[-1], out_query[-1], d_normed = tie(
        units_a, units_b, key_value_grad[-1], out_query[-1], d_normed
    )

    units_b = double(units_b, far_axis)
    owned_a = double(units_a, near_axis)
    grad_in = jnp.sum(d_normed * normal_one, axis=0)
    input_grad = d_residual + rms_back(d_normed * scale_in, normal_one, factor_one)
    once = jnp.where(lax.axis_index("tp") == 0, 1.0, 0.0)
    gain_grads = jnp.concatenate([grad_in * once, grad_post * once, gq_part[0], gk_part[0]])
    gain_grads = gain_grads.reshape(-1, HEAD)
    if shard_count != 2:
        gain_grads = lax.psum(gain_grads, "shard")
    out_query, key_value_grad = total(out_query), total(key_value_grad)
    rest_chain = [
        jnp.concatenate(
            [
                out_query[:, :heads_width],
                key_value_grad[:, :kv_width],
                out_query[:, heads_width:],
                key_value_grad[:, kv_width:],
            ],
            axis=1,
        )
    ]
    units_b, owned_a, rest_chain[0], gain_grads = tie(
        units_b, owned_a, rest_chain[0], gain_grads
    )

    owned_b = double(units_b, near_axis)
    rest_chain = total(halve(rest_chain, far_axis))
    gain_grads = gain_grads + swap(gain_grads, "tp")
    gain_grads = gain_grads + swap(gain_grads, "ctx", masks[0])
    grad_gate = owned_a[:, :units].astype(F32)
    owned_b, rest_chain, gain_grads, hidden, grad_gate = tie(
        owned_b, rest_chain, gain_grads, hidden, grad_gate
    )

    cut = rest_chain.shape[1] // 2
    rest_a, rest_b = rest_chain[:, :cut], rest_chain[:, cut:]
    rest_a = double(rest_a, far_axis)
    gain_grads = gain_grads + swap(gain_grads, "ctx", masks[1])
    mixed_part = product_nt((hidden, full_rest, 0))
    mixed = (residual + pair_total(mixed_part)).astype(BF16)
    grad_up = jnp.concatenate([owned_a[:, units:], owned_b[:, :middle]], axis=1).astype(F32)
    grad_down = owned_b[:, middle:].astype(F32).T
    rest_a, rest_b, gain_grads, mixed, grad_up, grad_down = tie(
        rest_a, rest_b, gain_grads, mixed, grad_up, grad_down
    )

    rest_b = double(rest_b, far_axis)
    rest_a = double(rest_a, near_axis)
    for mask in masks[2:]:
        gain_grads = gain_grads + swap(gain_grads, "ctx", mask)
    rest_a, rest_b, gain_grads = tie(rest_a, rest_b, gain_grads)

    rest_b = double(rest_b, near_axis)
    if shard_count == 2:
        gain_grads = gain_grads + swap(gain_grads, "shard")
    gain_grads = gain_grads.reshape(-1)
    own_gains = []
    for lo, size in ((0, model), (model, model), (2 * model, HEAD), (2 * model + HEAD, HEAD)):
        size = size // shard_count
        own_gains.append(lax.dynamic_slice_in_dim(gain_grads, lo + shard * size, size, 0))
    return (
        mixed,
        input_grad,
        rest_b[:, :heads_width].astype(F32),
        rest_a[:, heads_width:].astype(F32),
        rest_b[:, heads_width:].astype(F32),
        rest_a[:, :heads_width].astype(F32).T,
        grad_gate,
        grad_up,
        grad_down,
        *own_gains,
    )


def solution(mesh):
    placed = (
        P(("shard", "ctx"), None),
        P(("shard", "ctx"), None),
        P("shard", None),
        P(),
        P("shard", "tp"),
        P("shard", "tp"),
        P("shard", "tp"),
        P("tp", "shard"),
        P("shard", "tp"),
        P("shard", "tp"),
        P("tp", "shard"),
        P("shard"),
        P("shard"),
        P("shard"),
        P("shard"),
    )
    return jax.shard_map(
        body,
        mesh=mesh,
        in_specs=placed,
        out_specs=(
            P(("shard", "ctx"), None),
            P(("shard", "ctx"), None),
            P("shard", "tp"),
            P("shard", "tp"),
            P("shard", "tp"),
            P("tp", "shard"),
            P("shard", "tp"),
            P("shard", "tp"),
            P("tp", "shard"),
            P("shard"),
            P("shard"),
            P("shard"),
            P("shard"),
        ),
        check_vma=False,
    )
```
